32 devices in a mesh: grp: 8 (over z, core), cls: 4 (over y, x).
Axes of the slice: x: 2, y: 2, z: 4, core: 2. Of those that a mesh axis runs over, the one named last changes fastest.
Arguments:
- particles: bfloat16 [512, 16384], P(('grp', 'cls')), may hold values from -6 to 6
- candidates: int32 [512, 8], P(('grp', 'cls')), may hold values from 0 to 207, all different within a row; in each aligned block of 16 rows (0 to 15, 16 to 31, ...) at most 2 rows name the same one
- group_ids: int32 [512], P(('grp', 'cls')), may hold values from 0 to 63
- ctf_ids: int32 [512], P(('grp', 'cls')), may hold values from 0 to 255
- ctf_table: float32 [256, 64], replicated, may hold values from -1 to 1
- noise_prec: float32 [64, 64], replicated, may hold values from 0.02 to 0.2
- references: bfloat16 [208, 16384], P('cls'), may hold values from -3 to 3
- log_prior: bfloat16 [208], P('cls'), may hold values from -4 to 4
- reg: float32 [64], replicated, may hold values from 0.1 to 1
Outputs:
- averages: float32 [208, 16384], P('cls')
- class_share: float32 [208], P('cls')
- log_mass: float32 [512], P(('grp', 'cls'))
The draws below stay inside these ranges and needn't reach their ends.
Inputs may be any that keep to these rules, and one draw needn't show every extreme that they name: `candidates`: the 8 classes of a particle are distinct. Among the pairs of the rows of one device no class is named more than 2 times, a bound that some block reaches.
All inputs are finite; a program needn't handle non-finite values.
Results may differ from the reference program's by a relative error of at most 0.0046.
Values may be sent and summed in bfloat16 or wider, within the bound.
No kernel may reach another device: no remote copies, remote signals or barrier semaphores. Data moves between devices by JAX's collectives and lax.ppermute only.
A program may use at most 128 MiB of HBM per device.

```python
import math
import jax
import jax.numpy as jnp
import numpy as np
from jax import lax

SHELLS = 64
FREQ = 128
FEAT = 16384
ROTS = 64
K = 208
CAND = 8
NGROUPS = 64
NCTF = 256
DEVICE_PARTICLES = 16
MOST = 2
PARTICLES = 512
N_GRP = 8
N_CLS = 4


def draw_references(key, part):
    phase_key = jax.random.fold_in(key, 11)
    level_key = jax.random.fold_in(key, 12)
    base_key = jax.random.fold_in(key, 13)
    angle = jax.random.uniform(phase_key, (K, SHELLS, FREQ), jnp.float32, -math.pi, math.pi)
    base = jnp.exp(jax.random.uniform(base_key, (1, SHELLS, 1), jnp.float32, -0.5, 0.5))
    level = 1.0 + jax.random.uniform(level_key, (K, SHELLS, 1), jnp.float32, -0.1, 0.1)
    magnitude = base * jnp.sqrt(2.0 * level)
    real_part = magnitude * jnp.cos(angle)
    imag_part = magnitude * jnp.sin(angle)
    stacked = jnp.stack([real_part, imag_part], axis=1)
    return stacked.reshape(K, 2 * SHELLS * FREQ).astype(jnp.bfloat16)


def set_ends(array, stream_key, smallest, high):
    longest = array.shape.index(max(array.shape))
    spots = []
    for shift in (0, 1):
        where = [jax.random.randint(jax.random.fold_in(stream_key, axis), (), 0, length) for axis, length in enumerate(array.shape)]
        where[longest] = (where[longest] + shift) % array.shape[longest]
        spots.append(tuple(where))
    return array.at[spots[0]].set(smallest).at[spots[1]].set(high)


def steps_of(stream_key, dims, shards, least, high):
    def one(position, shards_of):
        draws = jax.random.uniform(jax.random.fold_in(jax.random.fold_in(stream_key, 6), position), (shards_of,), jnp.float32, least / len(shards), high / len(shards))
        return jnp.repeat(jnp.exp(draws), dims[position] // shards_of).reshape((-1,) + (1,) * (len(dims) - position - 1))

    loudness = one(*shards[0])
    for cut in shards[1:]:
        loudness = loudness * one(*cut)
    return loudness


def shared_out(own_key, own, number, rows, count, top, most, skew):
    order = jax.random.permutation(own_key, count)
    heavy_load, common = portions_of(count, rows * top, most, skew, True), portions_of(count, rows * top, most, skew, False)
    places = jnp.arange(count)

    def named(lengths, rotation):
        used = int((lengths > 0).sum())
        fixed = max(1, used // 4)
        moved = fixed + (places - fixed + rotation * (used - fixed)) % max(1, count - fixed)
        return jnp.zeros((count,), jnp.int32).at[order[jnp.where(places < fixed, places, moved)]].set(jnp.asarray(lengths, jnp.int32))

    lengths = jnp.where(number % 4 == 0, named(heavy_load, number // 4), named(common, number - number // 4 - 1))
    mixed = jax.random.permutation(jax.random.fold_in(own, 3), count)
    donor, sink = mixed[0:count // 2 * 2:2], mixed[1:count // 2 * 2:2]
    room = jnp.minimum(lengths[donor] - 1, most - lengths[sink]) // 2
    room = jnp.where((donor == order[0]) | (sink == order[0]) | (lengths[sink] == 0), 0, jnp.maximum(room, 0))
    moved = jax.random.randint(jax.random.fold_in(own, 4), (count // 2,), 0, 1 << 20) % (room + 1)
    lengths = lengths.at[donor].add(-moved).at[sink].add(moved)
    items = jnp.searchsorted(jnp.cumsum(lengths), jnp.arange(rows * top), side="right").astype(jnp.int32)
    grid = items.reshape(top, rows).T
    grid = grid[jax.random.permutation(jax.random.fold_in(own, 1), rows)]
    rotation = jax.random.randint(jax.random.fold_in(own, 2), (rows, 1), 0, top)
    return jnp.take_along_axis(grid, (jnp.arange(top)[None, :] + rotation) % top, axis=1)


def portions_of(count, total, reach, lean, full):
    portions = [(1 << 20) // math.isqrt(grade ** lean) + 1 for grade in range(1, count + 1)]
    largest = reach if full else min(reach, max(-(-total // count), total * portions[0] // sum(portions)))
    least = 1 if total - largest >= count - 1 else 0
    counts, spare = [largest] + [least] * (count - 1), total - largest - least * (count - 1)
    while spare > 0:
        movable = [i for i in range(1, count) if counts[i] < largest] or [i for i in range(1, count) if counts[i] < reach]
        mass, remaining = sum([portions[i] for i in movable]), spare
        for i in movable:
            more = min(reach - counts[i], max(1, remaining * portions[i] // mass), spare)
            counts[i] = counts[i] + more
            spare = spare - more
    return np.array(counts)


def scatter_about(rng, dims, spread, most, pieces=(), held_as=jnp.bfloat16):
    values = jax.random.normal(rng, dims, jnp.float32) * spread
    if len(pieces) > 0:
        values = steps_of(rng, dims, pieces, -0.22, 0.18) * values
    return jnp.clip(values, min=-most, max=most).astype(held_as)


def setup_inputs(seed: int = 0) -> dict:
    key_list = jax.random.split(jax.random.key(seed), 10)
    particles = scatter_about(key_list[0], (PARTICLES, FEAT), 1.0, 6.0, ((0, 32),))
    candidates_keys = jax.random.split(jax.random.fold_in(key_list[1], 1), PARTICLES // DEVICE_PARTICLES)
    candidates_turns = jax.random.permutation(jax.random.fold_in(key_list[1], 3), PARTICLES // DEVICE_PARTICLES)
    candidates = jax.vmap(lambda own, number: shared_out(jax.random.fold_in(key_list[1], 2), own, number, DEVICE_PARTICLES, K, CAND, MOST, 1))(candidates_keys, candidates_turns).reshape((PARTICLES, CAND))
    group_ids = set_ends(jax.random.randint(key_list[2], (PARTICLES,), 0, NGROUPS), jax.random.fold_in(key_list[2], 1), 0, NGROUPS - 1).astype(jnp.int32)
    ctf_ids = set_ends(jax.random.randint(key_list[3], (PARTICLES,), 0, NCTF), jax.random.fold_in(key_list[3], 1), 0, NCTF - 1).astype(jnp.int32)
    ctf_table = jnp.clip(jax.random.uniform(key_list[4], (NCTF, SHELLS), jnp.float32, -1.0, 1.0), -1.0, 1.0)
    noise_prec = jnp.clip(jnp.exp(jax.random.uniform(key_list[5], (NGROUPS, SHELLS), jnp.float32, math.log(0.02), math.log(0.2))), 0.02, 0.2)
    references = draw_references(jax.random.fold_in(key_list[9], 71), 0)
    log_prior = scatter_about(key_list[7], (K,), 1.0, 4.0, ((0, 4),))
    reg = jnp.clip(jnp.exp(jax.random.uniform(key_list[8], (SHELLS,), jnp.float32, math.log(0.1), math.log(1.0))), 0.1, 1.0)
    return dict(particles=particles, candidates=candidates, group_ids=group_ids, ctf_ids=ctf_ids, ctf_table=ctf_table, noise_prec=noise_prec, references=references, log_prior=log_prior, reg=reg)


def phase_tables():
    turns = jnp.arange(ROTS, dtype=jnp.int32)[:, None]
    orders = jnp.arange(FREQ, dtype=jnp.int32)[None, :]
    angles = ((turns * orders) % ROTS).astype(jnp.float32) * (2.0 * math.pi / ROTS)
    return jnp.cos(angles), jnp.sin(angles)


def cross_sums(rows, image):
    upper_limit = lax.Precision.HIGHEST
    count = rows.shape[0]
    particle_pieces = rows.astype(jnp.float32).reshape(count, 2, SHELLS, FREQ)
    image_components = image.astype(jnp.float32).reshape(2, SHELLS, FREQ)
    exchanged_rows = jnp.stack([image_components[1], -image_components[0]])
    inner_loop = jnp.einsum("kbqi,bqi->ki", particle_pieces, image_components, precision=upper_limit)
    outer_loop = jnp.einsum("kbqi,bqi->ki", particle_pieces, exchanged_rows, precision=upper_limit)
    return inner_loop, outer_loop


def rotation_scores(inner_loop, outer_loop, cos_tab, sin_tab):
    upper_limit = lax.Precision.HIGHEST
    return jnp.einsum("nf,jf->nj", inner_loop, cos_tab, precision=upper_limit) + jnp.einsum("nf,jf->nj", outer_loop, sin_tab, precision=upper_limit)


def reference(particles, candidates, group_ids, ctf_ids, ctf_table, noise_prec, references, log_prior, reg):
    cos_tab, sin_tab = phase_tables()
    pair_count = PARTICLES * CAND
    capacity = MOST * N_GRP * N_CLS
    precision_rows = noise_prec[group_ids]
    ctf_rows = ctf_table[ctf_ids]
    shell_weight = precision_rows * ctf_rows
    weighted = (particles.astype(jnp.float32).reshape(PARTICLES, 2, SHELLS, FREQ) * shell_weight[:, None, :, None]).reshape(PARTICLES, FEAT)
    weighted = lax.optimization_barrier(weighted.astype(jnp.bfloat16))
    shell_side = lax.optimization_barrier((precision_rows * ctf_rows * ctf_rows).astype(jnp.bfloat16))
    side_wide = shell_side.astype(jnp.float32)
    shell_power = jnp.sum(jnp.square(references.astype(jnp.float32)).reshape(K, 2, SHELLS, FREQ), axis=(1, 3))
    prior = log_prior.astype(jnp.float32)
    flat_class = candidates.reshape(pair_count).astype(jnp.int32)

    def members(class_index):
        found = jnp.nonzero(flat_class == class_index, size=capacity, fill_value=pair_count)[0].astype(jnp.int32)
        valid = found < pair_count
        clamped_values = jnp.minimum(found, pair_count - 1).astype(jnp.int32)
        return found, valid, clamped_values, clamped_values // CAND

    def score_class(carry, class_index):
        found, valid, clamped_values, row_index = members(class_index)
        picked = weighted[row_index]
        single = lax.dynamic_index_in_dim(references, class_index, 0, keepdims=False)
        inner_loop, outer_loop = cross_sums(picked, single)
        correlation = rotation_scores(inner_loop, outer_loop, cos_tab, sin_tab)
        penalty = jnp.sum(side_wide[row_index] * shell_power[class_index][None, :], axis=1)
        values = correlation - 0.5 * penalty[:, None] + prior[class_index]
        return carry.at[found].set(values, mode="drop"), None

    scores, unused = lax.scan(score_class, jnp.zeros((pair_count, ROTS), jnp.float32), jnp.arange(K, dtype=jnp.int32))
    scores = scores.reshape(PARTICLES, CAND * ROTS)
    best = jnp.max(scores, axis=1, keepdims=True)
    exponent = jnp.exp(scores - best)
    total_mass = jnp.sum(exponent, axis=1, keepdims=True)
    weights = lax.optimization_barrier((exponent / total_mass).astype(jnp.bfloat16))
    log_mass = jnp.log(total_mass[:, 0])
    pair_weights = weights.reshape(pair_count, ROTS).astype(jnp.float32)
    pair_sums = jnp.sum(pair_weights, axis=1)

    def gather_class(class_index):
        found, valid, clamped_values, row_index = members(class_index)
        chosen = jnp.where(valid[:, None], pair_weights[clamped_values], 0.0)
        wcos = lax.optimization_barrier(jnp.dot(chosen, cos_tab, precision=lax.Precision.HIGHEST).astype(jnp.bfloat16)).astype(jnp.float32)
        wsin = lax.optimization_barrier(jnp.dot(chosen, sin_tab, precision=lax.Precision.HIGHEST).astype(jnp.bfloat16)).astype(jnp.float32)
        particle_pieces = weighted[row_index].astype(jnp.float32).reshape(capacity, 2, SHELLS, FREQ)
        real_part = particle_pieces[:, 0]
        imag_part = particle_pieces[:, 1]
        upper_limit = lax.Precision.HIGHEST
        num_real = jnp.einsum("srf,sf->rf", real_part, wcos, precision=upper_limit) - jnp.einsum("srf,sf->rf", imag_part, wsin, precision=upper_limit)
        num_imag = jnp.einsum("srf,sf->rf", real_part, wsin, precision=upper_limit) + jnp.einsum("srf,sf->rf", imag_part, wcos, precision=upper_limit)
        numerator = jnp.stack([num_real, num_imag]).reshape(FEAT)
        sums = jnp.where(valid, pair_sums[clamped_values], 0.0)
        denominator = jnp.sum(sums[:, None] * side_wide[row_index], axis=0)
        return numerator, denominator, jnp.sum(sums)

    numerator, denominator, class_mass = lax.map(gather_class, jnp.arange(K, dtype=jnp.int32))
    divisor = denominator[:, None, :, None] + reg[None, None, :, None]
    averages = (numerator.reshape(K, 2, SHELLS, FREQ) / divisor).reshape(K, FEAT)
    class_share = class_mass * (K / PARTICLES)
    return averages, class_share, log_mass
```

```python
import functools
import math

import jax
import jax.numpy as jnp
import numpy as np
from jax import lax
from jax.experimental import pallas as pl
from jax.experimental.pallas import tpu as pltpu
from jax.sharding import PartitionSpec as P

SHELLS = 64
FREQ = 128
FEAT = 16384
ROTS = 64
K = 208
CAND = 8
IMG = 2 * SHELLS
UNROLL = 4
LOW = -1e30
HIGH = lax.Precision.HIGHEST
VMEM = pltpu.VMEM
SMEM = pltpu.SMEM


def tables():
    turns = np.arange(ROTS)[:, None]
    orders = np.arange(FREQ)[None, :]
    angles = ((turns * orders) % ROTS).astype(np.float32) * np.float32(2.0 * math.pi / ROTS)
    cos_tab = np.cos(angles).astype(np.float32)
    sin_tab = np.sin(angles).astype(np.float32)
    last = np.zeros((FREQ, ROTS), np.float32)
    last[:SHELLS] = -0.5
    last[SHELLS] = 1.0
    scoring = np.concatenate([cos_tab.T, sin_tab.T, last], axis=0)
    phases = np.concatenate([cos_tab, sin_tab], axis=1)
    return scoring, phases


def lanes_of(shape):
    return lax.broadcasted_iota(jnp.int32, shape, len(shape) - 1)


def prep_kernel(
    ids_s, ids_v, ctf, prec, refs, prior, first_s, rf_out, sw_out, side_out, pow_out, cls_out,
    rows_out, locs_out, counts_out, spread,
):
    count = ids_v.shape[0]
    cls_dev = refs.shape[0]
    pad = spread.shape[0] // IMG
    rows = count * CAND
    blocks = counts_out.shape[0]
    per = count // blocks
    first = first_s[0]
    slots = rows_out.shape[0] // blocks

    def block_list(b, _):
        def one(i, n):
            for t in range(CAND):
                local = ids_s[b * per + i, t] - first
                good = jnp.logical_and(local >= 0, local < cls_dev)
                rows_out[b * slots + n] = (b * per + i) * CAND + t
                locs_out[b * slots + n] = local
                n = n + good.astype(jnp.int32)
            return n

        n = lax.fori_loop(0, per, one, jnp.int32(0))
        for extra in range(UNROLL):
            rows_out[b * slots + n + extra] = rows
            locs_out[b * slots + n + extra] = 0
        counts_out[b] = (n + UNROLL - 1) // UNROLL
        return 0

    lax.fori_loop(0, blocks, block_list, 0)

    ids = ids_v[...]
    groups = (ids[:, CAND : CAND + 1] == lanes_of((count, prec.shape[0]))).astype(jnp.float32)
    entries = (ids[:, CAND + 1 : CAND + 2] == lanes_of((count, ctf.shape[0]))).astype(jnp.float32)
    prec_rows = jnp.dot(groups, prec[...], precision=HIGH, preferred_element_type=jnp.float32)
    ctf_rows = jnp.dot(entries, ctf[...], precision=HIGH, preferred_element_type=jnp.float32)
    weight = prec_rows * ctf_rows
    sw_out[...] = weight
    side = (weight * ctf_rows).astype(jnp.bfloat16).astype(jnp.float32)
    side_out[:, :SHELLS] = side
    side_out[:, SHELLS:] = (lanes_of((count, SHELLS)) == 0).astype(jnp.float32)

    cand = ids[:, :CAND].astype(jnp.float32)
    wide = jnp.broadcast_to(cand[:, None, :], (count, CAND, CAND)).reshape(rows, CAND)
    own = lax.broadcasted_iota(jnp.int32, (rows, CAND), 0) % CAND == lanes_of((rows, CAND))
    column = jnp.sum(jnp.where(own, wide, 0.0), axis=1, keepdims=True) - first.astype(jnp.float32)
    cls_out[...] = jnp.broadcast_to(column, (rows, FREQ))

    def shell(r, power):
        parts = []
        for x in range(2):
            piece = refs[:, pl.ds(pl.multiple_of((x * SHELLS + r) * FREQ, FREQ), FREQ)].astype(
                jnp.float32
            )
            spread[pl.ds(pl.multiple_of((x * SHELLS + r) * pad, 8), cls_dev), :] = piece
            parts.append(piece * piece)
        total = jnp.sum(parts[0] + parts[1], axis=1, keepdims=True)
        return jnp.where(lanes_of((cls_dev, FREQ)) == r, total, power)

    power = lax.fori_loop(0, SHELLS, shell, jnp.zeros((cls_dev, FREQ), jnp.float32))
    pow_out[...] = jnp.where(
        lanes_of((cls_dev, FREQ)) == SHELLS, prior[...].astype(jnp.float32), power
    )

    def image(k, _):
        rf_out[k] = spread[pl.ds(k, IMG, stride=pad), :]
        return 0

    lax.fori_loop(0, cls_dev, image, 0)


def score_kernel(
    blocks, rows_s, locs_s, counts_s, *refs,
):
    pieces = refs[:blocks]
    sw, side, power, rf, cls_f, scoring, w_out, scores_out, stats_out, spread, w32, ex = refs[blocks:]
    per = pieces[0].shape[0]
    count = per * blocks
    rows = count * CAND
    cls_dev = rf.shape[0]
    slots = rows_s.shape[0] // blocks

    for b in range(blocks):
        weight = sw[b * per : (b + 1) * per, :]
        for r in range(SHELLS):
            factor = weight[:, r : r + 1]
            for x in range(2):
                at = x * SHELLS + r
                piece = pieces[b][:, at * FREQ : (at + 1) * FREQ].astype(jnp.float32) * factor
                spread[at * per : (at + 1) * per, :] = piece.astype(jnp.bfloat16).astype(jnp.float32)

        def image(i, _):
            whole = spread[pl.ds(i, IMG, stride=per), :]
            w32[b * per + i] = whole
            w_out[b * per + i] = whole.astype(jnp.bfloat16)
            return 0

        lax.fori_loop(0, per, image, 0)

        def pairs(step, _):
            for u in range(UNROLL):
                row = rows_s[b * slots + step * UNROLL + u]
                k = locs_s[b * slots + step * UNROLL + u]
                i = jnp.minimum(row // CAND, count - 1)
                w_re, w_im = w32[i, :SHELLS], w32[i, SHELLS:]
                a_re, a_im = rf[k, :SHELLS], rf[k, SHELLS:]
                inner = jnp.sum(w_re * a_re + w_im * a_im, axis=0, keepdims=True)
                outer = jnp.sum(w_re * a_im - w_im * a_re, axis=0, keepdims=True)
                ex[0, pl.ds(row, 1), :] = inner
                ex[1, pl.ds(row, 1), :] = outer
                ex[2, pl.ds(row, 1), :] = side[pl.ds(i, 1), :] * power[pl.ds(k, 1), :]
            return 0

        lax.fori_loop(0, counts_s[b], pairs, 0)

    local = cls_f[:, :ROTS]
    good = jnp.logical_and(local >= 0, local < cls_dev)
    table = scoring[...]
    values = jnp.zeros((rows, ROTS), jnp.float32)
    for part in range(3):
        values = values + jnp.dot(
            jnp.where(good[:, :1], ex[part, :rows, :], 0.0),
            table[part * FREQ : (part + 1) * FREQ],
            precision=HIGH,
            preferred_element_type=jnp.float32,
        )
    scores = jnp.where(good, values, LOW)
    scores_out[...] = scores
    top = jnp.broadcast_to(jnp.max(scores, axis=1, keepdims=True), (rows, ROTS))
    best = jnp.max(top.reshape(count, CAND, ROTS), axis=1)
    best_rows = jnp.broadcast_to(best[:, None, :], (count, CAND, ROTS)).reshape(rows, ROTS)
    mass = jnp.where(good, jnp.exp(scores - best_rows), 0.0)
    mass = jnp.broadcast_to(jnp.sum(mass, axis=1, keepdims=True), (rows, ROTS))
    total = jnp.sum(mass.reshape(count, CAND, ROTS), axis=1)
    stats_out[:, :ROTS] = best
    stats_out[:, ROTS:] = total


def sum_kernel(
    blocks, slices, rows_s, locs_s, counts_s, *refs,
):
    stats = refs[:blocks]
    scores, w_in, side, cls_f, phases, msg_out, mass_out, wcs, num = refs[blocks:]
    count = w_in.shape[0]
    per = count // blocks
    rows = count * CAND
    cls_dev = num.shape[0]
    slots = rows_s.shape[0] // blocks
    width = SHELLS // slices

    best = stats[0][:, :ROTS]
    for one in stats[1:]:
        best = jnp.maximum(best, one[:, :ROTS])
    total = jnp.zeros((count, ROTS), jnp.float32)
    for one in stats:
        total = total + one[:, ROTS:] * jnp.exp(one[:, :ROTS] - best)
    mass_out[...] = jnp.log(total[:per, :])

    def over_rows(v):
        return jnp.broadcast_to(v[:, None, :], (count, CAND, ROTS)).reshape(rows, ROTS)

    local = cls_f[...]
    good = jnp.logical_and(local >= 0, local < cls_dev)
    weights = jnp.exp(scores[...] - over_rows(best)) / over_rows(total)
    weights = jnp.where(good[:, :ROTS], weights, 0.0).astype(jnp.bfloat16).astype(jnp.float32)
    both = jnp.dot(weights, phases[...], precision=HIGH, preferred_element_type=jnp.float32)
    both = both.astype(jnp.bfloat16).astype(jnp.float32)
    for part in range(2):
        wcs[part, :rows, :] = both[:, part * FREQ : (part + 1) * FREQ]
        wcs[part, rows:, :] = jnp.zeros((8, FREQ), jnp.float32)

    pair_sum = jnp.sum(weights, axis=1, keepdims=True)
    twice = (lanes_of((rows, FREQ)) % ROTS).astype(jnp.float32)
    chosen = jnp.where(twice == local, pair_sum, 0.0)
    by_particle = jnp.sum(chosen.reshape(count, CAND, FREQ), axis=1)
    den = lax.dot_general(
        side[...], by_particle, (((0,), (0,)), ((), ())), precision=HIGH,
        preferred_element_type=jnp.float32,
    )

    num[...] = jnp.zeros_like(num)

    for b in range(blocks):
        def pairs(step, _):
            for u in range(UNROLL):
                row = rows_s[b * slots + step * UNROLL + u]
                k = locs_s[b * slots + step * UNROLL + u]
                i = jnp.minimum(row // CAND, count - 1)
                c = wcs[0, pl.ds(row, 1), :]
                s = wcs[1, pl.ds(row, 1), :]
                w_re = w_in[i, :SHELLS].astype(jnp.float32)
                w_im = w_in[i, SHELLS:].astype(jnp.float32)
                num[k, :SHELLS] += w_re * c - w_im * s
                num[k, SHELLS:] += w_re * s + w_im * c
            return 0

        lax.fori_loop(0, counts_s[b], pairs, 0)

    def pack(k, _):
        for s in range(slices):
            msg_out[s, k, :width] = num[k, s * width : (s + 1) * width].astype(jnp.bfloat16)
            msg_out[s, k, width:] = num[
                k, SHELLS + s * width : SHELLS + (s + 1) * width
            ].astype(jnp.bfloat16)
        return 0

    lax.fori_loop(0, cls_dev, pack, 0)
    left = lanes_of((SHELLS, FREQ)) < ROTS
    high = den[:SHELLS].astype(jnp.bfloat16)
    low = (den[:SHELLS] - high.astype(jnp.float32)).astype(jnp.bfloat16)
    halves = jnp.where(left, high.astype(jnp.float32), low.astype(jnp.float32))
    mass = jnp.broadcast_to(jnp.sum(by_particle, axis=0, keepdims=True), (width, FREQ))
    mass_high = mass.astype(jnp.bfloat16).astype(jnp.float32)
    mass_low = (mass - mass_high).astype(jnp.bfloat16).astype(jnp.float32)
    mass_halves = jnp.where(left[:width], mass_high, mass_low)
    for s in range(slices):
        msg_out[s, cls_dev, :width] = halves[s * width : (s + 1) * width].astype(jnp.bfloat16)
        msg_out[s, cls_dev, width:] = mass_halves.astype(jnp.bfloat16)


def divide_kernel(scale, got, reg, avg_out, share_out):
    sources = got.shape[0]
    cls_dev = avg_out.shape[0]
    width = avg_out.shape[1] // 2
    tile = got[0, cls_dev].astype(jnp.float32)
    for s in range(1, sources):
        tile = tile + got[s, cls_dev].astype(jnp.float32)
    tile = tile + pltpu.roll(tile, ROTS, 1)
    divisor = tile[:width] + reg[...]
    share_out[...] = tile[width : width + 1] * scale
    inverse = 1.0 / divisor
    for k in range(cls_dev):
        total = got[0, k].astype(jnp.float32)
        for s in range(1, sources):
            total = total + got[s, k].astype(jnp.float32)
        factor = jnp.concatenate([inverse[:, k : k + 1]] * 2, axis=0)
        avg_out[k] = (total * factor).astype(jnp.bfloat16)


def spread_kernel(got, out, wide):
    slices, cls_dev, height, _ = got.shape
    width = height // 2
    pad = wide.shape[0] // IMG

    def one(k, _):
        for s in range(slices):
            piece = got[s, k].astype(jnp.float32)
            for x in range(2):
                at = x * SHELLS + s * width
                wide[pl.ds(k + at * pad, width, stride=pad), :] = piece[x * width : (x + 1) * width]
        return 0

    lax.fori_loop(0, cls_dev, one, 0)
    for at in range(IMG):
        out[:, at * FREQ : (at + 1) * FREQ] = wide[at * pad : at * pad + cls_dev, :]


def whole(space):
    return pl.BlockSpec(memory_space=space)


def params(mib):
    return pltpu.CompilerParams(vmem_limit_bytes=mib * 2**20)


def swap(value, axis, distance):
    size = lax.axis_size(axis)
    return lax.ppermute(value, axis, [(i, i ^ distance) for i in range(size)])


def per_device(
    particles, candidates, group_ids, ctf_ids, ctf_table, noise_prec, references, log_prior, reg
):
    n_cls = lax.axis_size("cls")
    n_grp = lax.axis_size("grp")
    per = particles.shape[0]
    cls_dev = references.shape[0]
    count = per * n_cls
    rows = count * CAND
    slots = per * CAND + 2 * UNROLL
    pad = -(-cls_dev // 8) * 8
    width = SHELLS // n_grp
    scoring, phases = (jnp.asarray(t) for t in tables())
    f32 = jnp.float32
    bf16 = jnp.bfloat16
    shape = jax.ShapeDtypeStruct

    ids = jnp.concatenate(
        [
            candidates,
            group_ids[:, None],
            ctf_ids[:, None],
            jnp.zeros((per, CAND - 2), jnp.int32),
        ],
        axis=1,
    )
    pieces = [particles] + [swap(particles, "cls", d) for d in range(1, n_cls)]
    all_ids = jnp.concatenate([ids] + [swap(ids, "cls", d) for d in range(1, n_cls)], axis=0)
    first = (lax.axis_index("cls") * cls_dev).astype(jnp.int32).reshape(1)

    rf, sw, side, power, cls_f, row_list, loc_list, counts = pl.pallas_call(
        prep_kernel,
        out_shape=(
            shape((cls_dev, IMG, FREQ), f32),
            shape((count, SHELLS), f32),
            shape((count, FREQ), f32),
            shape((cls_dev, FREQ), f32),
            shape((rows, FREQ), f32),
            shape((n_cls * slots,), jnp.int32),
            shape((n_cls * slots,), jnp.int32),
            shape((n_cls,), jnp.int32),
        ),
        in_specs=[whole(SMEM)] + [whole(VMEM)] * 5 + [whole(SMEM)],
        out_specs=tuple([whole(VMEM)] * 5 + [whole(SMEM)] * 3),
        scratch_shapes=[VMEM((IMG * pad, FREQ), f32)],
        compiler_params=params(40),
        name="prep",
    )(all_ids, all_ids, ctf_table, noise_prec, references, log_prior[:, None], first)

    weighted, scores, stats = pl.pallas_call(
        functools.partial(score_kernel, n_cls),
        out_shape=(
            shape((count, IMG, FREQ), bf16),
            shape((rows, ROTS), f32),
            shape((count, FREQ), f32),
        ),
        in_specs=[whole(SMEM)] * 3 + [whole(VMEM)] * (n_cls + 6),
        out_specs=tuple([whole(VMEM)] * 3),
        scratch_shapes=[
            VMEM((IMG * per, FREQ), f32),
            VMEM((count, IMG, FREQ), f32),
            VMEM((3, rows + 8, FREQ), f32),
        ],
        compiler_params=params(56),
        name="score",
    )(row_list, loc_list, counts, *pieces, sw, side, power, rf, cls_f, scoring)

    all_stats = [stats]
    for d in range(1, n_cls):
        got = swap(stats, "cls", d).reshape(n_cls, per, FREQ)
        order = [e ^ d for e in range(n_cls)]
        all_stats.append(jnp.concatenate([got[e] for e in order], axis=0))

    message, mass = pl.pallas_call(
        functools.partial(sum_kernel, n_cls, n_grp),
        out_shape=(
            shape((n_grp, cls_dev + 1, 2 * width, FREQ), bf16),
            shape((per, ROTS), f32),
        ),
        in_specs=[whole(SMEM)] * 3 + [whole(VMEM)] * (n_cls + 5),
        out_specs=tuple([whole(VMEM)] * 2),
        scratch_shapes=[
            VMEM((2, rows + 8, FREQ), f32),
            VMEM((cls_dev, IMG, FREQ), f32),
        ],
        compiler_params=params(56),
        name="sum",
    )(row_list, loc_list, counts, *all_stats, scores, weighted, side, cls_f, phases)

    received = lax.all_to_all(message, "grp", split_axis=0, concat_axis=0, tiled=True)
    own_reg = lax.dynamic_slice(reg, (lax.axis_index("grp") * width,), (width,))
    particle_total = per * n_grp * n_cls
    averaged, share = pl.pallas_call(
        functools.partial(divide_kernel, K / particle_total),
        out_shape=(
            shape((cls_dev, 2 * width, FREQ), bf16),
            shape((1, FREQ), f32),
        ),
        in_specs=[whole(VMEM)] * 2,
        out_specs=tuple([whole(VMEM)] * 2),
        compiler_params=params(40),
        name="divide",
    )(received, jnp.broadcast_to(own_reg[:, None], (width, FREQ)))
    gathered = lax.all_gather(averaged, "grp")
    averages = pl.pallas_call(
        spread_kernel,
        out_shape=shape((cls_dev, FEAT), f32),
        in_specs=[whole(VMEM)],
        out_specs=whole(VMEM),
        scratch_shapes=[VMEM((IMG * pad, FREQ), f32)],
        compiler_params=params(40),
        name="spread",
    )(gathered)
    return (averages, share[0, :cls_dev], mass[:, 0])


def solution(mesh):
    return jax.shard_map(
        per_device,
        mesh=mesh,
        in_specs=(
            P(("grp", "cls"), None),
            P(("grp", "cls"), None),
            P(("grp", "cls")),
            P(("grp", "cls")),
            P(),
            P(),
            P("cls", None),
            P("cls"),
            P(),
        ),
        out_specs=(P("cls", None), P("cls"), P(("grp", "cls"))),
        check_vma=False,
    )
```

```python
import functools
import math

import jax
import jax.numpy as jnp
import numpy as np
from jax import lax
from jax.experimental import pallas as pl
from jax.experimental.pallas import tpu as pltpu
from jax.sharding import PartitionSpec as P

SHELLS = 64
FREQ = 128
FEAT = 16384
ROTS = 64
K = 208
CAND = 8
IMG = 2 * SHELLS
UNROLL = 4
LOW = -1e30
HIGH = lax.Precision.HIGHEST
VMEM = pltpu.VMEM
SMEM = pltpu.SMEM
HBM = pltpu.HBM
F32 = jnp.float32
BF16 = jnp.bfloat16
SHAPE = jax.ShapeDtypeStruct


def tables():
    turns = np.arange(ROTS)[:, None]
    orders = np.arange(FREQ)[None, :]
    angles = ((turns * orders) % ROTS).astype(np.float32) * np.float32(2.0 * math.pi / ROTS)
    cos_tab = np.cos(angles).astype(np.float32)
    sin_tab = np.sin(angles).astype(np.float32)
    last = np.zeros((FREQ, ROTS), np.float32)
    last[:SHELLS] = -0.5
    last[SHELLS] = 1.0
    scoring = np.concatenate([cos_tab.T, sin_tab.T, last], axis=0)
    phases = np.concatenate([cos_tab, sin_tab], axis=1)
    return scoring, phases


def lanes_of(shape):
    return lax.broadcasted_iota(jnp.int32, shape, len(shape) - 1)


def rounded(v):
    return v.astype(BF16).astype(F32)


def chunks_of(cls_dev):
    cut = cls_dev // 2 // 8 * 8
    return ((cut, cls_dev - cut), (0, cut)) if cut else ((0, cls_dev),)


def weigh_kernel(
    particles_h, cand_h, groups_h, entries_h, ctf_h, prec_h, low_out, high_out,
    particles, cand, groups, entries, ctf, prec, hot_g, hot_e, spread, sem,
):
    copies = [
        pltpu.make_async_copy(a, b, sem.at[n])
        for n, (a, b) in enumerate(
            (
                (groups_h, groups), (entries_h, entries), (ctf_h, ctf), (prec_h, prec),
                (cand_h, cand), (particles_h, particles),
            )
        )
    ]
    for copy in copies:
        copy.start()
    per = particles.shape[0]
    half = per // 2
    for copy in copies[:2]:
        copy.wait()
    for i in range(per):
        hot_g[i : i + 1, :] = (lanes_of((1, hot_g.shape[1])) == groups[i]).astype(F32)
        hot_e[i : i + 1, :] = (lanes_of((1, hot_e.shape[1])) == entries[i]).astype(F32)
    for copy in copies[2:5]:
        copy.wait()
    p = jnp.dot(hot_g[...], prec[...], precision=HIGH, preferred_element_type=F32)
    c = lax.dot_general(
        hot_e[...], ctf[...], (((1,), (1,)), ((), ())), precision=HIGH, preferred_element_type=F32
    )
    eye = (lanes_of((per, per)) == lax.broadcasted_iota(jnp.int32, (per, per), 0)).astype(F32)
    named = lax.dot_general(
        eye, cand[...].astype(F32), (((1,), (1,)), ((), ())), precision=HIGH,
        preferred_element_type=F32,
    )
    factors = p * c
    extra = jnp.concatenate(
        [factors * c, named, jnp.zeros((per, FREQ - SHELLS - CAND), F32)], axis=1
    )
    low_out[half * IMG :, :] = extra.astype(BF16)
    copies[5].wait()
    for r in range(SHELLS):
        factor = jnp.broadcast_to(factors[:, r : r + 1], (per, FREQ))
        for x in range(2):
            at = x * SHELLS + r
            piece = particles[:, at * FREQ : (at + 1) * FREQ].astype(F32) * factor
            spread[at * per : (at + 1) * per, :] = rounded(piece)
    for i in range(per):
        out, at = (low_out, i) if i < half else (high_out, i - half)
        out[at * IMG : (at + 1) * IMG, :] = spread[i : i + IMG * per : per, :].astype(BF16)


def prep_kernel(
    refs_h, scoring_h, phases_h, prior, rf_out, pow_out, scoring_out, phases_out, refs, spread, sem
):
    cls_dev = refs.shape[0]
    pad = spread.shape[0] // IMG
    parts = sem.shape[0] - 2
    step = FEAT // parts
    tables_in = [
        pltpu.make_async_copy(scoring_h, scoring_out, sem.at[parts]),
        pltpu.make_async_copy(phases_h, phases_out, sem.at[parts + 1]),
    ]
    copies = [
        pltpu.make_async_copy(
            refs_h.at[:, pl.ds(n * step, step)], refs.at[:, pl.ds(n * step, step)], sem.at[n]
        )
        for n in range(parts)
    ]
    for copy in copies + tables_in:
        copy.start()
    for copy in copies:
        copy.wait()

    def shell(r, power):
        parts = []
        for x in range(2):
            at = x * SHELLS + r
            piece = refs[:, pl.ds(pl.multiple_of(at * FREQ, FREQ), FREQ)].astype(F32)
            spread[pl.ds(pl.multiple_of(at * pad, 8), cls_dev), :] = piece
            parts.append(piece * piece)
        total = jnp.sum(parts[0] + parts[1], axis=1, keepdims=True)
        return jnp.where(lanes_of((cls_dev, FREQ)) == r, total, power)

    power = lax.fori_loop(0, SHELLS, shell, jnp.zeros((cls_dev, FREQ), F32), unroll=4)
    pow_out[...] = jnp.where(lanes_of((cls_dev, FREQ)) == SHELLS, prior[...], power)

    def image(k, _):
        rf_out[k] = spread[pl.ds(k, IMG, stride=pad), :]
        return 0

    lax.fori_loop(0, cls_dev, image, 0, unroll=4)
    for copy in tables_in:
        copy.wait()


def score_kernel(blocks, chunks, first_s, *refs):
    messages = refs[: 2 * blocks]
    rf, power, scoring = refs[2 * blocks : 2 * blocks + 3]
    scores_out, stats_out, cls_out, rows_out, locs_out, counts_out = refs[2 * blocks + 3 : -6]
    cand_v, cand_s, side, ex, w32, sem = refs[-6:]
    half = messages[1].shape[0] // IMG
    per = 2 * half
    cls_dev = rf.shape[0]
    block_rows = per * CAND
    slots = rows_out.shape[0] // (blocks * len(chunks))
    first = first_s[0]
    table = scoring[...]

    for b in range(blocks):
        extra = messages[2 * b][half * IMG :, :].astype(F32)
        cand_v[b] = extra.astype(jnp.int32)
        lane = lanes_of((per, FREQ))
        side[b] = jnp.where(lane < SHELLS, extra, (lane == SHELLS).astype(F32))
    copies = [pltpu.make_async_copy(cand_v.at[b], cand_s.at[b], sem.at[b]) for b in range(blocks)]
    for copy in copies:
        copy.start()
    for b in range(blocks):

        def widen(i, _):
            at = pl.multiple_of(i * IMG, IMG)
            w32[b * per + i] = messages[2 * b][pl.ds(at, IMG), :].astype(F32)
            w32[b * per + half + i] = messages[2 * b + 1][pl.ds(at, IMG), :].astype(F32)
            return 0

        lax.fori_loop(0, half, widen, 0)
    for copy in copies:
        copy.wait()

    for b in range(blocks):
        base = b * len(chunks) * slots

        def one(i, n):
            for t in range(CAND):
                local = cand_s[b, i, SHELLS + t] - first
                good = jnp.logical_and(local >= 0, local < cls_dev)
                if len(chunks) == 1:
                    place, n = n[0], (n[0] + good.astype(jnp.int32),)
                else:
                    late = local < chunks[0][0]
                    place = jnp.where(late, slots + n[1], n[0])
                    n = (
                        n[0] + jnp.logical_and(good, jnp.logical_not(late)).astype(jnp.int32),
                        n[1] + jnp.logical_and(good, late).astype(jnp.int32),
                    )
                rows_out[base + place] = i * CAND + t
                locs_out[base + place] = local
            return n

        n = lax.fori_loop(0, per, one, (jnp.int32(0),) * len(chunks))
        for c, (start, _) in enumerate(chunks):
            for spare in range(UNROLL):
                rows_out[base + c * slots + n[c] + spare] = block_rows
                locs_out[base + c * slots + n[c] + spare] = start
            steps = (n[c] + UNROLL - 1) // UNROLL
            counts_out[b * len(chunks) + c] = steps

            def pairs(step, _):
                for u in range(UNROLL):
                    row = rows_out[base + c * slots + step * UNROLL + u]
                    k = locs_out[base + c * slots + step * UNROLL + u]
                    i = jnp.minimum(row // CAND, per - 1)
                    w_re, w_im = w32[b * per + i, :SHELLS], w32[b * per + i, SHELLS:]
                    a_re, a_im = rf[k, :SHELLS], rf[k, SHELLS:]
                    inner = jnp.sum(w_re * a_re + w_im * a_im, axis=0, keepdims=True)
                    outer = jnp.sum(w_re * a_im - w_im * a_re, axis=0, keepdims=True)
                    ex[0, pl.ds(row, 1), :] = inner
                    ex[1, pl.ds(row, 1), :] = outer
                    ex[2, pl.ds(row, 1), :] = side[b, pl.ds(i, 1), :] * power[pl.ds(k, 1), :]
                return 0

            lax.fori_loop(0, steps, pairs, 0)

        wide = jnp.broadcast_to(
            messages[2 * b][half * IMG :, :].astype(F32)[:, None, :], (per, CAND, FREQ)
        ).reshape(block_rows, FREQ)
        own = lanes_of((block_rows, FREQ)) == SHELLS + (
            lax.broadcasted_iota(jnp.int32, (block_rows, FREQ), 0) % CAND
        )
        column = jnp.sum(jnp.where(own, wide, 0.0), axis=1, keepdims=True) - first.astype(F32)
        cls_out[b * block_rows : (b + 1) * block_rows, :] = jnp.broadcast_to(
            column, (block_rows, FREQ)
        )
        good = jnp.logical_and(column >= 0, column < cls_dev)
        values = jnp.zeros((block_rows, ROTS), F32)
        for part in range(3):
            values = values + jnp.dot(
                jnp.where(good, ex[part, :block_rows, :], 0.0),
                table[part * FREQ : (part + 1) * FREQ],
                precision=HIGH,
                preferred_element_type=F32,
            )
        scores = jnp.where(good, values, LOW)
        scores_out[b * block_rows : (b + 1) * block_rows, :] = scores
        top = jnp.broadcast_to(jnp.max(scores, axis=1, keepdims=True), (block_rows, ROTS))
        best = jnp.max(top.reshape(per, CAND, ROTS), axis=1)
        best_rows = jnp.broadcast_to(best[:, None, :], (per, CAND, ROTS)).reshape(block_rows, ROTS)
        mass = jnp.where(good, jnp.exp(scores - best_rows), 0.0)
        mass = jnp.broadcast_to(jnp.sum(mass, axis=1, keepdims=True), (block_rows, ROTS))
        total = jnp.sum(mass.reshape(per, CAND, ROTS), axis=1)
        stats_out[b * per : (b + 1) * per, :ROTS] = best
        stats_out[b * per : (b + 1) * per, ROTS:] = total


def add_pairs(calls, chunk, chunks, messages, wcs, num):
    half = messages[1].shape[0] // IMG
    per = 2 * half
    block_rows = per * CAND
    start = chunks[chunk][0]
    groups, width = num.shape[2], num.shape[3]
    num[...] = jnp.zeros_like(num)
    block = 0
    for rows_s, locs_s, counts_s in calls:
        blocks = counts_s.shape[0] // len(chunks)
        slots = rows_s.shape[0] // (blocks * len(chunks))
        for b in range(blocks):
            low, high = messages[2 * block], messages[2 * block + 1]
            base = (b * len(chunks) + chunk) * slots
            row_base = block * (block_rows + 8)

            def pairs(step, _):
                for u in range(UNROLL):
                    row = rows_s[base + step * UNROLL + u]
                    k = locs_s[base + step * UNROLL + u] - start
                    i = jnp.minimum(row // CAND, per - 1)
                    at = pl.multiple_of((i % half) * IMG, IMG)
                    w = jnp.where(i < half, low[pl.ds(at, IMG), :], high[pl.ds(at, IMG), :])
                    w = w.astype(F32)
                    w_re = w[:SHELLS].reshape(groups, width, FREQ)
                    w_im = w[SHELLS:].reshape(groups, width, FREQ)
                    c = wcs[0, pl.ds(row_base + row, 1), :].reshape(1, 1, FREQ)
                    s = wcs[1, pl.ds(row_base + row, 1), :].reshape(1, 1, FREQ)
                    num[k, 0] += w_re * c - w_im * s
                    num[k, 1] += w_re * s + w_im * c
                return 0

            lax.fori_loop(0, counts_s[b * len(chunks) + chunk], pairs, 0)
            block += 1


def pack_sums(grp, num, own_out, sib_out):
    slices = own_out.shape[0]
    z, h = grp // 2, grp % 2

    def one(k, _):
        for d in range(slices):
            for out, core in ((own_out, h), (sib_out, 1 - h)):
                at = (z ^ d) * 2 + core
                out[d, k] = jnp.concatenate([num[k, 0, at], num[k, 1, at]], axis=0).astype(BF16)
        return 0

    lax.fori_loop(0, num.shape[0], one, 0)


def first_sum_kernel(calls, blocks, chunks, grp_s, *refs):
    lists = [refs[3 * c : 3 * c + 3] for c in range(calls)]
    refs = refs[3 * calls :]
    stats = refs[:blocks]
    scores = refs[blocks : blocks + calls]
    classes = refs[blocks + calls : blocks + 2 * calls]
    messages = refs[blocks + 2 * calls : 3 * blocks + 2 * calls]
    phases, own_out, sib_out, mass_out, wcs, num, halves = refs[3 * blocks + 2 * calls :]
    half = messages[1].shape[0] // IMG
    per = 2 * half
    block_rows = per * CAND
    groups, width = num.shape[2], num.shape[3]
    slices = own_out.shape[0]
    grp = grp_s[0]

    den = jnp.zeros((FREQ, FREQ), F32)
    mass = jnp.zeros((1, FREQ), F32)
    block = 0
    for scores_ref, cls_ref in zip(scores, classes):
        for b in range(scores_ref.shape[0] // block_rows):
            ones = [stats[d][(block ^ d) * per : ((block ^ d) + 1) * per, :] for d in range(blocks)]
            best = functools.reduce(jnp.maximum, [one[:, :ROTS] for one in ones])
            total = sum(one[:, ROTS:] * jnp.exp(one[:, :ROTS] - best) for one in ones)
            if block == 0:
                mass_out[...] = jnp.log(total)

            def over_rows(v):
                return jnp.broadcast_to(v[:, None, :], (per, CAND, ROTS)).reshape(block_rows, ROTS)

            at = slice(b * block_rows, (b + 1) * block_rows)
            weights = jnp.exp(scores_ref[at, :] - over_rows(best)) / over_rows(total)
            local = cls_ref[at, :]
            good = jnp.logical_and(local >= 0, local < sum(n for _, n in chunks))[:, :ROTS]
            weights = rounded(jnp.where(good, weights, 0.0))
            both = rounded(
                jnp.dot(weights, phases[...], precision=HIGH, preferred_element_type=F32)
            )
            row = block * (block_rows + 8)
            for part in range(2):
                wcs[part, row : row + block_rows, :] = both[:, part * FREQ : (part + 1) * FREQ]
                wcs[part, row + block_rows : row + block_rows + 8, :] = jnp.zeros((8, FREQ), F32)
            pair_sum = jnp.sum(weights, axis=1, keepdims=True)
            twice = (lanes_of((block_rows, FREQ)) % ROTS).astype(F32)
            chosen = jnp.where(twice == local, pair_sum, 0.0)
            by_particle = jnp.sum(chosen.reshape(per, CAND, FREQ), axis=1)
            side = messages[2 * block][half * IMG :, :].astype(F32)
            den = den + lax.dot_general(
                side, by_particle, (((0,), (0,)), ((), ())), precision=HIGH,
                preferred_element_type=F32,
            )
            mass = mass + jnp.sum(by_particle, axis=0, keepdims=True)
            block += 1

    add_pairs(lists, 0, chunks, messages, wcs, num)
    pack_sums(grp, num, own_out, sib_out)

    def two(v):
        left = lanes_of(v.shape) < ROTS
        return jnp.where(left, rounded(v), rounded(v - rounded(v)))

    halves[...] = two(den[:SHELLS]).reshape(groups, width, FREQ)
    mass_tile = two(jnp.broadcast_to(mass, (width, FREQ)))
    z, h = grp // 2, grp % 2
    for d in range(slices):
        for out, core in ((own_out, h), (sib_out, 1 - h)):
            tile = halves[(z ^ d) * 2 + core]
            out[d, chunks[0][1]] = jnp.concatenate([tile, mass_tile], axis=0).astype(BF16)


def next_sum_kernel(calls, blocks, chunk, chunks, grp_s, *refs):
    lists = [refs[3 * c : 3 * c + 3] for c in range(calls)]
    messages = refs[3 * calls : 3 * calls + 2 * blocks]
    wcs, own_out, sib_out, num = refs[3 * calls + 2 * blocks :]
    add_pairs(lists, chunk, chunks, messages, wcs, num)
    pack_sums(grp_s[0], num, own_out, sib_out)


def add_kernel(tail, own, sib, *outs):
    for d, out in enumerate(outs):
        out[...] = (own[d].astype(F32) + sib[d].astype(F32)).astype(BF16)
        if tail:
            total = own[d, out.shape[0] - 1].astype(F32) + sib[d, out.shape[0] - 1].astype(F32)
            total = total + pltpu.roll(total, ROTS, 1)
            left = lanes_of(total.shape) < ROTS
            high = rounded(total)
            out[out.shape[0] - 1] = jnp.where(left, high, total - high).astype(BF16)


def divide(got, inverse, start, avg_out):
    for k in range(avg_out.shape[0]):
        total = sum(one[k].astype(F32) for one in got)
        column = inverse[:, start + k : start + k + 1]
        factor = jnp.concatenate([column, column], axis=0)
        avg_out[k] = (total * factor).astype(BF16)


def first_divide_kernel(scale, start, *refs):
    got, (reg, avg_out, share_out, inverse_out) = refs[:-4], refs[-4:]
    cut = avg_out.shape[0]
    width = avg_out.shape[1] // 2
    tile = sum(one[cut].astype(F32) for one in got)
    tile = tile + pltpu.roll(tile, ROTS, 1)
    share_out[...] = tile[width : width + 1] * scale
    inverse = 1.0 / (tile[:width] + reg[...])
    inverse_out[...] = inverse
    divide(got, inverse, start, avg_out)


def next_divide_kernel(start, *refs):
    got, (inverse, avg_out) = refs[:-2], refs[-2:]
    divide(got, inverse[...], start, avg_out)


def spread_kernel(slices, start, has_out, grp_s, *refs):
    got = refs[: 2 * slices]
    out, wide, rows, sem = refs[2 * slices + has_out :]
    cut, height, _ = got[0].shape
    width = height // 2
    pad = wide.shape[0] // IMG
    z, h = grp_s[0] // 2, grp_s[0] % 2

    def one(k, _):
        for d in range(slices):
            for array, core in ((got[d], h), (got[slices + d], 1 - h)):
                piece = array[k].astype(F32)
                for x in range(2):
                    at = (x * SHELLS + ((z ^ d) * 2 + core) * width) * pad
                    wide[pl.ds(at + k, width, stride=pad), :] = piece[
                        x * width : (x + 1) * width
                    ]
        return 0

    lax.fori_loop(0, cut, one, 0)
    for at in range(IMG):
        rows[:, at * FREQ : (at + 1) * FREQ] = wide[at * pad : at * pad + cut, :]
    copy = pltpu.make_async_copy(rows, out.at[pl.ds(start, cut), :], sem)
    copy.start()
    copy.wait()


def whole(space):
    return pl.BlockSpec(memory_space=space)


def in_hbm(value):
    return pltpu.with_memory_space_constraint(value, HBM)


def call(kernel, name, ins, outs, scratch, mib, us, args, **more):
    cost = pl.CostEstimate(flops=0, bytes_accessed=int(us * 3.6e6), transcendentals=0)
    return pl.pallas_call(
        kernel,
        out_shape=tuple(s for s, _ in outs),
        in_specs=[whole(s) for s in ins],
        out_specs=tuple(whole(s) for _, s in outs),
        scratch_shapes=scratch,
        compiler_params=pltpu.CompilerParams(vmem_limit_bytes=mib * 2**20),
        name=name,
        cost_estimate=cost,
        **more,
    )(*args)


def swap(value, axis, distance):
    size = lax.axis_size(axis)
    return lax.ppermute(value, axis, [(i, i ^ distance) for i in range(size)])


def after(value, *others):
    return lax.optimization_barrier((value, *others))[0]


def per_device(
    particles, candidates, group_ids, ctf_ids, ctf_table, noise_prec, references, log_prior, reg
):
    n_cls = lax.axis_size("cls")
    n_grp = lax.axis_size("grp")
    per = particles.shape[0]
    half = per // 2
    cls_dev = references.shape[0]
    block_rows = per * CAND
    chunks = chunks_of(cls_dev)
    slots = block_rows + 2 * UNROLL
    pad = -(-cls_dev // 8) * 8
    width = SHELLS // n_grp
    nz = n_grp // 2
    scoring, phases = (jnp.asarray(t) for t in tables())
    first = (lax.axis_index("cls") * cls_dev).astype(jnp.int32).reshape(1)
    grp = lax.axis_index("grp").astype(jnp.int32).reshape(1)

    low, high = call(
        weigh_kernel, "weigh", [HBM] * 6,
        [(SHAPE((half * IMG + per, FREQ), BF16), VMEM), (SHAPE((half * IMG, FREQ), BF16), VMEM)],
        [
            VMEM(particles.shape, BF16),
            VMEM((CAND, per), jnp.int32),
            SMEM((per,), jnp.int32),
            SMEM((per,), jnp.int32),
            VMEM(ctf_table.shape[::-1], F32),
            VMEM(noise_prec.shape, F32),
            VMEM((per, noise_prec.shape[0]), F32),
            VMEM((per, ctf_table.shape[0]), F32),
            VMEM((IMG * per, FREQ), F32),
            pltpu.SemaphoreType.DMA((6,)),
        ],
        8, 3.0,
        tuple(
            in_hbm(a)
            for a in (particles, candidates.T, group_ids, ctf_ids, ctf_table.T, noise_prec)
        ),
    )

    if n_cls == 4:
        low_1, high_2 = swap(low, "cls", 1), swap(high, "cls", 2)
        high_1, low_2 = swap(high, "cls", 1), swap(low, "cls", 2)

    rf, power, scoring, phases = call(
        prep_kernel, "prep", [HBM, HBM, HBM, VMEM],
        [
            (SHAPE((cls_dev, IMG, FREQ), F32), VMEM),
            (SHAPE((cls_dev, FREQ), F32), VMEM),
            (SHAPE(scoring.shape, F32), VMEM),
            (SHAPE(phases.shape, F32), VMEM),
        ],
        [VMEM(references.shape, BF16), VMEM((IMG * pad, FREQ), F32), pltpu.SemaphoreType.DMA((6,))],
        14, 6.0,
        (
            in_hbm(references), in_hbm(scoring), in_hbm(phases),
            jnp.broadcast_to(log_prior.astype(F32)[:, None], (cls_dev, FREQ)),
        ),
    )

    def score(part):
        blocks = len(part)
        flat = [m for pair in part for m in pair]
        return call(
            functools.partial(score_kernel, blocks, chunks), "score",
            [SMEM] + [VMEM] * (2 * blocks + 3),
            [
                (SHAPE((blocks * block_rows, ROTS), F32), VMEM),
                (SHAPE((blocks * per, FREQ), F32), VMEM),
                (SHAPE((blocks * block_rows, FREQ), F32), VMEM),
                (SHAPE((blocks * len(chunks) * slots,), jnp.int32), SMEM),
                (SHAPE((blocks * len(chunks) * slots,), jnp.int32), SMEM),
                (SHAPE((blocks * len(chunks),), jnp.int32), SMEM),
            ],
            [
                VMEM((blocks, per, FREQ), jnp.int32),
                SMEM((blocks, per, FREQ), jnp.int32),
                VMEM((blocks, per, FREQ), F32),
                VMEM((3, block_rows + 8, FREQ), F32),
                VMEM((blocks * per, IMG, FREQ), F32),
                pltpu.SemaphoreType.DMA((blocks,)),
            ],
            12 if n_cls == 4 else 40, 3.0 * blocks, (first, *flat, rf, power, scoring),
        )

    if n_cls == 4:
        scored = [score([(low, high)])]
        low_1, high_2 = after(low_1, scored[0][1]), after(high_2, scored[0][1])
        low_3, high_3 = swap(low_1, "cls", 2), swap(high_2, "cls", 1)
        messages = [(low, high), (low_1, high_1), (low_2, high_2), (low_3, high_3)]
        scored += [score(messages[1:3]), score(messages[3:])]
    else:
        messages = [(low, high)]
        messages += [(swap(low, "cls", d), swap(high, "cls", d)) for d in range(1, n_cls)]
        scored = [score(messages)]
    stats = jnp.concatenate([s[1] for s in scored], axis=0) if len(scored) > 1 else scored[0][1]
    all_stats = [stats] + [swap(stats, "cls", d) for d in range(1, n_cls)]
    lists = [a for s in scored for a in s[3:]]
    flat = [m for pair in messages for m in pair]
    calls = len(scored)
    all_rows = n_cls * (block_rows + 8)
    tile = (2 * width, FREQ)

    def sums_out(rows):
        return [(SHAPE((nz, rows) + tile, BF16), VMEM)] * 2

    own, sib, mass, wcs = call(
        functools.partial(first_sum_kernel, calls, n_cls, chunks), "sum",
        [SMEM] * (1 + 3 * calls) + [VMEM] * (3 * n_cls + 2 * calls + 1),
        sums_out(chunks[0][1] + 1)
        + [(SHAPE((per, ROTS), F32), VMEM), (SHAPE((2, all_rows, FREQ), F32), VMEM)],
        [VMEM((chunks[0][1], 2, n_grp, width, FREQ), F32), VMEM((n_grp, width, FREQ), F32)],
        16 if n_cls == 4 else 32, 3.8,
        (grp, *lists, *all_stats, *(s[0] for s in scored), *(s[2] for s in scored), *flat, phases),
    )
    sums = [(own, sib)]
    for chunk in range(1, len(chunks)):
        sums.append(
            call(
                functools.partial(next_sum_kernel, calls, n_cls, chunk, chunks), "sum",
                [SMEM] * (1 + 3 * calls) + [VMEM] * (2 * n_cls + 1),
                sums_out(chunks[chunk][1]),
                [VMEM((chunks[chunk][1], 2, n_grp, width, FREQ), F32)],
                16, 3.0, (grp, *lists, *flat, wcs),
            )
        )

    own_reg = lax.dynamic_slice(reg, (lax.axis_index("grp") * width,), (width,))
    own_reg = jnp.broadcast_to(own_reg[:, None], (width, FREQ))
    particle_total = per * n_grp * n_cls
    averages, inverse, share = None, None, None
    for chunk, (own, sib) in enumerate(sums):
        rows = own.shape[1]
        start, cut = chunks[chunk]
        other = swap(sib, "grp", 1)
        added = call(
            functools.partial(add_kernel, chunk == 0), "add", [VMEM] * 2,
            [(SHAPE((rows,) + tile, BF16), VMEM)] * nz, [], 8, 0.8, (own, other),
        )
        got = [added[0]] + [swap(added[d], "grp", 2 * d) for d in range(1, nz)]
        averaged_out = (SHAPE((cut,) + tile, BF16), VMEM)
        if chunk == 0:
            averaged, share, inverse = call(
                functools.partial(first_divide_kernel, K / particle_total, start), "divide",
                [VMEM] * (nz + 1),
                [averaged_out, (SHAPE((1, FREQ), F32), VMEM), (SHAPE((width, FREQ), F32), VMEM)],
                [], 8, 1.0, (*got, own_reg),
            )
        else:
            (averaged,) = call(
                functools.partial(next_divide_kernel, start), "divide", [VMEM] * (nz + 1),
                [averaged_out], [], 8, 1.0, (*got, inverse),
            )
        slices = [averaged] + [swap(averaged, "grp", 2 * d) for d in range(1, nz)]
        slices = slices + [swap(s, "grp", 1) for s in slices]
        has_out = chunk > 0
        (averages,) = call(
            functools.partial(spread_kernel, nz, start, has_out), "spread",
            [SMEM] + [VMEM] * (2 * nz) + [HBM] * has_out,
            [(SHAPE((cls_dev, FEAT), F32), HBM)],
            [
                VMEM((IMG * (-(-cut // 8) * 8), FREQ), F32),
                VMEM((cut, FEAT), F32),
                pltpu.SemaphoreType.DMA,
            ],
            10, 2.0, (grp, *slices) + ((averages,) if has_out else ()),
            input_output_aliases={2 * nz + 1: 0} if has_out else {},
        )
    return (averages, share[0, :cls_dev], mass[:, 0])


def solution(mesh):
    return jax.shard_map(
        per_device,
        mesh=mesh,
        in_specs=(
            P(("grp", "cls"), None),
            P(("grp", "cls"), None),
            P(("grp", "cls")),
            P(("grp", "cls")),
            P(),
            P(),
            P("cls", None),
            P("cls"),
            P(),
        ),
        out_specs=(P("cls", None), P("cls"), P(("grp", "cls"))),
        check_vma=False,
    )
```

```python
import functools
import math

import jax
import jax.numpy as jnp
import numpy as np
from jax import lax
from jax.experimental import pallas as pl
from jax.experimental.pallas import tpu as pltpu
from jax.sharding import PartitionSpec as P

SHELLS = 64
FREQ = 128
FEAT = 16384
ROTS = 64
K = 208
CAND = 8
MOST = 2
IMG = 2 * SHELLS
UNROLL = 4
LOW = -1e30
HIGH = lax.Precision.HIGHEST
VMEM = pltpu.VMEM
SMEM = pltpu.SMEM
HBM = pltpu.HBM
F32 = jnp.float32
BF16 = jnp.bfloat16
SHAPE = jax.ShapeDtypeStruct


def tables():
    turns = np.arange(ROTS)[:, None]
    orders = np.arange(FREQ)[None, :]
    angles = ((turns * orders) % ROTS).astype(np.float32) * np.float32(2.0 * math.pi / ROTS)
    cos_tab = np.cos(angles).astype(np.float32)
    sin_tab = np.sin(angles).astype(np.float32)
    last = np.zeros((FREQ, ROTS), np.float32)
    last[:SHELLS] = -0.5
    last[SHELLS] = 1.0
    scoring = np.concatenate([cos_tab.T, sin_tab.T, last], axis=0)
    left = np.concatenate([cos_tab, sin_tab], axis=1)
    left = np.concatenate([left, left], axis=0)
    phases = []
    for _ in range(3):
        phases.append(left.astype(jnp.bfloat16))
        left = left - phases[-1].astype(np.float32)
    return (scoring, *phases)


def lanes_of(shape):
    return lax.broadcasted_iota(jnp.int32, shape, len(shape) - 1)


def list_spots(blocks, chunks):
    room = FREQ if max(n for _, n in chunks) * MOST + UNROLL > FREQ // 2 else FREQ // 2
    lines = -(-blocks * len(chunks) * room // FREQ)
    return room, lines, -(-(2 * lines + 1) // 8) * 8


def list_spot(block, chunk, blocks, chunks):
    room, lines, _ = list_spots(blocks, chunks)
    spot = block * len(chunks) + chunk
    line, lane = divmod(spot * room, FREQ)
    return line, lines + line, lane, 2 * lines, spot


def quot(v, n):
    return v >> (n.bit_length() - 1) if n & (n - 1) == 0 else v // n


def rest(v, n):
    return v & (n - 1) if n & (n - 1) == 0 else v % n


def rounded(v):
    return v.astype(BF16).astype(F32)


def row_of(x, r, depth):
    return r // depth * 2 * depth + x * depth + r % depth


def parts_of(image, depth):
    pieces = image.reshape(image.shape[0] // (2 * depth), 2, depth, FREQ)
    return pieces[:, 0], pieces[:, 1]


def chunks_of(cls_dev):
    cut = cls_dev // 2 // 8 * 8
    return ((cut, cls_dev - cut), (0, cut)) if cut else ((0, cls_dev),)


def weigh_kernel(
    slices, grp_s, particles_h, cand_h, groups_h, entries_h, ctf_h, prec_h, message_out, *refs
):
    slice_outs = refs[: slices - 1]
    particles, cand, groups, entries, ctf, prec, hot_g, hot_e, spread, sem = refs[slices - 1 :]
    depth = SHELLS // slices
    z = grp_s[0] // 2
    copies = [
        pltpu.make_async_copy(a, b, sem.at[n])
        for n, (a, b) in enumerate(
            (
                (groups_h, groups), (entries_h, entries), (ctf_h, ctf), (prec_h, prec),
                (cand_h, cand), (particles_h, particles),
            )
        )
    ]
    for copy in copies:
        copy.start()
    per = particles.shape[0]
    for copy in copies[:2]:
        copy.wait()
    for i in range(per):
        hot_g[i : i + 1, :] = (lanes_of((1, hot_g.shape[1])) == groups[i]).astype(F32)
        hot_e[i : i + 1, :] = (lanes_of((1, hot_e.shape[1])) == entries[i]).astype(F32)
    for copy in copies[2:5]:
        copy.wait()
    p = jnp.dot(hot_g[...], prec[...], precision=HIGH, preferred_element_type=F32)
    c = lax.dot_general(
        hot_e[...], ctf[...], (((1,), (1,)), ((), ())), precision=HIGH, preferred_element_type=F32
    )
    eye = (lanes_of((per, per)) == lax.broadcasted_iota(jnp.int32, (per, per), 0)).astype(F32)
    named = lax.dot_general(
        eye, cand[...].astype(F32), (((1,), (1,)), ((), ())), precision=HIGH,
        preferred_element_type=F32,
    )
    factors = p * c
    extra = jnp.concatenate(
        [factors * c, named, jnp.zeros((per, FREQ - SHELLS - CAND), F32)], axis=1
    )
    message_out[per * IMG :, :] = extra.astype(BF16)
    copies[5].wait()
    for r in range(SHELLS):
        factor = jnp.broadcast_to(factors[:, r : r + 1], (per, FREQ))
        for x in range(2):
            at = x * SHELLS + r
            piece = particles[:, at * FREQ : (at + 1) * FREQ].astype(F32) * factor
            at = row_of(x, r, depth)
            spread[at * per : (at + 1) * per, :] = rounded(piece)
    rows = 2 * depth
    for i in range(per):
        message_out[i * IMG : (i + 1) * IMG, :] = spread[i : i + IMG * per : per, :].astype(BF16)
        for d, out in enumerate(slice_outs, start=1):
            row = pl.multiple_of(i * IMG + (z ^ d) * rows, rows)
            out[i * rows : (i + 1) * rows, :] = message_out[pl.ds(row, rows), :]


def prep_kernel(depth, grp_s, refs_h, *rest_refs):
    tables_h, (reg_h, prior), rest_refs = rest_refs[:4], rest_refs[4:6], rest_refs[6:]
    (rf_out, pow_out), tables_out, (reg_out,) = rest_refs[:2], rest_refs[2:6], rest_refs[6:7]
    refs, spread, reg, sem = rest_refs[7:]
    cls_dev = refs.shape[0]
    pad = spread.shape[0] // IMG
    parts = sem.shape[0] - 5
    step = FEAT // parts
    tables_in = [
        pltpu.make_async_copy(a, b, sem.at[parts + n])
        for n, (a, b) in enumerate(zip((*tables_h, reg_h), (*tables_out, reg)))
    ]
    copies = [
        pltpu.make_async_copy(
            refs_h.at[:, pl.ds(n * step, step)], refs.at[:, pl.ds(n * step, step)], sem.at[n]
        )
        for n in range(parts)
    ]
    for copy in copies + tables_in:
        copy.start()
    for copy in copies:
        copy.wait()

    def shell(r, power):
        parts = []
        for x in range(2):
            at = x * SHELLS + r
            piece = refs[:, pl.ds(pl.multiple_of(at * FREQ, FREQ), FREQ)].astype(F32)
            at = row_of(x, r, depth)
            spread[pl.ds(pl.multiple_of(at * pad, 8), cls_dev), :] = piece
            parts.append(piece * piece)
        total = jnp.sum(parts[0] + parts[1], axis=1, keepdims=True)
        return jnp.where(lanes_of((cls_dev, FREQ)) == r, total, power)

    power = lax.fori_loop(0, SHELLS, shell, jnp.zeros((cls_dev, FREQ), F32), unroll=4)
    pow_out[...] = jnp.where(lanes_of((cls_dev, FREQ)) == SHELLS, prior[...], power)

    def image(k, _):
        rf_out[k] = spread[pl.ds(k, IMG, stride=pad), :]
        return 0

    lax.fori_loop(0, cls_dev, image, 0, unroll=4)
    for copy in tables_in:
        copy.wait()
    width = reg_out.shape[0]
    for r in range(width):
        reg_out[r : r + 1, :] = jnp.full((1, FREQ), reg[grp_s[0] * width + r], F32)


def take(refs, counts):
    taken = []
    for count in counts:
        taken.append(refs[:count])
        refs = refs[count:]
    return taken, refs


def score_kernel(arrays, earlier, depth, chunks, first_s, *refs):
    blocks = len(arrays)
    messages, refs = take(refs, arrays)
    (earlier_stats,), refs = take(refs, (earlier,))
    rf, power, scoring = refs[:3]
    scores_out, stats_out, cls_out, ints_out = refs[3:-7]
    cand_v, cand_s, ints_s, side, ex, w32, sem = refs[-7:]
    per = cand_v.shape[1]
    cls_dev = rf.shape[0]
    block_rows = per * CAND
    first = first_s[0]
    table = scoring[...]
    done = 0
    for one in earlier_stats:
        stats_out[done : done + one.shape[0], :] = one[...]
        done += one.shape[0]

    for b in range(blocks):
        extra = messages[b][-1][messages[b][-1].shape[0] - per :, :].astype(F32)
        cand_v[b] = extra.astype(jnp.int32)
        lane = lanes_of((per, FREQ))
        side[b] = jnp.where(lane < SHELLS, extra, (lane == SHELLS).astype(F32))
    copies = [pltpu.make_async_copy(cand_v.at[b], cand_s.at[b], sem.at[b]) for b in range(blocks)]
    for copy in copies:
        copy.start()
    for b in range(blocks):
        begin = 0
        for one in messages[b]:
            count = one.shape[0] // IMG

            def widen(i, _):
                w32[b * per + begin + i] = one[pl.ds(pl.multiple_of(i * IMG, IMG), IMG), :].astype(F32)
                return 0

            lax.fori_loop(0, count, widen, 0, unroll=2)
            begin += count
    for copy in copies:
        copy.wait()

    for b in range(blocks):
        spots = [list_spot(b, c, blocks, chunks) for c in range(len(chunks))]

        def put(place, lane, c, row, local):
            if len(chunks) == 1 or c is not None:
                spot = spots[c or 0]
                ints_s[spot[0], spot[2] + place] = row
                ints_s[spot[1], spot[2] + place] = local
            else:
                ints_s[spots[0][0] + lane[0], lane[1]] = row
                ints_s[spots[0][1] + lane[0], lane[1]] = local

        def one(i, n):
            for t in range(CAND):
                local = cand_s[b, i, SHELLS + t] - first
                good = jnp.logical_and(local >= 0, local < cls_dev)
                if len(chunks) == 1:
                    put(n[0], None, 0, i * CAND + t, local)
                    n = (n[0] + good.astype(jnp.int32),)
                else:
                    late = local < chunks[0][0]
                    line = jnp.where(late, spots[1][0] - spots[0][0], 0)
                    lane = jnp.where(late, spots[1][2] + n[1], spots[0][2] + n[0])
                    put(None, (line, lane), None, i * CAND + t, local)
                    n = (
                        n[0] + jnp.logical_and(good, jnp.logical_not(late)).astype(jnp.int32),
                        n[1] + jnp.logical_and(good, late).astype(jnp.int32),
                    )
            return n

        n = lax.fori_loop(0, per, one, (jnp.int32(0),) * len(chunks))
        for c, (start, _) in enumerate(chunks):
            for spare in range(UNROLL):
                put(n[c] + spare, None, c, block_rows, start)
            ints_s[spots[c][3], spots[c][4]] = quot(n[c] + UNROLL - 1, UNROLL)
    lists_copy = pltpu.make_async_copy(ints_s, ints_out, sem.at[blocks])
    lists_copy.start()

    for b in range(blocks):
        for c in range(len(chunks)):
            spot = list_spot(b, c, blocks, chunks)

            def pairs(step, _):
                for u in range(UNROLL):
                    row = ints_s[spot[0], spot[2] + step * UNROLL + u]
                    k = ints_s[spot[1], spot[2] + step * UNROLL + u]
                    i = jnp.minimum(quot(row, CAND), per - 1)
                    w_re, w_im = parts_of(w32[b * per + i], depth)
                    a_re, a_im = parts_of(rf[k], depth)
                    inner = (w_re * a_re + w_im * a_im).reshape(SHELLS, FREQ)
                    outer = (w_re * a_im - w_im * a_re).reshape(SHELLS, FREQ)
                    ex[0, pl.ds(row, 1), :] = jnp.sum(inner, axis=0, keepdims=True)
                    ex[1, pl.ds(row, 1), :] = jnp.sum(outer, axis=0, keepdims=True)
                    ex[2, pl.ds(row, 1), :] = side[b, pl.ds(i, 1), :] * power[pl.ds(k, 1), :]
                return 0

            lax.fori_loop(0, ints_s[spot[3], spot[4]], pairs, 0)

        wide = jnp.broadcast_to(
            messages[b][-1][messages[b][-1].shape[0] - per :, :].astype(F32)[:, None, :],
            (per, CAND, FREQ),
        ).reshape(block_rows, FREQ)
        own = lanes_of((block_rows, FREQ)) == SHELLS + (
            lax.broadcasted_iota(jnp.int32, (block_rows, FREQ), 0) % CAND
        )
        column = jnp.sum(jnp.where(own, wide, 0.0), axis=1, keepdims=True) - first.astype(F32)
        cls_out[b * block_rows : (b + 1) * block_rows, :] = jnp.broadcast_to(
            column, (block_rows, FREQ)
        )
        good = jnp.logical_and(column >= 0, column < cls_dev)
        values = jnp.zeros((block_rows, ROTS), F32)
        for part in range(3):
            values = values + jnp.dot(
                jnp.where(good, ex[part, :block_rows, :], 0.0),
                table[part * FREQ : (part + 1) * FREQ],
                precision=HIGH,
                preferred_element_type=F32,
            )
        scores = jnp.where(good, values, LOW)
        scores_out[b * block_rows : (b + 1) * block_rows, :] = scores
        top = jnp.broadcast_to(jnp.max(scores, axis=1, keepdims=True), (block_rows, ROTS))
        best = jnp.max(top.reshape(per, CAND, ROTS), axis=1)
        best_rows = jnp.broadcast_to(best[:, None, :], (per, CAND, ROTS)).reshape(block_rows, ROTS)
        mass = jnp.where(good, jnp.exp(scores - best_rows), 0.0)
        mass = jnp.broadcast_to(jnp.sum(mass, axis=1, keepdims=True), (block_rows, ROTS))
        total = jnp.sum(mass.reshape(per, CAND, ROTS), axis=1)
        stats_out[done + b * per : done + (b + 1) * per, :ROTS] = best
        stats_out[done + b * per : done + (b + 1) * per, ROTS:] = total
    lists_copy.wait()


def two(v):
    return jnp.where(lanes_of(v.shape) < ROTS, rounded(v), v - rounded(v))


def one_of_two(v):
    return v + pltpu.roll(v, ROTS, 1)


def weights_kernel(calls, blocks, slices, cls_dev, grp_s, *refs):
    stats = refs[:blocks]
    scores = refs[blocks : blocks + calls]
    classes = refs[blocks + calls : blocks + 2 * calls]
    extras = refs[blocks + 2 * calls : 2 * blocks + 2 * calls]
    refs = refs[2 * blocks + 2 * calls :]
    ints, refs = refs[:calls], refs[calls:]
    own_out, den_out, mass_out, log_out = refs[:4]
    message_outs = refs[4:-2]
    rows_v, den_v = refs[-2:]
    per = log_out.shape[0]
    block_rows = per * CAND
    depth = SHELLS // slices
    z = grp_s[0] // 2

    den = jnp.zeros((FREQ, FREQ), F32)
    mass = jnp.zeros((1, FREQ), F32)
    block = 0
    for scores_ref, cls_ref in zip(scores, classes):
        for b in range(scores_ref.shape[0] // block_rows):
            ones = [stats[d][(block ^ d) * per : ((block ^ d) + 1) * per, :] for d in range(blocks)]
            best = functools.reduce(jnp.maximum, [one[:, :ROTS] for one in ones])
            total = sum(one[:, ROTS:] * jnp.exp(one[:, :ROTS] - best) for one in ones)
            if block == 0:
                log_out[...] = jnp.log(total)

            def over_rows(v):
                return jnp.broadcast_to(v[:, None, :], (per, CAND, ROTS)).reshape(block_rows, ROTS)

            at = slice(b * block_rows, (b + 1) * block_rows)
            weights = jnp.exp(scores_ref[at, :] - over_rows(best)) / over_rows(total)
            local = cls_ref[at, :]
            good = jnp.logical_and(local >= 0, local < cls_dev)[:, :ROTS]
            weights = rounded(jnp.where(good, weights, 0.0))
            rows_v[block * block_rows : (block + 1) * block_rows, :] = weights
            pair_sum = jnp.sum(weights, axis=1, keepdims=True)
            twice = (lanes_of((block_rows, FREQ)) % ROTS).astype(F32)
            chosen = jnp.where(twice == local, pair_sum, 0.0)
            by_particle = jnp.sum(chosen.reshape(per, CAND, FREQ), axis=1)
            side = extras[block][extras[block].shape[0] - per :, :].astype(F32)
            den = den + lax.dot_general(
                side, by_particle, (((0,), (0,)), ((), ())), precision=HIGH,
                preferred_element_type=F32,
            )
            mass = mass + jnp.sum(by_particle, axis=0, keepdims=True)
            block += 1

    lines = rows_v.shape[0] // 2
    packed = jnp.concatenate([rows_v[:lines, :], rows_v[lines:, :]], axis=1).astype(BF16)
    own_out[...] = packed
    den_v[...] = den[:SHELLS].reshape(slices, depth, FREQ)
    mass_rows = jnp.broadcast_to(mass, (8, FREQ))
    mass_out[...] = mass_rows
    den_out[...] = den_v[z]
    tail = [two(mass_rows)] + [one[...].astype(F32) for one in ints]
    tail_rows = depth + sum(one.shape[0] for one in tail)
    spare = message_outs[0].shape[0] - lines - tail_rows
    if spare:
        tail.append(jnp.zeros((spare, FREQ), F32))
    for d, out in enumerate(message_outs, start=1):
        out[:lines, :] = packed
        out[lines:, :] = jnp.concatenate([two(den_v[z ^ d])] + tail, axis=0).astype(BF16)


def phase_rows(packed, phases):
    high, mid, low = phases
    halves = []
    for place in range(2):
        lanes = lanes_of(packed.shape) // ROTS == place
        picked = jnp.where(lanes, packed.astype(F32), 0.0).astype(BF16)
        halves.append(
            rounded(
                sum(
                    jnp.dot(picked, t[...], preferred_element_type=F32) for t in (low, mid, high)
                )
            )
        )
    return halves


def put_phases(packed, phases, wcs, base):
    lines = packed.shape[0]
    for place, both in enumerate(phase_rows(packed, phases)):
        for part in range(2):
            at = base + place * lines
            wcs[part, at : at + lines, :] = both[:, part * FREQ : (part + 1) * FREQ]
    for part in range(2):
        wcs[part, base + 2 * lines : base + 2 * lines + 8, :] = jnp.zeros((8, FREQ), F32)


def add_pair(image, row, k, wcs, num):
    shape = num.shape[1:]
    image = image.astype(F32)
    half = image.shape[0] // 2
    w_re, w_im = image[:half].reshape(shape[1:]), image[half:].reshape(shape[1:])
    c = wcs[0, pl.ds(row, 1), :].reshape(1, 1, FREQ)
    s = wcs[1, pl.ds(row, 1), :].reshape(1, 1, FREQ)
    num[k, 0] += w_re * c - w_im * s
    num[k, 1] += w_re * s + w_im * c


def pick_image(arrays, begin, i, rows, stride, offset):
    def rows_at(one, i):
        return one[pl.ds(pl.multiple_of(i * stride + offset, rows), rows), :]

    held = [one.shape[0] // stride for one in arrays]
    while len(arrays) > 1 and begin >= held[0]:
        arrays, begin, held = arrays[1:], begin - held[0], held[1:]
    if len(arrays) == 1:
        return rows_at(arrays[0], begin + i)
    cut = held[0] - begin
    return jnp.where(
        i < cut,
        rows_at(arrays[0], begin + jnp.minimum(i, cut - 1)),
        rows_at(arrays[1], jnp.maximum(i - cut, 0)),
    )


def own_sum_kernel(chunks, calls, arrays, grp_s, packed, *refs):
    (ints,), refs = take(refs, (len(calls),))
    messages, refs = take(refs, arrays)
    phases, (num, wcs, *ints_s, sem) = refs[:3], refs[3:]
    copies = [
        pltpu.make_async_copy(a, b, sem.at[n]) for n, (a, b) in enumerate(zip(ints, ints_s))
    ]
    for copy in copies:
        copy.start()
    per = sum(one.shape[0] for one in messages[0]) // (IMG + 1)
    rows = 2 * num.shape[2] * num.shape[3]
    z = grp_s[0] // 2
    put_phases(packed[...], phases, wcs, 0)
    num[...] = jnp.zeros_like(num)
    for copy in copies:
        copy.wait()
    block = 0
    for held, list_s in zip(calls, ints_s):
        for b in range(held):
            held_in = messages[block]
            base = block * per * CAND
            for c in range(len(chunks)):
                spot = list_spot(b, c, held, chunks)

                def pairs(step, _):
                    for u in range(UNROLL):
                        row = list_s[spot[0], spot[2] + step * UNROLL + u]
                        k = list_s[spot[1], spot[2] + step * UNROLL + u]
                        i = jnp.minimum(quot(row, CAND), per - 1)
                        row = jnp.where(row == per * CAND, wcs.shape[1] - 8, base + row)
                        image = pick_image(held_in, 0, i, rows, IMG, z * rows)
                        add_pair(image, row, k, wcs, num)
                    return 0

                lax.fori_loop(0, list_s[spot[3], spot[4]], pairs, 0)
            block += 1


def join_kernel(*refs):
    out = refs[-1]
    rows = refs[0].shape[0]
    for n, one in enumerate(refs[:-1]):
        out[n * rows : (n + 1) * rows, :] = one[...]


def sum_kernel(chunk, chunks, calls, slices, pieces, grp_s, *refs):
    images, refs = take(refs, pieces)
    messages, refs = refs[: slices - 1], refs[slices - 1 :]
    first, refs = refs[0], refs[1:]
    if chunk == 0:
        phases, (den_own, mass_own), refs = refs[:3], refs[3:5], refs[5:]
        own_out, sib_out, den_out, mass_out, wcs, num, den_v, ints_v, ints_s, sem = refs
    else:
        wcs, own_out, sib_out, num, ints_v, ints_s, sem = refs
    group_rows = wcs.shape[1] // (slices - 1)
    lines = (group_rows - 8) // 2
    core = grp_s[0] % 2
    start, size = chunks[chunk]
    depth = num.shape[2] * num.shape[3]
    rows = 2 * depth
    per = sum(one.shape[0] for one in images[0]) // ((slices - 1) * rows)
    total = ints_v.shape[1]

    for d in range(slices - 1):
        tail = messages[d][lines:, :].astype(F32)
        ints_v[d] = tail[depth + 8 : depth + 8 + total].astype(jnp.int32)
    copies = [
        pltpu.make_async_copy(ints_v.at[d], ints_s.at[d], sem.at[d]) for d in range(slices - 1)
    ]
    for copy in copies:
        copy.start()
    num[...] = first[start : start + size]
    if chunk == 0:
        den, mass = den_own[...], mass_own[...]
        for d in range(slices - 1):
            put_phases(messages[d][:lines, :], phases, wcs, d * group_rows)
            den = den + one_of_two(messages[d][lines:, :].astype(F32)[:depth])
            mass = mass + one_of_two(messages[d][lines:, :].astype(F32)[depth : depth + 8])
    for copy in copies:
        copy.wait()

    for d in range(slices - 1):
        block, line = 0, 0
        for held in calls:
            for b in range(held):
                spot = list_spot(b, chunk, held, chunks)
                held_in = images[block]
                base = d * group_rows + block * per * CAND
                blank = (d + 1) * group_rows - 8

                def pairs(step, _):
                    for u in range(UNROLL):
                        row = ints_s[d, line + spot[0], spot[2] + step * UNROLL + u]
                        k = ints_s[d, line + spot[1], spot[2] + step * UNROLL + u]
                        i = jnp.minimum(quot(row, CAND), per - 1)
                        row = jnp.where(row == per * CAND, blank, base + row)
                        image = pick_image(held_in, d * per, i, rows, rows, 0)
                        add_pair(image, row, k - start, wcs, num)
                    return 0

                lax.fori_loop(0, ints_s[d, line + spot[3], spot[4]], pairs, 0)
                block += 1
            line += list_spots(held, chunks)[2]

    def pack(k, _):
        own_out[k] = jnp.concatenate([num[k, 0, core], num[k, 1, core]], axis=0)
        other = jnp.concatenate([num[k, 0, 1 - core], num[k, 1, 1 - core]], axis=0)
        sib_out[k] = other.astype(BF16)
        return 0

    lax.fori_loop(0, size, pack, 0)
    if chunk == 0:
        width = num.shape[3]
        den_v[...] = den.reshape(2, width, FREQ)
        den_out[...] = den_v[core]
        mass_out[...] = mass
        sib_out[size] = jnp.concatenate([two(den_v[1 - core]), two(mass)[:width]], axis=0).astype(BF16)


def divide(own, sib, inverse, start, avg_out):
    for k in range(avg_out.shape[0]):
        column = inverse[:, start + k : start + k + 1]
        factor = jnp.concatenate([column, column], axis=0)
        avg_out[k] = ((own[k] + sib[k].astype(F32)) * factor).astype(BF16)


def first_divide_kernel(scale, start, own, sib, den, mass, reg, avg_out, share_out, inverse_out):
    cut = avg_out.shape[0]
    width = avg_out.shape[1] // 2
    tile = one_of_two(sib[cut].astype(F32))
    share_out[...] = (tile[width : width + 1] + mass[:1]) * scale
    inverse = 1.0 / (tile[:width] + den[...] + reg[...])
    inverse_out[...] = inverse
    divide(own, sib, inverse, start, avg_out)


def next_divide_kernel(start, own, sib, inverse, avg_out):
    divide(own, sib, inverse[...], start, avg_out)


def spread_kernel(slices, start, has_out, grp_s, *refs):
    got = refs[: 2 * slices]
    out, wide, rows, sem = refs[2 * slices + has_out :]
    cut, height, _ = got[0].shape
    width = height // 2
    pad = wide.shape[0] // IMG
    z, h = grp_s[0] // 2, grp_s[0] % 2

    def one(k, _):
        for d in range(slices):
            for array, core in ((got[d], h), (got[slices + d], 1 - h)):
                piece = array[k].astype(F32)
                for x in range(2):
                    at = (x * SHELLS + ((z ^ d) * 2 + core) * width) * pad
                    wide[pl.ds(at + k, width, stride=pad), :] = piece[
                        x * width : (x + 1) * width
                    ]
        return 0

    lax.fori_loop(0, cut, one, 0)
    for at in range(IMG):
        rows[:, at * FREQ : (at + 1) * FREQ] = wide[at * pad : at * pad + cut, :]
    copy = pltpu.make_async_copy(rows, out.at[pl.ds(start, cut), :], sem)
    copy.start()
    copy.wait()


def whole(space):
    return pl.BlockSpec(memory_space=space)


def in_hbm(value):
    return pltpu.with_memory_space_constraint(value, HBM)


def call(kernel, name, ins, outs, scratch, mib, us, args, **more):
    cost = pl.CostEstimate(flops=0, bytes_accessed=int(us * 3.6e6), transcendentals=0)
    return pl.pallas_call(
        kernel,
        out_shape=tuple(s for s, _ in outs),
        in_specs=[whole(s) for s in ins],
        out_specs=tuple(whole(s) for _, s in outs),
        scratch_shapes=scratch,
        compiler_params=pltpu.CompilerParams(vmem_limit_bytes=mib * 2**20),
        name=name,
        cost_estimate=cost,
        **more,
    )(*args)


def swap(value, axis, distance):
    size = lax.axis_size(axis)
    return lax.ppermute(value, axis, [(i, i ^ distance) for i in range(size)])


def after(value, *others):
    return lax.optimization_barrier((value, *others))[0]


def per_device(
    particles, candidates, group_ids, ctf_ids, ctf_table, noise_prec, references, log_prior, reg
):
    n_cls = lax.axis_size("cls")
    n_grp = lax.axis_size("grp")
    per = particles.shape[0]
    cls_dev = references.shape[0]
    block_rows = per * CAND
    chunks = chunks_of(cls_dev)
    pad = -(-cls_dev // 8) * 8
    width = SHELLS // n_grp
    nz = n_grp // 2
    scoring, *phases = (jnp.asarray(t) for t in tables())
    first = (lax.axis_index("cls") * cls_dev).astype(jnp.int32).reshape(1)
    grp = lax.axis_index("grp").astype(jnp.int32).reshape(1)

    depth = SHELLS // nz
    message, *sliced = call(
        functools.partial(weigh_kernel, nz), "weigh", [SMEM] + [HBM] * 6,
        [(SHAPE((per * (IMG + 1), FREQ), BF16), VMEM)]
        + [(SHAPE((per * 2 * depth, FREQ), BF16), VMEM)] * (nz - 1),
        [
            VMEM(particles.shape, BF16),
            VMEM((CAND, per), jnp.int32),
            SMEM((per,), jnp.int32),
            SMEM((per,), jnp.int32),
            VMEM(ctf_table.shape[::-1], F32),
            VMEM(noise_prec.shape, F32),
            VMEM((per, noise_prec.shape[0]), F32),
            VMEM((per, ctf_table.shape[0]), F32),
            VMEM((IMG * per, FREQ), F32),
            pltpu.SemaphoreType.DMA((6,)),
        ],
        5, 2.0,
        (grp,)
        + tuple(
            in_hbm(a)
            for a in (particles, candidates.T, group_ids, ctf_ids, ctf_table.T, noise_prec)
        ),
    )

    if n_cls == 4:
        message_1, message_2 = swap(message, "cls", 1), swap(message, "cls", 2)
    sliced = [swap(one, "grp", 2 * d) for d, one in enumerate(sliced, start=1)]

    rf, power, scoring, *phases, own_reg = call(
        functools.partial(prep_kernel, depth), "prep", [SMEM] + [HBM] * 6 + [VMEM],
        [(SHAPE((cls_dev, IMG, FREQ), F32), VMEM), (SHAPE((cls_dev, FREQ), F32), VMEM)]
        + [(SHAPE(t.shape, t.dtype), VMEM) for t in (scoring, *phases)]
        + [(SHAPE((width, FREQ), F32), VMEM)],
        [
            VMEM(references.shape, BF16),
            VMEM((IMG * pad, FREQ), F32),
            SMEM(reg.shape, F32),
            pltpu.SemaphoreType.DMA((9,)),
        ],
        8, 4.0,
        (grp,)
        + tuple(in_hbm(a) for a in (references, scoring, *phases, reg))
        + (jnp.broadcast_to(log_prior.astype(F32)[:, None], (cls_dev, FREQ)),),
    )

    def score(part, earlier=()):
        blocks = len(part)
        flat = [m for arrays in part for m in arrays]
        earlier = tuple(s[1] for s in earlier)
        ahead = sum(s.shape[0] for s in earlier)
        counts = tuple(len(arrays) for arrays in part)
        return call(
            functools.partial(score_kernel, counts, len(earlier), depth, chunks), "score",
            [SMEM] + [VMEM] * (len(flat) + len(earlier) + 3),
            [
                (SHAPE((blocks * block_rows, ROTS), F32), VMEM),
                (SHAPE((ahead + blocks * per, FREQ), F32), VMEM),
                (SHAPE((blocks * block_rows, FREQ), F32), VMEM),
                (SHAPE((list_spots(blocks, chunks)[2], FREQ), jnp.int32), VMEM),
            ],
            [
                VMEM((blocks, per, FREQ), jnp.int32),
                SMEM((blocks, per, FREQ), jnp.int32),
                SMEM((list_spots(blocks, chunks)[2], FREQ), jnp.int32),
                VMEM((blocks, per, FREQ), F32),
                VMEM((3, block_rows + 8, FREQ), F32),
                VMEM((blocks * per, IMG, FREQ), F32),
                pltpu.SemaphoreType.DMA((blocks + 1,)),
            ],
            6 if n_cls == 4 else 40, 3.0 * blocks, (first, *flat, *earlier, rf, power, scoring),
        )

    def join(got):
        (joined,) = call(
            join_kernel, "join", [VMEM] * (nz - 1),
            [(SHAPE(((nz - 1) * per * 2 * depth, FREQ), BF16), VMEM)], [], 2, 0.5, got,
        )
        return joined

    if n_cls == 4:
        cut = per // 2 * IMG
        scored = [score([(after(message, sliced[0]),)])]
        ready = (scored[0][1], sliced[1])
        message_1, message_2 = after(message_1, *ready), after(message_2, *ready)
        message_3 = (swap(message_1[:cut], "cls", 2), swap(message_2[cut:], "cls", 1))
        messages = [(message,), (message_1,), (message_2,), message_3]
        scored += [score(messages[1:3])]
        joined = join([after(sliced[0], scored[1][1], *message_3)] + sliced[1:])
        joined_1, joined_2 = swap(joined, "cls", 1), swap(joined, "cls", 2)
        scored += [score(messages[3:], scored)]
    else:
        messages = [(message,)] + [(swap(message, "cls", d),) for d in range(1, n_cls)]
        scored = [score(messages)]
        joined = join(sliced)
        images = [joined] + [swap(joined, "cls", d) for d in range(1, n_cls)]
        pieces = (1,) * n_cls
    calls = (1, 2, 1) if n_cls == 4 else (n_cls,)
    arrays = tuple(len(m) for m in messages)
    stats = scored[-1][1]
    all_stats = [stats] + [swap(stats, "cls", d) for d in range(1, n_cls)]
    ints = [s[3] for s in scored]
    list_lines = sum(one.shape[0] for one in ints)
    flat = [m for held in messages for m in held]

    lines = n_cls * block_rows // 2
    packed, den, mass, log_mass, *outgoing = call(
        functools.partial(weights_kernel, len(calls), n_cls, nz, cls_dev), "weights",
        [SMEM] + [VMEM] * (2 * n_cls + 3 * len(calls)),
        [
            (SHAPE((lines, FREQ), BF16), VMEM),
            (SHAPE((depth, FREQ), F32), VMEM),
            (SHAPE((8, FREQ), F32), VMEM),
            (SHAPE((per, ROTS), F32), VMEM),
        ]
        + [(SHAPE((-(-(lines + depth + 8 + list_lines) // 16) * 16, FREQ), BF16), VMEM)] * (nz - 1),
        [VMEM((2 * lines, ROTS), F32), VMEM((nz, depth, FREQ), F32)],
        4 if n_cls == 4 else 12, 2.0,
        (
            grp, *all_stats, *(s[0] for s in scored), *(s[2] for s in scored),
            *(held[-1] for held in messages), *ints,
        ),
    )
    incoming = [swap(one, "grp", 2 * d) for d, one in enumerate(outgoing, start=1)]
    if n_cls == 4:
        cut = joined.shape[0] // 2
        joined_1, joined_2 = after(joined_1, packed), after(joined_2, packed)
        joined_3 = [swap(joined_1[:cut], "cls", 2), swap(joined_2[cut:], "cls", 1)]
        images = [joined, joined_1, joined_2, *joined_3]
        pieces = (1, 1, 1, 2)
    (first_sums,) = call(
        functools.partial(own_sum_kernel, chunks, calls, arrays), "own_sum",
        [SMEM] + [VMEM] * (len(flat) + 4 + len(calls)),
        [(SHAPE((cls_dev, 2, 2, width, FREQ), F32), VMEM)],
        [
            VMEM((2, 2 * lines + 8, FREQ), F32),
            *(SMEM(one.shape, jnp.int32) for one in ints),
            pltpu.SemaphoreType.DMA((len(ints),)),
        ],
        4 if n_cls == 4 else 12, 3.0, (grp, packed, *ints, *flat, *phases),
    )
    tile = (2 * width, FREQ)
    sums = []
    for chunk, (start, size) in enumerate(chunks):
        more = chunk == 0
        outs = [
            (SHAPE((size,) + tile, F32), VMEM),
            (SHAPE((size + more,) + tile, BF16), VMEM),
        ]
        scratch = [
            VMEM((size, 2, 2, width, FREQ), F32),
            VMEM((nz - 1, list_lines, FREQ), jnp.int32),
            SMEM((nz - 1, list_lines, FREQ), jnp.int32),
            pltpu.SemaphoreType.DMA((nz - 1,)),
        ]
        if more:
            outs += [
                (SHAPE((width, FREQ), F32), VMEM),
                (SHAPE((8, FREQ), F32), VMEM),
                (SHAPE((2, (nz - 1) * (2 * lines + 8), FREQ), F32), VMEM),
            ]
            scratch = scratch[:1] + [VMEM((2, width, FREQ), F32)] + scratch[1:]
            args = (grp, *images, *incoming, first_sums, *phases, den, mass)
        else:
            args = (grp, *images, *incoming, first_sums, wcs)
        own, sib, *others = call(
            functools.partial(sum_kernel, chunk, chunks, calls, nz, pieces), "sum",
            [SMEM] + [VMEM] * (len(args) - 1), outs, scratch, 3 if n_cls == 4 else 24, 3.0, args,
        )
        if more:
            den, mass, wcs = others
        sums.append((own, sib))

    particle_total = per * n_grp * n_cls
    divided, inverse, share = [], None, None
    for chunk, (own, sib) in enumerate(sums):
        start, cut = chunks[chunk]
        other = swap(sib, "grp", 1)
        averaged_out = (SHAPE((cut,) + tile, BF16), VMEM)
        if chunk == 0:
            averaged, share, inverse = call(
                functools.partial(first_divide_kernel, K / particle_total, start), "divide",
                [VMEM] * 5,
                [averaged_out, (SHAPE((1, FREQ), F32), VMEM), (SHAPE((width, FREQ), F32), VMEM)],
                [], 2, 1.0, (own, other, den, mass, own_reg),
            )
        else:
            (averaged,) = call(
                functools.partial(next_divide_kernel, start), "divide", [VMEM] * 3,
                [averaged_out], [], 2, 1.0, (own, other, inverse),
            )
        divided.append(averaged)

    averages = None
    for chunk, averaged in enumerate(divided):
        start, cut = chunks[chunk]
        if nz == 4:
            across = swap(averaged, "grp", 4)
            across = after(across, averages if chunk > 0 else divided[-1])
            slices = [averaged, swap(averaged, "grp", 2), across, swap(across, "grp", 2)]
        else:
            slices = [averaged] + [swap(averaged, "grp", 2 * d) for d in range(1, nz)]
        has_out = chunk > 0
        slices = slices + [swap(s, "grp", 1) for s in slices]
        (averages,) = call(
            functools.partial(spread_kernel, nz, start, has_out), "spread",
            [SMEM] + [VMEM] * (2 * nz) + [HBM] * has_out,
            [(SHAPE((cls_dev, FEAT), F32), HBM)],
            [
                VMEM((IMG * (-(-cut // 8) * 8), FREQ), F32),
                VMEM((cut, FEAT), F32),
                pltpu.SemaphoreType.DMA,
            ],
            6, 2.0, (grp, *slices) + ((averages,) if has_out else ()),
            input_output_aliases={2 * nz + 1: 0} if has_out else {},
        )
    return (averages, share[0, :cls_dev], log_mass[:, 0])


def solution(mesh):
    return jax.shard_map(
        per_device,
        mesh=mesh,
        in_specs=(
            P(("grp", "cls"), None),
            P(("grp", "cls"), None),
            P(("grp", "cls")),
            P(("grp", "cls")),
            P(),
            P(),
            P("cls", None),
            P("cls"),
            P(),
        ),
        out_specs=(P("cls", None), P("cls"), P(("grp", "cls"))),
        check_vma=False,
    )
```

```python
import functools
import math

import jax
import jax.numpy as jnp
import numpy as np
from jax import lax
from jax.experimental import pallas as pl
from jax.experimental.pallas import tpu as pltpu
from jax.sharding import PartitionSpec as P

SHELLS = 64
FREQ = 128
FEAT = 16384
ROTS = 64
K = 208
CAND = 8
MOST = 2
IMG = 2 * SHELLS
UNROLL = 4
LOW = -1e30
HIGH = lax.Precision.HIGHEST
VMEM = pltpu.VMEM
SMEM = pltpu.SMEM
HBM = pltpu.HBM
F32 = jnp.float32
BF16 = jnp.bfloat16
SHAPE = jax.ShapeDtypeStruct


def tables():
    turns = np.arange(ROTS)[:, None]
    orders = np.arange(FREQ)[None, :]
    angles = ((turns * orders) % ROTS).astype(np.float32) * np.float32(2.0 * math.pi / ROTS)
    cos_tab = np.cos(angles).astype(np.float32)
    sin_tab = np.sin(angles).astype(np.float32)
    last = np.zeros((FREQ, ROTS), np.float32)
    last[:SHELLS] = -0.5
    last[SHELLS] = 1.0
    scoring = np.concatenate([cos_tab.T, sin_tab.T, last], axis=0)
    left = np.concatenate([cos_tab, sin_tab], axis=1)
    terms = []
    for _ in range(2):
        term = left.astype(jnp.bfloat16)
        left = left - term.astype(np.float32)
        blank = np.zeros_like(term)
        terms.append(np.block([[term, blank], [blank, term]]))
    return scoring, np.concatenate(terms, axis=0)


def lanes_of(shape):
    return lax.broadcasted_iota(jnp.int32, shape, len(shape) - 1)


def list_room(chunks):
    return FREQ if max(n for _, n in chunks) * MOST + UNROLL > FREQ // 2 else FREQ // 2


def list_lines(owners, chunks):
    lines = -(-owners * len(chunks) * list_room(chunks) // FREQ)
    return lines, -(-(2 * lines + 1) // 16) * 16


def list_spot(owner, chunk, chunks):
    number = owner * len(chunks) + chunk
    at = number * list_room(chunks)
    return number, quot(at, FREQ), rest(at, FREQ)


def quot(v, n):
    return v >> (n.bit_length() - 1) if n & (n - 1) == 0 else v // n


def rest(v, n):
    return v & (n - 1) if n & (n - 1) == 0 else v % n


def odd_tiles(rows):
    return (-(-rows // 8) | 1) * 8


def rounded(v):
    return v.astype(BF16).astype(F32)


def row_of(x, r, depth):
    return r // depth * 2 * depth + x * depth + r % depth


def parts_of(image, depth):
    pieces = image.reshape(image.shape[0] // (2 * depth), 2, depth, FREQ)
    return pieces[:, 0], pieces[:, 1]


def chunks_of(cls_dev):
    cut = cls_dev // 2 // 8 * 8
    return ((cut, cls_dev - cut), (0, cut)) if cut else ((0, cls_dev),)


def block_lists(named, owners, cls_dev, chunks):
    per = named.shape[0]
    pairs = per * CAND
    square = (pairs, pairs)
    wide = jnp.broadcast_to(named[:, None, :], (per, CAND, CAND)).reshape(pairs, CAND)
    own = lax.broadcasted_iota(jnp.int32, wide.shape, 0) % CAND == lanes_of(wide.shape)
    cls = jnp.broadcast_to(jnp.sum(jnp.where(own, wide, 0.0), axis=1, keepdims=True), square)
    owner = sum((cls >= o * cls_dev).astype(F32) for o in range(1, owners))
    local = cls - owner * cls_dev
    number = owner * len(chunks)
    if len(chunks) > 1:
        number = number + (local < chunks[0][0]).astype(F32)
    row = lax.broadcasted_iota(jnp.int32, square, 0)
    lane = lanes_of(square)

    def across(column):
        return jnp.sum(jnp.where(row == lane, column, 0.0), axis=0, keepdims=True)

    earlier = jnp.logical_and(number == across(number), lane < row)
    place = jnp.sum(earlier.astype(F32), axis=1, keepdims=True)
    room = list_room(chunks)
    lines, height = list_lines(owners, chunks)
    slots = lines * FREQ
    target = (number[:, :1] * room + place).astype(jnp.int32)
    hot = (target == lanes_of((pairs, slots))).astype(F32).astype(BF16)
    values = jnp.concatenate(
        [
            lanes_of((1, pairs)).astype(F32), across(local), jnp.ones((1, pairs), F32),
            jnp.zeros((5, pairs), F32),
        ],
        axis=0,
    ).astype(BF16)
    placed = jnp.dot(values, hot, preferred_element_type=F32)
    slot = lanes_of((1, slots))
    start = jnp.zeros((1, slots), F32)
    for c, (first, _) in enumerate(chunks):
        start = jnp.where(quot(slot, room) % len(chunks) == c, float(first), start)
    empty = 1.0 - placed[2:3]
    rows_line = placed[0:1] + empty * pairs
    cls_line = placed[1:2] + empty * start
    counts = jnp.sum((number == lane.astype(F32)).astype(F32), axis=0, keepdims=True)
    counts = quot(counts.astype(jnp.int32) + UNROLL - 1, UNROLL).astype(F32)
    cut = [v[:, n * FREQ : (n + 1) * FREQ] for v in (rows_line, cls_line) for n in range(lines)]
    return jnp.concatenate(
        cut + [counts, jnp.zeros((height - 2 * lines - 1, FREQ), F32)], axis=0
    )


def weigh_kernel(
    slices, owners, cls_dev, chunks, grp_s, particles_h, cand_h, groups_h, entries_h, ctf_h, prec_h, message_out, *refs
):
    slice_outs = refs[: slices - 1]
    particles, cand, groups, entries, ctf, prec, hot_g, hot_e, spread, sem = refs[slices - 1 :]
    depth = SHELLS // slices
    z = grp_s[0] // 2
    copies = [
        pltpu.make_async_copy(a, b, sem.at[n])
        for n, (a, b) in enumerate(
            (
                (groups_h, groups), (entries_h, entries), (ctf_h, ctf), (prec_h, prec),
                (cand_h, cand), (particles_h, particles),
            )
        )
    ]
    for copy in copies:
        copy.start()
    per = particles.shape[0]
    pad = spread.shape[0] // IMG
    for copy in copies[:2]:
        copy.wait()
    for i in range(per):
        hot_g[i : i + 1, :] = (lanes_of((1, hot_g.shape[1])) == groups[i]).astype(F32)
        hot_e[i : i + 1, :] = (lanes_of((1, hot_e.shape[1])) == entries[i]).astype(F32)
    for copy in copies[2:5]:
        copy.wait()
    p = jnp.dot(hot_g[...], prec[...], precision=HIGH, preferred_element_type=F32)
    c = lax.dot_general(
        hot_e[...], ctf[...], (((1,), (1,)), ((), ())), precision=HIGH, preferred_element_type=F32
    )
    eye = (lanes_of((per, per)) == lax.broadcasted_iota(jnp.int32, (per, per), 0)).astype(F32)
    named = lax.dot_general(
        eye, cand[...].astype(F32), (((1,), (1,)), ((), ())), precision=HIGH,
        preferred_element_type=F32,
    )
    factors = p * c
    extra = jnp.concatenate(
        [factors * c, named, jnp.zeros((per, FREQ - SHELLS - CAND), F32)], axis=1
    )
    message_out[per * IMG : per * (IMG + 1), :] = extra.astype(BF16)
    message_out[per * (IMG + 1) :, :] = block_lists(named, owners, cls_dev, chunks).astype(BF16)
    copies[5].wait()
    for r in range(SHELLS):
        factor = jnp.broadcast_to(factors[:, r : r + 1], (per, FREQ))
        for x in range(2):
            at = x * SHELLS + r
            piece = particles[:, at * FREQ : (at + 1) * FREQ].astype(F32) * factor
            at = row_of(x, r, depth)
            spread[at * pad : at * pad + per, :] = rounded(piece)
    rows = 2 * depth
    for i in range(per):
        message_out[i * IMG : (i + 1) * IMG, :] = spread[i : i + IMG * pad : pad, :].astype(BF16)
        for d, out in enumerate(slice_outs, start=1):
            row = pl.multiple_of(i * IMG + (z ^ d) * rows, rows)
            out[i * rows : (i + 1) * rows, :] = message_out[pl.ds(row, rows), :]


def prep_kernel(depth, grp_s, refs_h, *rest_refs):
    tables_h, (reg_h, prior), rest_refs = rest_refs[:2], rest_refs[2:4], rest_refs[4:]
    (rf_out, pow_out), tables_out, (reg_out,) = rest_refs[:2], rest_refs[2:4], rest_refs[4:5]
    refs, spread, reg, sem = rest_refs[5:]
    cls_dev = refs.shape[0]
    pad = spread.shape[0] // IMG
    parts = sem.shape[0] - 3
    step = FEAT // parts
    tables_in = [
        pltpu.make_async_copy(a, b, sem.at[parts + n])
        for n, (a, b) in enumerate(zip((*tables_h, reg_h), (*tables_out, reg)))
    ]
    copies = [
        pltpu.make_async_copy(
            refs_h.at[:, pl.ds(n * step, step)], refs.at[:, pl.ds(n * step, step)], sem.at[n]
        )
        for n in range(parts)
    ]
    turns = parts // 2
    for n in range(turns):
        copies[n].start()
        copies[n + turns].start()
    for copy in tables_in:
        copy.start()

    def shell(r, power):
        parts = []
        for x in range(2):
            at = x * SHELLS + r
            piece = refs[:, pl.ds(pl.multiple_of(at * FREQ, FREQ), FREQ)].astype(F32)
            at = row_of(x, r, depth)
            spread[pl.ds(pl.multiple_of(at * pad, 8), cls_dev), :] = piece
            parts.append(piece * piece)
        total = jnp.sum(parts[0] + parts[1], axis=1, keepdims=True)
        return jnp.where(lanes_of((cls_dev, FREQ)) == r, total, power)

    power = jnp.zeros((cls_dev, FREQ), F32)
    for n in range(turns):
        copies[n].wait()
        copies[n + turns].wait()
        low, high = n * SHELLS // turns, (n + 1) * SHELLS // turns
        power = lax.fori_loop(low, high, shell, power, unroll=4)
    line = jnp.broadcast_to(prior[...].astype(F32).reshape(1, cls_dev), (cls_dev, cls_dev))
    diagonal = lax.broadcasted_iota(jnp.int32, line.shape, 0) == lanes_of(line.shape)
    column = jnp.sum(jnp.where(diagonal, line, 0.0), axis=1, keepdims=True)
    pow_out[...] = jnp.where(lanes_of((cls_dev, FREQ)) == SHELLS, column, power)

    def image(k, _):
        rf_out[k] = spread[pl.ds(k, IMG, stride=pad), :]
        return 0

    lax.fori_loop(0, cls_dev, image, 0, unroll=4)
    for copy in tables_in:
        copy.wait()
    width = reg_out.shape[0]
    for r in range(width):
        reg_out[r : r + 1, :] = jnp.full((1, FREQ), reg[grp_s[0] * width + r], F32)


def take(refs, counts):
    taken = []
    for count in counts:
        taken.append(refs[:count])
        refs = refs[count:]
    return taken, refs


def score_kernel(arrays, earlier, depth, chunks, half, first_s, owner_s, *refs):
    blocks = len(arrays)
    messages, refs = take(refs, arrays)
    (earlier_stats,), refs = take(refs, (earlier,))
    rf, power, scoring = refs[:3]
    scores_out, stats_out, cls_out = refs[3:-6]
    ints_v, ints_s, side, ex, w32, sem = refs[-6:]
    per = side.shape[1]
    height = ints_v.shape[1]
    cls_dev = rf.shape[0]
    block_rows = per * CAND
    first = first_s[0]
    table = scoring[...]
    done = 0
    for one in earlier_stats:
        stats_out[done : done + one.shape[0], :] = one[...]
        done += one.shape[0]

    extras = []
    for b in range(blocks):
        last = messages[b][-1]
        end = last.shape[0] - height
        ints_v[b] = last[end:, :].astype(F32).astype(jnp.int32)
        extras.append(last[end - per : end, :].astype(F32))
    copies = [pltpu.make_async_copy(ints_v.at[b], ints_s.at[b], sem.at[b]) for b in range(blocks)]
    for copy in copies:
        copy.start()
    for b in range(blocks):
        lane = lanes_of((per, FREQ))
        side[b] = jnp.where(lane < SHELLS, extras[b], (lane == SHELLS).astype(F32))
        begin = 0
        for one in messages[b]:
            count = one.shape[0] // IMG

            def widen(i, _):
                w32[b * per + begin + i] = one[pl.ds(pl.multiple_of(i * IMG, IMG), IMG), :].astype(F32)
                return 0

            lax.fori_loop(0, count, widen, 0, unroll=2)
            begin += count
    for copy in copies:
        copy.wait()

    for b in range(blocks):
        for c in range(len(chunks)):
            number, line, lane = list_spot(owner_s[0], c, chunks)

            def pairs(step, _):
                for u in range(UNROLL):
                    row = ints_s[b, line, lane + step * UNROLL + u]
                    k = ints_s[b, line + half, lane + step * UNROLL + u]
                    i = jnp.minimum(quot(row, CAND), per - 1)
                    w_re, w_im = parts_of(w32[b * per + i], depth)
                    a_re, a_im = parts_of(rf[k], depth)
                    inner = (w_re * a_re + w_im * a_im).reshape(SHELLS, FREQ)
                    outer = (w_re * a_im - w_im * a_re).reshape(SHELLS, FREQ)
                    ex[0, pl.ds(row, 1), :] = jnp.sum(inner, axis=0, keepdims=True)
                    ex[1, pl.ds(row, 1), :] = jnp.sum(outer, axis=0, keepdims=True)
                    ex[2, pl.ds(row, 1), :] = side[b, pl.ds(i, 1), :] * power[pl.ds(k, 1), :]
                return 0

            lax.fori_loop(0, ints_s[b, 2 * half, number], pairs, 0)

        wide = jnp.broadcast_to(
            extras[b][:, None, :], (per, CAND, FREQ)
        ).reshape(block_rows, FREQ)
        own = lanes_of((block_rows, FREQ)) == SHELLS + (
            lax.broadcasted_iota(jnp.int32, (block_rows, FREQ), 0) % CAND
        )
        column = jnp.sum(jnp.where(own, wide, 0.0), axis=1, keepdims=True) - first.astype(F32)
        cls_out[b * block_rows : (b + 1) * block_rows, :] = jnp.broadcast_to(
            column, (block_rows, FREQ)
        )
        good = jnp.logical_and(column >= 0, column < cls_dev)
        values = jnp.zeros((block_rows, ROTS), F32)
        for part in range(3):
            values = values + jnp.dot(
                jnp.where(good, ex[part, :block_rows, :], 0.0),
                table[part * FREQ : (part + 1) * FREQ],
                precision=HIGH,
                preferred_element_type=F32,
            )
        scores = jnp.where(good, values, LOW)
        scores_out[b * block_rows : (b + 1) * block_rows, :] = scores
        top = jnp.broadcast_to(jnp.max(scores, axis=1, keepdims=True), (block_rows, ROTS))
        best = jnp.max(top.reshape(per, CAND, ROTS), axis=1)
        best_rows = jnp.broadcast_to(best[:, None, :], (per, CAND, ROTS)).reshape(block_rows, ROTS)
        mass = jnp.where(good, jnp.exp(scores - best_rows), 0.0)
        mass = jnp.broadcast_to(jnp.sum(mass, axis=1, keepdims=True), (block_rows, ROTS))
        total = jnp.sum(mass.reshape(per, CAND, ROTS), axis=1)
        stats_out[done + b * per : done + (b + 1) * per, :ROTS] = best
        stats_out[done + b * per : done + (b + 1) * per, ROTS:] = total


def two(v):
    return jnp.where(lanes_of(v.shape) < ROTS, rounded(v), v - rounded(v))


def one_of_two(v):
    return v + pltpu.roll(v, ROTS, 1)


def weights_kernel(calls, blocks, slices, cls_dev, chunks, grp_s, owner_s, *refs):
    stats = refs[:blocks]
    scores = refs[blocks : blocks + calls]
    classes = refs[blocks + calls : blocks + 2 * calls]
    extras = refs[blocks + 2 * calls : 2 * blocks + 2 * calls]
    refs = refs[2 * blocks + 2 * calls :]
    own_out, den_out, mass_out, log_out, ints_out = refs[:5]
    message_outs = refs[5:-3]
    rows_v, den_v, lists_v = refs[-3:]
    per = log_out.shape[0]
    block_rows = per * CAND
    depth = SHELLS // slices
    z = grp_s[0] // 2

    den = jnp.zeros((FREQ, FREQ), F32)
    mass = jnp.zeros((1, FREQ), F32)
    block = 0
    for scores_ref, cls_ref in zip(scores, classes):
        for b in range(scores_ref.shape[0] // block_rows):
            ones = [stats[d][(block ^ d) * per : ((block ^ d) + 1) * per, :] for d in range(blocks)]
            best = functools.reduce(jnp.maximum, [one[:, :ROTS] for one in ones])
            total = sum(one[:, ROTS:] * jnp.exp(one[:, :ROTS] - best) for one in ones)
            if block == 0:
                log_out[...] = jnp.log(total)

            def over_rows(v):
                return jnp.broadcast_to(v[:, None, :], (per, CAND, ROTS)).reshape(block_rows, ROTS)

            at = slice(b * block_rows, (b + 1) * block_rows)
            weights = jnp.exp(scores_ref[at, :] - over_rows(best)) / over_rows(total)
            local = cls_ref[at, :]
            good = jnp.logical_and(local >= 0, local < cls_dev)[:, :ROTS]
            weights = rounded(jnp.where(good, weights, 0.0))
            rows_v[block * block_rows : (block + 1) * block_rows, :] = weights
            pair_sum = jnp.sum(weights, axis=1, keepdims=True)
            twice = (lanes_of((block_rows, FREQ)) % ROTS).astype(F32)
            chosen = jnp.where(twice == local, pair_sum, 0.0)
            by_particle = jnp.sum(chosen.reshape(per, CAND, FREQ), axis=1)
            end = extras[block].shape[0] - lists_v.shape[0]
            side = extras[block][end - per : end, :].astype(F32)
            den = den + lax.dot_general(
                side, by_particle, (((0,), (0,)), ((), ())), precision=HIGH,
                preferred_element_type=F32,
            )
            mass = mass + jnp.sum(by_particle, axis=0, keepdims=True)
            block += 1

    lines = rows_v.shape[0] // 2
    packed = jnp.concatenate([rows_v[:lines, :], rows_v[lines:, :]], axis=1).astype(BF16)
    own_out[...] = packed
    den_v[...] = den[:SHELLS].reshape(slices, depth, FREQ)
    mass_rows = jnp.broadcast_to(mass, (8, FREQ))
    mass_out[...] = mass_rows
    den_out[...] = den_v[z]
    half = list_lines(blocks, chunks)[0]
    _, line, _ = list_spot(owner_s[0], 0, chunks)
    lists = []
    for one in extras:
        lists_v[...] = one[one.shape[0] - lists_v.shape[0] :, :].astype(F32)
        for at in (line, line + half, 2 * half):
            lists.append(lists_v[pl.ds(at, 1), :])
    if ints_out.shape[0] > len(lists):
        lists.append(jnp.zeros((ints_out.shape[0] - len(lists), FREQ), F32))
    lists = jnp.concatenate(lists, axis=0)
    ints_out[...] = lists.astype(jnp.int32)
    tail = [two(mass_rows), lists]
    tail_rows = depth + sum(one.shape[0] for one in tail)
    spare = message_outs[0].shape[0] - lines - tail_rows
    if spare:
        tail.append(jnp.zeros((spare, FREQ), F32))
    for d, out in enumerate(message_outs, start=1):
        out[:lines, :] = packed
        out[lines:, :] = jnp.concatenate([two(den_v[z ^ d])] + tail, axis=0).astype(BF16)


def put_phases(packed, table, wcs, base):
    lines = packed.shape[0]
    twice = jnp.concatenate([packed, packed], axis=1)
    both = rounded(jnp.dot(twice, table[...], preferred_element_type=F32))
    for place in range(2):
        for part in range(2):
            at = (2 * place + part) * FREQ
            row = base + place * lines
            wcs[part, row : row + lines, :] = both[:, at : at + FREQ]
    for part in range(2):
        wcs[part, base + 2 * lines : base + 2 * lines + 8, :] = jnp.zeros((8, FREQ), F32)


def add_pair(image, row, k, wcs, num):
    shape = num.shape[1:]
    image = image.astype(F32)
    half = image.shape[0] // 2
    w_re, w_im = image[:half].reshape(shape[1:]), image[half:].reshape(shape[1:])
    c = wcs[0, pl.ds(row, 1), :].reshape(1, 1, FREQ)
    s = wcs[1, pl.ds(row, 1), :].reshape(1, 1, FREQ)
    num[k, 0] += w_re * c - w_im * s
    num[k, 1] += w_re * s + w_im * c


def pick_image(arrays, begin, i, rows, stride, offset):
    def rows_at(one, i):
        return one[pl.ds(pl.multiple_of(i * stride + offset, rows), rows), :]

    held = [one.shape[0] // stride for one in arrays]
    while len(arrays) > 1 and begin >= held[0]:
        arrays, begin, held = arrays[1:], begin - held[0], held[1:]
    if len(arrays) == 1:
        return rows_at(arrays[0], begin + i)
    cut = held[0] - begin
    return jnp.where(
        i < cut,
        rows_at(arrays[0], begin + jnp.minimum(i, cut - 1)),
        rows_at(arrays[1], jnp.maximum(i - cut, 0)),
    )


def own_sum_kernel(chunks, arrays, grp_s, owner_s, packed, ints, *refs):
    messages, refs = take(refs, arrays)
    phases, (num, wcs, ints_s, sem) = refs[:1], refs[1:]
    copy = pltpu.make_async_copy(ints, ints_s, sem)
    copy.start()
    per = sum(one.shape[0] for one in messages[0]) // IMG
    rows = 2 * num.shape[2] * num.shape[3]
    z = grp_s[0] // 2
    put_phases(packed[...], phases[0], wcs, 0)
    num[...] = jnp.zeros_like(num)
    copy.wait()
    for block, held_in in enumerate(messages):
        base = block * per * CAND
        for c in range(len(chunks)):
            number, _, lane = list_spot(owner_s[0], c, chunks)

            def pairs(step, _):
                for u in range(UNROLL):
                    row = ints_s[3 * block, lane + step * UNROLL + u]
                    k = ints_s[3 * block + 1, lane + step * UNROLL + u]
                    i = jnp.minimum(quot(row, CAND), per - 1)
                    row = jnp.where(row == per * CAND, wcs.shape[1] - 8, base + row)
                    image = pick_image(held_in, 0, i, rows, IMG, z * rows)
                    add_pair(image, row, k, wcs, num)
                return 0

            lax.fori_loop(0, ints_s[3 * block + 2, number], pairs, 0)


def join_kernel(*refs):
    out = refs[-1]
    rows = refs[0].shape[0]
    for n, one in enumerate(refs[:-1]):
        out[n * rows : (n + 1) * rows, :] = one[...]


def sum_kernel(chunk, chunks, slices, pieces, grp_s, owner_s, *refs):
    images, refs = take(refs, pieces)
    messages, refs = refs[: slices - 1], refs[slices - 1 :]
    first, refs = refs[0], refs[1:]
    if chunk == 0:
        phases, (den_own, mass_own), refs = refs[:1], refs[1:3], refs[3:]
        own_out, sib_out, den_out, mass_out, wcs, ints_s, num, den_v, ints_v, sem = refs
    else:
        wcs, ints_s, own_out, sib_out, num = refs
    group_rows = wcs.shape[1] // (slices - 1)
    lines = (group_rows - 8) // 2
    core = grp_s[0] % 2
    start, size = chunks[chunk]
    depth = num.shape[2] * num.shape[3]
    rows = 2 * depth
    per = sum(one.shape[0] for one in images[0]) // ((slices - 1) * rows)
    if chunk == 0:
        total = ints_v.shape[1]
        for d in range(slices - 1):
            tail = messages[d][lines:, :].astype(F32)
            ints_v[d] = tail[depth + 8 : depth + 8 + total].astype(jnp.int32)
        copies = [
            pltpu.make_async_copy(ints_v.at[d], ints_s.at[d], sem.at[d]) for d in range(slices - 1)
        ]
        for copy in copies:
            copy.start()
    num[...] = first[start : start + size]
    if chunk == 0:
        den, mass = den_own[...], mass_own[...]
        for d in range(slices - 1):
            put_phases(messages[d][:lines, :], phases[0], wcs, d * group_rows)
            den = den + one_of_two(messages[d][lines:, :].astype(F32)[:depth])
            mass = mass + one_of_two(messages[d][lines:, :].astype(F32)[depth : depth + 8])
        for copy in copies:
            copy.wait()

    number, _, lane = list_spot(owner_s[0], chunk, chunks)
    for d in range(slices - 1):
        for block, held_in in enumerate(images):
            base = d * group_rows + block * per * CAND
            blank = (d + 1) * group_rows - 8

            def pairs(step, _):
                for u in range(UNROLL):
                    row = ints_s[d, 3 * block, lane + step * UNROLL + u]
                    k = ints_s[d, 3 * block + 1, lane + step * UNROLL + u]
                    i = jnp.minimum(quot(row, CAND), per - 1)
                    row = jnp.where(row == per * CAND, blank, base + row)
                    image = pick_image(held_in, d * per, i, rows, rows, 0)
                    add_pair(image, row, k - start, wcs, num)
                return 0

            lax.fori_loop(0, ints_s[d, 3 * block + 2, number], pairs, 0)

    def pack(k, _):
        own_out[k] = jnp.concatenate([num[k, 0, core], num[k, 1, core]], axis=0)
        other = jnp.concatenate([num[k, 0, 1 - core], num[k, 1, 1 - core]], axis=0)
        sib_out[k] = other.astype(BF16)
        return 0

    lax.fori_loop(0, size, pack, 0)
    if chunk == 0:
        width = num.shape[3]
        den_v[...] = den.reshape(2, width, FREQ)
        den_out[...] = den_v[core]
        mass_out[...] = mass
        sib_out[size] = jnp.concatenate([two(den_v[1 - core]), two(mass)[:width]], axis=0).astype(BF16)


def divide(own, sib, inverse, start, avg_out):
    for k in range(avg_out.shape[0]):
        column = inverse[:, start + k : start + k + 1]
        factor = jnp.concatenate([column, column], axis=0)
        avg_out[k] = ((own[k] + sib[k].astype(F32)) * factor).astype(BF16)


def first_divide_kernel(scale, start, own, sib, den, mass, reg, avg_out, share_out, inverse_out):
    cut = avg_out.shape[0]
    width = avg_out.shape[1] // 2
    tile = one_of_two(sib[cut].astype(F32))
    share_out[...] = (tile[width : width + 1] + mass[:1]) * scale
    inverse = 1.0 / (tile[:width] + den[...] + reg[...])
    inverse_out[...] = inverse
    divide(own, sib, inverse, start, avg_out)


def next_divide_kernel(start, own, sib, inverse, avg_out):
    divide(own, sib, inverse[...], start, avg_out)


def spread_kernel(planes, chunks, has_out, grp_s, *refs):
    held = 2 * len(planes) * len(chunks)
    arrays, (out, wide, columns, sem) = refs[:held], refs[held + has_out :]
    width = arrays[0].shape[1] // 2
    cls_dev = columns.shape[1]
    pad = wide.shape[0] // (len(planes) * 4 * width)
    z, h = grp_s[0] // 2, grp_s[0] % 2
    copies = []
    for n, d in enumerate(planes):
        for c, (start, cut) in enumerate(chunks):
            pair = arrays[2 * (n * len(chunks) + c) :][:2]

            def one(k, _):
                for side, array in enumerate(pair):
                    piece = array[k].astype(F32)
                    for x in range(2):
                        at = (n * 4 + side * 2 + x) * width * pad + start
                        wide[pl.ds(at + k, width, stride=pad), :] = piece[
                            x * width : (x + 1) * width
                        ]
                return 0

            lax.fori_loop(0, cut, one, 0, unroll=2)
        for side, core in enumerate((h, 1 - h)):
            for x in range(2):
                group = n * 4 + side * 2 + x
                for r in range(width):
                    at = (group * width + r) * pad
                    columns[group, :, r * FREQ : (r + 1) * FREQ] = wide[at : at + cls_dev, :]
                first = (x * SHELLS + ((z ^ d) * 2 + core) * width) * FREQ
                first = pl.multiple_of(first, width * FREQ)
                copies.append(
                    pltpu.make_async_copy(
                        columns.at[group], out.at[:, pl.ds(first, width * FREQ)], sem.at[group]
                    )
                )
                copies[-1].start()
    for copy in copies:
        copy.wait()


def whole(space):
    return pl.BlockSpec(memory_space=space)


def in_hbm(value):
    return pltpu.with_memory_space_constraint(value, HBM)


def call(kernel, name, ins, outs, scratch, mib, us, args, **more):
    cost = pl.CostEstimate(flops=0, bytes_accessed=int(us * 3.6e6), transcendentals=0)
    return pl.pallas_call(
        kernel,
        out_shape=tuple(s for s, _ in outs),
        in_specs=[whole(s) for s in ins],
        out_specs=tuple(whole(s) for _, s in outs),
        scratch_shapes=scratch,
        compiler_params=pltpu.CompilerParams(vmem_limit_bytes=mib * 2**20),
        name=name,
        cost_estimate=cost,
        **more,
    )(*args)


def swap(value, axis, distance):
    size = lax.axis_size(axis)
    return lax.ppermute(value, axis, [(i, i ^ distance) for i in range(size)])


def after(value, *others):
    return lax.optimization_barrier((value, *others))[0]


def per_device(
    particles, candidates, group_ids, ctf_ids, ctf_table, noise_prec, references, log_prior, reg
):
    n_cls = lax.axis_size("cls")
    n_grp = lax.axis_size("grp")
    per = particles.shape[0]
    cls_dev = references.shape[0]
    block_rows = per * CAND
    chunks = chunks_of(cls_dev)
    pad = odd_tiles(cls_dev)
    width = SHELLS // n_grp
    nz = n_grp // 2
    scoring, phases = (jnp.asarray(t) for t in tables())
    owner = lax.axis_index("cls").astype(jnp.int32).reshape(1)
    first = owner * cls_dev
    grp = lax.axis_index("grp").astype(jnp.int32).reshape(1)

    depth = SHELLS // nz
    message, *sliced = call(
        functools.partial(weigh_kernel, nz, n_cls, cls_dev, chunks), "weigh", [SMEM] + [HBM] * 6,
        [(SHAPE((per * (IMG + 1) + list_lines(n_cls, chunks)[1], FREQ), BF16), VMEM)]
        + [(SHAPE((per * 2 * depth, FREQ), BF16), VMEM)] * (nz - 1),
        [
            VMEM(particles.shape, BF16),
            VMEM((CAND, per), jnp.int32),
            SMEM((per,), jnp.int32),
            SMEM((per,), jnp.int32),
            VMEM(ctf_table.shape[::-1], F32),
            VMEM(noise_prec.shape, F32),
            VMEM((per, noise_prec.shape[0]), F32),
            VMEM((per, ctf_table.shape[0]), F32),
            VMEM((IMG * odd_tiles(per), FREQ), F32),
            pltpu.SemaphoreType.DMA((6,)),
        ],
        5, 2.0,
        (grp,)
        + tuple(
            in_hbm(a)
            for a in (particles, candidates.T, group_ids, ctf_ids, ctf_table.T, noise_prec)
        ),
    )

    if n_cls == 4:
        message_1, message_2 = swap(message, "cls", 1), swap(message, "cls", 2)
    sliced = [swap(one, "grp", 2 * d) for d, one in enumerate(sliced, start=1)]

    rf, power, scoring, phases, own_reg = call(
        functools.partial(prep_kernel, depth), "prep", [SMEM] + [HBM] * 4 + [VMEM],
        [(SHAPE((cls_dev, IMG, FREQ), F32), VMEM), (SHAPE((cls_dev, FREQ), F32), VMEM)]
        + [(SHAPE(t.shape, t.dtype), VMEM) for t in (scoring, phases)]
        + [(SHAPE((width, FREQ), F32), VMEM)],
        [
            VMEM(references.shape, BF16),
            VMEM((IMG * pad, FREQ), F32),
            SMEM(reg.shape, F32),
            pltpu.SemaphoreType.DMA((7,)),
        ],
        8, 4.0,
        (grp,)
        + tuple(in_hbm(a) for a in (references, scoring, phases, reg))
        + (log_prior,),
    )

    half, height = list_lines(n_cls, chunks)

    def score(part, earlier=()):
        blocks = len(part)
        flat = [m for arrays in part for m in arrays]
        earlier = tuple(s[1] for s in earlier)
        ahead = sum(s.shape[0] for s in earlier)
        counts = tuple(len(arrays) for arrays in part)
        return call(
            functools.partial(score_kernel, counts, len(earlier), depth, chunks, half), "score",
            [SMEM] * 2 + [VMEM] * (len(flat) + len(earlier) + 3),
            [
                (SHAPE((blocks * block_rows, ROTS), F32), VMEM),
                (SHAPE((ahead + blocks * per, FREQ), F32), VMEM),
                (SHAPE((blocks * block_rows, FREQ), F32), VMEM),
            ],
            [
                VMEM((blocks, height, FREQ), jnp.int32),
                SMEM((blocks, height, FREQ), jnp.int32),
                VMEM((blocks, per, FREQ), F32),
                VMEM((3, block_rows + 8, FREQ), F32),
                VMEM((blocks * per, IMG, FREQ), F32),
                pltpu.SemaphoreType.DMA((blocks,)),
            ],
            6 if n_cls == 4 else 40, 3.0 * blocks, (first, owner, *flat, *earlier, rf, power, scoring),
        )

    def join(got):
        (joined,) = call(
            join_kernel, "join", [VMEM] * (nz - 1),
            [(SHAPE(((nz - 1) * per * 2 * depth, FREQ), BF16), VMEM)], [], 2, 0.5, got,
        )
        return joined

    if n_cls == 4:
        cut = per // 2 * IMG
        scored = [score([(after(message, sliced[0]),)])]
        ready = (scored[0][1], sliced[1])
        message_1, message_2 = after(message_1, *ready), after(message_2, *ready)
        message_3 = (swap(message_1[:cut], "cls", 2), swap(message_2[cut:], "cls", 1))
        messages = [(message,), (message_1,), (message_2,), message_3]
        scored += [score(messages[1:3])]
        joined = join([after(sliced[0], scored[1][1], *message_3)] + sliced[1:])
        joined_1, joined_2 = swap(joined, "cls", 1), swap(joined, "cls", 2)
        scored += [score(messages[3:], scored)]
    else:
        messages = [(message,)] + [(swap(message, "cls", d),) for d in range(1, n_cls)]
        scored = [score(messages)]
        joined = join(sliced)
        images = [joined] + [swap(joined, "cls", d) for d in range(1, n_cls)]
        pieces = (1,) * n_cls
    arrays = tuple(len(m) for m in messages)
    stats = scored[-1][1]
    all_stats = [stats] + [swap(stats, "cls", d) for d in range(1, n_cls)]
    flat = [m for held in messages for m in held]

    lines = n_cls * block_rows // 2
    own_lists = SHAPE((-(-3 * n_cls // 8) * 8, FREQ), jnp.int32)
    outgoing_rows = -(-(lines + depth + 8 + own_lists.shape[0]) // 16) * 16
    packed, den, mass, log_mass, ints, *outgoing = call(
        functools.partial(weights_kernel, len(scored), n_cls, nz, cls_dev, chunks), "weights",
        [SMEM] * 2 + [VMEM] * (2 * n_cls + 2 * len(scored)),
        [
            (SHAPE((lines, FREQ), BF16), VMEM),
            (SHAPE((depth, FREQ), F32), VMEM),
            (SHAPE((8, FREQ), F32), VMEM),
            (SHAPE((per, ROTS), F32), VMEM),
            (own_lists, VMEM),
        ]
        + [(SHAPE((outgoing_rows, FREQ), BF16), VMEM)] * (nz - 1),
        [VMEM((2 * lines, ROTS), F32), VMEM((nz, depth, FREQ), F32), VMEM((height, FREQ), F32)],
        4 if n_cls == 4 else 12, 2.0,
        (
            grp, owner, *all_stats, *(s[0] for s in scored), *(s[2] for s in scored),
            *(held[-1] for held in messages),
        ),
    )
    incoming = [swap(one, "grp", 2 * d) for d, one in enumerate(outgoing, start=1)]
    if n_cls == 4:
        cut = joined.shape[0] // 2
        joined_1, joined_2 = after(joined_1, packed), after(joined_2, packed)
        joined_3 = [swap(joined_1[:cut], "cls", 2), swap(joined_2[cut:], "cls", 1)]
        images = [joined, joined_1, joined_2, *joined_3]
        pieces = (1, 1, 1, 2)
    (first_sums,) = call(
        functools.partial(own_sum_kernel, chunks, arrays), "own_sum",
        [SMEM] * 2 + [VMEM] * (len(flat) + 3),
        [(SHAPE((cls_dev, 2, 2, width, FREQ), F32), VMEM)],
        [
            VMEM((2, 2 * lines + 8, FREQ), F32),
            SMEM(own_lists.shape, jnp.int32),
            pltpu.SemaphoreType.DMA,
        ],
        4 if n_cls == 4 else 12, 3.0, (grp, owner, packed, ints, *flat, phases),
    )
    tile = (2 * width, FREQ)
    sums = []
    for chunk, (start, size) in enumerate(chunks):
        more = chunk == 0
        outs = [
            (SHAPE((size,) + tile, F32), VMEM),
            (SHAPE((size + more,) + tile, BF16), VMEM),
        ]
        scratch = [VMEM((size, 2, 2, width, FREQ), F32)]
        spaces = [SMEM] * 2 + [VMEM] * (sum(pieces) + nz)
        if more:
            outs += [
                (SHAPE((width, FREQ), F32), VMEM),
                (SHAPE((8, FREQ), F32), VMEM),
                (SHAPE((2, (nz - 1) * (2 * lines + 8), FREQ), F32), VMEM),
                (SHAPE((nz - 1,) + own_lists.shape, jnp.int32), SMEM),
            ]
            scratch += [
                VMEM((2, width, FREQ), F32),
                VMEM((nz - 1,) + own_lists.shape, jnp.int32),
                pltpu.SemaphoreType.DMA((nz - 1,)),
            ]
            spaces += [VMEM] * 3
            args = (grp, owner, *images, *incoming, first_sums, phases, den, mass)
        else:
            spaces += [VMEM, SMEM]
            args = (grp, owner, *images, *incoming, first_sums, wcs, lists)
        own, sib, *others = call(
            functools.partial(sum_kernel, chunk, chunks, nz, pieces), "sum",
            spaces, outs, scratch, 3 if n_cls == 4 else 24, 3.0, args,
        )
        if more:
            den, mass, wcs, lists = others
        sums.append((own, sib))

    particle_total = per * n_grp * n_cls
    divided, inverse, share = [], None, None
    for chunk, (own, sib) in enumerate(sums):
        start, cut = chunks[chunk]
        other = swap(sib, "grp", 1)
        averaged_out = (SHAPE((cut,) + tile, BF16), VMEM)
        if chunk == 0:
            averaged, share, inverse = call(
                functools.partial(first_divide_kernel, K / particle_total, start), "divide",
                [VMEM] * 5,
                [averaged_out, (SHAPE((1, FREQ), F32), VMEM), (SHAPE((width, FREQ), F32), VMEM)],
                [], 2, 0.05, (own, other, den, mass, own_reg),
            )
        else:
            (averaged,) = call(
                functools.partial(next_divide_kernel, start), "divide", [VMEM] * 3,
                [averaged_out], [], 2, 0.05, (own, other, inverse),
            )
        divided.append(averaged)

    if nz == 4:
        near = [swap(averaged, "grp", 2) for averaged in divided]
        across = [swap(averaged, "grp", 4) for averaged in divided]
        near, across = lax.optimization_barrier((near, across))
        relayed = [swap(one, "grp", 2) for one in across]
        planes = [list(held) for held in zip(divided, near, across, relayed)]
    else:
        planes = [
            [averaged] + [swap(averaged, "grp", 2 * d) for d in range(1, nz)]
            for averaged in divided
        ]
    averages = None
    for far in ((0, 1, 2), (3,)) if nz == 4 else (tuple(range(nz)),):
        arrays = []
        for d in far:
            for held in planes:
                one = held[d] if averages is None else after(held[d], averages)
                arrays += [one, swap(one, "grp", 1)]
        has_out = averages is not None
        groups = len(far) * 4
        (averages,) = call(
            functools.partial(spread_kernel, far, chunks, has_out), "spread",
            [SMEM] + [VMEM] * len(arrays) + [HBM] * has_out,
            [(SHAPE((cls_dev, FEAT), F32), HBM)],
            [
                VMEM((groups * width * odd_tiles(cls_dev), FREQ), F32),
                VMEM((groups, cls_dev, width * FREQ), F32),
                pltpu.SemaphoreType.DMA((groups,)),
            ],
            8, 0.05, (grp, *arrays) + ((averages,) if has_out else ()),
            input_output_aliases={len(arrays) + 1: 0} if has_out else {},
        )
    return (averages, share[0, :cls_dev], log_mass[:, 0])


def solution(mesh):
    return jax.shard_map(
        per_device,
        mesh=mesh,
        in_specs=(
            P(("grp", "cls"), None),
            P(("grp", "cls"), None),
            P(("grp", "cls")),
            P(("grp", "cls")),
            P(),
            P(),
            P("cls", None),
            P("cls"),
            P(),
        ),
        out_specs=(P("cls", None), P("cls"), P(("grp", "cls"))),
        check_vma=False,
    )
```

```python
import functools
import math

import jax
import jax.numpy as jnp
import numpy as np
from jax import lax
from jax.experimental import pallas as pl
from jax.experimental.pallas import tpu as pltpu
from jax.sharding import PartitionSpec as P

SHELLS = 64
FREQ = 128
FEAT = 16384
ROTS = 64
K = 208
CAND = 8
MOST = 2
IMG = 2 * SHELLS
UNROLL = 4
LOW = -1e30
HIGH = lax.Precision.HIGHEST
VMEM = pltpu.VMEM
SMEM = pltpu.SMEM
HBM = pltpu.HBM
F32 = jnp.float32
BF16 = jnp.bfloat16
SHAPE = jax.ShapeDtypeStruct


def tables():
    turns = np.arange(ROTS)[:, None]
    orders = np.arange(FREQ)[None, :]
    angles = ((turns * orders) % ROTS).astype(np.float32) * np.float32(2.0 * math.pi / ROTS)
    cos_tab = np.cos(angles).astype(np.float32)
    sin_tab = np.sin(angles).astype(np.float32)
    last = np.zeros((FREQ, ROTS), np.float32)
    last[:SHELLS] = -0.5
    last[SHELLS] = 1.0
    scoring = np.concatenate([cos_tab.T, sin_tab.T, last], axis=0)
    left = np.concatenate([cos_tab, sin_tab], axis=1)
    terms = []
    for _ in range(2):
        term = left.astype(jnp.bfloat16)
        left = left - term.astype(np.float32)
        blank = np.zeros_like(term)
        terms.append(np.block([[term, blank], [blank, term]]))
    return scoring, np.concatenate(terms, axis=0)


def lanes_of(shape):
    return lax.broadcasted_iota(jnp.int32, shape, len(shape) - 1)


def list_room(chunks):
    return FREQ if max(n for _, n in chunks) * MOST + UNROLL > FREQ // 2 else FREQ // 2


def list_lines(owners, chunks):
    lines = -(-owners * len(chunks) * list_room(chunks) // FREQ)
    return lines, -(-(2 * lines + 1) // 16) * 16


def list_spot(owner, chunk, chunks):
    number = owner * len(chunks) + chunk
    at = number * list_room(chunks)
    return number, quot(at, FREQ), rest(at, FREQ)


def quot(v, n):
    return v >> (n.bit_length() - 1) if n & (n - 1) == 0 else v // n


def rest(v, n):
    return v & (n - 1) if n & (n - 1) == 0 else v % n


def odd_tiles(rows):
    return (-(-rows // 8) | 1) * 8


def rounded(v):
    return v.astype(BF16).astype(F32)


def row_of(x, r, depth):
    return r // depth * 2 * depth + x * depth + r % depth


def parts_of(image, depth):
    pieces = image.reshape(image.shape[0] // (2 * depth), 2, depth, FREQ)
    return pieces[:, 0], pieces[:, 1]


def chunks_of(cls_dev):
    cut = cls_dev // 2 // 8 * 8
    return ((cut, cls_dev - cut), (0, cut)) if cut else ((0, cls_dev),)


def block_lists(named, owners, cls_dev, chunks):
    per = named.shape[0]
    pairs = per * CAND
    square = (pairs, pairs)
    wide = jnp.broadcast_to(named[:, None, :], (per, CAND, CAND)).reshape(pairs, CAND)
    own = lax.broadcasted_iota(jnp.int32, wide.shape, 0) % CAND == lanes_of(wide.shape)
    cls = jnp.broadcast_to(jnp.sum(jnp.where(own, wide, 0.0), axis=1, keepdims=True), square)
    owner = sum((cls >= o * cls_dev).astype(F32) for o in range(1, owners))
    local = cls - owner * cls_dev
    number = owner * len(chunks)
    if len(chunks) > 1:
        number = number + (local < chunks[0][0]).astype(F32)
    row = lax.broadcasted_iota(jnp.int32, square, 0)
    lane = lanes_of(square)

    def across(column):
        return jnp.sum(jnp.where(row == lane, column, 0.0), axis=0, keepdims=True)

    earlier = jnp.logical_and(number == across(number), lane < row)
    place = jnp.sum(earlier.astype(F32), axis=1, keepdims=True)
    room = list_room(chunks)
    lines, height = list_lines(owners, chunks)
    slots = lines * FREQ
    target = (number[:, :1] * room + place).astype(jnp.int32)
    hot = (target == lanes_of((pairs, slots))).astype(F32).astype(BF16)
    values = jnp.concatenate(
        [
            lanes_of((1, pairs)).astype(F32), across(local), jnp.ones((1, pairs), F32),
            jnp.zeros((5, pairs), F32),
        ],
        axis=0,
    ).astype(BF16)
    placed = jnp.dot(values, hot, preferred_element_type=F32)
    slot = lanes_of((1, slots))
    start = jnp.zeros((1, slots), F32)
    for c, (first, _) in enumerate(chunks):
        start = jnp.where(quot(slot, room) % len(chunks) == c, float(first), start)
    empty = 1.0 - placed[2:3]
    rows_line = placed[0:1] + empty * pairs
    cls_line = placed[1:2] + empty * start
    counts = jnp.sum((number == lane.astype(F32)).astype(F32), axis=0, keepdims=True)
    counts = quot(counts.astype(jnp.int32) + UNROLL - 1, UNROLL).astype(F32)
    cut = [v[:, n * FREQ : (n + 1) * FREQ] for v in (rows_line, cls_line) for n in range(lines)]
    return jnp.concatenate(
        cut + [counts, jnp.zeros((height - 2 * lines - 1, FREQ), F32)], axis=0
    )


def weigh_kernel(
    slices, owners, cls_dev, chunks, grp_s, particles_h, cand_h, groups_h, entries_h, ctf_h, prec_h, message_out, *refs
):
    slice_outs = refs[: slices - 1]
    particles, cand, groups, entries, ctf, prec, hot_g, hot_e, spread, sem = refs[slices - 1 :]
    depth = SHELLS // slices
    z = grp_s[0] // 2
    copies = [
        pltpu.make_async_copy(a, b, sem.at[n])
        for n, (a, b) in enumerate(
            (
                (groups_h, groups), (entries_h, entries), (ctf_h, ctf), (prec_h, prec),
                (cand_h, cand), (particles_h, particles),
            )
        )
    ]
    for copy in copies:
        copy.start()
    per = particles.shape[0]
    pad = spread.shape[0] // IMG
    for copy in copies[:2]:
        copy.wait()
    for i in range(per):
        hot_g[i : i + 1, :] = (lanes_of((1, hot_g.shape[1])) == groups[i]).astype(F32)
        hot_e[i : i + 1, :] = (lanes_of((1, hot_e.shape[1])) == entries[i]).astype(F32)
    for copy in copies[2:5]:
        copy.wait()
    p = jnp.dot(hot_g[...], prec[...], precision=HIGH, preferred_element_type=F32)
    c = lax.dot_general(
        hot_e[...], ctf[...], (((1,), (1,)), ((), ())), precision=HIGH, preferred_element_type=F32
    )
    eye = (lanes_of((per, per)) == lax.broadcasted_iota(jnp.int32, (per, per), 0)).astype(F32)
    named = lax.dot_general(
        eye, cand[...].astype(F32), (((1,), (1,)), ((), ())), precision=HIGH,
        preferred_element_type=F32,
    )
    factors = p * c
    extra = jnp.concatenate(
        [factors * c, named, jnp.zeros((per, FREQ - SHELLS - CAND), F32)], axis=1
    )
    message_out[per * IMG : per * (IMG + 1), :] = extra.astype(BF16)
    message_out[per * (IMG + 1) :, :] = block_lists(named, owners, cls_dev, chunks).astype(BF16)
    copies[5].wait()
    for r in range(SHELLS):
        factor = jnp.broadcast_to(factors[:, r : r + 1], (per, FREQ))
        for x in range(2):
            at = x * SHELLS + r
            piece = particles[:, at * FREQ : (at + 1) * FREQ].astype(F32) * factor
            at = row_of(x, r, depth)
            spread[at * pad : at * pad + per, :] = rounded(piece)
    rows = 2 * depth
    for i in range(per):
        message_out[i * IMG : (i + 1) * IMG, :] = spread[i : i + IMG * pad : pad, :].astype(BF16)
        for d, out in enumerate(slice_outs, start=1):
            row = pl.multiple_of(i * IMG + (z ^ d) * rows, rows)
            out[i * rows : (i + 1) * rows, :] = message_out[pl.ds(row, rows), :]


def prep_kernel(depth, grp_s, refs_h, *rest_refs):
    tables_h, (reg_h, prior), rest_refs = rest_refs[:2], rest_refs[2:4], rest_refs[4:]
    (rf_out, pow_out), tables_out, (reg_out,) = rest_refs[:2], rest_refs[2:4], rest_refs[4:5]
    refs, spread, reg, sem = rest_refs[5:]
    cls_dev = refs.shape[0]
    pad = spread.shape[0] // IMG
    parts = sem.shape[0] - 3
    step = FEAT // parts
    tables_in = [
        pltpu.make_async_copy(a, b, sem.at[parts + n])
        for n, (a, b) in enumerate(zip((*tables_h, reg_h), (*tables_out, reg)))
    ]
    copies = [
        pltpu.make_async_copy(
            refs_h.at[:, pl.ds(n * step, step)], refs.at[:, pl.ds(n * step, step)], sem.at[n]
        )
        for n in range(parts)
    ]
    turns = parts // 2
    for n in range(turns):
        copies[n].start()
        copies[n + turns].start()
    for copy in tables_in:
        copy.start()

    def shell(r, power):
        parts = []
        for x in range(2):
            at = x * SHELLS + r
            piece = refs[:, pl.ds(pl.multiple_of(at * FREQ, FREQ), FREQ)].astype(F32)
            at = row_of(x, r, depth)
            spread[pl.ds(pl.multiple_of(at * pad, 8), cls_dev), :] = piece
            parts.append(piece * piece)
        total = jnp.sum(parts[0] + parts[1], axis=1, keepdims=True)
        return jnp.where(lanes_of((cls_dev, FREQ)) == r, total, power)

    power = jnp.zeros((cls_dev, FREQ), F32)
    for n in range(turns):
        copies[n].wait()
        copies[n + turns].wait()
        low, high = n * SHELLS // turns, (n + 1) * SHELLS // turns
        power = lax.fori_loop(low, high, shell, power, unroll=4)
    line = jnp.broadcast_to(prior[...].astype(F32).reshape(1, cls_dev), (cls_dev, cls_dev))
    diagonal = lax.broadcasted_iota(jnp.int32, line.shape, 0) == lanes_of(line.shape)
    column = jnp.sum(jnp.where(diagonal, line, 0.0), axis=1, keepdims=True)
    pow_out[...] = jnp.where(lanes_of((cls_dev, FREQ)) == SHELLS, column, power)

    def image(k, _):
        rf_out[k] = spread[pl.ds(k, IMG, stride=pad), :]
        return 0

    lax.fori_loop(0, cls_dev, image, 0, unroll=4)
    for copy in tables_in:
        copy.wait()
    width = reg_out.shape[0]
    for r in range(width):
        reg_out[r : r + 1, :] = jnp.full((1, FREQ), reg[grp_s[0] * width + r], F32)


def take(refs, counts):
    taken = []
    for count in counts:
        taken.append(refs[:count])
        refs = refs[count:]
    return taken, refs


def score_kernel(arrays, earlier, depth, chunks, half, first_s, owner_s, *refs):
    blocks = len(arrays)
    messages, refs = take(refs, arrays)
    (earlier_stats,), refs = take(refs, (earlier,))
    rf, power, scoring = refs[:3]
    scores_out, stats_out, cls_out = refs[3:-6]
    ints_v, ints_s, side, ex, w32, sem = refs[-6:]
    per = side.shape[1]
    height = ints_v.shape[1]
    cls_dev = rf.shape[0]
    block_rows = per * CAND
    first = first_s[0]
    table = scoring[...]
    done = 0
    for one in earlier_stats:
        stats_out[done : done + one.shape[0], :] = one[...]
        done += one.shape[0]

    extras = []
    for b in range(blocks):
        last = messages[b][-1]
        end = last.shape[0] - height
        ints_v[b] = last[end:, :].astype(F32).astype(jnp.int32)
        extras.append(last[end - per : end, :].astype(F32))
    copies = [pltpu.make_async_copy(ints_v.at[b], ints_s.at[b], sem.at[b]) for b in range(blocks)]
    for copy in copies:
        copy.start()
    for b in range(blocks):
        lane = lanes_of((per, FREQ))
        side[b] = jnp.where(lane < SHELLS, extras[b], (lane == SHELLS).astype(F32))
        begin = 0
        for one in messages[b]:
            count = one.shape[0] // IMG

            def widen(i, _):
                w32[b * per + begin + i] = one[pl.ds(pl.multiple_of(i * IMG, IMG), IMG), :].astype(F32)
                return 0

            lax.fori_loop(0, count, widen, 0, unroll=2)
            begin += count
    for copy in copies:
        copy.wait()

    for b in range(blocks):
        for c in range(len(chunks)):
            number, line, lane = list_spot(owner_s[0], c, chunks)

            def pairs(step, _):
                for u in range(UNROLL):
                    row = ints_s[b, line, lane + step * UNROLL + u]
                    k = ints_s[b, line + half, lane + step * UNROLL + u]
                    i = jnp.minimum(quot(row, CAND), per - 1)
                    w_re, w_im = parts_of(w32[b * per + i], depth)
                    a_re, a_im = parts_of(rf[k], depth)
                    inner = (w_re * a_re + w_im * a_im).reshape(SHELLS, FREQ)
                    outer = (w_re * a_im - w_im * a_re).reshape(SHELLS, FREQ)
                    ex[0, pl.ds(row, 1), :] = jnp.sum(inner, axis=0, keepdims=True)
                    ex[1, pl.ds(row, 1), :] = jnp.sum(outer, axis=0, keepdims=True)
                    ex[2, pl.ds(row, 1), :] = side[b, pl.ds(i, 1), :] * power[pl.ds(k, 1), :]
                return 0

            lax.fori_loop(0, ints_s[b, 2 * half, number], pairs, 0)

        wide = jnp.broadcast_to(
            extras[b][:, None, :], (per, CAND, FREQ)
        ).reshape(block_rows, FREQ)
        own = lanes_of((block_rows, FREQ)) == SHELLS + (
            lax.broadcasted_iota(jnp.int32, (block_rows, FREQ), 0) % CAND
        )
        column = jnp.sum(jnp.where(own, wide, 0.0), axis=1, keepdims=True) - first.astype(F32)
        cls_out[b * block_rows : (b + 1) * block_rows, :] = jnp.broadcast_to(
            column, (block_rows, FREQ)
        )
        good = jnp.logical_and(column >= 0, column < cls_dev)
        values = jnp.zeros((block_rows, ROTS), F32)
        for part in range(3):
            values = values + jnp.dot(
                jnp.where(good, ex[part, :block_rows, :], 0.0),
                table[part * FREQ : (part + 1) * FREQ],
                precision=HIGH,
                preferred_element_type=F32,
            )
        scores = jnp.where(good, values, LOW)
        scores_out[b * block_rows : (b + 1) * block_rows, :] = scores
        top = jnp.broadcast_to(jnp.max(scores, axis=1, keepdims=True), (block_rows, ROTS))
        best = jnp.max(top.reshape(per, CAND, ROTS), axis=1)
        best_rows = jnp.broadcast_to(best[:, None, :], (per, CAND, ROTS)).reshape(block_rows, ROTS)
        mass = jnp.where(good, jnp.exp(scores - best_rows), 0.0)
        mass = jnp.broadcast_to(jnp.sum(mass, axis=1, keepdims=True), (block_rows, ROTS))
        total = jnp.sum(mass.reshape(per, CAND, ROTS), axis=1)
        stats_out[done + b * per : done + (b + 1) * per, :ROTS] = best
        stats_out[done + b * per : done + (b + 1) * per, ROTS:] = total


def two(v):
    return jnp.where(lanes_of(v.shape) < ROTS, rounded(v), v - rounded(v))


def one_of_two(v):
    return v + pltpu.roll(v, ROTS, 1)


def weights_kernel(calls, blocks, slices, cls_dev, chunks, grp_s, owner_s, *refs):
    stats = refs[:blocks]
    scores = refs[blocks : blocks + calls]
    classes = refs[blocks + calls : blocks + 2 * calls]
    extras = refs[blocks + 2 * calls : 2 * blocks + 2 * calls]
    refs = refs[2 * blocks + 2 * calls :]
    own_out, den_out, mass_out, log_out, ints_out = refs[:5]
    message_outs = refs[5:-3]
    rows_v, den_v, lists_v = refs[-3:]
    per = log_out.shape[0]
    block_rows = per * CAND
    depth = SHELLS // slices
    z = grp_s[0] // 2

    den = jnp.zeros((FREQ, FREQ), F32)
    mass = jnp.zeros((1, FREQ), F32)
    block = 0
    for scores_ref, cls_ref in zip(scores, classes):
        for b in range(scores_ref.shape[0] // block_rows):
            ones = [stats[d][(block ^ d) * per : ((block ^ d) + 1) * per, :] for d in range(blocks)]
            best = functools.reduce(jnp.maximum, [one[:, :ROTS] for one in ones])
            total = sum(one[:, ROTS:] * jnp.exp(one[:, :ROTS] - best) for one in ones)
            if block == 0:
                log_out[...] = jnp.log(total)

            def over_rows(v):
                return jnp.broadcast_to(v[:, None, :], (per, CAND, ROTS)).reshape(block_rows, ROTS)

            at = slice(b * block_rows, (b + 1) * block_rows)
            weights = jnp.exp(scores_ref[at, :] - over_rows(best)) / over_rows(total)
            local = cls_ref[at, :]
            good = jnp.logical_and(local >= 0, local < cls_dev)[:, :ROTS]
            weights = rounded(jnp.where(good, weights, 0.0))
            rows_v[block * block_rows : (block + 1) * block_rows, :] = weights
            pair_sum = jnp.sum(weights, axis=1, keepdims=True)
            twice = (lanes_of((block_rows, FREQ)) % ROTS).astype(F32)
            chosen = jnp.where(twice == local, pair_sum, 0.0)
            by_particle = jnp.sum(chosen.reshape(per, CAND, FREQ), axis=1)
            end = extras[block].shape[0] - lists_v.shape[0]
            side = extras[block][end - per : end, :].astype(F32)
            den = den + lax.dot_general(
                side, by_particle, (((0,), (0,)), ((), ())), precision=HIGH,
                preferred_element_type=F32,
            )
            mass = mass + jnp.sum(by_particle, axis=0, keepdims=True)
            block += 1

    lines = rows_v.shape[0] // 2
    packed = jnp.concatenate([rows_v[:lines, :], rows_v[lines:, :]], axis=1).astype(BF16)
    own_out[...] = packed
    den_v[...] = den[:SHELLS].reshape(slices, depth, FREQ)
    mass_rows = jnp.broadcast_to(mass, (8, FREQ))
    mass_out[...] = mass_rows
    den_out[...] = den_v[z]
    half = list_lines(blocks, chunks)[0]
    _, line, _ = list_spot(owner_s[0], 0, chunks)
    lists = []
    for one in extras:
        lists_v[...] = one[one.shape[0] - lists_v.shape[0] :, :].astype(F32)
        for at in (line, line + half, 2 * half):
            lists.append(lists_v[pl.ds(at, 1), :])
    if ints_out.shape[0] > len(lists):
        lists.append(jnp.zeros((ints_out.shape[0] - len(lists), FREQ), F32))
    lists = jnp.concatenate(lists, axis=0)
    ints_out[...] = lists.astype(jnp.int32)
    tail = [two(mass_rows), lists]
    tail_rows = depth + sum(one.shape[0] for one in tail)
    spare = message_outs[0].shape[0] - lines - tail_rows
    if spare:
        tail.append(jnp.zeros((spare, FREQ), F32))
    for d, out in enumerate(message_outs, start=1):
        out[:lines, :] = packed
        out[lines:, :] = jnp.concatenate([two(den_v[z ^ d])] + tail, axis=0).astype(BF16)


def put_phases(packed, table, wcs, base):
    lines = packed.shape[0]
    twice = jnp.concatenate([packed, packed], axis=1)
    both = rounded(jnp.dot(twice, table[...], preferred_element_type=F32))
    for place in range(2):
        for part in range(2):
            at = (2 * place + part) * FREQ
            row = base + place * lines
            wcs[part, row : row + lines, :] = both[:, at : at + FREQ]
    for part in range(2):
        wcs[part, base + 2 * lines : base + 2 * lines + 8, :] = jnp.zeros((8, FREQ), F32)


def add_pair(image, row, k, wcs, num):
    shape = num.shape[1:]
    image = image.astype(F32)
    half = image.shape[0] // 2
    w_re, w_im = image[:half].reshape(shape[1:]), image[half:].reshape(shape[1:])
    c = wcs[0, pl.ds(row, 1), :].reshape(1, 1, FREQ)
    s = wcs[1, pl.ds(row, 1), :].reshape(1, 1, FREQ)
    num[k, 0] += w_re * c - w_im * s
    num[k, 1] += w_re * s + w_im * c


def pick_image(arrays, begin, i, rows, stride, offset):
    def rows_at(one, i):
        return one[pl.ds(pl.multiple_of(i * stride + offset, rows), rows), :]

    held = [one.shape[0] // stride for one in arrays]
    while len(arrays) > 1 and begin >= held[0]:
        arrays, begin, held = arrays[1:], begin - held[0], held[1:]
    if len(arrays) == 1:
        return rows_at(arrays[0], begin + i)
    cut = held[0] - begin
    return jnp.where(
        i < cut,
        rows_at(arrays[0], begin + jnp.minimum(i, cut - 1)),
        rows_at(arrays[1], jnp.maximum(i - cut, 0)),
    )


def own_sum_kernel(chunks, arrays, grp_s, owner_s, packed, ints, *refs):
    messages, refs = take(refs, arrays)
    phases, (num, wcs, ints_s, sem) = refs[:1], refs[1:]
    copy = pltpu.make_async_copy(ints, ints_s, sem)
    copy.start()
    per = sum(one.shape[0] for one in messages[0]) // IMG
    rows = 2 * num.shape[2] * num.shape[3]
    z = grp_s[0] // 2
    put_phases(packed[...], phases[0], wcs, 0)
    num[...] = jnp.zeros_like(num)
    copy.wait()
    for block, held_in in enumerate(messages):
        base = block * per * CAND
        for c in range(len(chunks)):
            number, _, lane = list_spot(owner_s[0], c, chunks)

            def pairs(step, _):
                for u in range(UNROLL):
                    row = ints_s[3 * block, lane + step * UNROLL + u]
                    k = ints_s[3 * block + 1, lane + step * UNROLL + u]
                    i = jnp.minimum(quot(row, CAND), per - 1)
                    row = jnp.where(row == per * CAND, wcs.shape[1] - 8, base + row)
                    image = pick_image(held_in, 0, i, rows, IMG, z * rows)
                    add_pair(image, row, k, wcs, num)
                return 0

            lax.fori_loop(0, ints_s[3 * block + 2, number], pairs, 0)


def join_kernel(*refs):
    out = refs[-1]
    rows = refs[0].shape[0]
    for n, one in enumerate(refs[:-1]):
        out[n * rows : (n + 1) * rows, :] = one[...]


def read_tail(message, lines, depth, count):
    tail = message[lines:, :].astype(F32)
    den, mass = one_of_two(tail[:depth]), one_of_two(tail[depth : depth + 8])
    return den, mass, tail[depth + 8 : depth + 8 + count].astype(jnp.int32)


def add_plane(d, chunk, chunks, owner, images, ints, base, blank, wcs, num, first_class):
    number, _, lane = list_spot(owner, chunk, chunks)
    rows = 2 * num.shape[2] * num.shape[3]
    per = FREQ // CAND
    for block, held_in in enumerate(images):

        def pairs(step, _):
            for u in range(UNROLL):
                row = ints[3 * block, lane + step * UNROLL + u]
                k = ints[3 * block + 1, lane + step * UNROLL + u]
                i = jnp.minimum(quot(row, CAND), per - 1)
                row = jnp.where(row == per * CAND, blank, base + block * per * CAND + row)
                image = pick_image(held_in, d * per, i, rows, rows, 0)
                add_pair(image, row, k - first_class, wcs, num)
            return 0

        lax.fori_loop(0, ints[3 * block + 2, number], pairs, 0)


def near_sum_kernel(chunks, pieces, owner_s, *refs):
    images, refs = take(refs, pieces)
    message, first, phases, den_in, mass_in, num, den_out, mass_out, wcs, ints_v, ints_s, sem = refs
    lines = (wcs.shape[1] - 8) // 2
    depth = den_in.shape[0]
    den, mass, ints_v[...] = read_tail(message, lines, depth, ints_v.shape[0])
    copy = pltpu.make_async_copy(ints_v, ints_s, sem)
    copy.start()
    den_out[...] = den_in[...] + den
    mass_out[...] = mass_in[...] + mass
    put_phases(message[:lines, :], phases, wcs, 0)
    num[...] = first[...]
    copy.wait()
    for chunk in range(len(chunks)):
        add_plane(0, chunk, chunks, owner_s[0], images, ints_s, 0, 2 * lines, wcs, num, 0)


def sum_kernel(chunk, chunks, slices, pieces, grp_s, owner_s, *refs):
    images, refs = take(refs, pieces)
    messages, refs = refs[: slices - 2], refs[slices - 2 :]
    first, refs = refs[0], refs[1:]
    if chunk == 0:
        phases, (den_in, mass_in), refs = refs[0], refs[1:3], refs[3:]
        own_out, sib_out, den_out, mass_out, wcs, ints_s, num, den_v, ints_v, sem = refs
    else:
        wcs, ints_s, own_out, sib_out, num = refs
    group_rows = wcs.shape[1] // (slices - 2)
    lines = (group_rows - 8) // 2
    core = grp_s[0] % 2
    start, size = chunks[chunk]
    depth = num.shape[2] * num.shape[3]

    if chunk == 0:
        den, mass = den_in[...], mass_in[...]
        for n, message in enumerate(messages):
            more_den, more_mass, ints_v[n] = read_tail(message, lines, depth, ints_v.shape[1])
            den, mass = den + more_den, mass + more_mass
        copies = [
            pltpu.make_async_copy(ints_v.at[n], ints_s.at[n], sem.at[n])
            for n in range(slices - 2)
        ]
        for copy in copies:
            copy.start()
        for n, message in enumerate(messages):
            put_phases(message[:lines, :], phases, wcs, n * group_rows)
    num[...] = first[start : start + size]
    if chunk == 0:
        for copy in copies:
            copy.wait()
    for n in range(slices - 2):
        base = n * group_rows
        blank = base + group_rows - 8
        add_plane(
            n + 1, chunk, chunks, owner_s[0], images, ints_s.at[n], base, blank, wcs, num, start
        )

    def pack(k, _):
        own_out[k] = jnp.concatenate([num[k, 0, core], num[k, 1, core]], axis=0)
        other = jnp.concatenate([num[k, 0, 1 - core], num[k, 1, 1 - core]], axis=0)
        sib_out[k] = other.astype(BF16)
        return 0

    lax.fori_loop(0, size, pack, 0)
    if chunk == 0:
        width = num.shape[3]
        den_v[...] = den.reshape(2, width, FREQ)
        den_out[...] = den_v[core]
        mass_out[...] = mass
        sib_out[size] = jnp.concatenate([two(den_v[1 - core]), two(mass)[:width]], axis=0).astype(BF16)


def divide(own, sib, inverse, start, avg_out):
    for k in range(avg_out.shape[0]):
        column = inverse[:, start + k : start + k + 1]
        factor = jnp.concatenate([column, column], axis=0)
        avg_out[k] = ((own[k] + sib[k].astype(F32)) * factor).astype(BF16)


def first_divide_kernel(scale, start, own, sib, den, mass, reg, avg_out, share_out, inverse_out):
    cut = avg_out.shape[0]
    width = avg_out.shape[1] // 2
    tile = one_of_two(sib[cut].astype(F32))
    share_out[...] = (tile[width : width + 1] + mass[:1]) * scale
    inverse = 1.0 / (tile[:width] + den[...] + reg[...])
    inverse_out[...] = inverse
    divide(own, sib, inverse, start, avg_out)


def next_divide_kernel(start, own, sib, inverse, avg_out):
    divide(own, sib, inverse[...], start, avg_out)


def spread_kernel(planes, chunks, has_out, grp_s, *refs):
    held = 2 * len(planes) * len(chunks)
    arrays, (out, wide, columns, sem) = refs[:held], refs[held + has_out :]
    width = arrays[0].shape[1] // 2
    cls_dev = columns.shape[1]
    pad = wide.shape[0] // (len(planes) * 4 * width)
    z, h = grp_s[0] // 2, grp_s[0] % 2
    copies = []
    for n, d in enumerate(planes):
        for c, (start, cut) in enumerate(chunks):
            pair = arrays[2 * (n * len(chunks) + c) :][:2]

            def one(k, _):
                for side, array in enumerate(pair):
                    piece = array[k].astype(F32)
                    for x in range(2):
                        at = (n * 4 + side * 2 + x) * width * pad + start
                        wide[pl.ds(at + k, width, stride=pad), :] = piece[
                            x * width : (x + 1) * width
                        ]
                return 0

            lax.fori_loop(0, cut, one, 0, unroll=2)
        for side, core in enumerate((h, 1 - h)):
            for x in range(2):
                group = n * 4 + side * 2 + x
                for r in range(width):
                    at = (group * width + r) * pad
                    columns[group, :, r * FREQ : (r + 1) * FREQ] = wide[at : at + cls_dev, :]
                first = (x * SHELLS + ((z ^ d) * 2 + core) * width) * FREQ
                first = pl.multiple_of(first, width * FREQ)
                copies.append(
                    pltpu.make_async_copy(
                        columns.at[group], out.at[:, pl.ds(first, width * FREQ)], sem.at[group]
                    )
                )
                copies[-1].start()
    for copy in copies:
        copy.wait()


def whole(space):
    return pl.BlockSpec(memory_space=space)


def in_hbm(value):
    return pltpu.with_memory_space_constraint(value, HBM)


def call(kernel, name, ins, outs, scratch, mib, us, args, **more):
    cost = pl.CostEstimate(flops=0, bytes_accessed=int(us * 3.6e6), transcendentals=0)
    return pl.pallas_call(
        kernel,
        out_shape=tuple(s for s, _ in outs),
        in_specs=[whole(s) for s in ins],
        out_specs=tuple(whole(s) for _, s in outs),
        scratch_shapes=scratch,
        compiler_params=pltpu.CompilerParams(vmem_limit_bytes=mib * 2**20),
        name=name,
        cost_estimate=cost,
        **more,
    )(*args)


def swap(value, axis, distance):
    size = lax.axis_size(axis)
    return lax.ppermute(value, axis, [(i, i ^ distance) for i in range(size)])


def after(value, *others):
    return lax.optimization_barrier((value, *others))[0]


def per_device(
    particles, candidates, group_ids, ctf_ids, ctf_table, noise_prec, references, log_prior, reg
):
    n_cls = lax.axis_size("cls")
    n_grp = lax.axis_size("grp")
    per = particles.shape[0]
    cls_dev = references.shape[0]
    block_rows = per * CAND
    chunks = chunks_of(cls_dev)
    pad = odd_tiles(cls_dev)
    width = SHELLS // n_grp
    nz = n_grp // 2
    scoring, phases = (jnp.asarray(t) for t in tables())
    owner = lax.axis_index("cls").astype(jnp.int32).reshape(1)
    first = owner * cls_dev
    grp = lax.axis_index("grp").astype(jnp.int32).reshape(1)

    depth = SHELLS // nz
    message, *sliced = call(
        functools.partial(weigh_kernel, nz, n_cls, cls_dev, chunks), "weigh", [SMEM] + [HBM] * 6,
        [(SHAPE((per * (IMG + 1) + list_lines(n_cls, chunks)[1], FREQ), BF16), VMEM)]
        + [(SHAPE((per * 2 * depth, FREQ), BF16), VMEM)] * (nz - 1),
        [
            VMEM(particles.shape, BF16),
            VMEM((CAND, per), jnp.int32),
            SMEM((per,), jnp.int32),
            SMEM((per,), jnp.int32),
            VMEM(ctf_table.shape[::-1], F32),
            VMEM(noise_prec.shape, F32),
            VMEM((per, noise_prec.shape[0]), F32),
            VMEM((per, ctf_table.shape[0]), F32),
            VMEM((IMG * odd_tiles(per), FREQ), F32),
            pltpu.SemaphoreType.DMA((6,)),
        ],
        5, 2.0,
        (grp,)
        + tuple(
            in_hbm(a)
            for a in (particles, candidates.T, group_ids, ctf_ids, ctf_table.T, noise_prec)
        ),
    )

    if n_cls == 4:
        message_1, message_2 = swap(message, "cls", 1), swap(message, "cls", 2)
    sliced = [swap(one, "grp", 2 * d) for d, one in enumerate(sliced, start=1)]

    rf, power, scoring, phases, own_reg = call(
        functools.partial(prep_kernel, depth), "prep", [SMEM] + [HBM] * 4 + [VMEM],
        [(SHAPE((cls_dev, IMG, FREQ), F32), VMEM), (SHAPE((cls_dev, FREQ), F32), VMEM)]
        + [(SHAPE(t.shape, t.dtype), VMEM) for t in (scoring, phases)]
        + [(SHAPE((width, FREQ), F32), VMEM)],
        [
            VMEM(references.shape, BF16),
            VMEM((IMG * pad, FREQ), F32),
            SMEM(reg.shape, F32),
            pltpu.SemaphoreType.DMA((7,)),
        ],
        8, 4.0,
        (grp,)
        + tuple(in_hbm(a) for a in (references, scoring, phases, reg))
        + (log_prior,),
    )

    half, height = list_lines(n_cls, chunks)

    def score(part, earlier=()):
        blocks = len(part)
        flat = [m for arrays in part for m in arrays]
        earlier = tuple(s[1] for s in earlier)
        ahead = sum(s.shape[0] for s in earlier)
        counts = tuple(len(arrays) for arrays in part)
        return call(
            functools.partial(score_kernel, counts, len(earlier), depth, chunks, half), "score",
            [SMEM] * 2 + [VMEM] * (len(flat) + len(earlier) + 3),
            [
                (SHAPE((blocks * block_rows, ROTS), F32), VMEM),
                (SHAPE((ahead + blocks * per, FREQ), F32), VMEM),
                (SHAPE((blocks * block_rows, FREQ), F32), VMEM),
            ],
            [
                VMEM((blocks, height, FREQ), jnp.int32),
                SMEM((blocks, height, FREQ), jnp.int32),
                VMEM((blocks, per, FREQ), F32),
                VMEM((3, block_rows + 8, FREQ), F32),
                VMEM((blocks * per, IMG, FREQ), F32),
                pltpu.SemaphoreType.DMA((blocks,)),
            ],
            6 if n_cls == 4 else 40, 3.0 * blocks, (first, owner, *flat, *earlier, rf, power, scoring),
        )

    def join(got):
        (joined,) = call(
            join_kernel, "join", [VMEM] * (nz - 1),
            [(SHAPE(((nz - 1) * per * 2 * depth, FREQ), BF16), VMEM)], [], 2, 0.5, got,
        )
        return joined

    if n_cls == 4:
        cut = per // 2 * IMG
        scored = [score([(after(message, sliced[0]),)])]
        ready = (scored[0][1], sliced[1])
        message_1, message_2 = after(message_1, *ready), after(message_2, *ready)
        message_3 = (swap(message_1[:cut], "cls", 2), swap(message_2[cut:], "cls", 1))
        messages = [(message,), (message_1,), (message_2,), message_3]
        scored += [score(messages[1:3])]
        joined = join([after(sliced[0], scored[1][1], *message_3)] + sliced[1:])
        joined_1, joined_2 = swap(joined, "cls", 1), swap(joined, "cls", 2)
        scored += [score(messages[3:], scored)]
    else:
        messages = [(message,)] + [(swap(message, "cls", d),) for d in range(1, n_cls)]
        scored = [score(messages)]
        joined = join(sliced)
        images = [joined] + [swap(joined, "cls", d) for d in range(1, n_cls)]
        pieces = (1,) * n_cls
    arrays = tuple(len(m) for m in messages)
    stats = scored[-1][1]
    all_stats = [stats] + [swap(stats, "cls", d) for d in range(1, n_cls)]
    flat = [m for held in messages for m in held]

    lines = n_cls * block_rows // 2
    own_lists = SHAPE((-(-3 * n_cls // 8) * 8, FREQ), jnp.int32)
    outgoing_rows = -(-(lines + depth + 8 + own_lists.shape[0]) // 16) * 16
    packed, den, mass, log_mass, ints, *outgoing = call(
        functools.partial(weights_kernel, len(scored), n_cls, nz, cls_dev, chunks), "weights",
        [SMEM] * 2 + [VMEM] * (2 * n_cls + 2 * len(scored)),
        [
            (SHAPE((lines, FREQ), BF16), VMEM),
            (SHAPE((depth, FREQ), F32), VMEM),
            (SHAPE((8, FREQ), F32), VMEM),
            (SHAPE((per, ROTS), F32), VMEM),
            (own_lists, VMEM),
        ]
        + [(SHAPE((outgoing_rows, FREQ), BF16), VMEM)] * (nz - 1),
        [VMEM((2 * lines, ROTS), F32), VMEM((nz, depth, FREQ), F32), VMEM((height, FREQ), F32)],
        4 if n_cls == 4 else 12, 2.0,
        (
            grp, owner, *all_stats, *(s[0] for s in scored), *(s[2] for s in scored),
            *(held[-1] for held in messages),
        ),
    )
    incoming = [swap(one, "grp", 2 * d) for d, one in enumerate(outgoing, start=1)]
    if n_cls == 4:
        cut = joined.shape[0] // 2
        joined_1, joined_2 = after(joined_1, packed), after(joined_2, packed)
        joined_3 = [swap(joined_1[:cut], "cls", 2), swap(joined_2[cut:], "cls", 1)]
        images = [joined, joined_1, joined_2, *joined_3]
        pieces = (1, 1, 1, 2)
    (first_sums,) = call(
        functools.partial(own_sum_kernel, chunks, arrays), "own_sum",
        [SMEM] * 2 + [VMEM] * (len(flat) + 3),
        [(SHAPE((cls_dev, 2, 2, width, FREQ), F32), VMEM)],
        [
            VMEM((2, 2 * lines + 8, FREQ), F32),
            SMEM(own_lists.shape, jnp.int32),
            pltpu.SemaphoreType.DMA,
        ],
        4 if n_cls == 4 else 12, 3.0, (grp, owner, packed, ints, *flat, phases),
    )
    (near_sums, den, mass) = call(
        functools.partial(near_sum_kernel, chunks, pieces), "near_sum",
        [SMEM] + [VMEM] * (sum(pieces) + 5),
        [
            (SHAPE((cls_dev, 2, 2, width, FREQ), F32), VMEM),
            (SHAPE((depth, FREQ), F32), VMEM),
            (SHAPE((8, FREQ), F32), VMEM),
        ],
        [
            VMEM((2, 2 * lines + 8, FREQ), F32),
            VMEM(own_lists.shape, jnp.int32),
            SMEM(own_lists.shape, jnp.int32),
            pltpu.SemaphoreType.DMA,
        ],
        4 if n_cls == 4 else 12, 2.0,
        (owner, *images, incoming[0], first_sums, phases, den, mass),
    )
    tile = (2 * width, FREQ)
    sums = []
    for chunk, (start, size) in enumerate(chunks):
        more = chunk == 0
        outs = [
            (SHAPE((size,) + tile, F32), VMEM),
            (SHAPE((size + more,) + tile, BF16), VMEM),
        ]
        scratch = [VMEM((size, 2, 2, width, FREQ), F32)]
        spaces = [SMEM] * 2 + [VMEM] * (sum(pieces) + nz - 1)
        if more:
            outs += [
                (SHAPE((width, FREQ), F32), VMEM),
                (SHAPE((8, FREQ), F32), VMEM),
                (SHAPE((2, (nz - 2) * (2 * lines + 8), FREQ), F32), VMEM),
                (SHAPE((nz - 2,) + own_lists.shape, jnp.int32), SMEM),
            ]
            scratch += [
                VMEM((2, width, FREQ), F32),
                VMEM((nz - 2,) + own_lists.shape, jnp.int32),
                pltpu.SemaphoreType.DMA((nz - 2,)),
            ]
            spaces += [VMEM] * 3
            args = (grp, owner, *images, *incoming[1:], near_sums, phases, den, mass)
        else:
            spaces += [VMEM, SMEM]
            args = (grp, owner, *images, *incoming[1:], near_sums, wcs, lists)
        own, sib, *others = call(
            functools.partial(sum_kernel, chunk, chunks, nz, pieces), "sum",
            spaces, outs, scratch, 3 if n_cls == 4 else 24, 3.0, args,
        )
        if more:
            den, mass, wcs, lists = others
        sums.append((own, sib))

    particle_total = per * n_grp * n_cls
    divided, inverse, share = [], None, None
    for chunk, (own, sib) in enumerate(sums):
        start, cut = chunks[chunk]
        other = swap(sib, "grp", 1)
        averaged_out = (SHAPE((cut,) + tile, BF16), VMEM)
        if chunk == 0:
            averaged, share, inverse = call(
                functools.partial(first_divide_kernel, K / particle_total, start), "divide",
                [VMEM] * 5,
                [averaged_out, (SHAPE((1, FREQ), F32), VMEM), (SHAPE((width, FREQ), F32), VMEM)],
                [], 2, 0.05, (own, other, den, mass, own_reg),
            )
        else:
            (averaged,) = call(
                functools.partial(next_divide_kernel, start), "divide", [VMEM] * 3,
                [averaged_out], [], 2, 0.05, (own, other, inverse),
            )
        divided.append(averaged)

    if nz == 4:
        near = [swap(averaged, "grp", 2) for averaged in divided]
        across = [swap(averaged, "grp", 4) for averaged in divided]
        near, across = lax.optimization_barrier((near, across))
        relayed = [swap(one, "grp", 2) for one in across]
        planes = [list(held) for held in zip(divided, near, across, relayed)]
    else:
        planes = [
            [averaged] + [swap(averaged, "grp", 2 * d) for d in range(1, nz)]
            for averaged in divided
        ]
    averages = None
    for far in ((0, 1, 2), (3,)) if nz == 4 else (tuple(range(nz)),):
        arrays = []
        for d in far:
            for held in planes:
                one = held[d] if averages is None else after(held[d], averages)
                arrays += [one, swap(one, "grp", 1)]
        has_out = averages is not None
        groups = len(far) * 4
        (averages,) = call(
            functools.partial(spread_kernel, far, chunks, has_out), "spread",
            [SMEM] + [VMEM] * len(arrays) + [HBM] * has_out,
            [(SHAPE((cls_dev, FEAT), F32), HBM)],
            [
                VMEM((groups * width * odd_tiles(cls_dev), FREQ), F32),
                VMEM((groups, cls_dev, width * FREQ), F32),
                pltpu.SemaphoreType.DMA((groups,)),
            ],
            8, 0.05, (grp, *arrays) + ((averages,) if has_out else ()),
            input_output_aliases={len(arrays) + 1: 0} if has_out else {},
        )
    return (averages, share[0, :cls_dev], log_mass[:, 0])


def solution(mesh):
    return jax.shard_map(
        per_device,
        mesh=mesh,
        in_specs=(
            P(("grp", "cls"), None),
            P(("grp", "cls"), None),
            P(("grp", "cls")),
            P(("grp", "cls")),
            P(),
            P(),
            P("cls", None),
            P("cls"),
            P(),
        ),
        out_specs=(P("cls", None), P("cls"), P(("grp", "cls"))),
        check_vma=False,
    )
```

```python
import functools
import math

import jax
import jax.numpy as jnp
import numpy as np
from jax import lax
from jax.experimental import pallas as pl
from jax.experimental.pallas import tpu as pltpu
from jax.sharding import PartitionSpec as P

SHELLS = 64
FREQ = 128
FEAT = 16384
ROTS = 64
K = 208
CAND = 8
MOST = 2
IMG = 2 * SHELLS
UNROLL = 4
LOW = -1e30
HIGH = lax.Precision.HIGHEST
VMEM = pltpu.VMEM
SMEM = pltpu.SMEM
HBM = pltpu.HBM
F32 = jnp.float32
BF16 = jnp.bfloat16
SHAPE = jax.ShapeDtypeStruct


def tables():
    turns = np.arange(ROTS)[:, None]
    orders = np.arange(FREQ)[None, :]
    angles = ((turns * orders) % ROTS).astype(np.float32) * np.float32(2.0 * math.pi / ROTS)
    cos_tab = np.cos(angles).astype(np.float32)
    sin_tab = np.sin(angles).astype(np.float32)
    last = np.zeros((FREQ, ROTS), np.float32)
    last[:SHELLS] = -0.5
    last[SHELLS] = 1.0
    scoring = np.concatenate([cos_tab.T, sin_tab.T, last], axis=0)
    left = np.concatenate([cos_tab, sin_tab], axis=1)
    terms = []
    for _ in range(2):
        term = left.astype(jnp.bfloat16)
        left = left - term.astype(np.float32)
        blank = np.zeros_like(term)
        terms.append(np.block([[term, blank], [blank, term]]))
    return scoring, np.concatenate(terms, axis=0)


def lanes_of(shape):
    return lax.broadcasted_iota(jnp.int32, shape, len(shape) - 1)


def list_room(chunks):
    return FREQ if max(n for _, n in chunks) * MOST + UNROLL > FREQ // 2 else FREQ // 2


def list_lines(owners, chunks):
    lines = -(-owners * len(chunks) * list_room(chunks) // FREQ)
    return lines, -(-(2 * lines + 1) // 16) * 16


def list_spot(owner, chunk, chunks):
    number = owner * len(chunks) + chunk
    at = number * list_room(chunks)
    return number, quot(at, FREQ), rest(at, FREQ)


def quot(v, n):
    return v >> (n.bit_length() - 1) if n & (n - 1) == 0 else v // n


def rest(v, n):
    return v & (n - 1) if n & (n - 1) == 0 else v % n


def odd_tiles(rows):
    return (-(-rows // 8) | 1) * 8


def rounded(v):
    return v.astype(BF16).astype(F32)


def row_of(x, r, depth):
    return r // depth * 2 * depth + x * depth + r % depth


def parts_of(image, depth):
    pieces = image.reshape(image.shape[0] // (2 * depth), 2, depth, FREQ)
    return pieces[:, 0], pieces[:, 1]


def chunks_of(cls_dev):
    return ((0, cls_dev),)


def block_lists(named, owners, cls_dev, chunks):
    per = named.shape[0]
    pairs = per * CAND
    square = (pairs, pairs)
    wide = jnp.broadcast_to(named[:, None, :], (per, CAND, CAND)).reshape(pairs, CAND)
    own = lax.broadcasted_iota(jnp.int32, wide.shape, 0) % CAND == lanes_of(wide.shape)
    cls = jnp.broadcast_to(jnp.sum(jnp.where(own, wide, 0.0), axis=1, keepdims=True), square)
    owner = sum((cls >= o * cls_dev).astype(F32) for o in range(1, owners))
    local = cls - owner * cls_dev
    number = owner * len(chunks)
    if len(chunks) > 1:
        number = number + (local < chunks[0][0]).astype(F32)
    row = lax.broadcasted_iota(jnp.int32, square, 0)
    lane = lanes_of(square)

    def across(column):
        return jnp.sum(jnp.where(row == lane, column, 0.0), axis=0, keepdims=True)

    same = (number == across(number)).astype(F32)
    place = jnp.sum(jnp.where(lane < row, same, 0.0), axis=1, keepdims=True)
    held = jnp.sum(same, axis=1, keepdims=True).astype(jnp.int32)
    place = place + rest(UNROLL - rest(held, UNROLL), UNROLL).astype(F32)
    room = list_room(chunks)
    lines, height = list_lines(owners, chunks)
    slots = lines * FREQ
    target = (number[:, :1] * room + place).astype(jnp.int32)
    hot = (target == lanes_of((pairs, slots))).astype(F32).astype(BF16)
    values = jnp.concatenate(
        [
            lanes_of((1, pairs)).astype(F32), across(local), jnp.ones((1, pairs), F32),
            jnp.zeros((5, pairs), F32),
        ],
        axis=0,
    ).astype(BF16)
    placed = jnp.dot(values, hot, preferred_element_type=F32)
    rows_line = placed[0:1]
    cls_line = placed[1:2] + (1.0 - placed[2:3]) * cls_dev
    counts = jnp.sum((number == lane.astype(F32)).astype(F32), axis=0, keepdims=True)
    counts = quot(counts.astype(jnp.int32) + UNROLL - 1, UNROLL).astype(F32)
    cut = [v[:, n * FREQ : (n + 1) * FREQ] for v in (rows_line, cls_line) for n in range(lines)]
    return jnp.concatenate(
        cut + [counts, jnp.zeros((height - 2 * lines - 1, FREQ), F32)], axis=0
    )


def weigh_kernel(
    slices, owners, cls_dev, chunks, grp_s, particles_h, cand_h, groups_h, entries_h, ctf_h, prec_h, message_out, *refs
):
    slice_outs = refs[: slices - 1]
    particles, cand, groups, entries, ctf, prec, hot_g, hot_e, spread, sem = refs[slices - 1 :]
    depth = SHELLS // slices
    z = grp_s[0] // 2
    copies = [
        pltpu.make_async_copy(a, b, sem.at[n])
        for n, (a, b) in enumerate(
            (
                (groups_h, groups), (entries_h, entries), (ctf_h, ctf), (prec_h, prec),
                (cand_h, cand), (particles_h, particles),
            )
        )
    ]
    for copy in copies:
        copy.start()
    per = particles.shape[0]
    pad = spread.shape[0] // IMG
    for copy in copies[:2]:
        copy.wait()
    for i in range(per):
        hot_g[i : i + 1, :] = (lanes_of((1, hot_g.shape[1])) == groups[i]).astype(F32)
        hot_e[i : i + 1, :] = (lanes_of((1, hot_e.shape[1])) == entries[i]).astype(F32)
    for copy in copies[2:5]:
        copy.wait()
    p = jnp.dot(hot_g[...], prec[...], precision=HIGH, preferred_element_type=F32)
    c = lax.dot_general(
        hot_e[...], ctf[...], (((1,), (1,)), ((), ())), precision=HIGH, preferred_element_type=F32
    )
    eye = (lanes_of((per, per)) == lax.broadcasted_iota(jnp.int32, (per, per), 0)).astype(F32)
    named = lax.dot_general(
        eye, cand[...].astype(F32), (((1,), (1,)), ((), ())), precision=HIGH,
        preferred_element_type=F32,
    )
    factors = p * c
    extra = jnp.concatenate(
        [factors * c, named, jnp.zeros((per, FREQ - SHELLS - CAND), F32)], axis=1
    )
    message_out[per * IMG : per * (IMG + 1), :] = extra.astype(BF16)
    message_out[per * (IMG + 1) :, :] = block_lists(named, owners, cls_dev, chunks).astype(BF16)
    copies[5].wait()
    for r in range(SHELLS):
        factor = jnp.broadcast_to(factors[:, r : r + 1], (per, FREQ))
        for x in range(2):
            at = x * SHELLS + r
            piece = particles[:, at * FREQ : (at + 1) * FREQ].astype(F32) * factor
            at = row_of(x, r, depth)
            spread[at * pad : at * pad + per, :] = rounded(piece)
    rows = 2 * depth
    for i in range(per):
        message_out[i * IMG : (i + 1) * IMG, :] = spread[i : i + IMG * pad : pad, :].astype(BF16)
        for d, out in enumerate(slice_outs, start=1):
            row = pl.multiple_of(i * IMG + (z ^ d) * rows, rows)
            out[i * rows : (i + 1) * rows, :] = message_out[pl.ds(row, rows), :]


def prep_kernel(depth, grp_s, refs_h, *rest_refs):
    tables_h, (reg_h, prior), rest_refs = rest_refs[:2], rest_refs[2:4], rest_refs[4:]
    (rf_out, pow_out), tables_out, (reg_out,) = rest_refs[:2], rest_refs[2:4], rest_refs[4:5]
    refs, spread, reg, sem = rest_refs[5:]
    cls_dev = refs.shape[0]
    pow_out[cls_dev:, :] = jnp.zeros((pow_out.shape[0] - cls_dev, FREQ), F32)
    pad = spread.shape[0] // IMG
    parts = sem.shape[0] - 3
    step = FEAT // parts
    tables_in = [
        pltpu.make_async_copy(a, b, sem.at[parts + n])
        for n, (a, b) in enumerate(zip((*tables_h, reg_h), (*tables_out, reg)))
    ]
    copies = [
        pltpu.make_async_copy(
            refs_h.at[:, pl.ds(n * step, step)], refs.at[:, pl.ds(n * step, step)], sem.at[n]
        )
        for n in range(parts)
    ]
    turns = parts // 2
    for n in range(turns):
        copies[n].start()
        copies[n + turns].start()
    for copy in tables_in:
        copy.start()

    def shell(r, power):
        parts = []
        for x in range(2):
            at = x * SHELLS + r
            piece = refs[:, pl.ds(pl.multiple_of(at * FREQ, FREQ), FREQ)].astype(F32)
            at = row_of(x, r, depth)
            spread[pl.ds(pl.multiple_of(at * pad, 8), cls_dev), :] = piece
            parts.append(piece * piece)
        total = jnp.sum(parts[0] + parts[1], axis=1, keepdims=True)
        return jnp.where(lanes_of((cls_dev, FREQ)) == r, total, power)

    power = jnp.zeros((cls_dev, FREQ), F32)
    for n in range(turns):
        copies[n].wait()
        copies[n + turns].wait()
        low, high = n * SHELLS // turns, (n + 1) * SHELLS // turns
        power = lax.fori_loop(low, high, shell, power, unroll=4)
    line = jnp.broadcast_to(prior[...].astype(F32).reshape(1, cls_dev), (cls_dev, cls_dev))
    diagonal = lax.broadcasted_iota(jnp.int32, line.shape, 0) == lanes_of(line.shape)
    column = jnp.sum(jnp.where(diagonal, line, 0.0), axis=1, keepdims=True)
    pow_out[:cls_dev, :] = jnp.where(lanes_of((cls_dev, FREQ)) == SHELLS, column, power)

    def image(k, _):
        rf_out[k] = spread[pl.ds(k, IMG, stride=pad), :]
        return 0

    lax.fori_loop(0, cls_dev, image, 0, unroll=4)
    for copy in tables_in:
        copy.wait()
    width = reg_out.shape[0]
    for r in range(width):
        reg_out[r : r + 1, :] = jnp.full((1, FREQ), reg[grp_s[0] * width + r], F32)


def take(refs, counts):
    taken = []
    for count in counts:
        taken.append(refs[:count])
        refs = refs[count:]
    return taken, refs


def score_kernel(arrays, earlier, depth, chunks, half, first_s, owner_s, *refs):
    blocks = len(arrays)
    messages, refs = take(refs, arrays)
    (earlier_stats,), refs = take(refs, (earlier,))
    rf, power, scoring = refs[:3]
    scores_out, stats_out, cls_out = refs[3:-6]
    ints_v, ints_s, side, ex, w32, sem = refs[-6:]
    per = side.shape[1]
    height = ints_v.shape[1]
    cls_dev = rf.shape[0] - 1
    block_rows = per * CAND
    first = first_s[0]
    table = scoring[...]
    done = 0
    for one in earlier_stats:
        stats_out[done : done + one.shape[0], :] = one[...]
        done += one.shape[0]

    extras = []
    for b in range(blocks):
        last = messages[b][-1]
        end = last.shape[0] - height
        ints_v[b] = last[end:, :].astype(F32).astype(jnp.int32)
        extras.append(last[end - per : end, :].astype(F32))
    copies = [pltpu.make_async_copy(ints_v.at[b], ints_s.at[b], sem.at[b]) for b in range(blocks)]
    for copy in copies:
        copy.start()
    for b in range(blocks):
        lane = lanes_of((per, FREQ))
        side[b] = jnp.where(lane < SHELLS, extras[b], (lane == SHELLS).astype(F32))
        begin = 0
        for one in messages[b]:
            count = one.shape[0] // IMG

            def widen(i, _):
                w32[b * per + begin + i] = one[pl.ds(pl.multiple_of(i * IMG, IMG), IMG), :].astype(F32)
                return 0

            lax.fori_loop(0, count, widen, 0, unroll=2)
            begin += count
    for copy in copies:
        copy.wait()

    for b in range(blocks):
        for c in range(len(chunks)):
            number, line, lane = list_spot(owner_s[0], c, chunks)

            def pairs(step, _):
                for u in range(UNROLL):
                    row = ints_s[b, line, lane + step * UNROLL + u]
                    k = ints_s[b, line + half, lane + step * UNROLL + u]
                    i = quot(row, CAND)
                    w_re, w_im = parts_of(w32[b * per + i], depth)
                    a_re, a_im = parts_of(rf[k], depth)
                    inner = (w_re * a_re + w_im * a_im).reshape(SHELLS, FREQ)
                    outer = (w_re * a_im - w_im * a_re).reshape(SHELLS, FREQ)
                    ex[0, pl.ds(row, 1), :] = jnp.sum(inner, axis=0, keepdims=True)
                    ex[1, pl.ds(row, 1), :] = jnp.sum(outer, axis=0, keepdims=True)
                    ex[2, pl.ds(row, 1), :] = side[b, pl.ds(i, 1), :] * power[pl.ds(k, 1), :]
                return 0

            lax.fori_loop(0, ints_s[b, 2 * half, number], pairs, 0)

        wide = jnp.broadcast_to(
            extras[b][:, None, :], (per, CAND, FREQ)
        ).reshape(block_rows, FREQ)
        own = lanes_of((block_rows, FREQ)) == SHELLS + (
            lax.broadcasted_iota(jnp.int32, (block_rows, FREQ), 0) % CAND
        )
        column = jnp.sum(jnp.where(own, wide, 0.0), axis=1, keepdims=True) - first.astype(F32)
        cls_out[b * block_rows : (b + 1) * block_rows, :] = jnp.broadcast_to(
            column, (block_rows, FREQ)
        )
        good = jnp.logical_and(column >= 0, column < cls_dev)
        values = jnp.zeros((block_rows, ROTS), F32)
        for part in range(3):
            values = values + jnp.dot(
                jnp.where(good, ex[part, :block_rows, :], 0.0),
                table[part * FREQ : (part + 1) * FREQ],
                precision=HIGH,
                preferred_element_type=F32,
            )
        scores = jnp.where(good, values, LOW)
        scores_out[b * block_rows : (b + 1) * block_rows, :] = scores
        top = jnp.broadcast_to(jnp.max(scores, axis=1, keepdims=True), (block_rows, ROTS))
        best = jnp.max(top.reshape(per, CAND, ROTS), axis=1)
        best_rows = jnp.broadcast_to(best[:, None, :], (per, CAND, ROTS)).reshape(block_rows, ROTS)
        mass = jnp.where(good, jnp.exp(scores - best_rows), 0.0)
        mass = jnp.broadcast_to(jnp.sum(mass, axis=1, keepdims=True), (block_rows, ROTS))
        total = jnp.sum(mass.reshape(per, CAND, ROTS), axis=1)
        stats_out[done + b * per : done + (b + 1) * per, :ROTS] = best
        stats_out[done + b * per : done + (b + 1) * per, ROTS:] = total


def two(v):
    return jnp.where(lanes_of(v.shape) < ROTS, rounded(v), v - rounded(v))


def one_of_two(v):
    return v + pltpu.roll(v, ROTS, 1)


def weights_kernel(calls, blocks, slices, cls_dev, chunks, grp_s, owner_s, *refs):
    stats = refs[:blocks]
    scores = refs[blocks : blocks + calls]
    classes = refs[blocks + calls : blocks + 2 * calls]
    extras = refs[blocks + 2 * calls : 2 * blocks + 2 * calls]
    refs = refs[2 * blocks + 2 * calls :]
    own_out, den_out, mass_out, log_out, ints_out = refs[:5]
    message_outs = refs[5:-3]
    rows_v, den_v, lists_v = refs[-3:]
    per = log_out.shape[0]
    block_rows = per * CAND
    depth = SHELLS // slices
    z = grp_s[0] // 2

    den = jnp.zeros((FREQ, FREQ), F32)
    mass = jnp.zeros((1, FREQ), F32)
    block = 0
    for scores_ref, cls_ref in zip(scores, classes):
        for b in range(scores_ref.shape[0] // block_rows):
            ones = [stats[d][(block ^ d) * per : ((block ^ d) + 1) * per, :] for d in range(blocks)]
            best = functools.reduce(jnp.maximum, [one[:, :ROTS] for one in ones])
            total = sum(one[:, ROTS:] * jnp.exp(one[:, :ROTS] - best) for one in ones)
            if block == 0:
                log_out[...] = jnp.log(total)

            def over_rows(v):
                return jnp.broadcast_to(v[:, None, :], (per, CAND, ROTS)).reshape(block_rows, ROTS)

            at = slice(b * block_rows, (b + 1) * block_rows)
            weights = jnp.exp(scores_ref[at, :] - over_rows(best)) / over_rows(total)
            local = cls_ref[at, :]
            good = jnp.logical_and(local >= 0, local < cls_dev)[:, :ROTS]
            weights = rounded(jnp.where(good, weights, 0.0))
            rows_v[block * block_rows : (block + 1) * block_rows, :] = weights
            pair_sum = jnp.sum(weights, axis=1, keepdims=True)
            twice = (lanes_of((block_rows, FREQ)) % ROTS).astype(F32)
            chosen = jnp.where(twice == local, pair_sum, 0.0)
            by_particle = jnp.sum(chosen.reshape(per, CAND, FREQ), axis=1)
            end = extras[block].shape[0] - lists_v.shape[0]
            side = extras[block][end - per : end, :].astype(F32)
            den = den + lax.dot_general(
                side, by_particle, (((0,), (0,)), ((), ())), precision=HIGH,
                preferred_element_type=F32,
            )
            mass = mass + jnp.sum(by_particle, axis=0, keepdims=True)
            block += 1

    lines = rows_v.shape[0] // 2
    packed = jnp.concatenate([rows_v[:lines, :], rows_v[lines:, :]], axis=1).astype(BF16)
    own_out[...] = packed
    den_v[...] = den[:SHELLS].reshape(slices, depth, FREQ)
    mass_rows = jnp.broadcast_to(mass, (8, FREQ))
    mass_out[...] = mass_rows
    den_out[...] = den_v[z]
    half = list_lines(blocks, chunks)[0]
    _, line, _ = list_spot(owner_s[0], 0, chunks)
    lists = []
    for one in extras:
        lists_v[...] = one[one.shape[0] - lists_v.shape[0] :, :].astype(F32)
        for at in (line, line + half, 2 * half):
            lists.append(lists_v[pl.ds(at, 1), :])
    if ints_out.shape[0] > len(lists):
        lists.append(jnp.zeros((ints_out.shape[0] - len(lists), FREQ), F32))
    lists = jnp.concatenate(lists, axis=0)
    ints_out[...] = lists.astype(jnp.int32)
    tail = [two(mass_rows), lists]
    tail_rows = depth + sum(one.shape[0] for one in tail)
    spare = message_outs[0].shape[0] - lines - tail_rows
    if spare:
        tail.append(jnp.zeros((spare, FREQ), F32))
    for d, out in enumerate(message_outs, start=1):
        out[:lines, :] = packed
        out[lines:, :] = jnp.concatenate([two(den_v[z ^ d])] + tail, axis=0).astype(BF16)


def put_phases(packed, table, wcs, base):
    lines = packed.shape[0]
    twice = jnp.concatenate([packed, packed], axis=1)
    both = rounded(jnp.dot(twice, table[...], preferred_element_type=F32))
    for place in range(2):
        for part in range(2):
            at = (2 * place + part) * FREQ
            row = base + place * lines
            wcs[part, row : row + lines, :] = both[:, at : at + FREQ]


def add_pair(image, row, k, wcs, num):
    shape = num.shape[1:]
    image = image.astype(F32)
    half = image.shape[0] // 2
    w_re, w_im = image[:half].reshape(shape[1:]), image[half:].reshape(shape[1:])
    c = wcs[0, pl.ds(row, 1), :].reshape(1, 1, FREQ)
    s = wcs[1, pl.ds(row, 1), :].reshape(1, 1, FREQ)
    num[k, 0] += w_re * c - w_im * s
    num[k, 1] += w_re * s + w_im * c


def pick_image(arrays, begin, i, rows, stride, offset):
    def rows_at(one, i):
        return one[pl.ds(pl.multiple_of(i * stride + offset, rows), rows), :]

    held = [one.shape[0] // stride for one in arrays]
    while len(arrays) > 1 and begin >= held[0]:
        arrays, begin, held = arrays[1:], begin - held[0], held[1:]
    if len(arrays) == 1:
        return rows_at(arrays[0], begin + i)
    cut = held[0] - begin
    return jnp.where(
        i < cut,
        rows_at(arrays[0], begin + jnp.minimum(i, cut - 1)),
        rows_at(arrays[1], jnp.maximum(i - cut, 0)),
    )


def own_sum_kernel(chunks, arrays, grp_s, owner_s, packed, ints, *refs):
    messages, refs = take(refs, arrays)
    phases, (num, wcs, ints_s, sem) = refs[:1], refs[1:]
    copy = pltpu.make_async_copy(ints, ints_s, sem)
    copy.start()
    per = sum(one.shape[0] for one in messages[0]) // IMG
    rows = 2 * num.shape[2] * num.shape[3]
    z = grp_s[0] // 2
    put_phases(packed[...], phases[0], wcs, 0)
    num[...] = jnp.zeros_like(num)
    copy.wait()
    for block, held_in in enumerate(messages):
        base = block * per * CAND
        for c in range(len(chunks)):
            number, _, lane = list_spot(owner_s[0], c, chunks)

            def pairs(step, _):
                for u in range(UNROLL):
                    row = ints_s[3 * block, lane + step * UNROLL + u]
                    k = ints_s[3 * block + 1, lane + step * UNROLL + u]
                    image = pick_image(held_in, 0, quot(row, CAND), rows, IMG, z * rows)
                    add_pair(image, base + row, k, wcs, num)
                return 0

            lax.fori_loop(0, ints_s[3 * block + 2, number], pairs, 0)


def join_kernel(*refs):
    out = refs[-1]
    rows = refs[0].shape[0]
    for n, one in enumerate(refs[:-1]):
        out[n * rows : (n + 1) * rows, :] = one[...]


def read_tail(message, lines, depth, count):
    tail = message[lines:, :].astype(F32)
    den, mass = one_of_two(tail[:depth]), one_of_two(tail[depth : depth + 8])
    return den, mass, tail[depth + 8 : depth + 8 + count].astype(jnp.int32)


def add_plane(d, chunk, chunks, owner, images, ints, base, wcs, num):
    number, _, lane = list_spot(owner, chunk, chunks)
    rows = 2 * num.shape[2] * num.shape[3]
    per = FREQ // CAND
    for block, held_in in enumerate(images):

        def pairs(step, _):
            for u in range(UNROLL):
                row = ints[3 * block, lane + step * UNROLL + u]
                k = ints[3 * block + 1, lane + step * UNROLL + u]
                image = pick_image(held_in, d * per, quot(row, CAND), rows, rows, 0)
                add_pair(image, base + block * per * CAND + row, k, wcs, num)
            return 0

        lax.fori_loop(0, ints[3 * block + 2, number], pairs, 0)


def near_sum_kernel(chunks, pieces, owner_s, *refs):
    images, refs = take(refs, pieces)
    message, first, phases, den_in, mass_in, num, den_out, mass_out, wcs, ints_v, ints_s, sem = refs
    lines = wcs.shape[1] // 2
    depth = den_in.shape[0]
    den, mass, ints_v[...] = read_tail(message, lines, depth, ints_v.shape[0])
    copy = pltpu.make_async_copy(ints_v, ints_s, sem)
    copy.start()
    den_out[...] = den_in[...] + den
    mass_out[...] = mass_in[...] + mass
    put_phases(message[:lines, :], phases, wcs, 0)
    num[...] = first[...]
    copy.wait()
    for chunk in range(len(chunks)):
        add_plane(0, chunk, chunks, owner_s[0], images, ints_s, 0, wcs, num)


def sum_kernel(chunk, chunks, slices, pieces, grp_s, owner_s, *refs):
    images, refs = take(refs, pieces)
    messages, refs = refs[: slices - 2], refs[slices - 2 :]
    first, refs = refs[0], refs[1:]
    if chunk == 0:
        phases, (den_in, mass_in), refs = refs[0], refs[1:3], refs[3:]
        own_out, sib_out, den_out, mass_out, wcs, ints_s, num, den_v, ints_v, sem = refs
    else:
        wcs, ints_s, own_out, sib_out, num = refs
    group_rows = wcs.shape[1] // (slices - 2)
    lines = group_rows // 2
    core = grp_s[0] % 2
    start, size = chunks[chunk]
    depth = num.shape[2] * num.shape[3]

    if chunk == 0:
        den, mass = den_in[...], mass_in[...]
        for n, message in enumerate(messages):
            more_den, more_mass, ints_v[n] = read_tail(message, lines, depth, ints_v.shape[1])
            den, mass = den + more_den, mass + more_mass
        copies = [
            pltpu.make_async_copy(ints_v.at[n], ints_s.at[n], sem.at[n])
            for n in range(slices - 2)
        ]
        for copy in copies:
            copy.start()
        for n, message in enumerate(messages):
            put_phases(message[:lines, :], phases, wcs, n * group_rows)
    num[...] = first[...]
    if chunk == 0:
        for copy in copies:
            copy.wait()
    for n in range(slices - 2):
        add_plane(
            n + 1, chunk, chunks, owner_s[0], images, ints_s.at[n], n * group_rows, wcs, num
        )

    def pack(k, _):
        own_out[k] = jnp.concatenate([num[k, 0, core], num[k, 1, core]], axis=0)
        other = jnp.concatenate([num[k, 0, 1 - core], num[k, 1, 1 - core]], axis=0)
        sib_out[k] = other.astype(BF16)
        return 0

    lax.fori_loop(0, size, pack, 0, unroll=4)
    if chunk == 0:
        width = num.shape[3]
        den_v[...] = den.reshape(2, width, FREQ)
        den_out[...] = den_v[core]
        mass_out[...] = mass
        sib_out[size] = jnp.concatenate([two(den_v[1 - core]), two(mass)[:width]], axis=0).astype(BF16)


def divide(own, sib, inverse, start, avg_out):
    for k in range(avg_out.shape[0]):
        column = inverse[:, start + k : start + k + 1]
        factor = jnp.concatenate([column, column], axis=0)
        avg_out[k] = ((own[k] + sib[k].astype(F32)) * factor).astype(BF16)


def first_divide_kernel(scale, start, own, sib, den, mass, reg, avg_out, share_out, inverse_out):
    cut = avg_out.shape[0]
    width = avg_out.shape[1] // 2
    tile = one_of_two(sib[cut].astype(F32))
    share_out[...] = (tile[width : width + 1] + mass[:1]) * scale
    inverse = 1.0 / (tile[:width] + den[...] + reg[...])
    inverse_out[...] = inverse
    divide(own, sib, inverse, start, avg_out)


def next_divide_kernel(start, own, sib, inverse, avg_out):
    divide(own, sib, inverse[...], start, avg_out)


def spread_kernel(planes, chunks, has_out, grp_s, *refs):
    held = 2 * len(planes) * len(chunks)
    arrays, (out, wide, columns, sem) = refs[:held], refs[held + has_out :]
    width = arrays[0].shape[1] // 2
    cls_dev = columns.shape[1]
    pad = wide.shape[0] // (len(planes) * 4 * width)
    z, h = grp_s[0] // 2, grp_s[0] % 2
    copies = []
    for n, d in enumerate(planes):
        for c, (start, cut) in enumerate(chunks):
            pair = arrays[2 * (n * len(chunks) + c) :][:2]

            def one(k, _):
                for side, array in enumerate(pair):
                    piece = array[k].astype(F32)
                    for x in range(2):
                        at = (n * 4 + side * 2 + x) * width * pad + start
                        wide[pl.ds(at + k, width, stride=pad), :] = piece[
                            x * width : (x + 1) * width
                        ]
                return 0

            lax.fori_loop(0, cut, one, 0, unroll=2)
        for side, core in enumerate((h, 1 - h)):
            for x in range(2):
                group = n * 4 + side * 2 + x
                for r in range(width):
                    at = (group * width + r) * pad
                    columns[group, :, r * FREQ : (r + 1) * FREQ] = wide[at : at + cls_dev, :]
                first = (x * SHELLS + ((z ^ d) * 2 + core) * width) * FREQ
                first = pl.multiple_of(first, width * FREQ)
                copies.append(
                    pltpu.make_async_copy(
                        columns.at[group], out.at[:, pl.ds(first, width * FREQ)], sem.at[group]
                    )
                )
                copies[-1].start()
    for copy in copies:
        copy.wait()


def whole(space):
    return pl.BlockSpec(memory_space=space)


def in_hbm(value):
    return pltpu.with_memory_space_constraint(value, HBM)


def call(kernel, name, ins, outs, scratch, mib, us, args, **more):
    cost = pl.CostEstimate(flops=0, bytes_accessed=int(us * 3.6e6), transcendentals=0)
    return pl.pallas_call(
        kernel,
        out_shape=tuple(s for s, _ in outs),
        in_specs=[whole(s) for s in ins],
        out_specs=tuple(whole(s) for _, s in outs),
        scratch_shapes=scratch,
        compiler_params=pltpu.CompilerParams(vmem_limit_bytes=mib * 2**20),
        name=name,
        cost_estimate=cost,
        **more,
    )(*args)


def swap(value, axis, distance):
    size = lax.axis_size(axis)
    return lax.ppermute(value, axis, [(i, i ^ distance) for i in range(size)])


def after(value, *others):
    return lax.optimization_barrier((value, *others))[0]


def per_device(
    particles, candidates, group_ids, ctf_ids, ctf_table, noise_prec, references, log_prior, reg
):
    n_cls = lax.axis_size("cls")
    n_grp = lax.axis_size("grp")
    per = particles.shape[0]
    cls_dev = references.shape[0]
    block_rows = per * CAND
    chunks = chunks_of(cls_dev)
    pad = odd_tiles(cls_dev)
    width = SHELLS // n_grp
    nz = n_grp // 2
    scoring, phases = (jnp.asarray(t) for t in tables())
    owner = lax.axis_index("cls").astype(jnp.int32).reshape(1)
    first = owner * cls_dev
    grp = lax.axis_index("grp").astype(jnp.int32).reshape(1)

    depth = SHELLS // nz
    message, *sliced = call(
        functools.partial(weigh_kernel, nz, n_cls, cls_dev, chunks), "weigh", [SMEM] + [HBM] * 6,
        [(SHAPE((per * (IMG + 1) + list_lines(n_cls, chunks)[1], FREQ), BF16), VMEM)]
        + [(SHAPE((per * 2 * depth, FREQ), BF16), VMEM)] * (nz - 1),
        [
            VMEM(particles.shape, BF16),
            VMEM((CAND, per), jnp.int32),
            SMEM((per,), jnp.int32),
            SMEM((per,), jnp.int32),
            VMEM(ctf_table.shape[::-1], F32),
            VMEM(noise_prec.shape, F32),
            VMEM((per, noise_prec.shape[0]), F32),
            VMEM((per, ctf_table.shape[0]), F32),
            VMEM((IMG * odd_tiles(per), FREQ), F32),
            pltpu.SemaphoreType.DMA((6,)),
        ],
        5, 2.0,
        (grp,)
        + tuple(
            in_hbm(a)
            for a in (particles, candidates.T, group_ids, ctf_ids, ctf_table.T, noise_prec)
        ),
    )

    if n_cls == 4:
        message_1, message_2 = swap(message, "cls", 1), swap(message, "cls", 2)
    sliced = [swap(one, "grp", 2 * d) for d, one in enumerate(sliced, start=1)]

    rf, power, scoring, phases, own_reg = call(
        functools.partial(prep_kernel, depth), "prep", [SMEM] + [HBM] * 4 + [VMEM],
        [(SHAPE((cls_dev + 1, IMG, FREQ), F32), VMEM), (SHAPE((cls_dev + 1, FREQ), F32), VMEM)]
        + [(SHAPE(t.shape, t.dtype), VMEM) for t in (scoring, phases)]
        + [(SHAPE((width, FREQ), F32), VMEM)],
        [
            VMEM(references.shape, BF16),
            VMEM((IMG * pad, FREQ), F32),
            SMEM(reg.shape, F32),
            pltpu.SemaphoreType.DMA((7,)),
        ],
        8, 4.0,
        (grp,)
        + tuple(in_hbm(a) for a in (references, scoring, phases, reg))
        + (log_prior,),
    )

    half, height = list_lines(n_cls, chunks)

    def score(part, earlier=()):
        blocks = len(part)
        flat = [m for arrays in part for m in arrays]
        earlier = tuple(s[1] for s in earlier)
        ahead = sum(s.shape[0] for s in earlier)
        counts = tuple(len(arrays) for arrays in part)
        return call(
            functools.partial(score_kernel, counts, len(earlier), depth, chunks, half), "score",
            [SMEM] * 2 + [VMEM] * (len(flat) + len(earlier) + 3),
            [
                (SHAPE((blocks * block_rows, ROTS), F32), VMEM),
                (SHAPE((ahead + blocks * per, FREQ), F32), VMEM),
                (SHAPE((blocks * block_rows, FREQ), F32), VMEM),
            ],
            [
                VMEM((blocks, height, FREQ), jnp.int32),
                SMEM((blocks, height, FREQ), jnp.int32),
                VMEM((blocks, per, FREQ), F32),
                VMEM((3, block_rows, FREQ), F32),
                VMEM((blocks * per, IMG, FREQ), F32),
                pltpu.SemaphoreType.DMA((blocks,)),
            ],
            6 if n_cls == 4 else 40, 3.0 * blocks, (first, owner, *flat, *earlier, rf, power, scoring),
        )

    def join(got):
        (joined,) = call(
            join_kernel, "join", [VMEM] * (nz - 1),
            [(SHAPE(((nz - 1) * per * 2 * depth, FREQ), BF16), VMEM)], [], 2, 0.5, got,
        )
        return joined

    if n_cls == 4:
        cut = per // 2 * IMG
        scored = [score([(after(message, sliced[0]),)])]
        ready = (scored[0][1], sliced[1])
        message_1, message_2 = after(message_1, *ready), after(message_2, *ready)
        message_3 = (swap(message_1[:cut], "cls", 2), swap(message_2[cut:], "cls", 1))
        messages = [(message,), (message_1,), (message_2,), message_3]
        scored += [score(messages[1:3])]
        joined = join([after(sliced[0], scored[1][1], *message_3)] + sliced[1:])
        joined_1, joined_2 = swap(joined, "cls", 1), swap(joined, "cls", 2)
        scored += [score(messages[3:], scored)]
    else:
        messages = [(message,)] + [(swap(message, "cls", d),) for d in range(1, n_cls)]
        scored = [score(messages)]
        joined = join(sliced)
        images = [joined] + [swap(joined, "cls", d) for d in range(1, n_cls)]
        pieces = (1,) * n_cls
    arrays = tuple(len(m) for m in messages)
    stats = scored[-1][1]
    all_stats = [stats] + [swap(stats, "cls", d) for d in range(1, n_cls)]
    flat = [m for held in messages for m in held]

    lines = n_cls * block_rows // 2
    own_lists = SHAPE((-(-3 * n_cls // 8) * 8, FREQ), jnp.int32)
    outgoing_rows = -(-(lines + depth + 8 + own_lists.shape[0]) // 16) * 16
    packed, den, mass, log_mass, ints, *outgoing = call(
        functools.partial(weights_kernel, len(scored), n_cls, nz, cls_dev, chunks), "weights",
        [SMEM] * 2 + [VMEM] * (2 * n_cls + 2 * len(scored)),
        [
            (SHAPE((lines, FREQ), BF16), VMEM),
            (SHAPE((depth, FREQ), F32), VMEM),
            (SHAPE((8, FREQ), F32), VMEM),
            (SHAPE((per, ROTS), F32), VMEM),
            (own_lists, VMEM),
        ]
        + [(SHAPE((outgoing_rows, FREQ), BF16), VMEM)] * (nz - 1),
        [VMEM((2 * lines, ROTS), F32), VMEM((nz, depth, FREQ), F32), VMEM((height, FREQ), F32)],
        4 if n_cls == 4 else 12, 2.0,
        (
            grp, owner, *all_stats, *(s[0] for s in scored), *(s[2] for s in scored),
            *(held[-1] for held in messages),
        ),
    )
    incoming = [swap(one, "grp", 2 * d) for d, one in enumerate(outgoing, start=1)]
    if n_cls == 4:
        cut = joined.shape[0] // 2
        joined_1, joined_2 = after(joined_1, packed), after(joined_2, packed)
        joined_3 = [swap(joined_1[:cut], "cls", 2), swap(joined_2[cut:], "cls", 1)]
        images = [joined, joined_1, joined_2, *joined_3]
        pieces = (1, 1, 1, 2)
    (first_sums,) = call(
        functools.partial(own_sum_kernel, chunks, arrays), "own_sum",
        [SMEM] * 2 + [VMEM] * (len(flat) + 3),
        [(SHAPE((cls_dev + 1, 2, 2, width, FREQ), F32), VMEM)],
        [
            VMEM((2, 2 * lines, FREQ), F32),
            SMEM(own_lists.shape, jnp.int32),
            pltpu.SemaphoreType.DMA,
        ],
        4 if n_cls == 4 else 12, 3.0, (grp, owner, packed, ints, *flat, phases),
    )
    (near_sums, den, mass) = call(
        functools.partial(near_sum_kernel, chunks, pieces), "near_sum",
        [SMEM] + [VMEM] * (sum(pieces) + 5),
        [
            (SHAPE((cls_dev + 1, 2, 2, width, FREQ), F32), VMEM),
            (SHAPE((depth, FREQ), F32), VMEM),
            (SHAPE((8, FREQ), F32), VMEM),
        ],
        [
            VMEM((2, 2 * lines, FREQ), F32),
            VMEM(own_lists.shape, jnp.int32),
            SMEM(own_lists.shape, jnp.int32),
            pltpu.SemaphoreType.DMA,
        ],
        4 if n_cls == 4 else 12, 2.0,
        (owner, *images, incoming[0], first_sums, phases, den, mass),
    )
    tile = (2 * width, FREQ)
    sums = []
    for chunk, (start, size) in enumerate(chunks):
        more = chunk == 0
        outs = [
            (SHAPE((size,) + tile, F32), VMEM),
            (SHAPE((size + more,) + tile, BF16), VMEM),
        ]
        scratch = [VMEM((size + 1, 2, 2, width, FREQ), F32)]
        spaces = [SMEM] * 2 + [VMEM] * (sum(pieces) + nz - 1)
        if more:
            outs += [
                (SHAPE((width, FREQ), F32), VMEM),
                (SHAPE((8, FREQ), F32), VMEM),
                (SHAPE((2, (nz - 2) * (2 * lines), FREQ), F32), VMEM),
                (SHAPE((nz - 2,) + own_lists.shape, jnp.int32), SMEM),
            ]
            scratch += [
                VMEM((2, width, FREQ), F32),
                VMEM((nz - 2,) + own_lists.shape, jnp.int32),
                pltpu.SemaphoreType.DMA((nz - 2,)),
            ]
            spaces += [VMEM] * 3
            args = (grp, owner, *images, *incoming[1:], near_sums, phases, den, mass)
        else:
            spaces += [VMEM, SMEM]
            args = (grp, owner, *images, *incoming[1:], near_sums, wcs, lists)
        own, sib, *others = call(
            functools.partial(sum_kernel, chunk, chunks, nz, pieces), "sum",
            spaces, outs, scratch, 3 if n_cls == 4 else 24, 3.0, args,
        )
        if more:
            den, mass, wcs, lists = others
        sums.append((own, sib))

    particle_total = per * n_grp * n_cls
    divided, inverse, share = [], None, None
    for chunk, (own, sib) in enumerate(sums):
        start, cut = chunks[chunk]
        other = swap(sib, "grp", 1)
        averaged_out = (SHAPE((cut,) + tile, BF16), VMEM)
        if chunk == 0:
            averaged, share, inverse = call(
                functools.partial(first_divide_kernel, K / particle_total, start), "divide",
                [VMEM] * 5,
                [averaged_out, (SHAPE((1, FREQ), F32), VMEM), (SHAPE((width, FREQ), F32), VMEM)],
                [], 2, 0.05, (own, other, den, mass, own_reg),
            )
        else:
            (averaged,) = call(
                functools.partial(next_divide_kernel, start), "divide", [VMEM] * 3,
                [averaged_out], [], 2, 0.05, (own, other, inverse),
            )
        divided.append(averaged)

    if nz == 4:
        near = [swap(averaged, "grp", 2) for averaged in divided]
        across = [swap(averaged, "grp", 4) for averaged in divided]
        near, across = lax.optimization_barrier((near, across))
        relayed = [swap(one, "grp", 2) for one in across]
        planes = [list(held) for held in zip(divided, near, across, relayed)]
    else:
        planes = [
            [averaged] + [swap(averaged, "grp", 2 * d) for d in range(1, nz)]
            for averaged in divided
        ]
    averages = None
    for far in ((0, 1, 2), (3,)) if nz == 4 else (tuple(range(nz)),):
        arrays = []
        for d in far:
            for held in planes:
                one = held[d] if averages is None else after(held[d], averages)
                arrays += [one, swap(one, "grp", 1)]
        has_out = averages is not None
        groups = len(far) * 4
        (averages,) = call(
            functools.partial(spread_kernel, far, chunks, has_out), "spread",
            [SMEM] + [VMEM] * len(arrays) + [HBM] * has_out,
            [(SHAPE((cls_dev, FEAT), F32), HBM)],
            [
                VMEM((groups * width * odd_tiles(cls_dev), FREQ), F32),
                VMEM((groups, cls_dev, width * FREQ), F32),
                pltpu.SemaphoreType.DMA((groups,)),
            ],
            8, 0.05, (grp, *arrays) + ((averages,) if has_out else ()),
            input_output_aliases={len(arrays) + 1: 0} if has_out else {},
        )
    return (averages, share[0, :cls_dev], log_mass[:, 0])


def solution(mesh):
    return jax.shard_map(
        per_device,
        mesh=mesh,
        in_specs=(
            P(("grp", "cls"), None),
            P(("grp", "cls"), None),
            P(("grp", "cls")),
            P(("grp", "cls")),
            P(),
            P(),
            P("cls", None),
            P("cls"),
            P(),
        ),
        out_specs=(P("cls", None), P("cls"), P(("grp", "cls"))),
        check_vma=False,
    )
```

```python
import functools
import math

import jax
import jax.numpy as jnp
import numpy as np
from jax import lax
from jax.experimental import pallas as pl
from jax.experimental.pallas import tpu as pltpu
from jax.sharding import PartitionSpec as P

SHELLS = 64
FREQ = 128
FEAT = 16384
ROTS = 64
K = 208
CAND = 8
MOST = 2
IMG = 2 * SHELLS
UNROLL = 4
LOW = -1e30
HIGH = lax.Precision.HIGHEST
VMEM = pltpu.VMEM
SMEM = pltpu.SMEM
HBM = pltpu.HBM
F32 = jnp.float32
BF16 = jnp.bfloat16
SHAPE = jax.ShapeDtypeStruct


def tables():
    turns = np.arange(ROTS)[:, None]
    orders = np.arange(FREQ)[None, :]
    angles = ((turns * orders) % ROTS).astype(np.float32) * np.float32(2.0 * math.pi / ROTS)
    cos_tab = np.cos(angles).astype(np.float32)
    sin_tab = np.sin(angles).astype(np.float32)
    last = np.zeros((FREQ, ROTS), np.float32)
    last[:SHELLS] = -0.5
    last[SHELLS] = 1.0
    scoring = np.concatenate([cos_tab.T, sin_tab.T, last], axis=0)
    left = np.concatenate([cos_tab, sin_tab], axis=1)
    terms = []
    for _ in range(2):
        term = left.astype(jnp.bfloat16)
        left = left - term.astype(np.float32)
        blank = np.zeros_like(term)
        terms.append(np.block([[term, blank], [blank, term]]))
    return scoring, np.concatenate(terms, axis=0)


def lanes_of(shape):
    return lax.broadcasted_iota(jnp.int32, shape, len(shape) - 1)


def list_room(chunks):
    return FREQ if max(n for _, n in chunks) * MOST + UNROLL > FREQ // 2 else FREQ // 2


def list_lines(owners, chunks):
    lines = -(-owners * len(chunks) * list_room(chunks) // FREQ)
    return lines, -(-(2 * lines + 1) // 16) * 16


def list_spot(owner, chunk, chunks):
    number = owner * len(chunks) + chunk
    at = number * list_room(chunks)
    return number, quot(at, FREQ), rest(at, FREQ)


def list_slots(cls_dev):
    return -(-cls_dev * MOST // 8) * 8


def quot(v, n):
    return v >> (n.bit_length() - 1) if n & (n - 1) == 0 else v // n


def rest(v, n):
    return v & (n - 1) if n & (n - 1) == 0 else v % n


def odd_tiles(rows):
    return (-(-rows // 8) | 1) * 8


def rounded(v):
    return v.astype(BF16).astype(F32)


def row_of(x, r, depth):
    return r // depth * 2 * depth + x * depth + r % depth


def parts_of(image, depth):
    pieces = image.reshape(image.shape[0] // (2 * depth), 2, depth, FREQ)
    return pieces[:, 0], pieces[:, 1]


def chunks_of(cls_dev):
    return ((0, cls_dev),)


def block_lists(named, owners, cls_dev, chunks):
    per = named.shape[0]
    pairs = per * CAND
    square = (pairs, pairs)
    wide = jnp.broadcast_to(named[:, None, :], (per, CAND, CAND)).reshape(pairs, CAND)
    own = lax.broadcasted_iota(jnp.int32, wide.shape, 0) % CAND == lanes_of(wide.shape)
    cls = jnp.broadcast_to(jnp.sum(jnp.where(own, wide, 0.0), axis=1, keepdims=True), square)
    owner = sum((cls >= o * cls_dev).astype(F32) for o in range(1, owners))
    local = cls - owner * cls_dev
    number = owner * len(chunks)
    if len(chunks) > 1:
        number = number + (local < chunks[0][0]).astype(F32)
    row = lax.broadcasted_iota(jnp.int32, square, 0)
    lane = lanes_of(square)

    def across(column):
        return jnp.sum(jnp.where(row == lane, column, 0.0), axis=0, keepdims=True)

    same = (number == across(number)).astype(F32)
    place = jnp.sum(jnp.where(lane < row, same, 0.0), axis=1, keepdims=True)
    held = jnp.sum(same, axis=1, keepdims=True).astype(jnp.int32)
    place = place + rest(UNROLL - rest(held, UNROLL), UNROLL).astype(F32)
    room = list_room(chunks)
    lines, height = list_lines(owners, chunks)
    slots = lines * FREQ
    target = (number[:, :1] * room + place).astype(jnp.int32)
    hot = (target == lanes_of((pairs, slots))).astype(F32).astype(BF16)
    values = jnp.concatenate(
        [
            lanes_of((1, pairs)).astype(F32), across(local), jnp.ones((1, pairs), F32),
            jnp.zeros((5, pairs), F32),
        ],
        axis=0,
    ).astype(BF16)
    placed = jnp.dot(values, hot, preferred_element_type=F32)
    rows_line = placed[0:1]
    cls_line = placed[1:2] + (1.0 - placed[2:3]) * cls_dev
    counts = jnp.sum((number == lane.astype(F32)).astype(F32), axis=0, keepdims=True)
    counts = quot(counts.astype(jnp.int32) + UNROLL - 1, UNROLL).astype(F32)
    cut = [v[:, n * FREQ : (n + 1) * FREQ] for v in (rows_line, cls_line) for n in range(lines)]
    return jnp.concatenate(
        cut + [counts, jnp.zeros((height - 2 * lines - 1, FREQ), F32)], axis=0
    )


def weigh_kernel(
    slices, owners, cls_dev, chunks, grp_s, particles_h, cand_h, groups_h, entries_h, ctf_h, prec_h, message_out, *refs
):
    slice_outs = refs[: slices - 1]
    particles, cand, groups, entries, ctf, prec, hot_g, hot_e, spread, sem = refs[slices - 1 :]
    depth = SHELLS // slices
    z = grp_s[0] // 2
    copies = [
        pltpu.make_async_copy(a, b, sem.at[n])
        for n, (a, b) in enumerate(
            (
                (groups_h, groups), (entries_h, entries), (ctf_h, ctf), (prec_h, prec),
                (cand_h, cand), (particles_h, particles),
            )
        )
    ]
    for copy in copies:
        copy.start()
    per = particles.shape[0]
    pad = spread.shape[0] // (IMG + 1)
    for copy in copies[:2]:
        copy.wait()
    for i in range(per):
        hot_g[i : i + 1, :] = (lanes_of((1, hot_g.shape[1])) == groups[i]).astype(F32)
        hot_e[i : i + 1, :] = (lanes_of((1, hot_e.shape[1])) == entries[i]).astype(F32)
    for copy in copies[2:5]:
        copy.wait()
    p = jnp.dot(hot_g[...], prec[...], precision=HIGH, preferred_element_type=F32)
    c = lax.dot_general(
        hot_e[...], ctf[...], (((1,), (1,)), ((), ())), precision=HIGH, preferred_element_type=F32
    )
    eye = (lanes_of((per, per)) == lax.broadcasted_iota(jnp.int32, (per, per), 0)).astype(F32)
    named = lax.dot_general(
        eye, cand[...].astype(F32), (((1,), (1,)), ((), ())), precision=HIGH,
        preferred_element_type=F32,
    )
    factors = p * c
    extra = jnp.concatenate(
        [factors * c, named, jnp.zeros((per, FREQ - SHELLS - CAND), F32)], axis=1
    )
    message_out[per * IMG : per * (IMG + 1), :] = extra.astype(BF16)
    message_out[per * (IMG + 1) :, :] = block_lists(named, owners, cls_dev, chunks).astype(BF16)
    copies[5].wait()
    for r in range(SHELLS):
        factor = jnp.broadcast_to(factors[:, r : r + 1], (per, FREQ))
        for x in range(2):
            at = x * SHELLS + r
            piece = particles[:, at * FREQ : (at + 1) * FREQ].astype(F32) * factor
            at = row_of(x, r, depth)
            spread[at * pad : at * pad + per, :] = rounded(piece)
    rows = 2 * depth
    for i in range(per):
        message_out[i * IMG : (i + 1) * IMG, :] = spread[i : i + IMG * pad : pad, :].astype(BF16)
        for d, out in enumerate(slice_outs, start=1):
            row = pl.multiple_of(i * IMG + (z ^ d) * rows, rows)
            out[i * rows : (i + 1) * rows, :] = message_out[pl.ds(row, rows), :]


def prep_kernel(depth, grp_s, refs_h, *rest_refs):
    tables_h, (reg_h, prior), rest_refs = rest_refs[:2], rest_refs[2:4], rest_refs[4:]
    (rf_out, pow_out), tables_out, (reg_out,) = rest_refs[:2], rest_refs[2:4], rest_refs[4:5]
    refs, spread, reg, sem = rest_refs[5:]
    cls_dev = refs.shape[0]
    pow_out[cls_dev:, :] = jnp.zeros((pow_out.shape[0] - cls_dev, FREQ), F32)
    pad = spread.shape[0] // (IMG + 1)
    parts = sem.shape[0] - 3
    step = FEAT // parts
    tables_in = [
        pltpu.make_async_copy(a, b, sem.at[parts + n])
        for n, (a, b) in enumerate(zip((*tables_h, reg_h), (*tables_out, reg)))
    ]
    copies = [
        pltpu.make_async_copy(
            refs_h.at[:, pl.ds(n * step, step)], refs.at[:, pl.ds(n * step, step)], sem.at[n]
        )
        for n in range(parts)
    ]
    turns = parts // 2
    for n in range(turns):
        copies[n].start()
        copies[n + turns].start()
    for copy in tables_in:
        copy.start()

    def shell(r, power):
        parts = []
        for x in range(2):
            at = x * SHELLS + r
            piece = refs[:, pl.ds(pl.multiple_of(at * FREQ, FREQ), FREQ)].astype(F32)
            at = row_of(x, r, depth)
            spread[pl.ds(pl.multiple_of(at * pad, 8), cls_dev), :] = piece
            parts.append(piece * piece)
        total = jnp.sum(parts[0] + parts[1], axis=1, keepdims=True)
        return jnp.where(lanes_of((cls_dev, FREQ)) == r, total, power)

    power = jnp.zeros((cls_dev, FREQ), F32)
    for n in range(turns):
        copies[n].wait()
        copies[n + turns].wait()
        low, high = n * SHELLS // turns, (n + 1) * SHELLS // turns
        power = lax.fori_loop(low, high, shell, power, unroll=4)
    line = jnp.broadcast_to(prior[...].astype(F32).reshape(1, cls_dev), (cls_dev, cls_dev))
    diagonal = lax.broadcasted_iota(jnp.int32, line.shape, 0) == lanes_of(line.shape)
    column = jnp.sum(jnp.where(diagonal, line, 0.0), axis=1, keepdims=True)
    pow_out[:cls_dev, :] = jnp.where(lanes_of((cls_dev, FREQ)) == SHELLS, column, power)

    def image(k, _):
        rf_out[k] = spread[pl.ds(k, IMG, stride=pad), :]
        return 0

    lax.fori_loop(0, cls_dev, image, 0, unroll=4)
    for copy in tables_in:
        copy.wait()
    width = reg_out.shape[0]
    for r in range(width):
        reg_out[r : r + 1, :] = jnp.full((1, FREQ), reg[grp_s[0] * width + r], F32)


def take(refs, counts):
    taken = []
    for count in counts:
        taken.append(refs[:count])
        refs = refs[count:]
    return taken, refs


def score_kernel(arrays, earlier, depth, chunks, half, first_s, owner_s, *refs):
    blocks = len(arrays)
    messages, refs = take(refs, arrays)
    (earlier_stats,), refs = take(refs, (earlier,))
    rf, power, scoring = refs[:3]
    scores_out, stats_out, cls_out = refs[3:-6]
    ints_v, ints_s, side, ex, w32, sem = refs[-6:]
    per = side.shape[1]
    height = ints_v.shape[1]
    cls_dev = rf.shape[0] - 1
    block_rows = per * CAND
    first = first_s[0]
    table = scoring[...]
    done = 0
    for one in earlier_stats:
        stats_out[done : done + one.shape[0], :] = one[...]
        done += one.shape[0]

    extras = []
    for b in range(blocks):
        last = messages[b][-1]
        end = last.shape[0] - height
        ints_v[b] = last[end:, :].astype(F32).astype(jnp.int32)
        extras.append(last[end - per : end, :].astype(F32))
    copies = [pltpu.make_async_copy(ints_v.at[b], ints_s.at[b], sem.at[b]) for b in range(blocks)]
    for copy in copies:
        copy.start()
    for b in range(blocks):
        lane = lanes_of((per, FREQ))
        side[b] = jnp.where(lane < SHELLS, extras[b], (lane == SHELLS).astype(F32))
        begin = 0
        for one in messages[b]:
            count = one.shape[0] // IMG

            def widen(i, _):
                w32[b * per + begin + i] = one[pl.ds(pl.multiple_of(i * IMG, IMG), IMG), :].astype(F32)
                return 0

            lax.fori_loop(0, count, widen, 0, unroll=2)
            begin += count
    for copy in copies:
        copy.wait()

    for b in range(blocks):
        for c in range(len(chunks)):
            number, line, lane = list_spot(owner_s[0], c, chunks)

            def pairs(step, _):
                for u in range(UNROLL):
                    row = ints_s[b, line, lane + step * UNROLL + u]
                    k = ints_s[b, line + half, lane + step * UNROLL + u]
                    i = quot(row, CAND)
                    w_re, w_im = parts_of(w32[b * per + i], depth)
                    a_re, a_im = parts_of(rf[k], depth)
                    inner = (w_re * a_re + w_im * a_im).reshape(SHELLS, FREQ)
                    outer = (w_re * a_im - w_im * a_re).reshape(SHELLS, FREQ)
                    ex[0, pl.ds(row, 1), :] = jnp.sum(inner, axis=0, keepdims=True)
                    ex[1, pl.ds(row, 1), :] = jnp.sum(outer, axis=0, keepdims=True)
                    ex[2, pl.ds(row, 1), :] = side[b, pl.ds(i, 1), :] * power[pl.ds(k, 1), :]
                return 0

            lax.fori_loop(0, ints_s[b, 2 * half, number], pairs, 0)

        wide = jnp.broadcast_to(
            extras[b][:, None, :], (per, CAND, FREQ)
        ).reshape(block_rows, FREQ)
        own = lanes_of((block_rows, FREQ)) == SHELLS + (
            lax.broadcasted_iota(jnp.int32, (block_rows, FREQ), 0) % CAND
        )
        column = jnp.sum(jnp.where(own, wide, 0.0), axis=1, keepdims=True) - first.astype(F32)
        cls_out[b * block_rows : (b + 1) * block_rows, :] = jnp.broadcast_to(
            column, (block_rows, FREQ)
        )
        good = jnp.logical_and(column >= 0, column < cls_dev)
        values = jnp.zeros((block_rows, ROTS), F32)
        for part in range(3):
            values = values + jnp.dot(
                jnp.where(good, ex[part, :block_rows, :], 0.0),
                table[part * FREQ : (part + 1) * FREQ],
                precision=HIGH,
                preferred_element_type=F32,
            )
        scores = jnp.where(good, values, LOW)
        scores_out[b * block_rows : (b + 1) * block_rows, :] = scores
        top = jnp.broadcast_to(jnp.max(scores, axis=1, keepdims=True), (block_rows, ROTS))
        best = jnp.max(top.reshape(per, CAND, ROTS), axis=1)
        best_rows = jnp.broadcast_to(best[:, None, :], (per, CAND, ROTS)).reshape(block_rows, ROTS)
        mass = jnp.where(good, jnp.exp(scores - best_rows), 0.0)
        mass = jnp.broadcast_to(jnp.sum(mass, axis=1, keepdims=True), (block_rows, ROTS))
        total = jnp.sum(mass.reshape(per, CAND, ROTS), axis=1)
        stats_out[done + b * per : done + (b + 1) * per, :ROTS] = best
        stats_out[done + b * per : done + (b + 1) * per, ROTS:] = total


def two(v):
    return jnp.where(lanes_of(v.shape) < ROTS, rounded(v), v - rounded(v))


def one_of_two(v):
    return v + pltpu.roll(v, ROTS, 1)


def weights_kernel(calls, blocks, slices, cls_dev, chunks, grp_s, owner_s, *refs):
    stats = refs[:blocks]
    scores = refs[blocks : blocks + calls]
    classes = refs[blocks + calls : blocks + 2 * calls]
    extras = refs[blocks + 2 * calls : 2 * blocks + 2 * calls]
    refs = refs[2 * blocks + 2 * calls :]
    own_out, den_out, mass_out, log_out, ints_out = refs[:5]
    message_outs = refs[5:-4]
    rows_v, den_v, lists_v, picked_v = refs[-4:]
    per = log_out.shape[0]
    block_rows = per * CAND
    depth = SHELLS // slices
    z = grp_s[0] // 2

    half = list_lines(blocks, chunks)[0]
    _, line, lane = list_spot(owner_s[0], 0, chunks)
    slots = list_slots(cls_dev)
    lists = []

    den = jnp.zeros((FREQ, FREQ), F32)
    mass = jnp.zeros((1, FREQ), F32)
    block = 0
    for scores_ref, cls_ref in zip(scores, classes):
        for b in range(scores_ref.shape[0] // block_rows):
            ones = [stats[d][(block ^ d) * per : ((block ^ d) + 1) * per, :] for d in range(blocks)]
            best = functools.reduce(jnp.maximum, [one[:, :ROTS] for one in ones])
            total = sum(one[:, ROTS:] * jnp.exp(one[:, :ROTS] - best) for one in ones)
            if block == 0:
                log_out[...] = jnp.log(total)

            def over_rows(v):
                return jnp.broadcast_to(v[:, None, :], (per, CAND, ROTS)).reshape(block_rows, ROTS)

            at = slice(b * block_rows, (b + 1) * block_rows)
            weights = jnp.exp(scores_ref[at, :] - over_rows(best)) / over_rows(total)
            local = cls_ref[at, :]
            good = jnp.logical_and(local >= 0, local < cls_dev)[:, :ROTS]
            weights = rounded(jnp.where(good, weights, 0.0))
            lists_v[...] = extras[block][extras[block].shape[0] - lists_v.shape[0] :, :].astype(F32)
            named = jnp.broadcast_to(lists_v[pl.ds(line, 1), :], (block_rows, FREQ))
            row = lax.broadcasted_iota(jnp.int32, named.shape, 0).astype(F32)
            picked_v[...] = lax.dot_general(
                (named == row).astype(F32).astype(BF16), weights.astype(BF16),
                (((0,), (0,)), ((), ())), preferred_element_type=F32,
            )
            at = block * slots
            rows_v[at : at + slots, :] = picked_v[pl.ds(pl.multiple_of(lane, 8), slots), :]
            for source in (line, line + half, 2 * half):
                lists.append(lists_v[pl.ds(source, 1), :])
            pair_sum = jnp.sum(weights, axis=1, keepdims=True)
            twice = (lanes_of((block_rows, FREQ)) % ROTS).astype(F32)
            chosen = jnp.where(twice == local, pair_sum, 0.0)
            by_particle = jnp.sum(chosen.reshape(per, CAND, FREQ), axis=1)
            end = extras[block].shape[0] - lists_v.shape[0]
            side = extras[block][end - per : end, :].astype(F32)
            den = den + lax.dot_general(
                side, by_particle, (((0,), (0,)), ((), ())), precision=HIGH,
                preferred_element_type=F32,
            )
            mass = mass + jnp.sum(by_particle, axis=0, keepdims=True)
            block += 1

    lines = rows_v.shape[0] // 2
    packed = jnp.concatenate([rows_v[:lines, :], rows_v[lines:, :]], axis=1).astype(BF16)
    own_out[...] = packed
    den_v[...] = den[:SHELLS].reshape(slices, depth, FREQ)
    mass_rows = jnp.broadcast_to(mass, (8, FREQ))
    mass_out[...] = mass_rows
    den_out[...] = den_v[z]
    if ints_out.shape[0] > len(lists):
        lists.append(jnp.zeros((ints_out.shape[0] - len(lists), FREQ), F32))
    lists = jnp.concatenate(lists, axis=0)
    ints_out[...] = lists.astype(jnp.int32)
    tail = [two(mass_rows), lists]
    tail_rows = depth + sum(one.shape[0] for one in tail)
    spare = message_outs[0].shape[0] - lines - tail_rows
    if spare:
        tail.append(jnp.zeros((spare, FREQ), F32))
    for d, out in enumerate(message_outs, start=1):
        out[:lines, :] = packed
        out[lines:, :] = jnp.concatenate([two(den_v[z ^ d])] + tail, axis=0).astype(BF16)


def put_phases(packed, table, wcs, base):
    lines = packed.shape[0]
    twice = jnp.concatenate([packed, packed], axis=1)
    both = rounded(jnp.dot(twice, table[...], preferred_element_type=F32))
    for place in range(2):
        for part in range(2):
            at = (2 * place + part) * FREQ
            row = base + place * lines
            wcs[part, row : row + lines, :] = both[:, at : at + FREQ]


def add_pair(image, row, k, wcs, num):
    shape = num.shape[1:]
    image = image.astype(F32)
    half = image.shape[0] // 2
    w_re, w_im = image[:half].reshape(shape[1:]), image[half:].reshape(shape[1:])
    c = wcs[0, pl.ds(row, 1), :].reshape(1, 1, FREQ)
    s = wcs[1, pl.ds(row, 1), :].reshape(1, 1, FREQ)
    num[k, 0] += w_re * c - w_im * s
    num[k, 1] += w_re * s + w_im * c


def pick_image(arrays, begin, i, rows, stride, offset):
    def rows_at(one, i):
        return one[pl.ds(pl.multiple_of(i * stride + offset, rows), rows), :]

    held = [one.shape[0] // stride for one in arrays]
    while len(arrays) > 1 and begin >= held[0]:
        arrays, begin, held = arrays[1:], begin - held[0], held[1:]
    if len(arrays) == 1:
        return rows_at(arrays[0], begin + i)
    cut = held[0] - begin
    return jnp.where(
        i < cut,
        rows_at(arrays[0], begin + jnp.minimum(i, cut - 1)),
        rows_at(arrays[1], jnp.maximum(i - cut, 0)),
    )


def own_sum_kernel(chunks, arrays, grp_s, owner_s, packed, ints, *refs):
    messages, refs = take(refs, arrays)
    phases, (num, wcs, ints_s, sem) = refs[:1], refs[1:]
    copy = pltpu.make_async_copy(ints, ints_s, sem)
    copy.start()
    per = sum(one.shape[0] for one in messages[0]) // IMG
    rows = 2 * num.shape[2] * num.shape[3]
    z = grp_s[0] // 2
    put_phases(packed[...], phases[0], wcs, 0)
    num[...] = jnp.zeros_like(num)
    copy.wait()
    for block, held_in in enumerate(messages):
        base = block * list_slots(num.shape[0] - 1)
        for c in range(len(chunks)):
            number, _, lane = list_spot(owner_s[0], c, chunks)

            def pairs(step, _):
                for u in range(UNROLL):
                    row = ints_s[3 * block, lane + step * UNROLL + u]
                    k = ints_s[3 * block + 1, lane + step * UNROLL + u]
                    image = pick_image(held_in, 0, quot(row, CAND), rows, IMG, z * rows)
                    add_pair(image, base + step * UNROLL + u, k, wcs, num)
                return 0

            lax.fori_loop(0, ints_s[3 * block + 2, number], pairs, 0)


def join_kernel(*refs):
    out = refs[-1]
    rows = refs[0].shape[0]
    for n, one in enumerate(refs[:-1]):
        out[n * rows : (n + 1) * rows, :] = one[...]


def read_tail(message, lines, depth, count):
    tail = message[lines:, :].astype(F32)
    den, mass = one_of_two(tail[:depth]), one_of_two(tail[depth : depth + 8])
    return den, mass, tail[depth + 8 : depth + 8 + count].astype(jnp.int32)


def add_plane(d, chunk, chunks, owner, images, ints, base, wcs, num):
    number, _, lane = list_spot(owner, chunk, chunks)
    rows = 2 * num.shape[2] * num.shape[3]
    per = FREQ // CAND
    for block, held_in in enumerate(images):
        start = base + block * list_slots(num.shape[0] - 1)

        def pairs(step, _):
            for u in range(UNROLL):
                row = ints[3 * block, lane + step * UNROLL + u]
                k = ints[3 * block + 1, lane + step * UNROLL + u]
                image = pick_image(held_in, d * per, quot(row, CAND), rows, rows, 0)
                add_pair(image, start + step * UNROLL + u, k, wcs, num)
            return 0

        lax.fori_loop(0, ints[3 * block + 2, number], pairs, 0)


def near_sum_kernel(chunks, pieces, owner_s, *refs):
    images, refs = take(refs, pieces)
    message, first, phases, den_in, mass_in, num, den_out, mass_out, wcs, ints_v, ints_s, sem = refs
    lines = wcs.shape[1] // 2
    depth = den_in.shape[0]
    den, mass, ints_v[...] = read_tail(message, lines, depth, ints_v.shape[0])
    copy = pltpu.make_async_copy(ints_v, ints_s, sem)
    copy.start()
    den_out[...] = den_in[...] + den
    mass_out[...] = mass_in[...] + mass
    put_phases(message[:lines, :], phases, wcs, 0)
    num[...] = first[...]
    copy.wait()
    for chunk in range(len(chunks)):
        add_plane(0, chunk, chunks, owner_s[0], images, ints_s, 0, wcs, num)


def sum_kernel(chunk, chunks, slices, pieces, grp_s, owner_s, *refs):
    images, refs = take(refs, pieces)
    messages, refs = refs[: slices - 2], refs[slices - 2 :]
    first, refs = refs[0], refs[1:]
    if chunk == 0:
        phases, (den_in, mass_in), refs = refs[0], refs[1:3], refs[3:]
        own_out, sib_out, den_out, mass_out, wcs, ints_s, num, den_v, ints_v, sem = refs
    else:
        wcs, ints_s, own_out, sib_out, num = refs
    group_rows = wcs.shape[1] // (slices - 2)
    lines = group_rows // 2
    core = grp_s[0] % 2
    start, size = chunks[chunk]
    depth = num.shape[2] * num.shape[3]

    if chunk == 0:
        den, mass = den_in[...], mass_in[...]
        for n, message in enumerate(messages):
            more_den, more_mass, ints_v[n] = read_tail(message, lines, depth, ints_v.shape[1])
            den, mass = den + more_den, mass + more_mass
        copies = [
            pltpu.make_async_copy(ints_v.at[n], ints_s.at[n], sem.at[n])
            for n in range(slices - 2)
        ]
        for copy in copies:
            copy.start()
        for n, message in enumerate(messages):
            put_phases(message[:lines, :], phases, wcs, n * group_rows)
    num[...] = first[...]
    if chunk == 0:
        for copy in copies:
            copy.wait()
    for n in range(slices - 2):
        add_plane(
            n + 1, chunk, chunks, owner_s[0], images, ints_s.at[n], n * group_rows, wcs, num
        )

    def pack(k, _):
        own_out[k] = jnp.concatenate([num[k, 0, core], num[k, 1, core]], axis=0)
        other = jnp.concatenate([num[k, 0, 1 - core], num[k, 1, 1 - core]], axis=0)
        sib_out[k] = other.astype(BF16)
        return 0

    lax.fori_loop(0, size, pack, 0, unroll=4)
    if chunk == 0:
        width = num.shape[3]
        den_v[...] = den.reshape(2, width, FREQ)
        den_out[...] = den_v[core]
        mass_out[...] = mass
        sib_out[size] = jnp.concatenate([two(den_v[1 - core]), two(mass)[:width]], axis=0).astype(BF16)


def divide(own, sib, inverse, start, avg_out):
    for k in range(avg_out.shape[0]):
        column = inverse[:, start + k : start + k + 1]
        factor = jnp.concatenate([column, column], axis=0)
        avg_out[k] = ((own[k] + sib[k].astype(F32)) * factor).astype(BF16)


def first_divide_kernel(scale, start, own, sib, den, mass, reg, avg_out, share_out, inverse_out):
    cut = avg_out.shape[0]
    width = avg_out.shape[1] // 2
    tile = one_of_two(sib[cut].astype(F32))
    share_out[...] = (tile[width : width + 1] + mass[:1]) * scale
    inverse = 1.0 / (tile[:width] + den[...] + reg[...])
    inverse_out[...] = inverse
    divide(own, sib, inverse, start, avg_out)


def next_divide_kernel(start, own, sib, inverse, avg_out):
    divide(own, sib, inverse[...], start, avg_out)


def spread_kernel(planes, chunks, has_out, grp_s, *refs):
    held = 2 * len(planes) * len(chunks)
    arrays, (out, wide, columns, sem) = refs[:held], refs[held + has_out :]
    width = arrays[0].shape[1] // 2
    cls_dev = columns.shape[1]
    pad = wide.shape[0] // (len(planes) * 4 * width + 1)
    z, h = grp_s[0] // 2, grp_s[0] % 2
    copies = []
    for n, d in enumerate(planes):
        for c, (start, cut) in enumerate(chunks):
            pair = arrays[2 * (n * len(chunks) + c) :][:2]

            def one(k, _):
                for side, array in enumerate(pair):
                    piece = array[k].astype(F32)
                    for x in range(2):
                        at = (n * 4 + side * 2 + x) * width * pad + start
                        wide[pl.ds(at + k, width, stride=pad), :] = piece[
                            x * width : (x + 1) * width
                        ]
                return 0

            lax.fori_loop(0, cut, one, 0, unroll=2)
        for side, core in enumerate((h, 1 - h)):
            for x in range(2):
                group = n * 4 + side * 2 + x
                for r in range(width):
                    at = (group * width + r) * pad
                    columns[group, :, r * FREQ : (r + 1) * FREQ] = wide[at : at + cls_dev, :]
                first = (x * SHELLS + ((z ^ d) * 2 + core) * width) * FREQ
                first = pl.multiple_of(first, width * FREQ)
                copies.append(
                    pltpu.make_async_copy(
                        columns.at[group], out.at[:, pl.ds(first, width * FREQ)], sem.at[group]
                    )
                )
                copies[-1].start()
    for copy in copies:
        copy.wait()


def whole(space):
    return pl.BlockSpec(memory_space=space)


def in_hbm(value):
    return pltpu.with_memory_space_constraint(value, HBM)


def call(kernel, name, ins, outs, scratch, mib, us, args, **more):
    cost = pl.CostEstimate(flops=0, bytes_accessed=int(us * 3.6e6), transcendentals=0)
    return pl.pallas_call(
        kernel,
        out_shape=tuple(s for s, _ in outs),
        in_specs=[whole(s) for s in ins],
        out_specs=tuple(whole(s) for _, s in outs),
        scratch_shapes=scratch,
        compiler_params=pltpu.CompilerParams(vmem_limit_bytes=mib * 2**20),
        name=name,
        cost_estimate=cost,
        **more,
    )(*args)


def swap(value, axis, distance):
    size = lax.axis_size(axis)
    return lax.ppermute(value, axis, [(i, i ^ distance) for i in range(size)])


def after(value, *others):
    return lax.optimization_barrier((value, *others))[0]


def per_device(
    particles, candidates, group_ids, ctf_ids, ctf_table, noise_prec, references, log_prior, reg
):
    n_cls = lax.axis_size("cls")
    n_grp = lax.axis_size("grp")
    per = particles.shape[0]
    cls_dev = references.shape[0]
    block_rows = per * CAND
    chunks = chunks_of(cls_dev)
    pad = odd_tiles(cls_dev)
    width = SHELLS // n_grp
    nz = n_grp // 2
    scoring, phases = (jnp.asarray(t) for t in tables())
    owner = lax.axis_index("cls").astype(jnp.int32).reshape(1)
    first = owner * cls_dev
    grp = lax.axis_index("grp").astype(jnp.int32).reshape(1)

    depth = SHELLS // nz
    message, *sliced = call(
        functools.partial(weigh_kernel, nz, n_cls, cls_dev, chunks), "weigh", [SMEM] + [HBM] * 6,
        [(SHAPE((per * (IMG + 1) + list_lines(n_cls, chunks)[1], FREQ), BF16), VMEM)]
        + [(SHAPE((per * 2 * depth, FREQ), BF16), VMEM)] * (nz - 1),
        [
            VMEM(particles.shape, BF16),
            VMEM((CAND, per), jnp.int32),
            SMEM((per,), jnp.int32),
            SMEM((per,), jnp.int32),
            VMEM(ctf_table.shape[::-1], F32),
            VMEM(noise_prec.shape, F32),
            VMEM((per, noise_prec.shape[0]), F32),
            VMEM((per, ctf_table.shape[0]), F32),
            VMEM(((IMG + 1) * odd_tiles(per), FREQ), F32),
            pltpu.SemaphoreType.DMA((6,)),
        ],
        5, 2.0,
        (grp,)
        + tuple(
            in_hbm(a)
            for a in (particles, candidates.T, group_ids, ctf_ids, ctf_table.T, noise_prec)
        ),
    )

    if n_cls == 4:
        message_1, message_2 = swap(message, "cls", 1), swap(message, "cls", 2)
    sliced = [swap(one, "grp", 2 * d) for d, one in enumerate(sliced, start=1)]

    rf, power, scoring, phases, own_reg = call(
        functools.partial(prep_kernel, depth), "prep", [SMEM] + [HBM] * 4 + [VMEM],
        [(SHAPE((cls_dev + 1, IMG, FREQ), F32), VMEM), (SHAPE((cls_dev + 1, FREQ), F32), VMEM)]
        + [(SHAPE(t.shape, t.dtype), VMEM) for t in (scoring, phases)]
        + [(SHAPE((width, FREQ), F32), VMEM)],
        [
            VMEM(references.shape, BF16),
            VMEM(((IMG + 1) * pad, FREQ), F32),
            SMEM(reg.shape, F32),
            pltpu.SemaphoreType.DMA((7,)),
        ],
        8, 4.0,
        (grp,)
        + tuple(in_hbm(a) for a in (references, scoring, phases, reg))
        + (log_prior,),
    )

    half, height = list_lines(n_cls, chunks)

    def score(part, earlier=()):
        blocks = len(part)
        flat = [m for arrays in part for m in arrays]
        earlier = tuple(s[1] for s in earlier)
        ahead = sum(s.shape[0] for s in earlier)
        counts = tuple(len(arrays) for arrays in part)
        return call(
            functools.partial(score_kernel, counts, len(earlier), depth, chunks, half), "score",
            [SMEM] * 2 + [VMEM] * (len(flat) + len(earlier) + 3),
            [
                (SHAPE((blocks * block_rows, ROTS), F32), VMEM),
                (SHAPE((ahead + blocks * per, FREQ), F32), VMEM),
                (SHAPE((blocks * block_rows, FREQ), F32), VMEM),
            ],
            [
                VMEM((blocks, height, FREQ), jnp.int32),
                SMEM((blocks, height, FREQ), jnp.int32),
                VMEM((blocks, per, FREQ), F32),
                VMEM((3, block_rows, FREQ), F32),
                VMEM((blocks * per, IMG, FREQ), F32),
                pltpu.SemaphoreType.DMA((blocks,)),
            ],
            6 if n_cls == 4 else 40, 3.0 * blocks, (first, owner, *flat, *earlier, rf, power, scoring),
        )

    def join(got):
        (joined,) = call(
            join_kernel, "join", [VMEM] * (nz - 1),
            [(SHAPE(((nz - 1) * per * 2 * depth, FREQ), BF16), VMEM)], [], 2, 0.5, got,
        )
        return joined

    if n_cls == 4:
        cut = per // 2 * IMG
        scored = [score([(after(message, sliced[0]),)])]
        ready = (scored[0][1], sliced[1])
        message_1, message_2 = after(message_1, *ready), after(message_2, *ready)
        message_3 = (swap(message_1[:cut], "cls", 2), swap(message_2[cut:], "cls", 1))
        messages = [(message,), (message_1,), (message_2,), message_3]
        scored += [score(messages[1:3])]
        joined = join([after(sliced[0], scored[1][1], *message_3)] + sliced[1:])
        joined_1, joined_2 = swap(joined, "cls", 1), swap(joined, "cls", 2)
        scored += [score(messages[3:], scored)]
    else:
        messages = [(message,)] + [(swap(message, "cls", d),) for d in range(1, n_cls)]
        scored = [score(messages)]
        joined = join(sliced)
        images = [joined] + [swap(joined, "cls", d) for d in range(1, n_cls)]
        pieces = (1,) * n_cls
    arrays = tuple(len(m) for m in messages)
    stats = scored[-1][1]
    all_stats = [stats] + [swap(stats, "cls", d) for d in range(1, n_cls)]
    flat = [m for held in messages for m in held]

    lines = n_cls * list_slots(cls_dev) // 2
    own_lists = SHAPE((-(-3 * n_cls // 8) * 8, FREQ), jnp.int32)
    outgoing_rows = -(-(lines + depth + 8 + own_lists.shape[0]) // 16) * 16
    packed, den, mass, log_mass, ints, *outgoing = call(
        functools.partial(weights_kernel, len(scored), n_cls, nz, cls_dev, chunks), "weights",
        [SMEM] * 2 + [VMEM] * (2 * n_cls + 2 * len(scored)),
        [
            (SHAPE((lines, FREQ), BF16), VMEM),
            (SHAPE((depth, FREQ), F32), VMEM),
            (SHAPE((8, FREQ), F32), VMEM),
            (SHAPE((per, ROTS), F32), VMEM),
            (own_lists, VMEM),
        ]
        + [(SHAPE((outgoing_rows, FREQ), BF16), VMEM)] * (nz - 1),
        [
            VMEM((2 * lines, ROTS), F32),
            VMEM((nz, depth, FREQ), F32),
            VMEM((height, FREQ), F32),
            VMEM((block_rows, ROTS), F32),
        ],
        4 if n_cls == 4 else 12, 2.0,
        (
            grp, owner, *all_stats, *(s[0] for s in scored), *(s[2] for s in scored),
            *(held[-1] for held in messages),
        ),
    )
    incoming = [swap(one, "grp", 2 * d) for d, one in enumerate(outgoing, start=1)]
    if n_cls == 4:
        cut = joined.shape[0] // 2
        joined_1, joined_2 = after(joined_1, packed), after(joined_2, packed)
        joined_3 = [swap(joined_1[:cut], "cls", 2), swap(joined_2[cut:], "cls", 1)]
        images = [joined, joined_1, joined_2, *joined_3]
        pieces = (1, 1, 1, 2)
    (first_sums,) = call(
        functools.partial(own_sum_kernel, chunks, arrays), "own_sum",
        [SMEM] * 2 + [VMEM] * (len(flat) + 3),
        [(SHAPE((cls_dev + 1, 2, 2, width, FREQ), F32), VMEM)],
        [
            VMEM((2, 2 * lines, FREQ), F32),
            SMEM(own_lists.shape, jnp.int32),
            pltpu.SemaphoreType.DMA,
        ],
        4 if n_cls == 4 else 12, 3.0, (grp, owner, packed, ints, *flat, phases),
    )
    (near_sums, den, mass) = call(
        functools.partial(near_sum_kernel, chunks, pieces), "near_sum",
        [SMEM] + [VMEM] * (sum(pieces) + 5),
        [
            (SHAPE((cls_dev + 1, 2, 2, width, FREQ), F32), VMEM),
            (SHAPE((depth, FREQ), F32), VMEM),
            (SHAPE((8, FREQ), F32), VMEM),
        ],
        [
            VMEM((2, 2 * lines, FREQ), F32),
            VMEM(own_lists.shape, jnp.int32),
            SMEM(own_lists.shape, jnp.int32),
            pltpu.SemaphoreType.DMA,
        ],
        4 if n_cls == 4 else 12, 2.0,
        (owner, *images, incoming[0], first_sums, phases, den, mass),
    )
    tile = (2 * width, FREQ)
    sums = []
    for chunk, (start, size) in enumerate(chunks):
        more = chunk == 0
        outs = [
            (SHAPE((size,) + tile, F32), VMEM),
            (SHAPE((size + more,) + tile, BF16), VMEM),
        ]
        scratch = [VMEM((size + 1, 2, 2, width, FREQ), F32)]
        spaces = [SMEM] * 2 + [VMEM] * (sum(pieces) + nz - 1)
        if more:
            outs += [
                (SHAPE((width, FREQ), F32), VMEM),
                (SHAPE((8, FREQ), F32), VMEM),
                (SHAPE((2, (nz - 2) * (2 * lines), FREQ), F32), VMEM),
                (SHAPE((nz - 2,) + own_lists.shape, jnp.int32), SMEM),
            ]
            scratch += [
                VMEM((2, width, FREQ), F32),
                VMEM((nz - 2,) + own_lists.shape, jnp.int32),
                pltpu.SemaphoreType.DMA((nz - 2,)),
            ]
            spaces += [VMEM] * 3
            args = (grp, owner, *images, *incoming[1:], near_sums, phases, den, mass)
        else:
            spaces += [VMEM, SMEM]
            args = (grp, owner, *images, *incoming[1:], near_sums, wcs, lists)
        own, sib, *others = call(
            functools.partial(sum_kernel, chunk, chunks, nz, pieces), "sum",
            spaces, outs, scratch, 3 if n_cls == 4 else 24, 3.0, args,
        )
        if more:
            den, mass, wcs, lists = others
        sums.append((own, sib))

    particle_total = per * n_grp * n_cls
    divided, inverse, share = [], None, None
    for chunk, (own, sib) in enumerate(sums):
        start, cut = chunks[chunk]
        other = swap(sib, "grp", 1)
        averaged_out = (SHAPE((cut,) + tile, BF16), VMEM)
        if chunk == 0:
            averaged, share, inverse = call(
                functools.partial(first_divide_kernel, K / particle_total, start), "divide",
                [VMEM] * 5,
                [averaged_out, (SHAPE((1, FREQ), F32), VMEM), (SHAPE((width, FREQ), F32), VMEM)],
                [], 2, 0.05, (own, other, den, mass, own_reg),
            )
        else:
            (averaged,) = call(
                functools.partial(next_divide_kernel, start), "divide", [VMEM] * 3,
                [averaged_out], [], 2, 0.05, (own, other, inverse),
            )
        divided.append(averaged)

    if nz == 4:
        near = [swap(averaged, "grp", 2) for averaged in divided]
        across = [swap(averaged, "grp", 4) for averaged in divided]
        near, across = lax.optimization_barrier((near, across))
        relayed = [swap(one, "grp", 2) for one in across]
        planes = [list(held) for held in zip(divided, near, across, relayed)]
    else:
        planes = [
            [averaged] + [swap(averaged, "grp", 2 * d) for d in range(1, nz)]
            for averaged in divided
        ]
    averages = None
    for far in ((0, 1, 2), (3,)) if nz == 4 else (tuple(range(nz)),):
        arrays = []
        for d in far:
            for held in planes:
                one = held[d] if averages is None else after(held[d], averages)
                arrays += [one, swap(one, "grp", 1)]
        has_out = averages is not None
        groups = len(far) * 4
        (averages,) = call(
            functools.partial(spread_kernel, far, chunks, has_out), "spread",
            [SMEM] + [VMEM] * len(arrays) + [HBM] * has_out,
            [(SHAPE((cls_dev, FEAT), F32), HBM)],
            [
                VMEM(((groups * width + 1) * odd_tiles(cls_dev), FREQ), F32),
                VMEM((groups, cls_dev, width * FREQ), F32),
                pltpu.SemaphoreType.DMA((groups,)),
            ],
            8, 0.05, (grp, *arrays) + ((averages,) if has_out else ()),
            input_output_aliases={len(arrays) + 1: 0} if has_out else {},
        )
    return (averages, share[0, :cls_dev], log_mass[:, 0])


def solution(mesh):
    return jax.shard_map(
        per_device,
        mesh=mesh,
        in_specs=(
            P(("grp", "cls"), None),
            P(("grp", "cls"), None),
            P(("grp", "cls")),
            P(("grp", "cls")),
            P(),
            P(),
            P("cls", None),
            P("cls"),
            P(),
        ),
        out_specs=(P("cls", None), P("cls"), P(("grp", "cls"))),
        check_vma=False,
    )
```

```python
import functools
import math

import jax
import jax.numpy as jnp
import numpy as np
from jax import lax
from jax.experimental import pallas as pl
from jax.experimental.pallas import tpu as pltpu
from jax.sharding import PartitionSpec as P

SHELLS = 64
FREQ = 128
FEAT = 16384
ROTS = 64
K = 208
CAND = 8
MOST = 2
IMG = 2 * SHELLS
UNROLL = 4
LOW = -1e30
HIGH = lax.Precision.HIGHEST
VMEM = pltpu.VMEM
SMEM = pltpu.SMEM
HBM = pltpu.HBM
F32 = jnp.float32
BF16 = jnp.bfloat16
SHAPE = jax.ShapeDtypeStruct


def tables():
    turns = np.arange(ROTS)[:, None]
    orders = np.arange(FREQ)[None, :]
    angles = ((turns * orders) % ROTS).astype(np.float32) * np.float32(2.0 * math.pi / ROTS)
    cos_tab = np.cos(angles).astype(np.float32)
    sin_tab = np.sin(angles).astype(np.float32)
    last = np.zeros((FREQ, ROTS), np.float32)
    last[:SHELLS] = -0.5
    last[SHELLS] = 1.0
    scoring = np.concatenate([cos_tab.T, sin_tab.T, last], axis=0)
    left = np.concatenate([cos_tab, sin_tab], axis=1)
    terms = []
    for _ in range(2):
        term = left.astype(jnp.bfloat16)
        left = left - term.astype(np.float32)
        blank = np.zeros_like(term)
        terms.append(np.block([[term, blank], [blank, term]]))
    return scoring, np.concatenate(terms, axis=0)


def lanes_of(shape):
    return lax.broadcasted_iota(jnp.int32, shape, len(shape) - 1)


def list_room(chunks):
    return FREQ if max(n for _, n in chunks) * MOST + UNROLL > FREQ // 2 else FREQ // 2


def list_lines(owners, chunks):
    lines = -(-owners * len(chunks) * list_room(chunks) // FREQ)
    return lines, -(-(2 * lines + 1) // 16) * 16


def list_spot(owner, chunk, chunks):
    number = owner * len(chunks) + chunk
    at = number * list_room(chunks)
    return number, quot(at, FREQ), rest(at, FREQ)


def list_slots(cls_dev):
    return -(-cls_dev * MOST // 8) * 8


def quot(v, n):
    return v >> (n.bit_length() - 1) if n & (n - 1) == 0 else v // n


def rest(v, n):
    return v & (n - 1) if n & (n - 1) == 0 else v % n


def odd_tiles(rows):
    return (-(-rows // 8) | 1) * 8


def rounded(v):
    return v.astype(BF16).astype(F32)


def row_of(x, r, depth):
    return r // depth * 2 * depth + x * depth + r % depth


def parts_of(image, depth):
    pieces = image.reshape(image.shape[0] // (2 * depth), 2, depth, FREQ)
    return pieces[:, 0], pieces[:, 1]


def chunks_of(cls_dev):
    return ((0, cls_dev),)


def block_lists(named, owners, cls_dev, chunks):
    per = named.shape[0]
    pairs = per * CAND
    square = (pairs, pairs)
    wide = jnp.broadcast_to(named[:, None, :], (per, CAND, CAND)).reshape(pairs, CAND)
    own = lax.broadcasted_iota(jnp.int32, wide.shape, 0) % CAND == lanes_of(wide.shape)
    cls = jnp.broadcast_to(jnp.sum(jnp.where(own, wide, 0.0), axis=1, keepdims=True), square)
    owner = sum((cls >= o * cls_dev).astype(F32) for o in range(1, owners))
    local = cls - owner * cls_dev
    number = owner * len(chunks)
    if len(chunks) > 1:
        number = number + (local < chunks[0][0]).astype(F32)
    row = lax.broadcasted_iota(jnp.int32, square, 0)
    lane = lanes_of(square)

    def across(column):
        return jnp.sum(jnp.where(row == lane, column, 0.0), axis=0, keepdims=True)

    same = (number == across(number)).astype(F32)
    place = jnp.sum(jnp.where(lane < row, same, 0.0), axis=1, keepdims=True)
    held = jnp.sum(same, axis=1, keepdims=True).astype(jnp.int32)
    place = place + rest(UNROLL - rest(held, UNROLL), UNROLL).astype(F32)
    room = list_room(chunks)
    lines, height = list_lines(owners, chunks)
    slots = lines * FREQ
    target = (number[:, :1] * room + place).astype(jnp.int32)
    hot = (target == lanes_of((pairs, slots))).astype(F32).astype(BF16)
    values = jnp.concatenate(
        [
            lanes_of((1, pairs)).astype(F32), across(local), jnp.ones((1, pairs), F32),
            jnp.zeros((5, pairs), F32),
        ],
        axis=0,
    ).astype(BF16)
    placed = jnp.dot(values, hot, preferred_element_type=F32)
    rows_line = placed[0:1]
    cls_line = placed[1:2] + (1.0 - placed[2:3]) * cls_dev
    counts = jnp.sum((number == lane.astype(F32)).astype(F32), axis=0, keepdims=True)
    counts = quot(counts.astype(jnp.int32) + UNROLL - 1, UNROLL).astype(F32)
    cut = [v[:, n * FREQ : (n + 1) * FREQ] for v in (rows_line, cls_line) for n in range(lines)]
    return jnp.concatenate(
        cut + [counts, jnp.zeros((height - 2 * lines - 1, FREQ), F32)], axis=0
    )


def weigh_kernel(
    slices, owners, cls_dev, chunks, grp_s, particles_h, cand_h, groups_h, entries_h, ctf_h, prec_h, message_out, *refs
):
    slice_outs = refs[: slices - 1]
    particles, cand, groups, entries, ctf, prec, hot_g, hot_e, spread, sem = refs[slices - 1 :]
    depth = SHELLS // slices
    z = grp_s[0] // 2
    copies = [
        pltpu.make_async_copy(a, b, sem.at[n])
        for n, (a, b) in enumerate(
            (
                (groups_h, groups), (entries_h, entries), (ctf_h, ctf), (prec_h, prec),
                (cand_h, cand), (particles_h, particles),
            )
        )
    ]
    for copy in copies:
        copy.start()
    per = particles.shape[0]
    pad = spread.shape[0] // (IMG + 1)
    for copy in copies[:2]:
        copy.wait()
    for i in range(per):
        hot_g[i : i + 1, :] = (lanes_of((1, hot_g.shape[1])) == groups[i]).astype(F32)
        hot_e[i : i + 1, :] = (lanes_of((1, hot_e.shape[1])) == entries[i]).astype(F32)
    for copy in copies[2:5]:
        copy.wait()
    p = jnp.dot(hot_g[...], prec[...], precision=HIGH, preferred_element_type=F32)
    c = lax.dot_general(
        hot_e[...], ctf[...], (((1,), (1,)), ((), ())), precision=HIGH, preferred_element_type=F32
    )
    eye = (lanes_of((per, per)) == lax.broadcasted_iota(jnp.int32, (per, per), 0)).astype(F32)
    named = lax.dot_general(
        eye, cand[...].astype(F32), (((1,), (1,)), ((), ())), precision=HIGH,
        preferred_element_type=F32,
    )
    factors = p * c
    extra = jnp.concatenate(
        [factors * c, named, jnp.zeros((per, FREQ - SHELLS - CAND), F32)], axis=1
    )
    message_out[per * IMG : per * (IMG + 1), :] = extra.astype(BF16)
    message_out[per * (IMG + 1) :, :] = block_lists(named, owners, cls_dev, chunks).astype(BF16)
    copies[5].wait()
    for r in range(SHELLS):
        factor = jnp.broadcast_to(factors[:, r : r + 1], (per, FREQ))
        for x in range(2):
            at = x * SHELLS + r
            piece = particles[:, at * FREQ : (at + 1) * FREQ].astype(F32) * factor
            at = row_of(x, r, depth)
            spread[at * pad : at * pad + per, :] = rounded(piece)
    rows = 2 * depth
    for i in range(per):
        message_out[i * IMG : (i + 1) * IMG, :] = spread[i : i + IMG * pad : pad, :].astype(BF16)
        for d, out in enumerate(slice_outs, start=1):
            row = pl.multiple_of(i * IMG + (z ^ d) * rows, rows)
            out[i * rows : (i + 1) * rows, :] = message_out[pl.ds(row, rows), :]


def prep_kernel(depth, grp_s, refs_h, *rest_refs):
    tables_h, (reg_h, prior), rest_refs = rest_refs[:2], rest_refs[2:4], rest_refs[4:]
    (rf_out, pow_out), tables_out, (reg_out,) = rest_refs[:2], rest_refs[2:4], rest_refs[4:5]
    refs, spread, reg, sem = rest_refs[5:]
    cls_dev = refs.shape[0]
    pow_out[cls_dev:, :] = jnp.zeros((pow_out.shape[0] - cls_dev, FREQ), F32)
    pad = spread.shape[0] // (IMG + 1)
    parts = sem.shape[0] - 3
    step = FEAT // parts
    tables_in = [
        pltpu.make_async_copy(a, b, sem.at[parts + n])
        for n, (a, b) in enumerate(zip((*tables_h, reg_h), (*tables_out, reg)))
    ]
    copies = [
        pltpu.make_async_copy(
            refs_h.at[:, pl.ds(n * step, step)], refs.at[:, pl.ds(n * step, step)], sem.at[n]
        )
        for n in range(parts)
    ]
    turns = parts // 2
    for n in range(turns):
        copies[n].start()
        copies[n + turns].start()
    for copy in tables_in:
        copy.start()

    def shell(r, power):
        parts = []
        for x in range(2):
            at = x * SHELLS + r
            piece = refs[:, pl.ds(pl.multiple_of(at * FREQ, FREQ), FREQ)].astype(F32)
            at = row_of(x, r, depth)
            spread[pl.ds(pl.multiple_of(at * pad, 8), cls_dev), :] = piece
            parts.append(piece * piece)
        total = jnp.sum(parts[0] + parts[1], axis=1, keepdims=True)
        return jnp.where(lanes_of((cls_dev, FREQ)) == r, total, power)

    power = jnp.zeros((cls_dev, FREQ), F32)
    for n in range(turns):
        copies[n].wait()
        copies[n + turns].wait()
        low, high = n * SHELLS // turns, (n + 1) * SHELLS // turns
        power = lax.fori_loop(low, high, shell, power, unroll=4)
    line = jnp.broadcast_to(prior[...].astype(F32).reshape(1, cls_dev), (cls_dev, cls_dev))
    diagonal = lax.broadcasted_iota(jnp.int32, line.shape, 0) == lanes_of(line.shape)
    column = jnp.sum(jnp.where(diagonal, line, 0.0), axis=1, keepdims=True)
    pow_out[:cls_dev, :] = jnp.where(lanes_of((cls_dev, FREQ)) == SHELLS, column, power)

    def image(k, _):
        rf_out[k] = spread[pl.ds(k, IMG, stride=pad), :]
        return 0

    lax.fori_loop(0, cls_dev, image, 0, unroll=4)
    for copy in tables_in:
        copy.wait()
    width = reg_out.shape[0]
    for r in range(width):
        reg_out[r : r + 1, :] = jnp.full((1, FREQ), reg[grp_s[0] * width + r], F32)


def take(refs, counts):
    taken = []
    for count in counts:
        taken.append(refs[:count])
        refs = refs[count:]
    return taken, refs


def score_kernel(arrays, earlier, depth, chunks, half, first_s, owner_s, *refs):
    blocks = len(arrays)
    messages, refs = take(refs, arrays)
    (earlier_stats,), refs = take(refs, (earlier,))
    rf, power, scoring = refs[:3]
    scores_out, stats_out, cls_out = refs[3:-6]
    ints_v, ints_s, side, ex, w32, sem = refs[-6:]
    per = side.shape[1]
    height = ints_v.shape[1]
    cls_dev = rf.shape[0] - 1
    block_rows = per * CAND
    first = first_s[0]
    table = scoring[...]
    done = 0
    for one in earlier_stats:
        stats_out[done : done + one.shape[0], :] = one[...]
        done += one.shape[0]

    extras = []
    for b in range(blocks):
        last = messages[b][-1]
        end = last.shape[0] - height
        ints_v[b] = last[end:, :].astype(F32).astype(jnp.int32)
        extras.append(last[end - per : end, :].astype(F32))
    copies = [pltpu.make_async_copy(ints_v.at[b], ints_s.at[b], sem.at[b]) for b in range(blocks)]
    for copy in copies:
        copy.start()
    for b in range(blocks):
        lane = lanes_of((per, FREQ))
        side[b] = jnp.where(lane < SHELLS, extras[b], (lane == SHELLS).astype(F32))
        begin = 0
        for one in messages[b]:
            count = one.shape[0] // IMG

            def widen(i, _):
                w32[b * per + begin + i] = one[pl.ds(pl.multiple_of(i * IMG, IMG), IMG), :].astype(F32)
                return 0

            lax.fori_loop(0, count, widen, 0, unroll=2)
            begin += count
    for copy in copies:
        copy.wait()

    for b in range(blocks):
        for c in range(len(chunks)):
            number, line, lane = list_spot(owner_s[0], c, chunks)

            def pairs(step, _):
                for u in range(UNROLL):
                    row = ints_s[b, line, lane + step * UNROLL + u]
                    k = ints_s[b, line + half, lane + step * UNROLL + u]
                    i = quot(row, CAND)
                    w_re, w_im = parts_of(w32[b * per + i], depth)
                    a_re, a_im = parts_of(rf[k], depth)
                    inner = (w_re * a_re + w_im * a_im).reshape(SHELLS, FREQ)
                    outer = (w_re * a_im - w_im * a_re).reshape(SHELLS, FREQ)
                    ex[0, pl.ds(row, 1), :] = jnp.sum(inner, axis=0, keepdims=True)
                    ex[1, pl.ds(row, 1), :] = jnp.sum(outer, axis=0, keepdims=True)
                    ex[2, pl.ds(row, 1), :] = side[b, pl.ds(i, 1), :] * power[pl.ds(k, 1), :]
                return 0

            lax.fori_loop(0, ints_s[b, 2 * half, number], pairs, 0)

        wide = jnp.broadcast_to(
            extras[b][:, None, :], (per, CAND, FREQ)
        ).reshape(block_rows, FREQ)
        own = lanes_of((block_rows, FREQ)) == SHELLS + (
            lax.broadcasted_iota(jnp.int32, (block_rows, FREQ), 0) % CAND
        )
        column = jnp.sum(jnp.where(own, wide, 0.0), axis=1, keepdims=True) - first.astype(F32)
        cls_out[b * block_rows : (b + 1) * block_rows, :] = jnp.broadcast_to(
            column, (block_rows, FREQ)
        )
        good = jnp.logical_and(column >= 0, column < cls_dev)
        values = jnp.zeros((block_rows, ROTS), F32)
        for part in range(3):
            values = values + jnp.dot(
                jnp.where(good, ex[part, :block_rows, :], 0.0),
                table[part * FREQ : (part + 1) * FREQ],
                precision=HIGH,
                preferred_element_type=F32,
            )
        scores = jnp.where(good, values, LOW)
        scores_out[b * block_rows : (b + 1) * block_rows, :] = scores
        top = jnp.broadcast_to(jnp.max(scores, axis=1, keepdims=True), (block_rows, ROTS))
        best = jnp.max(top.reshape(per, CAND, ROTS), axis=1)
        best_rows = jnp.broadcast_to(best[:, None, :], (per, CAND, ROTS)).reshape(block_rows, ROTS)
        mass = jnp.where(good, jnp.exp(scores - best_rows), 0.0)
        mass = jnp.broadcast_to(jnp.sum(mass, axis=1, keepdims=True), (block_rows, ROTS))
        total = jnp.sum(mass.reshape(per, CAND, ROTS), axis=1)
        stats_out[done + b * per : done + (b + 1) * per, :ROTS] = best
        stats_out[done + b * per : done + (b + 1) * per, ROTS:] = total


def two(v):
    return jnp.where(lanes_of(v.shape) < ROTS, rounded(v), v - rounded(v))


def one_of_two(v):
    return v + pltpu.roll(v, ROTS, 1)


def weights_kernel(calls, blocks, slices, cls_dev, chunks, grp_s, owner_s, *refs):
    stats = refs[:blocks]
    scores = refs[blocks : blocks + calls]
    classes = refs[blocks + calls : blocks + 2 * calls]
    extras = refs[blocks + 2 * calls : 2 * blocks + 2 * calls]
    refs = refs[2 * blocks + 2 * calls :]
    own_out, den_out, mass_out, log_out, ints_out = refs[:5]
    message_outs = refs[5:-4]
    rows_v, den_v, lists_v, picked_v = refs[-4:]
    per = log_out.shape[0]
    block_rows = per * CAND
    depth = SHELLS // slices
    z = grp_s[0] // 2

    half = list_lines(blocks, chunks)[0]
    _, line, lane = list_spot(owner_s[0], 0, chunks)
    slots = list_slots(cls_dev)
    lists = []

    den = jnp.zeros((FREQ, FREQ), F32)
    mass = jnp.zeros((1, FREQ), F32)
    block = 0
    for scores_ref, cls_ref in zip(scores, classes):
        for b in range(scores_ref.shape[0] // block_rows):
            ones = [stats[d][(block ^ d) * per : ((block ^ d) + 1) * per, :] for d in range(blocks)]
            best = functools.reduce(jnp.maximum, [one[:, :ROTS] for one in ones])
            total = sum(one[:, ROTS:] * jnp.exp(one[:, :ROTS] - best) for one in ones)
            if block == 0:
                log_out[...] = jnp.log(total)

            def over_rows(v):
                return jnp.broadcast_to(v[:, None, :], (per, CAND, ROTS)).reshape(block_rows, ROTS)

            at = slice(b * block_rows, (b + 1) * block_rows)
            weights = jnp.exp(scores_ref[at, :] - over_rows(best)) / over_rows(total)
            local = cls_ref[at, :]
            good = jnp.logical_and(local >= 0, local < cls_dev)[:, :ROTS]
            weights = rounded(jnp.where(good, weights, 0.0))
            lists_v[...] = extras[block][extras[block].shape[0] - lists_v.shape[0] :, :].astype(F32)
            named = jnp.broadcast_to(lists_v[pl.ds(line, 1), :], (block_rows, FREQ))
            row = lax.broadcasted_iota(jnp.int32, named.shape, 0).astype(F32)
            picked_v[...] = lax.dot_general(
                (named == row).astype(F32).astype(BF16), weights.astype(BF16),
                (((0,), (0,)), ((), ())), preferred_element_type=F32,
            )
            at = block * slots
            rows_v[at : at + slots, :] = picked_v[pl.ds(pl.multiple_of(lane, 8), slots), :]
            for source in (line, line + half, 2 * half):
                lists.append(lists_v[pl.ds(source, 1), :])
            pair_sum = jnp.sum(weights, axis=1, keepdims=True)
            twice = (lanes_of((block_rows, FREQ)) % ROTS).astype(F32)
            chosen = jnp.where(twice == local, pair_sum, 0.0)
            by_particle = jnp.sum(chosen.reshape(per, CAND, FREQ), axis=1)
            end = extras[block].shape[0] - lists_v.shape[0]
            side = extras[block][end - per : end, :].astype(F32)
            den = den + lax.dot_general(
                side, by_particle, (((0,), (0,)), ((), ())), precision=HIGH,
                preferred_element_type=F32,
            )
            mass = mass + jnp.sum(by_particle, axis=0, keepdims=True)
            block += 1

    lines = rows_v.shape[0] // 2
    packed = jnp.concatenate([rows_v[:lines, :], rows_v[lines:, :]], axis=1).astype(BF16)
    own_out[...] = packed
    den_v[...] = den[:SHELLS].reshape(slices, depth, FREQ)
    mass_rows = jnp.broadcast_to(mass, (8, FREQ))
    mass_out[...] = mass_rows
    den_out[...] = den_v[z]
    if ints_out.shape[0] > len(lists):
        lists.append(jnp.zeros((ints_out.shape[0] - len(lists), FREQ), F32))
    lists = jnp.concatenate(lists, axis=0)
    ints_out[...] = lists.astype(jnp.int32)
    tail = [two(mass_rows), lists]
    tail_rows = depth + sum(one.shape[0] for one in tail)
    spare = message_outs[0].shape[0] - lines - tail_rows
    if spare:
        tail.append(jnp.zeros((spare, FREQ), F32))
    for d, out in enumerate(message_outs, start=1):
        out[:lines, :] = packed
        out[lines:, :] = jnp.concatenate([two(den_v[z ^ d])] + tail, axis=0).astype(BF16)


def put_phases(packed, table, wcs, base):
    lines = packed.shape[0]
    twice = jnp.concatenate([packed, packed], axis=1)
    both = rounded(jnp.dot(twice, table[...], preferred_element_type=F32))
    for place in range(2):
        for part in range(2):
            at = (2 * place + part) * FREQ
            row = base + place * lines
            wcs[part, row : row + lines, :] = both[:, at : at + FREQ]


def add_pair(image, row, k, wcs, num):
    shape = num.shape[1:]
    image = image.astype(F32)
    half = image.shape[0] // 2
    w_re, w_im = image[:half].reshape(shape[1:]), image[half:].reshape(shape[1:])
    c = wcs[0, pl.ds(row, 1), :].reshape(1, 1, FREQ)
    s = wcs[1, pl.ds(row, 1), :].reshape(1, 1, FREQ)
    num[k, 0] += w_re * c - w_im * s
    num[k, 1] += w_re * s + w_im * c


def pick_image(arrays, begin, i, rows, stride, offset):
    def rows_at(one, i):
        return one[pl.ds(pl.multiple_of(i * stride + offset, rows), rows), :]

    held = [one.shape[0] // stride for one in arrays]
    while len(arrays) > 1 and begin >= held[0]:
        arrays, begin, held = arrays[1:], begin - held[0], held[1:]
    if len(arrays) == 1:
        return rows_at(arrays[0], begin + i)
    cut = held[0] - begin
    return jnp.where(
        i < cut,
        rows_at(arrays[0], begin + jnp.minimum(i, cut - 1)),
        rows_at(arrays[1], jnp.maximum(i - cut, 0)),
    )


def own_sum_kernel(chunks, arrays, grp_s, owner_s, packed, ints, *refs):
    messages, refs = take(refs, arrays)
    phases, (num, wcs, ints_s, sem) = refs[:1], refs[1:]
    copy = pltpu.make_async_copy(ints, ints_s, sem)
    copy.start()
    per = sum(one.shape[0] for one in messages[0]) // IMG
    rows = 2 * num.shape[2] * num.shape[3]
    z = grp_s[0] // 2
    put_phases(packed[...], phases[0], wcs, 0)
    num[...] = jnp.zeros_like(num)
    copy.wait()
    for block, held_in in enumerate(messages):
        base = block * list_slots(num.shape[0] - 1)
        for c in range(len(chunks)):
            number, _, lane = list_spot(owner_s[0], c, chunks)

            def pairs(step, _):
                for u in range(UNROLL):
                    row = ints_s[3 * block, lane + step * UNROLL + u]
                    k = ints_s[3 * block + 1, lane + step * UNROLL + u]
                    image = pick_image(held_in, 0, quot(row, CAND), rows, IMG, z * rows)
                    add_pair(image, base + step * UNROLL + u, k, wcs, num)
                return 0

            lax.fori_loop(0, ints_s[3 * block + 2, number], pairs, 0)


def join_kernel(*refs):
    out = refs[-1]
    rows = refs[0].shape[0]
    for n, one in enumerate(refs[:-1]):
        out[n * rows : (n + 1) * rows, :] = one[...]


def read_tail(message, lines, depth, count):
    tail = message[lines:, :].astype(F32)
    den, mass = one_of_two(tail[:depth]), one_of_two(tail[depth : depth + 8])
    return den, mass, tail[depth + 8 : depth + 8 + count].astype(jnp.int32)


def add_planes(planes, owner, chunks, images, wcs, *nums):
    number, _, lane = list_spot(owner, 0, chunks)
    num = nums[0]
    slots = list_slots(num.shape[0] - 1)
    rows = 2 * num.shape[2] * num.shape[3]
    per = FREQ // CAND
    for first in range(0, len(images), 2):
        group = [
            (d, ints, base + block * slots, block)
            for d, ints, base in planes
            for block in range(first, min(first + 2, len(images)))
        ]
        counts = [ints[3 * block + 2, number] for _, ints, _, block in group]

        def pairs(step, _):
            for d, ints, start, block in group:
                for u in range(UNROLL):
                    slot = step * UNROLL + u
                    row = ints[3 * block, lane + slot]
                    k = ints[3 * block + 1, lane + slot]
                    image = pick_image(images[block], d * per, quot(row, CAND), rows, rows, 0)
                    add_pair(image, start + slot, k, wcs, nums[u % len(nums)])
            return 0

        lax.fori_loop(0, functools.reduce(jnp.maximum, counts), pairs, 0)


def near_sum_kernel(chunks, pieces, owner_s, *refs):
    images, refs = take(refs, pieces)
    message, first, phases, den_in, mass_in, num, den_out, mass_out, wcs, ints_v, ints_s, sem = refs
    lines = wcs.shape[1] // 2
    depth = den_in.shape[0]
    den, mass, ints_v[...] = read_tail(message, lines, depth, ints_v.shape[0])
    copy = pltpu.make_async_copy(ints_v, ints_s, sem)
    copy.start()
    den_out[...] = den_in[...] + den
    mass_out[...] = mass_in[...] + mass
    put_phases(message[:lines, :], phases, wcs, 0)
    num[...] = first[...]
    copy.wait()
    add_planes([(0, ints_s, 0)], owner_s[0], chunks, images, wcs, num)


def sum_kernel(chunk, chunks, slices, pieces, grp_s, owner_s, *refs):
    images, refs = take(refs, pieces)
    messages, refs = refs[: slices - 2], refs[slices - 2 :]
    first, refs = refs[0], refs[1:]
    if chunk == 0:
        phases, (den_in, mass_in), refs = refs[0], refs[1:3], refs[3:]
        own_out, sib_out, den_out, mass_out, wcs, ints_s, num, more, den_v, ints_v, sem = refs
    else:
        wcs, ints_s, own_out, sib_out, num, more = refs
    group_rows = wcs.shape[1] // (slices - 2)
    lines = group_rows // 2
    core = grp_s[0] % 2
    start, size = chunks[chunk]
    depth = num.shape[2] * num.shape[3]

    if chunk == 0:
        den, mass = den_in[...], mass_in[...]
        for n, message in enumerate(messages):
            more_den, more_mass, ints_v[n] = read_tail(message, lines, depth, ints_v.shape[1])
            den, mass = den + more_den, mass + more_mass
        copies = [
            pltpu.make_async_copy(ints_v.at[n], ints_s.at[n], sem.at[n])
            for n in range(slices - 2)
        ]
        for copy in copies:
            copy.start()
        for n, message in enumerate(messages):
            put_phases(message[:lines, :], phases, wcs, n * group_rows)
    num[...] = first[...]
    more[...] = jnp.zeros_like(more)
    if chunk == 0:
        for copy in copies:
            copy.wait()
    planes = [(n + 1, ints_s.at[n], n * group_rows) for n in range(slices - 2)]
    add_planes(planes, owner_s[0], chunks, images, wcs, num, more)

    def pack(k, _):
        for out, at in ((own_out, core), (sib_out, 1 - core)):
            halves = [num[k, x, at] + more[k, x, at] for x in range(2)]
            out[k] = jnp.concatenate(halves, axis=0).astype(out.dtype)
        return 0

    lax.fori_loop(0, size, pack, 0, unroll=4)
    if chunk == 0:
        width = num.shape[3]
        den_v[...] = den.reshape(2, width, FREQ)
        den_out[...] = den_v[core]
        mass_out[...] = mass
        sib_out[size] = jnp.concatenate([two(den_v[1 - core]), two(mass)[:width]], axis=0).astype(BF16)


def divide(own, sib, inverse, start, avg_out):
    for k in range(avg_out.shape[0]):
        column = inverse[:, start + k : start + k + 1]
        factor = jnp.concatenate([column, column], axis=0)
        avg_out[k] = ((own[k] + sib[k].astype(F32)) * factor).astype(BF16)


def first_divide_kernel(scale, start, own, sib, den, mass, reg, avg_out, share_out, inverse_out):
    cut = avg_out.shape[0]
    width = avg_out.shape[1] // 2
    tile = one_of_two(sib[cut].astype(F32))
    share_out[...] = (tile[width : width + 1] + mass[:1]) * scale
    inverse = 1.0 / (tile[:width] + den[...] + reg[...])
    inverse_out[...] = inverse
    divide(own, sib, inverse, start, avg_out)


def next_divide_kernel(start, own, sib, inverse, avg_out):
    divide(own, sib, inverse[...], start, avg_out)


def spread_kernel(planes, chunks, has_out, grp_s, *refs):
    held = 2 * len(planes) * len(chunks)
    arrays, (out, wide, columns, sem) = refs[:held], refs[held + has_out :]
    width = arrays[0].shape[1] // 2
    cls_dev = columns.shape[1]
    pad = wide.shape[0] // (len(planes) * 4 * width + 1)
    z, h = grp_s[0] // 2, grp_s[0] % 2
    copies = []
    for n, d in enumerate(planes):
        for c, (start, cut) in enumerate(chunks):
            pair = arrays[2 * (n * len(chunks) + c) :][:2]

            def one(k, _):
                for side, array in enumerate(pair):
                    piece = array[k].astype(F32)
                    for x in range(2):
                        at = (n * 4 + side * 2 + x) * width * pad + start
                        wide[pl.ds(at + k, width, stride=pad), :] = piece[
                            x * width : (x + 1) * width
                        ]
                return 0

            lax.fori_loop(0, cut, one, 0, unroll=2)
        for side, core in enumerate((h, 1 - h)):
            for x in range(2):
                group = n * 4 + side * 2 + x
                for r in range(width):
                    at = (group * width + r) * pad
                    columns[group, :, r * FREQ : (r + 1) * FREQ] = wide[at : at + cls_dev, :]
                first = (x * SHELLS + ((z ^ d) * 2 + core) * width) * FREQ
                first = pl.multiple_of(first, width * FREQ)
                copies.append(
                    pltpu.make_async_copy(
                        columns.at[group], out.at[:, pl.ds(first, width * FREQ)], sem.at[group]
                    )
                )
                copies[-1].start()
    for copy in copies:
        copy.wait()


def whole(space):
    return pl.BlockSpec(memory_space=space)


def in_hbm(value):
    return pltpu.with_memory_space_constraint(value, HBM)


def call(kernel, name, ins, outs, scratch, mib, us, args, **more):
    cost = pl.CostEstimate(flops=0, bytes_accessed=int(us * 3.6e6), transcendentals=0)
    return pl.pallas_call(
        kernel,
        out_shape=tuple(s for s, _ in outs),
        in_specs=[whole(s) for s in ins],
        out_specs=tuple(whole(s) for _, s in outs),
        scratch_shapes=scratch,
        compiler_params=pltpu.CompilerParams(vmem_limit_bytes=mib * 2**20),
        name=name,
        cost_estimate=cost,
        **more,
    )(*args)


def swap(value, axis, distance):
    size = lax.axis_size(axis)
    return lax.ppermute(value, axis, [(i, i ^ distance) for i in range(size)])


def after(value, *others):
    return lax.optimization_barrier((value, *others))[0]


def per_device(
    particles, candidates, group_ids, ctf_ids, ctf_table, noise_prec, references, log_prior, reg
):
    n_cls = lax.axis_size("cls")
    n_grp = lax.axis_size("grp")
    per = particles.shape[0]
    cls_dev = references.shape[0]
    block_rows = per * CAND
    chunks = chunks_of(cls_dev)
    pad = odd_tiles(cls_dev)
    width = SHELLS // n_grp
    nz = n_grp // 2
    scoring, phases = (jnp.asarray(t) for t in tables())
    owner = lax.axis_index("cls").astype(jnp.int32).reshape(1)
    first = owner * cls_dev
    grp = lax.axis_index("grp").astype(jnp.int32).reshape(1)

    depth = SHELLS // nz
    message, *sliced = call(
        functools.partial(weigh_kernel, nz, n_cls, cls_dev, chunks), "weigh", [SMEM] + [HBM] * 6,
        [(SHAPE((per * (IMG + 1) + list_lines(n_cls, chunks)[1], FREQ), BF16), VMEM)]
        + [(SHAPE((per * 2 * depth, FREQ), BF16), VMEM)] * (nz - 1),
        [
            VMEM(particles.shape, BF16),
            VMEM((CAND, per), jnp.int32),
            SMEM((per,), jnp.int32),
            SMEM((per,), jnp.int32),
            VMEM(ctf_table.shape[::-1], F32),
            VMEM(noise_prec.shape, F32),
            VMEM((per, noise_prec.shape[0]), F32),
            VMEM((per, ctf_table.shape[0]), F32),
            VMEM(((IMG + 1) * odd_tiles(per), FREQ), F32),
            pltpu.SemaphoreType.DMA((6,)),
        ],
        5, 2.0,
        (grp,)
        + tuple(
            in_hbm(a)
            for a in (particles, candidates.T, group_ids, ctf_ids, ctf_table.T, noise_prec)
        ),
    )

    if n_cls == 4:
        message_1, message_2 = swap(message, "cls", 1), swap(message, "cls", 2)
    sliced = [swap(one, "grp", 2 * d) for d, one in enumerate(sliced, start=1)]

    rf, power, scoring, phases, own_reg = call(
        functools.partial(prep_kernel, depth), "prep", [SMEM] + [HBM] * 4 + [VMEM],
        [(SHAPE((cls_dev + 1, IMG, FREQ), F32), VMEM), (SHAPE((cls_dev + 1, FREQ), F32), VMEM)]
        + [(SHAPE(t.shape, t.dtype), VMEM) for t in (scoring, phases)]
        + [(SHAPE((width, FREQ), F32), VMEM)],
        [
            VMEM(references.shape, BF16),
            VMEM(((IMG + 1) * pad, FREQ), F32),
            SMEM(reg.shape, F32),
            pltpu.SemaphoreType.DMA((7,)),
        ],
        8, 4.0,
        (grp,)
        + tuple(in_hbm(a) for a in (references, scoring, phases, reg))
        + (log_prior,),
    )

    half, height = list_lines(n_cls, chunks)

    def score(part, earlier=()):
        blocks = len(part)
        flat = [m for arrays in part for m in arrays]
        earlier = tuple(s[1] for s in earlier)
        ahead = sum(s.shape[0] for s in earlier)
        counts = tuple(len(arrays) for arrays in part)
        return call(
            functools.partial(score_kernel, counts, len(earlier), depth, chunks, half), "score",
            [SMEM] * 2 + [VMEM] * (len(flat) + len(earlier) + 3),
            [
                (SHAPE((blocks * block_rows, ROTS), F32), VMEM),
                (SHAPE((ahead + blocks * per, FREQ), F32), VMEM),
                (SHAPE((blocks * block_rows, FREQ), F32), VMEM),
            ],
            [
                VMEM((blocks, height, FREQ), jnp.int32),
                SMEM((blocks, height, FREQ), jnp.int32),
                VMEM((blocks, per, FREQ), F32),
                VMEM((3, block_rows, FREQ), F32),
                VMEM((blocks * per, IMG, FREQ), F32),
                pltpu.SemaphoreType.DMA((blocks,)),
            ],
            6 if n_cls == 4 else 40, 3.0 * blocks, (first, owner, *flat, *earlier, rf, power, scoring),
        )

    def join(got):
        (joined,) = call(
            join_kernel, "join", [VMEM] * (nz - 1),
            [(SHAPE(((nz - 1) * per * 2 * depth, FREQ), BF16), VMEM)], [], 2, 0.5, got,
        )
        return joined

    if n_cls == 4:
        cut = per // 2 * IMG
        scored = [score([(after(message, sliced[0]),)])]
        ready = (scored[0][1], sliced[1])
        message_1, message_2 = after(message_1, *ready), after(message_2, *ready)
        message_3 = (swap(message_1[:cut], "cls", 2), swap(message_2[cut:], "cls", 1))
        messages = [(message,), (message_1,), (message_2,), message_3]
        scored += [score(messages[1:3])]
        joined = join([after(sliced[0], scored[1][1], *message_3)] + sliced[1:])
        joined_1, joined_2 = swap(joined, "cls", 1), swap(joined, "cls", 2)
        scored += [score(messages[3:], scored)]
    else:
        messages = [(message,)] + [(swap(message, "cls", d),) for d in range(1, n_cls)]
        scored = [score(messages)]
        joined = join(sliced)
        images = [joined] + [swap(joined, "cls", d) for d in range(1, n_cls)]
        pieces = (1,) * n_cls
    arrays = tuple(len(m) for m in messages)
    stats = scored[-1][1]
    all_stats = [stats] + [swap(stats, "cls", d) for d in range(1, n_cls)]
    flat = [m for held in messages for m in held]

    lines = n_cls * list_slots(cls_dev) // 2
    own_lists = SHAPE((-(-3 * n_cls // 8) * 8, FREQ), jnp.int32)
    outgoing_rows = -(-(lines + depth + 8 + own_lists.shape[0]) // 16) * 16
    packed, den, mass, log_mass, ints, *outgoing = call(
        functools.partial(weights_kernel, len(scored), n_cls, nz, cls_dev, chunks), "weights",
        [SMEM] * 2 + [VMEM] * (2 * n_cls + 2 * len(scored)),
        [
            (SHAPE((lines, FREQ), BF16), VMEM),
            (SHAPE((depth, FREQ), F32), VMEM),
            (SHAPE((8, FREQ), F32), VMEM),
            (SHAPE((per, ROTS), F32), VMEM),
            (own_lists, VMEM),
        ]
        + [(SHAPE((outgoing_rows, FREQ), BF16), VMEM)] * (nz - 1),
        [
            VMEM((2 * lines, ROTS), F32),
            VMEM((nz, depth, FREQ), F32),
            VMEM((height, FREQ), F32),
            VMEM((block_rows, ROTS), F32),
        ],
        4 if n_cls == 4 else 12, 2.0,
        (
            grp, owner, *all_stats, *(s[0] for s in scored), *(s[2] for s in scored),
            *(held[-1] for held in messages),
        ),
    )
    incoming = [swap(one, "grp", 2 * d) for d, one in enumerate(outgoing, start=1)]
    if n_cls == 4:
        cut = joined.shape[0] // 2
        joined_1, joined_2 = after(joined_1, packed), after(joined_2, packed)
        joined_3 = [swap(joined_1[:cut], "cls", 2), swap(joined_2[cut:], "cls", 1)]
        images = [joined, joined_1, joined_2, *joined_3]
        pieces = (1, 1, 1, 2)
    (first_sums,) = call(
        functools.partial(own_sum_kernel, chunks, arrays), "own_sum",
        [SMEM] * 2 + [VMEM] * (len(flat) + 3),
        [(SHAPE((cls_dev + 1, 2, 2, width, FREQ), F32), VMEM)],
        [
            VMEM((2, 2 * lines, FREQ), F32),
            SMEM(own_lists.shape, jnp.int32),
            pltpu.SemaphoreType.DMA,
        ],
        4 if n_cls == 4 else 12, 3.0, (grp, owner, packed, ints, *flat, phases),
    )
    (near_sums, den, mass) = call(
        functools.partial(near_sum_kernel, chunks, pieces), "near_sum",
        [SMEM] + [VMEM] * (sum(pieces) + 5),
        [
            (SHAPE((cls_dev + 1, 2, 2, width, FREQ), F32), VMEM),
            (SHAPE((depth, FREQ), F32), VMEM),
            (SHAPE((8, FREQ), F32), VMEM),
        ],
        [
            VMEM((2, 2 * lines, FREQ), F32),
            VMEM(own_lists.shape, jnp.int32),
            SMEM(own_lists.shape, jnp.int32),
            pltpu.SemaphoreType.DMA,
        ],
        4 if n_cls == 4 else 12, 2.0,
        (owner, *images, incoming[0], first_sums, phases, den, mass),
    )
    tile = (2 * width, FREQ)
    sums = []
    for chunk, (start, size) in enumerate(chunks):
        more = chunk == 0
        outs = [
            (SHAPE((size,) + tile, F32), VMEM),
            (SHAPE((size + more,) + tile, BF16), VMEM),
        ]
        scratch = [VMEM((size + 1, 2, 2, width, FREQ), F32)] * 2
        spaces = [SMEM] * 2 + [VMEM] * (sum(pieces) + nz - 1)
        if more:
            outs += [
                (SHAPE((width, FREQ), F32), VMEM),
                (SHAPE((8, FREQ), F32), VMEM),
                (SHAPE((2, (nz - 2) * (2 * lines), FREQ), F32), VMEM),
                (SHAPE((nz - 2,) + own_lists.shape, jnp.int32), SMEM),
            ]
            scratch += [
                VMEM((2, width, FREQ), F32),
                VMEM((nz - 2,) + own_lists.shape, jnp.int32),
                pltpu.SemaphoreType.DMA((nz - 2,)),
            ]
            spaces += [VMEM] * 3
            args = (grp, owner, *images, *incoming[1:], near_sums, phases, den, mass)
        else:
            spaces += [VMEM, SMEM]
            args = (grp, owner, *images, *incoming[1:], near_sums, wcs, lists)
        own, sib, *others = call(
            functools.partial(sum_kernel, chunk, chunks, nz, pieces), "sum",
            spaces, outs, scratch, 5 if n_cls == 4 else 24, 3.0, args,
        )
        if more:
            den, mass, wcs, lists = others
        sums.append((own, sib))

    particle_total = per * n_grp * n_cls
    divided, inverse, share = [], None, None
    for chunk, (own, sib) in enumerate(sums):
        start, cut = chunks[chunk]
        other = swap(sib, "grp", 1)
        averaged_out = (SHAPE((cut,) + tile, BF16), VMEM)
        if chunk == 0:
            averaged, share, inverse = call(
                functools.partial(first_divide_kernel, K / particle_total, start), "divide",
                [VMEM] * 5,
                [averaged_out, (SHAPE((1, FREQ), F32), VMEM), (SHAPE((width, FREQ), F32), VMEM)],
                [], 2, 0.05, (own, other, den, mass, own_reg),
            )
        else:
            (averaged,) = call(
                functools.partial(next_divide_kernel, start), "divide", [VMEM] * 3,
                [averaged_out], [], 2, 0.05, (own, other, inverse),
            )
        divided.append(averaged)

    if nz == 4:
        near = [swap(averaged, "grp", 2) for averaged in divided]
        across = [swap(averaged, "grp", 4) for averaged in divided]
        near, across = lax.optimization_barrier((near, across))
        relayed = [swap(one, "grp", 2) for one in across]
        planes = [list(held) for held in zip(divided, near, across, relayed)]
    else:
        planes = [
            [averaged] + [swap(averaged, "grp", 2 * d) for d in range(1, nz)]
            for averaged in divided
        ]
    averages = None
    for far in ((0, 1, 2), (3,)) if nz == 4 else (tuple(range(nz)),):
        arrays = []
        for d in far:
            for held in planes:
                one = held[d] if averages is None else after(held[d], averages)
                arrays += [one, swap(one, "grp", 1)]
        has_out = averages is not None
        groups = len(far) * 4
        (averages,) = call(
            functools.partial(spread_kernel, far, chunks, has_out), "spread",
            [SMEM] + [VMEM] * len(arrays) + [HBM] * has_out,
            [(SHAPE((cls_dev, FEAT), F32), HBM)],
            [
                VMEM(((groups * width + 1) * odd_tiles(cls_dev), FREQ), F32),
                VMEM((groups, cls_dev, width * FREQ), F32),
                pltpu.SemaphoreType.DMA((groups,)),
            ],
            8, 0.05, (grp, *arrays) + ((averages,) if has_out else ()),
            input_output_aliases={len(arrays) + 1: 0} if has_out else {},
        )
    return (averages, share[0, :cls_dev], log_mass[:, 0])


def solution(mesh):
    return jax.shard_map(
        per_device,
        mesh=mesh,
        in_specs=(
            P(("grp", "cls"), None),
            P(("grp", "cls"), None),
            P(("grp", "cls")),
            P(("grp", "cls")),
            P(),
            P(),
            P("cls", None),
            P("cls"),
            P(),
        ),
        out_specs=(P("cls", None), P("cls"), P(("grp", "cls"))),
        check_vma=False,
    )
```

```python
import functools
import math

import jax
import jax.numpy as jnp
import numpy as np
from jax import lax
from jax.experimental import pallas as pl
from jax.experimental.pallas import tpu as pltpu
from jax.sharding import PartitionSpec as P

SHELLS = 64
FREQ = 128
FEAT = 16384
ROTS = 64
K = 208
CAND = 8
MOST = 2
IMG = 2 * SHELLS
UNROLL = 4
LOW = -1e30
HIGH = lax.Precision.HIGHEST
VMEM = pltpu.VMEM
SMEM = pltpu.SMEM
HBM = pltpu.HBM
F32 = jnp.float32
BF16 = jnp.bfloat16
SHAPE = jax.ShapeDtypeStruct


def tables():
    turns = np.arange(ROTS)[:, None]
    orders = np.arange(FREQ)[None, :]
    angles = ((turns * orders) % ROTS).astype(np.float32) * np.float32(2.0 * math.pi / ROTS)
    cos_tab = np.cos(angles).astype(np.float32)
    sin_tab = np.sin(angles).astype(np.float32)
    last = np.zeros((FREQ, ROTS), np.float32)
    last[:SHELLS] = -0.5
    last[SHELLS] = 1.0
    scoring = np.concatenate([cos_tab.T, sin_tab.T, last], axis=0)
    left = np.concatenate([cos_tab, sin_tab], axis=1)
    terms = []
    for _ in range(2):
        term = left.astype(jnp.bfloat16)
        left = left - term.astype(np.float32)
        blank = np.zeros_like(term)
        terms.append(np.block([[term, blank], [blank, term]]))
    return scoring, np.concatenate(terms, axis=0)


def lanes_of(shape):
    return lax.broadcasted_iota(jnp.int32, shape, len(shape) - 1)


def list_room(chunks):
    return FREQ if max(n for _, n in chunks) * MOST + UNROLL > FREQ // 2 else FREQ // 2


def list_lines(owners, chunks):
    lines = -(-owners * len(chunks) * list_room(chunks) // FREQ)
    return lines, -(-(2 * lines + 1) // 16) * 16


def list_spot(owner, chunk, chunks):
    number = owner * len(chunks) + chunk
    at = number * list_room(chunks)
    return number, quot(at, FREQ), rest(at, FREQ)


def list_slots(cls_dev):
    return -(-cls_dev * MOST // 8) * 8


def quot(v, n):
    return v >> (n.bit_length() - 1) if n & (n - 1) == 0 else v // n


def rest(v, n):
    return v & (n - 1) if n & (n - 1) == 0 else v % n


def odd_tiles(rows):
    return (-(-rows // 8) | 1) * 8


def rounded(v):
    return v.astype(BF16).astype(F32)


def row_of(x, r, depth):
    return r // depth * 2 * depth + x * depth + r % depth


def parts_of(image, depth):
    pieces = image.reshape(image.shape[0] // (2 * depth), 2, depth, FREQ)
    return pieces[:, 0], pieces[:, 1]


def chunks_of(cls_dev):
    return ((0, cls_dev),)


def block_lists(named, owners, cls_dev, chunks):
    per = named.shape[0]
    pairs = per * CAND
    square = (pairs, pairs)
    wide = jnp.broadcast_to(named[:, None, :], (per, CAND, CAND)).reshape(pairs, CAND)
    own = lax.broadcasted_iota(jnp.int32, wide.shape, 0) % CAND == lanes_of(wide.shape)
    cls = jnp.broadcast_to(jnp.sum(jnp.where(own, wide, 0.0), axis=1, keepdims=True), square)
    owner = sum((cls >= o * cls_dev).astype(F32) for o in range(1, owners))
    local = cls - owner * cls_dev
    number = owner * len(chunks)
    if len(chunks) > 1:
        number = number + (local < chunks[0][0]).astype(F32)
    row = lax.broadcasted_iota(jnp.int32, square, 0)
    lane = lanes_of(square)

    def across(column):
        return jnp.sum(jnp.where(row == lane, column, 0.0), axis=0, keepdims=True)

    same = (number == across(number)).astype(F32)
    place = jnp.sum(jnp.where(lane < row, same, 0.0), axis=1, keepdims=True)
    held = jnp.sum(same, axis=1, keepdims=True).astype(jnp.int32)
    place = place + rest(UNROLL - rest(held, UNROLL), UNROLL).astype(F32)
    room = list_room(chunks)
    lines, height = list_lines(owners, chunks)
    slots = lines * FREQ
    target = (number[:, :1] * room + place).astype(jnp.int32)
    hot = (target == lanes_of((pairs, slots))).astype(F32).astype(BF16)
    values = jnp.concatenate(
        [
            lanes_of((1, pairs)).astype(F32), across(local), jnp.ones((1, pairs), F32),
            jnp.zeros((5, pairs), F32),
        ],
        axis=0,
    ).astype(BF16)
    placed = jnp.dot(values, hot, preferred_element_type=F32)
    rows_line = placed[0:1]
    cls_line = placed[1:2] + (1.0 - placed[2:3]) * cls_dev
    counts = jnp.sum((number == lane.astype(F32)).astype(F32), axis=0, keepdims=True)
    counts = quot(counts.astype(jnp.int32) + UNROLL - 1, UNROLL).astype(F32)
    cut = [v[:, n * FREQ : (n + 1) * FREQ] for v in (rows_line, cls_line) for n in range(lines)]
    return jnp.concatenate(
        cut + [counts, jnp.zeros((height - 2 * lines - 1, FREQ), F32)], axis=0
    )


def weigh_kernel(
    slices, owners, cls_dev, chunks, grp_s, particles_h, cand_h, groups_h, entries_h, ctf_h, prec_h, message_out, *refs
):
    slice_outs = refs[: slices - 1]
    particles, cand, groups, entries, ctf, prec, hot_g, hot_e, spread, sem = refs[slices - 1 :]
    depth = SHELLS // slices
    z = grp_s[0] // 2
    copies = [
        pltpu.make_async_copy(a, b, sem.at[n])
        for n, (a, b) in enumerate(
            (
                (groups_h, groups), (entries_h, entries), (ctf_h, ctf), (prec_h, prec),
                (cand_h, cand), (particles_h, particles),
            )
        )
    ]
    for copy in copies:
        copy.start()
    per = particles.shape[0]
    pad = spread.shape[0] // (IMG + 1)
    for copy in copies[:2]:
        copy.wait()
    for i in range(per):
        hot_g[i : i + 1, :] = (lanes_of((1, hot_g.shape[1])) == groups[i]).astype(F32)
        hot_e[i : i + 1, :] = (lanes_of((1, hot_e.shape[1])) == entries[i]).astype(F32)
    for copy in copies[2:5]:
        copy.wait()
    p = jnp.dot(hot_g[...], prec[...], precision=HIGH, preferred_element_type=F32)
    c = lax.dot_general(
        hot_e[...], ctf[...], (((1,), (1,)), ((), ())), precision=HIGH, preferred_element_type=F32
    )
    eye = (lanes_of((per, per)) == lax.broadcasted_iota(jnp.int32, (per, per), 0)).astype(F32)
    named = lax.dot_general(
        eye, cand[...].astype(F32), (((1,), (1,)), ((), ())), precision=HIGH,
        preferred_element_type=F32,
    )
    factors = p * c
    extra = jnp.concatenate(
        [factors * c, named, jnp.zeros((per, FREQ - SHELLS - CAND), F32)], axis=1
    )
    message_out[per * IMG : per * (IMG + 1), :] = extra.astype(BF16)
    message_out[per * (IMG + 1) :, :] = block_lists(named, owners, cls_dev, chunks).astype(BF16)
    copies[5].wait()
    for r in range(SHELLS):
        factor = jnp.broadcast_to(factors[:, r : r + 1], (per, FREQ))
        for x in range(2):
            at = x * SHELLS + r
            piece = particles[:, at * FREQ : (at + 1) * FREQ].astype(F32) * factor
            at = row_of(x, r, depth)
            spread[at * pad : at * pad + per, :] = rounded(piece)
    rows = 2 * depth
    for i in range(per):
        message_out[i * IMG : (i + 1) * IMG, :] = spread[i : i + IMG * pad : pad, :].astype(BF16)
        for d, out in enumerate(slice_outs, start=1):
            row = pl.multiple_of(i * IMG + (z ^ d) * rows, rows)
            out[i * rows : (i + 1) * rows, :] = message_out[pl.ds(row, rows), :]


def prep_kernel(depth, grp_s, refs_h, *rest_refs):
    tables_h, (reg_h, prior), rest_refs = rest_refs[:2], rest_refs[2:4], rest_refs[4:]
    (rf_out, pow_out), tables_out, (reg_out,) = rest_refs[:2], rest_refs[2:4], rest_refs[4:5]
    refs, spread, reg, sem = rest_refs[5:]
    cls_dev = refs.shape[0]
    pow_out[cls_dev:, :] = jnp.zeros((pow_out.shape[0] - cls_dev, FREQ), F32)
    pad = spread.shape[0] // (IMG + 1)
    parts = sem.shape[0] - 3
    step = FEAT // parts
    tables_in = [
        pltpu.make_async_copy(a, b, sem.at[parts + n])
        for n, (a, b) in enumerate(zip((*tables_h, reg_h), (*tables_out, reg)))
    ]
    copies = [
        pltpu.make_async_copy(
            refs_h.at[:, pl.ds(n * step, step)], refs.at[:, pl.ds(n * step, step)], sem.at[n]
        )
        for n in range(parts)
    ]
    turns = parts // 2
    for n in range(turns):
        copies[n].start()
        copies[n + turns].start()
    for copy in tables_in:
        copy.start()

    def shell(r, power):
        parts = []
        for x in range(2):
            at = x * SHELLS + r
            piece = refs[:, pl.ds(pl.multiple_of(at * FREQ, FREQ), FREQ)].astype(F32)
            at = row_of(x, r, depth)
            spread[pl.ds(pl.multiple_of(at * pad, 8), cls_dev), :] = piece
            parts.append(piece * piece)
        total = jnp.sum(parts[0] + parts[1], axis=1, keepdims=True)
        return jnp.where(lanes_of((cls_dev, FREQ)) == r, total, power)

    power = jnp.zeros((cls_dev, FREQ), F32)
    for n in range(turns):
        copies[n].wait()
        copies[n + turns].wait()
        low, high = n * SHELLS // turns, (n + 1) * SHELLS // turns
        power = lax.fori_loop(low, high, shell, power, unroll=4)
    line = jnp.broadcast_to(prior[...].astype(F32).reshape(1, cls_dev), (cls_dev, cls_dev))
    diagonal = lax.broadcasted_iota(jnp.int32, line.shape, 0) == lanes_of(line.shape)
    column = jnp.sum(jnp.where(diagonal, line, 0.0), axis=1, keepdims=True)
    pow_out[:cls_dev, :] = jnp.where(lanes_of((cls_dev, FREQ)) == SHELLS, column, power)

    def image(k, _):
        rf_out[k] = spread[pl.ds(k, IMG, stride=pad), :]
        return 0

    lax.fori_loop(0, cls_dev, image, 0, unroll=4)
    for copy in tables_in:
        copy.wait()
    width = reg_out.shape[0]
    for r in range(width):
        reg_out[r : r + 1, :] = jnp.full((1, FREQ), reg[grp_s[0] * width + r], F32)


def take(refs, counts):
    taken = []
    for count in counts:
        taken.append(refs[:count])
        refs = refs[count:]
    return taken, refs


def score_kernel(arrays, earlier, depth, chunks, half, first_s, owner_s, *refs):
    blocks = len(arrays)
    messages, refs = take(refs, arrays)
    (earlier_stats,), refs = take(refs, (earlier,))
    rf, power, scoring = refs[:3]
    scores_out, stats_out, cls_out = refs[3:-6]
    ints_v, ints_s, side, ex, w32, sem = refs[-6:]
    per = side.shape[1]
    height = ints_v.shape[1]
    cls_dev = rf.shape[0] - 1
    block_rows = per * CAND
    first = first_s[0]
    table = scoring[...]
    done = 0
    for one in earlier_stats:
        stats_out[done : done + one.shape[0], :] = one[...]
        done += one.shape[0]

    extras = []
    for b in range(blocks):
        last = messages[b][-1]
        end = last.shape[0] - height
        ints_v[b] = last[end:, :].astype(F32).astype(jnp.int32)
        extras.append(last[end - per : end, :].astype(F32))
    copies = [pltpu.make_async_copy(ints_v.at[b], ints_s.at[b], sem.at[b]) for b in range(blocks)]
    for copy in copies:
        copy.start()
    for b in range(blocks):
        lane = lanes_of((per, FREQ))
        side[b] = jnp.where(lane < SHELLS, extras[b], (lane == SHELLS).astype(F32))
        begin = 0
        for one in messages[b]:
            count = one.shape[0] // IMG

            def widen(i, _):
                w32[b * per + begin + i] = one[pl.ds(pl.multiple_of(i * IMG, IMG), IMG), :].astype(F32)
                return 0

            lax.fori_loop(0, count, widen, 0, unroll=2)
            begin += count
    for copy in copies:
        copy.wait()

    for b in range(blocks):
        for c in range(len(chunks)):
            number, line, lane = list_spot(owner_s[0], c, chunks)

            def pairs(step, _):
                for u in range(UNROLL):
                    row = ints_s[b, line, lane + step * UNROLL + u]
                    k = ints_s[b, line + half, lane + step * UNROLL + u]
                    i = quot(row, CAND)
                    w_re, w_im = parts_of(w32[b * per + i], depth)
                    a_re, a_im = parts_of(rf[k], depth)
                    inner = (w_re * a_re + w_im * a_im).reshape(SHELLS, FREQ)
                    outer = (w_re * a_im - w_im * a_re).reshape(SHELLS, FREQ)
                    ex[0, pl.ds(row, 1), :] = jnp.sum(inner, axis=0, keepdims=True)
                    ex[1, pl.ds(row, 1), :] = jnp.sum(outer, axis=0, keepdims=True)
                    ex[2, pl.ds(row, 1), :] = side[b, pl.ds(i, 1), :] * power[pl.ds(k, 1), :]
                return 0

            lax.fori_loop(0, ints_s[b, 2 * half, number], pairs, 0)

        wide = jnp.broadcast_to(
            extras[b][:, None, :], (per, CAND, FREQ)
        ).reshape(block_rows, FREQ)
        own = lanes_of((block_rows, FREQ)) == SHELLS + (
            lax.broadcasted_iota(jnp.int32, (block_rows, FREQ), 0) % CAND
        )
        column = jnp.sum(jnp.where(own, wide, 0.0), axis=1, keepdims=True) - first.astype(F32)
        cls_out[b * block_rows : (b + 1) * block_rows, :] = jnp.broadcast_to(
            column, (block_rows, FREQ)
        )
        good = jnp.logical_and(column >= 0, column < cls_dev)
        values = jnp.zeros((block_rows, ROTS), F32)
        for part in range(3):
            values = values + jnp.dot(
                jnp.where(good, ex[part, :block_rows, :], 0.0),
                table[part * FREQ : (part + 1) * FREQ],
                precision=HIGH,
                preferred_element_type=F32,
            )
        scores = jnp.where(good, values, LOW)
        scores_out[b * block_rows : (b + 1) * block_rows, :] = scores
        top = jnp.broadcast_to(jnp.max(scores, axis=1, keepdims=True), (block_rows, ROTS))
        best = jnp.max(top.reshape(per, CAND, ROTS), axis=1)
        best_rows = jnp.broadcast_to(best[:, None, :], (per, CAND, ROTS)).reshape(block_rows, ROTS)
        mass = jnp.where(good, jnp.exp(scores - best_rows), 0.0)
        mass = jnp.broadcast_to(jnp.sum(mass, axis=1, keepdims=True), (block_rows, ROTS))
        total = jnp.sum(mass.reshape(per, CAND, ROTS), axis=1)
        stats_out[done + b * per : done + (b + 1) * per, :ROTS] = best
        stats_out[done + b * per : done + (b + 1) * per, ROTS:] = total


def two(v):
    return jnp.where(lanes_of(v.shape) < ROTS, rounded(v), v - rounded(v))


def one_of_two(v):
    return v + pltpu.roll(v, ROTS, 1)


def weights_kernel(calls, blocks, slices, cls_dev, chunks, grp_s, owner_s, *refs):
    stats = refs[:blocks]
    scores = refs[blocks : blocks + calls]
    classes = refs[blocks + calls : blocks + 2 * calls]
    extras = refs[blocks + 2 * calls : 2 * blocks + 2 * calls]
    refs = refs[2 * blocks + 2 * calls :]
    own_out, den_out, mass_out, log_out, ints_out = refs[:5]
    message_outs = refs[5:-4]
    rows_v, den_v, lists_v, picked_v = refs[-4:]
    per = log_out.shape[0]
    block_rows = per * CAND
    depth = SHELLS // slices
    z = grp_s[0] // 2

    half = list_lines(blocks, chunks)[0]
    _, line, lane = list_spot(owner_s[0], 0, chunks)
    slots = list_slots(cls_dev)
    lists = []

    den = jnp.zeros((FREQ, FREQ), F32)
    mass = jnp.zeros((1, FREQ), F32)
    block = 0
    for scores_ref, cls_ref in zip(scores, classes):
        for b in range(scores_ref.shape[0] // block_rows):
            ones = [stats[d][(block ^ d) * per : ((block ^ d) + 1) * per, :] for d in range(blocks)]
            best = functools.reduce(jnp.maximum, [one[:, :ROTS] for one in ones])
            total = sum(one[:, ROTS:] * jnp.exp(one[:, :ROTS] - best) for one in ones)
            if block == 0:
                log_out[...] = jnp.log(total)

            def over_rows(v):
                return jnp.broadcast_to(v[:, None, :], (per, CAND, ROTS)).reshape(block_rows, ROTS)

            at = slice(b * block_rows, (b + 1) * block_rows)
            weights = jnp.exp(scores_ref[at, :] - over_rows(best)) / over_rows(total)
            local = cls_ref[at, :]
            good = jnp.logical_and(local >= 0, local < cls_dev)[:, :ROTS]
            weights = rounded(jnp.where(good, weights, 0.0))
            lists_v[...] = extras[block][extras[block].shape[0] - lists_v.shape[0] :, :].astype(F32)
            named = jnp.broadcast_to(lists_v[pl.ds(line, 1), :], (block_rows, FREQ))
            row = lax.broadcasted_iota(jnp.int32, named.shape, 0).astype(F32)
            picked_v[...] = lax.dot_general(
                (named == row).astype(F32).astype(BF16), weights.astype(BF16),
                (((0,), (0,)), ((), ())), preferred_element_type=F32,
            )
            at = block * slots
            rows_v[at : at + slots, :] = picked_v[pl.ds(pl.multiple_of(lane, 8), slots), :]
            for source in (line, line + half, 2 * half):
                lists.append(lists_v[pl.ds(source, 1), :])
            pair_sum = jnp.sum(weights, axis=1, keepdims=True)
            twice = (lanes_of((block_rows, FREQ)) % ROTS).astype(F32)
            chosen = jnp.where(twice == local, pair_sum, 0.0)
            by_particle = jnp.sum(chosen.reshape(per, CAND, FREQ), axis=1)
            end = extras[block].shape[0] - lists_v.shape[0]
            side = extras[block][end - per : end, :].astype(F32)
            den = den + lax.dot_general(
                side, by_particle, (((0,), (0,)), ((), ())), precision=HIGH,
                preferred_element_type=F32,
            )
            mass = mass + jnp.sum(by_particle, axis=0, keepdims=True)
            block += 1

    lines = rows_v.shape[0] // 2
    packed = jnp.concatenate([rows_v[:lines, :], rows_v[lines:, :]], axis=1).astype(BF16)
    own_out[...] = packed
    den_v[...] = den[:SHELLS].reshape(slices, depth, FREQ)
    mass_rows = jnp.broadcast_to(mass, (8, FREQ))
    mass_out[...] = mass_rows
    den_out[...] = den_v[z]
    if ints_out.shape[0] > len(lists):
        lists.append(jnp.zeros((ints_out.shape[0] - len(lists), FREQ), F32))
    lists = jnp.concatenate(lists, axis=0)
    ints_out[...] = lists.astype(jnp.int32)
    tail = [two(mass_rows), lists]
    tail_rows = depth + sum(one.shape[0] for one in tail)
    spare = message_outs[0].shape[0] - lines - tail_rows
    if spare:
        tail.append(jnp.zeros((spare, FREQ), F32))
    for d, out in enumerate(message_outs, start=1):
        out[:lines, :] = packed
        out[lines:, :] = jnp.concatenate([two(den_v[z ^ d])] + tail, axis=0).astype(BF16)


def put_phases(packed, table, wcs, base):
    lines = packed.shape[0]
    twice = jnp.concatenate([packed, packed], axis=1)
    both = rounded(jnp.dot(twice, table[...], preferred_element_type=F32))
    for place in range(2):
        for part in range(2):
            at = (2 * place + part) * FREQ
            row = base + place * lines
            wcs[part, row : row + lines, :] = both[:, at : at + FREQ]


def add_pair(image, row, k, wcs, num):
    shape = num.shape[1:]
    image = image.astype(F32)
    half = image.shape[0] // 2
    w_re, w_im = image[:half].reshape(shape[1:]), image[half:].reshape(shape[1:])
    c = wcs[0, pl.ds(row, 1), :].reshape(1, 1, FREQ)
    s = wcs[1, pl.ds(row, 1), :].reshape(1, 1, FREQ)
    num[k, 0] += w_re * c - w_im * s
    num[k, 1] += w_re * s + w_im * c


def pick_image(arrays, begin, i, rows, stride, offset):
    def rows_at(one, i):
        return one[pl.ds(pl.multiple_of(i * stride + offset, rows), rows), :]

    held = [one.shape[0] // stride for one in arrays]
    while len(arrays) > 1 and begin >= held[0]:
        arrays, begin, held = arrays[1:], begin - held[0], held[1:]
    if len(arrays) == 1:
        return rows_at(arrays[0], begin + i)
    cut = held[0] - begin
    return jnp.where(
        i < cut,
        rows_at(arrays[0], begin + jnp.minimum(i, cut - 1)),
        rows_at(arrays[1], jnp.maximum(i - cut, 0)),
    )


def own_sum_kernel(chunks, arrays, grp_s, owner_s, packed, ints, *refs):
    messages, refs = take(refs, arrays)
    phases, (num, wcs, ints_s, sem) = refs[:1], refs[1:]
    copy = pltpu.make_async_copy(ints, ints_s, sem)
    copy.start()
    per = sum(one.shape[0] for one in messages[0]) // IMG
    rows = 2 * num.shape[2] * num.shape[3]
    z = grp_s[0] // 2
    put_phases(packed[...], phases[0], wcs, 0)
    num[...] = jnp.zeros_like(num)
    copy.wait()
    for block, held_in in enumerate(messages):
        base = block * list_slots(num.shape[0] - 1)
        for c in range(len(chunks)):
            number, _, lane = list_spot(owner_s[0], c, chunks)

            def pairs(step, _):
                for u in range(UNROLL):
                    row = ints_s[3 * block, lane + step * UNROLL + u]
                    k = ints_s[3 * block + 1, lane + step * UNROLL + u]
                    image = pick_image(held_in, 0, quot(row, CAND), rows, IMG, z * rows)
                    add_pair(image, base + step * UNROLL + u, k, wcs, num)
                return 0

            lax.fori_loop(0, ints_s[3 * block + 2, number], pairs, 0)


def join_kernel(*refs):
    out = refs[-1]
    rows = refs[0].shape[0]
    for n, one in enumerate(refs[:-1]):
        out[n * rows : (n + 1) * rows, :] = one[...]


def read_tail(message, lines, depth, count):
    tail = message[lines:, :].astype(F32)
    den, mass = one_of_two(tail[:depth]), one_of_two(tail[depth : depth + 8])
    return den, mass, tail[depth + 8 : depth + 8 + count].astype(jnp.int32)


def add_planes(planes, owner, chunks, images, wcs, *nums):
    number, _, lane = list_spot(owner, 0, chunks)
    num = nums[0]
    slots = list_slots(num.shape[0] - 1)
    rows = 2 * num.shape[2] * num.shape[3]
    per = FREQ // CAND
    for first in range(0, len(images), 2):
        group = [
            (d, ints, base + block * slots, block)
            for d, ints, base in planes
            for block in range(first, min(first + 2, len(images)))
        ]
        counts = [ints[3 * block + 2, number] for _, ints, _, block in group]

        def pairs(step, _):
            for d, ints, start, block in group:
                for u in range(UNROLL):
                    slot = step * UNROLL + u
                    row = ints[3 * block, lane + slot]
                    k = ints[3 * block + 1, lane + slot]
                    image = pick_image(images[block], d * per, quot(row, CAND), rows, rows, 0)
                    add_pair(image, start + slot, k, wcs, nums[u % len(nums)])
            return 0

        lax.fori_loop(0, functools.reduce(jnp.maximum, counts), pairs, 0)


def near_sum_kernel(chunks, pieces, owner_s, *refs):
    images, refs = take(refs, pieces)
    message, first, phases, den_in, mass_in, num, den_out, mass_out, wcs, ints_v, ints_s, sem = refs
    lines = wcs.shape[1] // 2
    depth = den_in.shape[0]
    den, mass, ints_v[...] = read_tail(message, lines, depth, ints_v.shape[0])
    copy = pltpu.make_async_copy(ints_v, ints_s, sem)
    copy.start()
    den_out[...] = den_in[...] + den
    mass_out[...] = mass_in[...] + mass
    put_phases(message[:lines, :], phases, wcs, 0)
    num[...] = first[...]
    copy.wait()
    add_planes([(0, ints_s, 0)], owner_s[0], chunks, images, wcs, num)


def sum_kernel(chunk, chunks, slices, pieces, grp_s, owner_s, *refs):
    images, refs = take(refs, pieces)
    messages, refs = refs[: slices - 2], refs[slices - 2 :]
    first, refs = refs[0], refs[1:]
    if chunk == 0:
        phases, (den_in, mass_in), refs = refs[0], refs[1:3], refs[3:]
        own_out, sib_out, den_out, mass_out, wcs, ints_s, num, more, den_v, ints_v, sem = refs
    else:
        wcs, ints_s, own_out, sib_out, num, more = refs
    group_rows = wcs.shape[1] // (slices - 2)
    lines = group_rows // 2
    core = grp_s[0] % 2
    start, size = chunks[chunk]
    depth = num.shape[2] * num.shape[3]

    if chunk == 0:
        den, mass = den_in[...], mass_in[...]
        for n, message in enumerate(messages):
            more_den, more_mass, ints_v[n] = read_tail(message, lines, depth, ints_v.shape[1])
            den, mass = den + more_den, mass + more_mass
        copies = [
            pltpu.make_async_copy(ints_v.at[n], ints_s.at[n], sem.at[n])
            for n in range(slices - 2)
        ]
        for copy in copies:
            copy.start()
        for n, message in enumerate(messages):
            put_phases(message[:lines, :], phases, wcs, n * group_rows)
    num[...] = first[...]
    more[...] = jnp.zeros_like(more)
    if chunk == 0:
        for copy in copies:
            copy.wait()
    planes = [(n + 1, ints_s.at[n], n * group_rows) for n in range(slices - 2)]
    add_planes(planes, owner_s[0], chunks, images, wcs, num, more)

    def pack(k, _):
        for out, at in ((own_out, core), (sib_out, 1 - core)):
            halves = [num[k, x, at] + more[k, x, at] for x in range(2)]
            out[k] = jnp.concatenate(halves, axis=0).astype(out.dtype)
        return 0

    lax.fori_loop(0, size, pack, 0, unroll=13)
    if chunk == 0:
        width = num.shape[3]
        den_v[...] = den.reshape(2, width, FREQ)
        den_out[...] = den_v[core]
        mass_out[...] = mass
        sib_out[size] = jnp.concatenate([two(den_v[1 - core]), two(mass)[:width]], axis=0).astype(BF16)


def divide(own, sib, inverse, start, avg_out):
    for k in range(avg_out.shape[0]):
        column = inverse[:, start + k : start + k + 1]
        factor = jnp.broadcast_to(column, inverse.shape)
        total = own[k] + sib[k].astype(F32)
        width = inverse.shape[0]
        parts = [total[:width] * factor, total[width:] * factor]
        avg_out[k] = jnp.concatenate(parts, axis=0).astype(BF16)


def first_divide_kernel(scale, start, own, sib, den, mass, reg, avg_out, share_out, inverse_out):
    cut = avg_out.shape[0]
    width = avg_out.shape[1] // 2
    tile = one_of_two(sib[cut].astype(F32))
    share_out[...] = (tile[width : width + 1] + mass[:1]) * scale
    inverse = 1.0 / (tile[:width] + den[...] + reg[...])
    inverse_out[...] = inverse
    divide(own, sib, inverse, start, avg_out)


def next_divide_kernel(start, own, sib, inverse, avg_out):
    divide(own, sib, inverse[...], start, avg_out)


def spread_kernel(planes, chunks, has_out, grp_s, *refs):
    held = 2 * len(planes) * len(chunks)
    arrays, (out, wide, columns, sem) = refs[:held], refs[held + has_out :]
    width = arrays[0].shape[1] // 2
    cls_dev = columns.shape[1]
    pad = wide.shape[0] // (len(planes) * 4 * width + 1)
    z, h = grp_s[0] // 2, grp_s[0] % 2
    copies = []
    for n, d in enumerate(planes):
        for c, (start, cut) in enumerate(chunks):
            pair = arrays[2 * (n * len(chunks) + c) :][:2]

            def one(k, _):
                for side, array in enumerate(pair):
                    piece = array[k].astype(F32)
                    for x in range(2):
                        at = (n * 4 + side * 2 + x) * width * pad + start
                        wide[pl.ds(at + k, width, stride=pad), :] = piece[
                            x * width : (x + 1) * width
                        ]
                return 0

            lax.fori_loop(0, cut, one, 0, unroll=2)
        for side, core in enumerate((h, 1 - h)):
            for x in range(2):
                group = n * 4 + side * 2 + x
                for r in range(width):
                    at = (group * width + r) * pad
                    columns[group, :, r * FREQ : (r + 1) * FREQ] = wide[at : at + cls_dev, :]
                first = (x * SHELLS + ((z ^ d) * 2 + core) * width) * FREQ
                first = pl.multiple_of(first, width * FREQ)
                copies.append(
                    pltpu.make_async_copy(
                        columns.at[group], out.at[:, pl.ds(first, width * FREQ)], sem.at[group]
                    )
                )
                copies[-1].start()
    for copy in copies:
        copy.wait()


def whole(space):
    return pl.BlockSpec(memory_space=space)


def in_hbm(value):
    return pltpu.with_memory_space_constraint(value, HBM)


def call(kernel, name, ins, outs, scratch, mib, us, args, **more):
    cost = pl.CostEstimate(flops=0, bytes_accessed=int(us * 3.6e6), transcendentals=0)
    return pl.pallas_call(
        kernel,
        out_shape=tuple(s for s, _ in outs),
        in_specs=[whole(s) for s in ins],
        out_specs=tuple(whole(s) for _, s in outs),
        scratch_shapes=scratch,
        compiler_params=pltpu.CompilerParams(vmem_limit_bytes=mib * 2**20),
        name=name,
        cost_estimate=cost,
        **more,
    )(*args)


def swap(value, axis, distance):
    size = lax.axis_size(axis)
    return lax.ppermute(value, axis, [(i, i ^ distance) for i in range(size)])


def after(value, *others):
    return lax.optimization_barrier((value, *others))[0]


def per_device(
    particles, candidates, group_ids, ctf_ids, ctf_table, noise_prec, references, log_prior, reg
):
    n_cls = lax.axis_size("cls")
    n_grp = lax.axis_size("grp")
    per = particles.shape[0]
    cls_dev = references.shape[0]
    block_rows = per * CAND
    chunks = chunks_of(cls_dev)
    pad = odd_tiles(cls_dev)
    width = SHELLS // n_grp
    nz = n_grp // 2
    scoring, phases = (jnp.asarray(t) for t in tables())
    owner = lax.axis_index("cls").astype(jnp.int32).reshape(1)
    first = owner * cls_dev
    grp = lax.axis_index("grp").astype(jnp.int32).reshape(1)

    depth = SHELLS // nz
    message, *sliced = call(
        functools.partial(weigh_kernel, nz, n_cls, cls_dev, chunks), "weigh", [SMEM] + [HBM] * 6,
        [(SHAPE((per * (IMG + 1) + list_lines(n_cls, chunks)[1], FREQ), BF16), VMEM)]
        + [(SHAPE((per * 2 * depth, FREQ), BF16), VMEM)] * (nz - 1),
        [
            VMEM(particles.shape, BF16),
            VMEM((CAND, per), jnp.int32),
            SMEM((per,), jnp.int32),
            SMEM((per,), jnp.int32),
            VMEM(ctf_table.shape[::-1], F32),
            VMEM(noise_prec.shape, F32),
            VMEM((per, noise_prec.shape[0]), F32),
            VMEM((per, ctf_table.shape[0]), F32),
            VMEM(((IMG + 1) * odd_tiles(per), FREQ), F32),
            pltpu.SemaphoreType.DMA((6,)),
        ],
        5, 2.0,
        (grp,)
        + tuple(
            in_hbm(a)
            for a in (particles, candidates.T, group_ids, ctf_ids, ctf_table.T, noise_prec)
        ),
    )

    if n_cls == 4:
        message_1, message_2 = swap(message, "cls", 1), swap(message, "cls", 2)
    sliced = [swap(one, "grp", 2 * d) for d, one in enumerate(sliced, start=1)]

    rf, power, scoring, phases, own_reg = call(
        functools.partial(prep_kernel, depth), "prep", [SMEM] + [HBM] * 4 + [VMEM],
        [(SHAPE((cls_dev + 1, IMG, FREQ), F32), VMEM), (SHAPE((cls_dev + 1, FREQ), F32), VMEM)]
        + [(SHAPE(t.shape, t.dtype), VMEM) for t in (scoring, phases)]
        + [(SHAPE((width, FREQ), F32), VMEM)],
        [
            VMEM(references.shape, BF16),
            VMEM(((IMG + 1) * pad, FREQ), F32),
            SMEM(reg.shape, F32),
            pltpu.SemaphoreType.DMA((7,)),
        ],
        8, 4.0,
        (grp,)
        + tuple(in_hbm(a) for a in (references, scoring, phases, reg))
        + (log_prior,),
    )

    half, height = list_lines(n_cls, chunks)

    def score(part, earlier=()):
        blocks = len(part)
        flat = [m for arrays in part for m in arrays]
        earlier = tuple(s[1] for s in earlier)
        ahead = sum(s.shape[0] for s in earlier)
        counts = tuple(len(arrays) for arrays in part)
        return call(
            functools.partial(score_kernel, counts, len(earlier), depth, chunks, half), "score",
            [SMEM] * 2 + [VMEM] * (len(flat) + len(earlier) + 3),
            [
                (SHAPE((blocks * block_rows, ROTS), F32), VMEM),
                (SHAPE((ahead + blocks * per, FREQ), F32), VMEM),
                (SHAPE((blocks * block_rows, FREQ), F32), VMEM),
            ],
            [
                VMEM((blocks, height, FREQ), jnp.int32),
                SMEM((blocks, height, FREQ), jnp.int32),
                VMEM((blocks, per, FREQ), F32),
                VMEM((3, block_rows, FREQ), F32),
                VMEM((blocks * per, IMG, FREQ), F32),
                pltpu.SemaphoreType.DMA((blocks,)),
            ],
            6 if n_cls == 4 else 40, 3.0 * blocks, (first, owner, *flat, *earlier, rf, power, scoring),
        )

    def join(got):
        (joined,) = call(
            join_kernel, "join", [VMEM] * (nz - 1),
            [(SHAPE(((nz - 1) * per * 2 * depth, FREQ), BF16), VMEM)], [], 2, 0.5, got,
        )
        return joined

    if n_cls == 4:
        cut = per // 2 * IMG
        scored = [score([(after(message, sliced[0]),)])]
        ready = (scored[0][1], sliced[1])
        message_1, message_2 = after(message_1, *ready), after(message_2, *ready)
        message_3 = (swap(message_1[:cut], "cls", 2), swap(message_2[cut:], "cls", 1))
        messages = [(message,), (message_1,), (message_2,), message_3]
        scored += [score(messages[1:3])]
        joined = join([after(sliced[0], scored[1][1], *message_3)] + sliced[1:])
        joined_1, joined_2 = swap(joined, "cls", 1), swap(joined, "cls", 2)
        scored += [score(messages[3:], scored)]
    else:
        messages = [(message,)] + [(swap(message, "cls", d),) for d in range(1, n_cls)]
        scored = [score(messages)]
        joined = join(sliced)
        images = [joined] + [swap(joined, "cls", d) for d in range(1, n_cls)]
        pieces = (1,) * n_cls
    arrays = tuple(len(m) for m in messages)
    stats = scored[-1][1]
    all_stats = [stats] + [swap(stats, "cls", d) for d in range(1, n_cls)]
    flat = [m for held in messages for m in held]

    lines = n_cls * list_slots(cls_dev) // 2
    own_lists = SHAPE((-(-3 * n_cls // 8) * 8, FREQ), jnp.int32)
    outgoing_rows = -(-(lines + depth + 8 + own_lists.shape[0]) // 16) * 16
    packed, den, mass, log_mass, ints, *outgoing = call(
        functools.partial(weights_kernel, len(scored), n_cls, nz, cls_dev, chunks), "weights",
        [SMEM] * 2 + [VMEM] * (2 * n_cls + 2 * len(scored)),
        [
            (SHAPE((lines, FREQ), BF16), VMEM),
            (SHAPE((depth, FREQ), F32), VMEM),
            (SHAPE((8, FREQ), F32), VMEM),
            (SHAPE((per, ROTS), F32), VMEM),
            (own_lists, VMEM),
        ]
        + [(SHAPE((outgoing_rows, FREQ), BF16), VMEM)] * (nz - 1),
        [
            VMEM((2 * lines, ROTS), F32),
            VMEM((nz, depth, FREQ), F32),
            VMEM((height, FREQ), F32),
            VMEM((block_rows, ROTS), F32),
        ],
        4 if n_cls == 4 else 12, 2.0,
        (
            grp, owner, *all_stats, *(s[0] for s in scored), *(s[2] for s in scored),
            *(held[-1] for held in messages),
        ),
    )
    incoming = [swap(one, "grp", 2 * d) for d, one in enumerate(outgoing, start=1)]
    if n_cls == 4:
        cut = joined.shape[0] // 2
        joined_1, joined_2 = after(joined_1, packed), after(joined_2, packed)
        joined_3 = [swap(joined_1[:cut], "cls", 2), swap(joined_2[cut:], "cls", 1)]
        images = [joined, joined_1, joined_2, *joined_3]
        pieces = (1, 1, 1, 2)
    (first_sums,) = call(
        functools.partial(own_sum_kernel, chunks, arrays), "own_sum",
        [SMEM] * 2 + [VMEM] * (len(flat) + 3),
        [(SHAPE((cls_dev + 1, 2, 2, width, FREQ), F32), VMEM)],
        [
            VMEM((2, 2 * lines, FREQ), F32),
            SMEM(own_lists.shape, jnp.int32),
            pltpu.SemaphoreType.DMA,
        ],
        4 if n_cls == 4 else 12, 3.0, (grp, owner, packed, ints, *flat, phases),
    )
    (near_sums, den, mass) = call(
        functools.partial(near_sum_kernel, chunks, pieces), "near_sum",
        [SMEM] + [VMEM] * (sum(pieces) + 5),
        [
            (SHAPE((cls_dev + 1, 2, 2, width, FREQ), F32), VMEM),
            (SHAPE((depth, FREQ), F32), VMEM),
            (SHAPE((8, FREQ), F32), VMEM),
        ],
        [
            VMEM((2, 2 * lines, FREQ), F32),
            VMEM(own_lists.shape, jnp.int32),
            SMEM(own_lists.shape, jnp.int32),
            pltpu.SemaphoreType.DMA,
        ],
        4 if n_cls == 4 else 12, 2.0,
        (owner, *images, incoming[0], first_sums, phases, den, mass),
    )
    tile = (2 * width, FREQ)
    sums = []
    for chunk, (start, size) in enumerate(chunks):
        more = chunk == 0
        outs = [
            (SHAPE((size,) + tile, F32), VMEM),
            (SHAPE((size + more,) + tile, BF16), VMEM),
        ]
        scratch = [VMEM((size + 1, 2, 2, width, FREQ), F32)] * 2
        spaces = [SMEM] * 2 + [VMEM] * (sum(pieces) + nz - 1)
        if more:
            outs += [
                (SHAPE((width, FREQ), F32), VMEM),
                (SHAPE((8, FREQ), F32), VMEM),
                (SHAPE((2, (nz - 2) * (2 * lines), FREQ), F32), VMEM),
                (SHAPE((nz - 2,) + own_lists.shape, jnp.int32), SMEM),
            ]
            scratch += [
                VMEM((2, width, FREQ), F32),
                VMEM((nz - 2,) + own_lists.shape, jnp.int32),
                pltpu.SemaphoreType.DMA((nz - 2,)),
            ]
            spaces += [VMEM] * 3
            args = (grp, owner, *images, *incoming[1:], near_sums, phases, den, mass)
        else:
            spaces += [VMEM, SMEM]
            args = (grp, owner, *images, *incoming[1:], near_sums, wcs, lists)
        own, sib, *others = call(
            functools.partial(sum_kernel, chunk, chunks, nz, pieces), "sum",
            spaces, outs, scratch, 5 if n_cls == 4 else 24, 3.0, args,
        )
        if more:
            den, mass, wcs, lists = others
        sums.append((own, sib))

    particle_total = per * n_grp * n_cls
    divided, inverse, share = [], None, None
    for chunk, (own, sib) in enumerate(sums):
        start, cut = chunks[chunk]
        other = swap(sib, "grp", 1)
        averaged_out = (SHAPE((cut,) + tile, BF16), VMEM)
        if chunk == 0:
            averaged, share, inverse = call(
                functools.partial(first_divide_kernel, K / particle_total, start), "divide",
                [VMEM] * 5,
                [averaged_out, (SHAPE((1, FREQ), F32), VMEM), (SHAPE((width, FREQ), F32), VMEM)],
                [], 2, 0.05, (own, other, den, mass, own_reg),
            )
        else:
            (averaged,) = call(
                functools.partial(next_divide_kernel, start), "divide", [VMEM] * 3,
                [averaged_out], [], 2, 0.05, (own, other, inverse),
            )
        divided.append(averaged)

    if nz == 4:
        near = [swap(averaged, "grp", 2) for averaged in divided]
        across = [swap(averaged, "grp", 4) for averaged in divided]
        near, across = lax.optimization_barrier((near, across))
        relayed = [swap(one, "grp", 2) for one in across]
        planes = [list(held) for held in zip(divided, near, across, relayed)]
    else:
        planes = [
            [averaged] + [swap(averaged, "grp", 2 * d) for d in range(1, nz)]
            for averaged in divided
        ]
    averages = None
    for far in ((0, 1, 2), (3,)) if nz == 4 else (tuple(range(nz)),):
        arrays = []
        for d in far:
            for held in planes:
                one = held[d] if averages is None else after(held[d], averages)
                arrays += [one, swap(one, "grp", 1)]
        has_out = averages is not None
        groups = len(far) * 4
        (averages,) = call(
            functools.partial(spread_kernel, far, chunks, has_out), "spread",
            [SMEM] + [VMEM] * len(arrays) + [HBM] * has_out,
            [(SHAPE((cls_dev, FEAT), F32), HBM)],
            [
                VMEM(((groups * width + 1) * odd_tiles(cls_dev), FREQ), F32),
                VMEM((groups, cls_dev, width * FREQ), F32),
                pltpu.SemaphoreType.DMA((groups,)),
            ],
            8, 0.05, (grp, *arrays) + ((averages,) if has_out else ()),
            input_output_aliases={len(arrays) + 1: 0} if has_out else {},
        )
    return (averages, share[0, :cls_dev], log_mass[:, 0])


def solution(mesh):
    return jax.shard_map(
        per_device,
        mesh=mesh,
        in_specs=(
            P(("grp", "cls"), None),
            P(("grp", "cls"), None),
            P(("grp", "cls")),
            P(("grp", "cls")),
            P(),
            P(),
            P("cls", None),
            P("cls"),
            P(),
        ),
        out_specs=(P("cls", None), P("cls"), P(("grp", "cls"))),
        check_vma=False,
    )
```

```python
import functools
import math

import jax
import jax.numpy as jnp
import numpy as np
from jax import lax
from jax.experimental import pallas as pl
from jax.experimental.pallas import tpu as pltpu
from jax.sharding import PartitionSpec as P

SHELLS = 64
FREQ = 128
FEAT = 16384
ROTS = 64
K = 208
CAND = 8
MOST = 2
IMG = 2 * SHELLS
UNROLL = 4
LOW = -1e30
HIGH = lax.Precision.HIGHEST
VMEM = pltpu.VMEM
SMEM = pltpu.SMEM
HBM = pltpu.HBM
F32 = jnp.float32
BF16 = jnp.bfloat16
SHAPE = jax.ShapeDtypeStruct


def tables():
    turns = np.arange(ROTS)[:, None]
    orders = np.arange(FREQ)[None, :]
    angles = ((turns * orders) % ROTS).astype(np.float32) * np.float32(2.0 * math.pi / ROTS)
    cos_tab = np.cos(angles).astype(np.float32)
    sin_tab = np.sin(angles).astype(np.float32)
    last = np.zeros((FREQ, ROTS), np.float32)
    last[:SHELLS] = -0.5
    last[SHELLS] = 1.0
    scoring = np.concatenate([cos_tab.T, sin_tab.T, last], axis=0)
    left = np.concatenate([cos_tab, sin_tab], axis=1)
    terms = []
    for _ in range(2):
        term = left.astype(jnp.bfloat16)
        left = left - term.astype(np.float32)
        blank = np.zeros_like(term)
        terms.append(np.block([[term, blank], [blank, term]]))
    return scoring, np.concatenate(terms, axis=0)


def lanes_of(shape):
    return lax.broadcasted_iota(jnp.int32, shape, len(shape) - 1)


def list_room(chunks):
    return FREQ if max(n for _, n in chunks) * MOST + UNROLL > FREQ // 2 else FREQ // 2


def list_lines(owners, chunks):
    lines = -(-owners * len(chunks) * list_room(chunks) // FREQ)
    return lines, -(-(2 * lines + 1) // 16) * 16


def list_spot(owner, chunk, chunks):
    number = owner * len(chunks) + chunk
    at = number * list_room(chunks)
    return number, quot(at, FREQ), rest(at, FREQ)


def list_slots(cls_dev):
    return -(-cls_dev * MOST // 8) * 8


def quot(v, n):
    return v >> (n.bit_length() - 1) if n & (n - 1) == 0 else v // n


def rest(v, n):
    return v & (n - 1) if n & (n - 1) == 0 else v % n


def odd_tiles(rows):
    return (-(-rows // 8) | 1) * 8


def rounded(v):
    return v.astype(BF16).astype(F32)


def row_of(x, r, depth):
    return r // depth * 2 * depth + x * depth + r % depth


def parts_of(image, depth):
    pieces = image.reshape(image.shape[0] // (2 * depth), 2, depth, FREQ)
    return pieces[:, 0], pieces[:, 1]


def chunks_of(cls_dev):
    return ((0, cls_dev),)


def block_lists(named, owners, cls_dev, chunks):
    per = named.shape[0]
    pairs = per * CAND
    square = (pairs, pairs)
    wide = jnp.broadcast_to(named[:, None, :], (per, CAND, CAND)).reshape(pairs, CAND)
    own = lax.broadcasted_iota(jnp.int32, wide.shape, 0) % CAND == lanes_of(wide.shape)
    cls = jnp.broadcast_to(jnp.sum(jnp.where(own, wide, 0.0), axis=1, keepdims=True), square)
    owner = sum((cls >= o * cls_dev).astype(F32) for o in range(1, owners))
    local = cls - owner * cls_dev
    number = owner * len(chunks)
    if len(chunks) > 1:
        number = number + (local < chunks[0][0]).astype(F32)
    row = lax.broadcasted_iota(jnp.int32, square, 0)
    lane = lanes_of(square)

    def across(column):
        return jnp.sum(jnp.where(row == lane, column, 0.0), axis=0, keepdims=True)

    same = (number == across(number)).astype(F32)
    place = jnp.sum(jnp.where(lane < row, same, 0.0), axis=1, keepdims=True)
    held = jnp.sum(same, axis=1, keepdims=True).astype(jnp.int32)
    place = place + rest(UNROLL - rest(held, UNROLL), UNROLL).astype(F32)
    room = list_room(chunks)
    lines, height = list_lines(owners, chunks)
    slots = lines * FREQ
    target = (number[:, :1] * room + place).astype(jnp.int32)
    hot = (target == lanes_of((pairs, slots))).astype(F32).astype(BF16)
    values = jnp.concatenate(
        [
            lanes_of((1, pairs)).astype(F32), across(local), jnp.ones((1, pairs), F32),
            jnp.zeros((5, pairs), F32),
        ],
        axis=0,
    ).astype(BF16)
    placed = jnp.dot(values, hot, preferred_element_type=F32)
    rows_line = placed[0:1]
    cls_line = placed[1:2] + (1.0 - placed[2:3]) * cls_dev
    counts = jnp.sum((number == lane.astype(F32)).astype(F32), axis=0, keepdims=True)
    counts = quot(counts.astype(jnp.int32) + UNROLL - 1, UNROLL).astype(F32)
    cut = [v[:, n * FREQ : (n + 1) * FREQ] for v in (rows_line, cls_line) for n in range(lines)]
    return jnp.concatenate(
        cut + [counts, jnp.zeros((height - 2 * lines - 1, FREQ), F32)], axis=0
    )


def weigh_kernel(
    slices, owners, cls_dev, chunks, grp_s, particles_h, cand_h, groups_h, entries_h, ctf_h, prec_h, message_out, *refs
):
    slice_outs = refs[: slices - 1]
    particles, cand, groups, entries, ctf, prec, hot_g, hot_e, spread, sem = refs[slices - 1 :]
    depth = SHELLS // slices
    z = grp_s[0] // 2
    copies = [
        pltpu.make_async_copy(a, b, sem.at[n])
        for n, (a, b) in enumerate(
            (
                (groups_h, groups), (entries_h, entries), (ctf_h, ctf), (prec_h, prec),
                (cand_h, cand), (particles_h, particles),
            )
        )
    ]
    for copy in copies:
        copy.start()
    per = particles.shape[0]
    pad = spread.shape[0] // (IMG + 1)
    for copy in copies[:2]:
        copy.wait()
    for i in range(per):
        hot_g[i : i + 1, :] = (lanes_of((1, hot_g.shape[1])) == groups[i]).astype(F32)
        hot_e[i : i + 1, :] = (lanes_of((1, hot_e.shape[1])) == entries[i]).astype(F32)
    for copy in copies[2:5]:
        copy.wait()
    p = jnp.dot(hot_g[...], prec[...], precision=HIGH, preferred_element_type=F32)
    c = lax.dot_general(
        hot_e[...], ctf[...], (((1,), (1,)), ((), ())), precision=HIGH, preferred_element_type=F32
    )
    eye = (lanes_of((per, per)) == lax.broadcasted_iota(jnp.int32, (per, per), 0)).astype(F32)
    named = lax.dot_general(
        eye, cand[...].astype(F32), (((1,), (1,)), ((), ())), precision=HIGH,
        preferred_element_type=F32,
    )
    factors = p * c
    extra = jnp.concatenate(
        [factors * c, named, jnp.zeros((per, FREQ - SHELLS - CAND), F32)], axis=1
    )
    message_out[per * IMG : per * (IMG + 1), :] = extra.astype(BF16)
    message_out[per * (IMG + 1) :, :] = block_lists(named, owners, cls_dev, chunks).astype(BF16)
    copies[5].wait()
    for r in range(SHELLS):
        factor = jnp.broadcast_to(factors[:, r : r + 1], (per, FREQ))
        for x in range(2):
            at = x * SHELLS + r
            piece = particles[:, at * FREQ : (at + 1) * FREQ].astype(F32) * factor
            at = row_of(x, r, depth)
            spread[at * pad : at * pad + per, :] = rounded(piece)
    rows = 2 * depth
    for i in range(per):
        message_out[i * IMG : (i + 1) * IMG, :] = spread[i : i + IMG * pad : pad, :].astype(BF16)
        for d, out in enumerate(slice_outs, start=1):
            row = pl.multiple_of(i * IMG + (z ^ d) * rows, rows)
            out[i * rows : (i + 1) * rows, :] = message_out[pl.ds(row, rows), :]


def prep_kernel(depth, grp_s, refs_h, *rest_refs):
    tables_h, (reg_h, prior), rest_refs = rest_refs[:2], rest_refs[2:4], rest_refs[4:]
    (rf_out, pow_out), tables_out, (reg_out,) = rest_refs[:2], rest_refs[2:4], rest_refs[4:5]
    refs, spread, reg, sem = rest_refs[5:]
    cls_dev = refs.shape[0]
    pow_out[cls_dev:, :] = jnp.zeros((pow_out.shape[0] - cls_dev, FREQ), F32)
    pad = spread.shape[0] // (IMG + 1)
    parts = sem.shape[0] - 3
    step = FEAT // parts
    tables_in = [
        pltpu.make_async_copy(a, b, sem.at[parts + n])
        for n, (a, b) in enumerate(zip((*tables_h, reg_h), (*tables_out, reg)))
    ]
    copies = [
        pltpu.make_async_copy(
            refs_h.at[:, pl.ds(n * step, step)], refs.at[:, pl.ds(n * step, step)], sem.at[n]
        )
        for n in range(parts)
    ]
    turns = parts // 2
    for n in range(turns):
        copies[n].start()
        copies[n + turns].start()
    for copy in tables_in:
        copy.start()

    def shell(r, power):
        parts = []
        for x in range(2):
            at = x * SHELLS + r
            piece = refs[:, pl.ds(pl.multiple_of(at * FREQ, FREQ), FREQ)].astype(F32)
            at = row_of(x, r, depth)
            spread[pl.ds(pl.multiple_of(at * pad, 8), cls_dev), :] = piece
            parts.append(piece * piece)
        total = jnp.sum(parts[0] + parts[1], axis=1, keepdims=True)
        return jnp.where(lanes_of((cls_dev, FREQ)) == r, total, power)

    power = jnp.zeros((cls_dev, FREQ), F32)
    for n in range(turns):
        copies[n].wait()
        copies[n + turns].wait()
        low, high = n * SHELLS // turns, (n + 1) * SHELLS // turns
        power = lax.fori_loop(low, high, shell, power, unroll=4)
    line = jnp.broadcast_to(prior[...].astype(F32).reshape(1, cls_dev), (cls_dev, cls_dev))
    diagonal = lax.broadcasted_iota(jnp.int32, line.shape, 0) == lanes_of(line.shape)
    column = jnp.sum(jnp.where(diagonal, line, 0.0), axis=1, keepdims=True)
    pow_out[:cls_dev, :] = jnp.where(lanes_of((cls_dev, FREQ)) == SHELLS, column, power)

    def image(k, _):
        rf_out[k] = spread[pl.ds(k, IMG, stride=pad), :]
        return 0

    lax.fori_loop(0, cls_dev, image, 0, unroll=4)
    for copy in tables_in:
        copy.wait()
    width = reg_out.shape[0]
    for r in range(width):
        reg_out[r : r + 1, :] = jnp.full((1, FREQ), reg[grp_s[0] * width + r], F32)


def take(refs, counts):
    taken = []
    for count in counts:
        taken.append(refs[:count])
        refs = refs[count:]
    return taken, refs


def score_kernel(arrays, earlier, depth, chunks, half, first_s, owner_s, *refs):
    blocks = len(arrays)
    messages, refs = take(refs, arrays)
    (earlier_stats,), refs = take(refs, (earlier,))
    rf, power, scoring = refs[:3]
    scores_out, stats_out, cls_out = refs[3:-6]
    ints_v, ints_s, side, ex, w32, sem = refs[-6:]
    per = side.shape[1]
    height = ints_v.shape[1]
    cls_dev = rf.shape[0] - 1
    block_rows = per * CAND
    first = first_s[0]
    table = scoring[...]
    done = 0
    for one in earlier_stats:
        stats_out[done : done + one.shape[0], :] = one[...]
        done += one.shape[0]

    extras = []
    for b in range(blocks):
        last = messages[b][-1]
        end = last.shape[0] - height
        ints_v[b] = last[end:, :].astype(F32).astype(jnp.int32)
        extras.append(last[end - per : end, :].astype(F32))
    copies = [pltpu.make_async_copy(ints_v.at[b], ints_s.at[b], sem.at[b]) for b in range(blocks)]
    for copy in copies:
        copy.start()
    for b in range(blocks):
        lane = lanes_of((per, FREQ))
        side[b] = jnp.where(lane < SHELLS, extras[b], (lane == SHELLS).astype(F32))
        begin = 0
        for one in messages[b]:
            count = one.shape[0] // IMG

            def widen(i, _):
                w32[b * per + begin + i] = one[pl.ds(pl.multiple_of(i * IMG, IMG), IMG), :].astype(F32)
                return 0

            lax.fori_loop(0, count, widen, 0, unroll=2)
            begin += count
    for copy in copies:
        copy.wait()

    for b in range(blocks):
        for c in range(len(chunks)):
            number, line, lane = list_spot(owner_s[0], c, chunks)

            def pairs(step, _):
                for u in range(UNROLL):
                    row = ints_s[b, line, lane + step * UNROLL + u]
                    k = ints_s[b, line + half, lane + step * UNROLL + u]
                    i = quot(row, CAND)
                    w_re, w_im = parts_of(w32[b * per + i], depth)
                    a_re, a_im = parts_of(rf[k], depth)
                    inner = (w_re * a_re + w_im * a_im).reshape(SHELLS, FREQ)
                    outer = (w_re * a_im - w_im * a_re).reshape(SHELLS, FREQ)
                    ex[0, pl.ds(row, 1), :] = jnp.sum(inner, axis=0, keepdims=True)
                    ex[1, pl.ds(row, 1), :] = jnp.sum(outer, axis=0, keepdims=True)
                    ex[2, pl.ds(row, 1), :] = side[b, pl.ds(i, 1), :] * power[pl.ds(k, 1), :]
                return 0

            lax.fori_loop(0, ints_s[b, 2 * half, number], pairs, 0)

        wide = jnp.broadcast_to(
            extras[b][:, None, :], (per, CAND, FREQ)
        ).reshape(block_rows, FREQ)
        own = lanes_of((block_rows, FREQ)) == SHELLS + (
            lax.broadcasted_iota(jnp.int32, (block_rows, FREQ), 0) % CAND
        )
        column = jnp.sum(jnp.where(own, wide, 0.0), axis=1, keepdims=True) - first.astype(F32)
        cls_out[b * block_rows : (b + 1) * block_rows, :] = jnp.broadcast_to(
            column, (block_rows, FREQ)
        )
        good = jnp.logical_and(column >= 0, column < cls_dev)
        values = jnp.zeros((block_rows, ROTS), F32)
        for part in range(3):
            values = values + jnp.dot(
                jnp.where(good, ex[part, :block_rows, :], 0.0),
                table[part * FREQ : (part + 1) * FREQ],
                precision=HIGH,
                preferred_element_type=F32,
            )
        scores = jnp.where(good, values, LOW)
        scores_out[b * block_rows : (b + 1) * block_rows, :] = scores
        top = jnp.broadcast_to(jnp.max(scores, axis=1, keepdims=True), (block_rows, ROTS))
        best = jnp.max(top.reshape(per, CAND, ROTS), axis=1)
        best_rows = jnp.broadcast_to(best[:, None, :], (per, CAND, ROTS)).reshape(block_rows, ROTS)
        mass = jnp.where(good, jnp.exp(scores - best_rows), 0.0)
        mass = jnp.broadcast_to(jnp.sum(mass, axis=1, keepdims=True), (block_rows, ROTS))
        total = jnp.sum(mass.reshape(per, CAND, ROTS), axis=1)
        stats_out[done + b * per : done + (b + 1) * per, :ROTS] = best
        stats_out[done + b * per : done + (b + 1) * per, ROTS:] = total


def two(v):
    return jnp.where(lanes_of(v.shape) < ROTS, rounded(v), v - rounded(v))


def one_of_two(v):
    return v + pltpu.roll(v, ROTS, 1)


def weights_kernel(calls, blocks, slices, cls_dev, chunks, grp_s, owner_s, *refs):
    stats = refs[:blocks]
    scores = refs[blocks : blocks + calls]
    classes = refs[blocks + calls : blocks + 2 * calls]
    extras = refs[blocks + 2 * calls : 2 * blocks + 2 * calls]
    refs = refs[2 * blocks + 2 * calls :]
    own_out, den_out, mass_out, log_out, ints_out = refs[:5]
    message_outs = refs[5:-4]
    rows_v, den_v, lists_v, picked_v = refs[-4:]
    per = log_out.shape[0]
    block_rows = per * CAND
    depth = SHELLS // slices
    z = grp_s[0] // 2

    half = list_lines(blocks, chunks)[0]
    _, line, lane = list_spot(owner_s[0], 0, chunks)
    slots = list_slots(cls_dev)
    lists = []

    den = jnp.zeros((FREQ, FREQ), F32)
    mass = jnp.zeros((1, FREQ), F32)
    block = 0
    for scores_ref, cls_ref in zip(scores, classes):
        for b in range(scores_ref.shape[0] // block_rows):
            ones = [stats[d][(block ^ d) * per : ((block ^ d) + 1) * per, :] for d in range(blocks)]
            best = functools.reduce(jnp.maximum, [one[:, :ROTS] for one in ones])
            total = sum(one[:, ROTS:] * jnp.exp(one[:, :ROTS] - best) for one in ones)
            if block == 0:
                log_out[...] = jnp.log(total)

            def over_rows(v):
                return jnp.broadcast_to(v[:, None, :], (per, CAND, ROTS)).reshape(block_rows, ROTS)

            at = slice(b * block_rows, (b + 1) * block_rows)
            weights = jnp.exp(scores_ref[at, :] - over_rows(best)) / over_rows(total)
            local = cls_ref[at, :]
            good = jnp.logical_and(local >= 0, local < cls_dev)[:, :ROTS]
            weights = rounded(jnp.where(good, weights, 0.0))
            lists_v[...] = extras[block][extras[block].shape[0] - lists_v.shape[0] :, :].astype(F32)
            named = jnp.broadcast_to(lists_v[pl.ds(line, 1), :], (block_rows, FREQ))
            row = lax.broadcasted_iota(jnp.int32, named.shape, 0).astype(F32)
            picked_v[...] = lax.dot_general(
                (named == row).astype(F32).astype(BF16), weights.astype(BF16),
                (((0,), (0,)), ((), ())), preferred_element_type=F32,
            )
            at = block * slots
            rows_v[at : at + slots, :] = picked_v[pl.ds(pl.multiple_of(lane, 8), slots), :]
            for source in (line, line + half, 2 * half):
                lists.append(lists_v[pl.ds(source, 1), :])
            pair_sum = jnp.sum(weights, axis=1, keepdims=True)
            twice = (lanes_of((block_rows, FREQ)) % ROTS).astype(F32)
            chosen = jnp.where(twice == local, pair_sum, 0.0)
            by_particle = jnp.sum(chosen.reshape(per, CAND, FREQ), axis=1)
            end = extras[block].shape[0] - lists_v.shape[0]
            side = extras[block][end - per : end, :].astype(F32)
            den = den + lax.dot_general(
                side, by_particle, (((0,), (0,)), ((), ())), precision=HIGH,
                preferred_element_type=F32,
            )
            mass = mass + jnp.sum(by_particle, axis=0, keepdims=True)
            block += 1

    lines = rows_v.shape[0] // 2
    packed = jnp.concatenate([rows_v[:lines, :], rows_v[lines:, :]], axis=1).astype(BF16)
    own_out[...] = packed
    den_v[...] = den[:SHELLS].reshape(slices, depth, FREQ)
    mass_rows = jnp.broadcast_to(mass, (8, FREQ))
    mass_out[...] = mass_rows
    den_out[...] = den_v[z]
    if ints_out.shape[0] > len(lists):
        lists.append(jnp.zeros((ints_out.shape[0] - len(lists), FREQ), F32))
    lists = jnp.concatenate(lists, axis=0)
    ints_out[...] = lists.astype(jnp.int32)
    tail = [two(mass_rows), lists]
    tail_rows = depth + sum(one.shape[0] for one in tail)
    spare = message_outs[0].shape[0] - lines - tail_rows
    if spare:
        tail.append(jnp.zeros((spare, FREQ), F32))
    for d, out in enumerate(message_outs, start=1):
        out[:lines, :] = packed
        out[lines:, :] = jnp.concatenate([two(den_v[z ^ d])] + tail, axis=0).astype(BF16)


def put_phases(packed, table, wcs, base):
    lines = packed.shape[0]
    twice = jnp.concatenate([packed, packed], axis=1)
    both = rounded(jnp.dot(twice, table[...], preferred_element_type=F32))
    for place in range(2):
        for part in range(2):
            at = (2 * place + part) * FREQ
            row = base + place * lines
            wcs[part, row : row + lines, :] = both[:, at : at + FREQ]


def add_pair(image, row, k, wcs, num):
    shape = num.shape[1:]
    image = image.astype(F32)
    half = image.shape[0] // 2
    w_re, w_im = image[:half].reshape(shape[1:]), image[half:].reshape(shape[1:])
    c = wcs[0, pl.ds(row, 1), :].reshape(1, 1, FREQ)
    s = wcs[1, pl.ds(row, 1), :].reshape(1, 1, FREQ)
    num[k, 0] += w_re * c - w_im * s
    num[k, 1] += w_re * s + w_im * c


def pick_image(arrays, begin, i, rows, stride, offset):
    def rows_at(one, i):
        return one[pl.ds(pl.multiple_of(i * stride + offset, rows), rows), :]

    held = [one.shape[0] // stride for one in arrays]
    while len(arrays) > 1 and begin >= held[0]:
        arrays, begin, held = arrays[1:], begin - held[0], held[1:]
    if len(arrays) == 1:
        return rows_at(arrays[0], begin + i)
    cut = held[0] - begin
    return jnp.where(
        i < cut,
        rows_at(arrays[0], begin + jnp.minimum(i, cut - 1)),
        rows_at(arrays[1], jnp.maximum(i - cut, 0)),
    )


def own_sum_kernel(chunks, arrays, grp_s, owner_s, packed, ints, *refs):
    messages, refs = take(refs, arrays)
    phases, (num, wcs, ints_s, sem) = refs[:1], refs[1:]
    copy = pltpu.make_async_copy(ints, ints_s, sem)
    copy.start()
    per = sum(one.shape[0] for one in messages[0]) // IMG
    rows = 2 * num.shape[2] * num.shape[3]
    z = grp_s[0] // 2
    put_phases(packed[...], phases[0], wcs, 0)
    num[...] = jnp.zeros_like(num)
    copy.wait()
    for block, held_in in enumerate(messages):
        base = block * list_slots(num.shape[0] - 1)
        for c in range(len(chunks)):
            number, _, lane = list_spot(owner_s[0], c, chunks)

            def pairs(step, _):
                for u in range(UNROLL):
                    row = ints_s[3 * block, lane + step * UNROLL + u]
                    k = ints_s[3 * block + 1, lane + step * UNROLL + u]
                    image = pick_image(held_in, 0, quot(row, CAND), rows, IMG, z * rows)
                    add_pair(image, base + step * UNROLL + u, k, wcs, num)
                return 0

            lax.fori_loop(0, ints_s[3 * block + 2, number], pairs, 0)


def join_kernel(*refs):
    out = refs[-1]
    rows = refs[0].shape[0]
    for n, one in enumerate(refs[:-1]):
        out[n * rows : (n + 1) * rows, :] = one[...]


def read_tail(message, lines, depth, count):
    tail = message[lines:, :].astype(F32)
    den, mass = one_of_two(tail[:depth]), one_of_two(tail[depth : depth + 8])
    return den, mass, tail[depth + 8 : depth + 8 + count].astype(jnp.int32)


def add_planes(planes, owner, chunks, images, wcs, *nums):
    number, _, lane = list_spot(owner, 0, chunks)
    num = nums[0]
    slots = list_slots(num.shape[0] - 1)
    rows = 2 * num.shape[2] * num.shape[3]
    per = FREQ // CAND
    for first in range(0, len(images), 2):
        group = [
            (d, ints, base + block * slots, block)
            for d, ints, base in planes
            for block in range(first, min(first + 2, len(images)))
        ]
        counts = [ints[3 * block + 2, number] for _, ints, _, block in group]

        def pairs(step, _):
            for d, ints, start, block in group:
                for u in range(UNROLL):
                    slot = step * UNROLL + u
                    row = ints[3 * block, lane + slot]
                    k = ints[3 * block + 1, lane + slot]
                    image = pick_image(images[block], d * per, quot(row, CAND), rows, rows, 0)
                    add_pair(image, start + slot, k, wcs, nums[u % len(nums)])
            return 0

        lax.fori_loop(0, functools.reduce(jnp.maximum, counts), pairs, 0)


def near_sum_kernel(chunks, pieces, owner_s, *refs):
    images, refs = take(refs, pieces)
    message, first, phases, den_in, mass_in, num, den_out, mass_out, wcs, ints_v, ints_s, sem = refs
    lines = wcs.shape[1] // 2
    depth = den_in.shape[0]
    den, mass, ints_v[...] = read_tail(message, lines, depth, ints_v.shape[0])
    copy = pltpu.make_async_copy(ints_v, ints_s, sem)
    copy.start()
    den_out[...] = den_in[...] + den
    mass_out[...] = mass_in[...] + mass
    put_phases(message[:lines, :], phases, wcs, 0)
    num[...] = first[...]
    copy.wait()
    add_planes([(0, ints_s, 0)], owner_s[0], chunks, images, wcs, num)


def sum_kernel(chunk, chunks, slices, pieces, grp_s, owner_s, *refs):
    images, refs = take(refs, pieces)
    messages, refs = refs[: slices - 2], refs[slices - 2 :]
    first, refs = refs[0], refs[1:]
    if chunk == 0:
        phases, (den_in, mass_in), refs = refs[0], refs[1:3], refs[3:]
        own_out, sib_out, den_out, mass_out, wcs, ints_s, num, more, den_v, ints_v, sem = refs
    else:
        wcs, ints_s, own_out, sib_out, num, more = refs
    group_rows = wcs.shape[1] // (slices - 2)
    lines = group_rows // 2
    core = grp_s[0] % 2
    start, size = chunks[chunk]
    depth = num.shape[2] * num.shape[3]

    if chunk == 0:
        den, mass = den_in[...], mass_in[...]
        for n, message in enumerate(messages):
            more_den, more_mass, ints_v[n] = read_tail(message, lines, depth, ints_v.shape[1])
            den, mass = den + more_den, mass + more_mass
        copies = [
            pltpu.make_async_copy(ints_v.at[n], ints_s.at[n], sem.at[n])
            for n in range(slices - 2)
        ]
        for copy in copies:
            copy.start()
        for n, message in enumerate(messages):
            put_phases(message[:lines, :], phases, wcs, n * group_rows)
    num[...] = first[...]
    more[...] = jnp.zeros_like(more)
    if chunk == 0:
        for copy in copies:
            copy.wait()
    planes = [(n + 1, ints_s.at[n], n * group_rows) for n in range(slices - 2)]
    add_planes(planes, owner_s[0], chunks, images, wcs, num, more)

    def pack(k, _):
        for out, at in ((own_out, core), (sib_out, 1 - core)):
            halves = [num[k, x, at] + more[k, x, at] for x in range(2)]
            out[k] = jnp.concatenate(halves, axis=0).astype(out.dtype)
        return 0

    lax.fori_loop(0, size, pack, 0, unroll=13)
    if chunk == 0:
        width = num.shape[3]
        den_v[...] = den.reshape(2, width, FREQ)
        den_out[...] = den_v[core]
        mass_out[...] = mass
        sib_out[size] = jnp.concatenate([two(den_v[1 - core]), two(mass)[:width]], axis=0).astype(BF16)


def divide(own, sib, inverse, start, avg_out):
    for k in range(avg_out.shape[0]):
        column = inverse[:, start + k : start + k + 1]
        factor = jnp.broadcast_to(column, inverse.shape)
        total = own[k] + sib[k].astype(F32)
        width = inverse.shape[0]
        parts = [total[:width] * factor, total[width:] * factor]
        avg_out[k] = jnp.concatenate(parts, axis=0).astype(BF16)


def first_divide_kernel(scale, start, own, sib, den, mass, reg, avg_out, share_out, inverse_out):
    cut = avg_out.shape[0]
    width = avg_out.shape[1] // 2
    tile = one_of_two(sib[cut].astype(F32))
    share_out[...] = (tile[width : width + 1] + mass[:1]) * scale
    inverse = 1.0 / (tile[:width] + den[...] + reg[...])
    inverse_out[...] = inverse
    divide(own, sib, inverse, start, avg_out)


def next_divide_kernel(start, own, sib, inverse, avg_out):
    divide(own, sib, inverse[...], start, avg_out)


def spread_kernel(planes, counts, has_out, grp_s, *refs):
    taken, (out, wide, columns, sem) = refs[: 2 * sum(counts)], refs[2 * sum(counts) + has_out :]
    arrays, _ = take(taken, [2 * count for count in counts])
    width = taken[0].shape[1] // 2
    cls_dev = columns.shape[1]
    pad = wide.shape[0] // (len(planes) * 4 * width + 1)
    z, h = grp_s[0] // 2, grp_s[0] % 2
    copies = []
    for n, d in enumerate(planes):
        start = 0
        for c in range(counts[n]):
            pair = arrays[n][2 * c : 2 * c + 2]
            cut = pair[0].shape[0]

            def one(k, _):
                for side, array in enumerate(pair):
                    piece = array[k].astype(F32)
                    for x in range(2):
                        at = (n * 4 + side * 2 + x) * width * pad + start
                        wide[pl.ds(at + k, width, stride=pad), :] = piece[
                            x * width : (x + 1) * width
                        ]
                return 0

            lax.fori_loop(0, cut, one, 0, unroll=2)
            start += cut
        for side, core in enumerate((h, 1 - h)):
            for x in range(2):
                group = n * 4 + side * 2 + x
                for r in range(width):
                    at = (group * width + r) * pad
                    columns[group, :, r * FREQ : (r + 1) * FREQ] = wide[at : at + cls_dev, :]
                first = (x * SHELLS + ((z ^ d) * 2 + core) * width) * FREQ
                first = pl.multiple_of(first, width * FREQ)
                copies.append(
                    pltpu.make_async_copy(
                        columns.at[group], out.at[:, pl.ds(first, width * FREQ)], sem.at[group]
                    )
                )
                copies[-1].start()
    for copy in copies:
        copy.wait()


def whole(space):
    return pl.BlockSpec(memory_space=space)


def in_hbm(value):
    return pltpu.with_memory_space_constraint(value, HBM)


def call(kernel, name, ins, outs, scratch, mib, us, args, **more):
    cost = pl.CostEstimate(flops=0, bytes_accessed=int(us * 3.6e6), transcendentals=0)
    return pl.pallas_call(
        kernel,
        out_shape=tuple(s for s, _ in outs),
        in_specs=[whole(s) for s in ins],
        out_specs=tuple(whole(s) for _, s in outs),
        scratch_shapes=scratch,
        compiler_params=pltpu.CompilerParams(vmem_limit_bytes=mib * 2**20),
        name=name,
        cost_estimate=cost,
        **more,
    )(*args)


def swap(value, axis, distance):
    size = lax.axis_size(axis)
    return lax.ppermute(value, axis, [(i, i ^ distance) for i in range(size)])


def after(value, *others):
    return lax.optimization_barrier((value, *others))[0]


def per_device(
    particles, candidates, group_ids, ctf_ids, ctf_table, noise_prec, references, log_prior, reg
):
    n_cls = lax.axis_size("cls")
    n_grp = lax.axis_size("grp")
    per = particles.shape[0]
    cls_dev = references.shape[0]
    block_rows = per * CAND
    chunks = chunks_of(cls_dev)
    pad = odd_tiles(cls_dev)
    width = SHELLS // n_grp
    nz = n_grp // 2
    scoring, phases = (jnp.asarray(t) for t in tables())
    owner = lax.axis_index("cls").astype(jnp.int32).reshape(1)
    first = owner * cls_dev
    grp = lax.axis_index("grp").astype(jnp.int32).reshape(1)

    depth = SHELLS // nz
    message, *sliced = call(
        functools.partial(weigh_kernel, nz, n_cls, cls_dev, chunks), "weigh", [SMEM] + [HBM] * 6,
        [(SHAPE((per * (IMG + 1) + list_lines(n_cls, chunks)[1], FREQ), BF16), VMEM)]
        + [(SHAPE((per * 2 * depth, FREQ), BF16), VMEM)] * (nz - 1),
        [
            VMEM(particles.shape, BF16),
            VMEM((CAND, per), jnp.int32),
            SMEM((per,), jnp.int32),
            SMEM((per,), jnp.int32),
            VMEM(ctf_table.shape[::-1], F32),
            VMEM(noise_prec.shape, F32),
            VMEM((per, noise_prec.shape[0]), F32),
            VMEM((per, ctf_table.shape[0]), F32),
            VMEM(((IMG + 1) * odd_tiles(per), FREQ), F32),
            pltpu.SemaphoreType.DMA((6,)),
        ],
        5, 2.0,
        (grp,)
        + tuple(
            in_hbm(a)
            for a in (particles, candidates.T, group_ids, ctf_ids, ctf_table.T, noise_prec)
        ),
    )

    if n_cls == 4:
        message_1, message_2 = swap(message, "cls", 1), swap(message, "cls", 2)
    sliced = [swap(one, "grp", 2 * d) for d, one in enumerate(sliced, start=1)]

    rf, power, scoring, phases, own_reg = call(
        functools.partial(prep_kernel, depth), "prep", [SMEM] + [HBM] * 4 + [VMEM],
        [(SHAPE((cls_dev + 1, IMG, FREQ), F32), VMEM), (SHAPE((cls_dev + 1, FREQ), F32), VMEM)]
        + [(SHAPE(t.shape, t.dtype), VMEM) for t in (scoring, phases)]
        + [(SHAPE((width, FREQ), F32), VMEM)],
        [
            VMEM(references.shape, BF16),
            VMEM(((IMG + 1) * pad, FREQ), F32),
            SMEM(reg.shape, F32),
            pltpu.SemaphoreType.DMA((7,)),
        ],
        8, 4.0,
        (grp,)
        + tuple(in_hbm(a) for a in (references, scoring, phases, reg))
        + (log_prior,),
    )

    half, height = list_lines(n_cls, chunks)

    def score(part, earlier=()):
        blocks = len(part)
        flat = [m for arrays in part for m in arrays]
        earlier = tuple(s[1] for s in earlier)
        ahead = sum(s.shape[0] for s in earlier)
        counts = tuple(len(arrays) for arrays in part)
        return call(
            functools.partial(score_kernel, counts, len(earlier), depth, chunks, half), "score",
            [SMEM] * 2 + [VMEM] * (len(flat) + len(earlier) + 3),
            [
                (SHAPE((blocks * block_rows, ROTS), F32), VMEM),
                (SHAPE((ahead + blocks * per, FREQ), F32), VMEM),
                (SHAPE((blocks * block_rows, FREQ), F32), VMEM),
            ],
            [
                VMEM((blocks, height, FREQ), jnp.int32),
                SMEM((blocks, height, FREQ), jnp.int32),
                VMEM((blocks, per, FREQ), F32),
                VMEM((3, block_rows, FREQ), F32),
                VMEM((blocks * per, IMG, FREQ), F32),
                pltpu.SemaphoreType.DMA((blocks,)),
            ],
            6 if n_cls == 4 else 40, 3.0 * blocks, (first, owner, *flat, *earlier, rf, power, scoring),
        )

    def join(got):
        (joined,) = call(
            join_kernel, "join", [VMEM] * (nz - 1),
            [(SHAPE(((nz - 1) * per * 2 * depth, FREQ), BF16), VMEM)], [], 2, 0.5, got,
        )
        return joined

    if n_cls == 4:
        cut = per // 2 * IMG
        scored = [score([(after(message, sliced[0]),)])]
        ready = (scored[0][1], sliced[1])
        message_1, message_2 = after(message_1, *ready), after(message_2, *ready)
        message_3 = (swap(message_1[:cut], "cls", 2), swap(message_2[cut:], "cls", 1))
        messages = [(message,), (message_1,), (message_2,), message_3]
        scored += [score(messages[1:3])]
        joined = join([after(sliced[0], scored[1][1], *message_3)] + sliced[1:])
        joined_1, joined_2 = swap(joined, "cls", 1), swap(joined, "cls", 2)
        scored += [score(messages[3:], scored)]
    else:
        messages = [(message,)] + [(swap(message, "cls", d),) for d in range(1, n_cls)]
        scored = [score(messages)]
        joined = join(sliced)
        images = [joined] + [swap(joined, "cls", d) for d in range(1, n_cls)]
        pieces = (1,) * n_cls
    arrays = tuple(len(m) for m in messages)
    stats = scored[-1][1]
    all_stats = [stats] + [swap(stats, "cls", d) for d in range(1, n_cls)]
    flat = [m for held in messages for m in held]

    lines = n_cls * list_slots(cls_dev) // 2
    own_lists = SHAPE((-(-3 * n_cls // 8) * 8, FREQ), jnp.int32)
    outgoing_rows = -(-(lines + depth + 8 + own_lists.shape[0]) // 16) * 16
    packed, den, mass, log_mass, ints, *outgoing = call(
        functools.partial(weights_kernel, len(scored), n_cls, nz, cls_dev, chunks), "weights",
        [SMEM] * 2 + [VMEM] * (2 * n_cls + 2 * len(scored)),
        [
            (SHAPE((lines, FREQ), BF16), VMEM),
            (SHAPE((depth, FREQ), F32), VMEM),
            (SHAPE((8, FREQ), F32), VMEM),
            (SHAPE((per, ROTS), F32), VMEM),
            (own_lists, VMEM),
        ]
        + [(SHAPE((outgoing_rows, FREQ), BF16), VMEM)] * (nz - 1),
        [
            VMEM((2 * lines, ROTS), F32),
            VMEM((nz, depth, FREQ), F32),
            VMEM((height, FREQ), F32),
            VMEM((block_rows, ROTS), F32),
        ],
        4 if n_cls == 4 else 12, 2.0,
        (
            grp, owner, *all_stats, *(s[0] for s in scored), *(s[2] for s in scored),
            *(held[-1] for held in messages),
        ),
    )
    incoming = [swap(one, "grp", 2 * d) for d, one in enumerate(outgoing, start=1)]
    if n_cls == 4:
        cut = joined.shape[0] // 2
        joined_1, joined_2 = after(joined_1, packed), after(joined_2, packed)
        joined_3 = [swap(joined_1[:cut], "cls", 2), swap(joined_2[cut:], "cls", 1)]
        images = [joined, joined_1, joined_2, *joined_3]
        pieces = (1, 1, 1, 2)
    (first_sums,) = call(
        functools.partial(own_sum_kernel, chunks, arrays), "own_sum",
        [SMEM] * 2 + [VMEM] * (len(flat) + 3),
        [(SHAPE((cls_dev + 1, 2, 2, width, FREQ), F32), VMEM)],
        [
            VMEM((2, 2 * lines, FREQ), F32),
            SMEM(own_lists.shape, jnp.int32),
            pltpu.SemaphoreType.DMA,
        ],
        4 if n_cls == 4 else 12, 3.0, (grp, owner, packed, ints, *flat, phases),
    )
    (near_sums, den, mass) = call(
        functools.partial(near_sum_kernel, chunks, pieces), "near_sum",
        [SMEM] + [VMEM] * (sum(pieces) + 5),
        [
            (SHAPE((cls_dev + 1, 2, 2, width, FREQ), F32), VMEM),
            (SHAPE((depth, FREQ), F32), VMEM),
            (SHAPE((8, FREQ), F32), VMEM),
        ],
        [
            VMEM((2, 2 * lines, FREQ), F32),
            VMEM(own_lists.shape, jnp.int32),
            SMEM(own_lists.shape, jnp.int32),
            pltpu.SemaphoreType.DMA,
        ],
        4 if n_cls == 4 else 12, 2.0,
        (owner, *images, incoming[0], first_sums, phases, den, mass),
    )
    tile = (2 * width, FREQ)
    sums = []
    for chunk, (start, size) in enumerate(chunks):
        more = chunk == 0
        outs = [
            (SHAPE((size,) + tile, F32), VMEM),
            (SHAPE((size + more,) + tile, BF16), VMEM),
        ]
        scratch = [VMEM((size + 1, 2, 2, width, FREQ), F32)] * 2
        spaces = [SMEM] * 2 + [VMEM] * (sum(pieces) + nz - 1)
        if more:
            outs += [
                (SHAPE((width, FREQ), F32), VMEM),
                (SHAPE((8, FREQ), F32), VMEM),
                (SHAPE((2, (nz - 2) * (2 * lines), FREQ), F32), VMEM),
                (SHAPE((nz - 2,) + own_lists.shape, jnp.int32), SMEM),
            ]
            scratch += [
                VMEM((2, width, FREQ), F32),
                VMEM((nz - 2,) + own_lists.shape, jnp.int32),
                pltpu.SemaphoreType.DMA((nz - 2,)),
            ]
            spaces += [VMEM] * 3
            args = (grp, owner, *images, *incoming[1:], near_sums, phases, den, mass)
        else:
            spaces += [VMEM, SMEM]
            args = (grp, owner, *images, *incoming[1:], near_sums, wcs, lists)
        own, sib, *others = call(
            functools.partial(sum_kernel, chunk, chunks, nz, pieces), "sum",
            spaces, outs, scratch, 5 if n_cls == 4 else 24, 3.0, args,
        )
        if more:
            den, mass, wcs, lists = others
        sums.append((own, sib))

    particle_total = per * n_grp * n_cls
    divided, inverse, share = [], None, None
    for chunk, (own, sib) in enumerate(sums):
        start, cut = chunks[chunk]
        other = swap(sib, "grp", 1)
        averaged_out = (SHAPE((cut,) + tile, BF16), VMEM)
        if chunk == 0:
            averaged, share, inverse = call(
                functools.partial(first_divide_kernel, K / particle_total, start), "divide",
                [VMEM] * 5,
                [averaged_out, (SHAPE((1, FREQ), F32), VMEM), (SHAPE((width, FREQ), F32), VMEM)],
                [], 2, 0.05, (own, other, den, mass, own_reg),
            )
        else:
            (averaged,) = call(
                functools.partial(next_divide_kernel, start), "divide", [VMEM] * 3,
                [averaged_out], [], 2, 0.05, (own, other, inverse),
            )
        divided.append(averaged)

    (averaged,) = divided
    if nz == 4:
        near, across = lax.optimization_barrier(
            (swap(averaged, "grp", 2), swap(averaged, "grp", 4))
        )
        cut = cls_dev - cls_dev // 13 * 4
        relayed = [swap(part, "grp", 2) for part in (across[:cut], across[cut:])]
        planes = [[averaged], [near], [across], relayed]
    else:
        planes = [[averaged]] + [[swap(averaged, "grp", 2 * d)] for d in range(1, nz)]
    averages = None
    for far in ((0, 1, 2), (3,)) if nz == 4 else (tuple(range(nz)),):
        arrays = []
        for d in far:
            for one in planes[d]:
                one = one if averages is None else after(one, averages)
                arrays += [one, swap(one, "grp", 1)]
        counts = tuple(len(planes[d]) for d in far)
        has_out = averages is not None
        groups = len(far) * 4
        (averages,) = call(
            functools.partial(spread_kernel, far, counts, has_out), "spread",
            [SMEM] + [VMEM] * len(arrays) + [HBM] * has_out,
            [(SHAPE((cls_dev, FEAT), F32), HBM)],
            [
                VMEM(((groups * width + 1) * odd_tiles(cls_dev), FREQ), F32),
                VMEM((groups, cls_dev, width * FREQ), F32),
                pltpu.SemaphoreType.DMA((groups,)),
            ],
            8, 0.05, (grp, *arrays) + ((averages,) if has_out else ()),
            input_output_aliases={len(arrays) + 1: 0} if has_out else {},
        )
    return (averages, share[0, :cls_dev], log_mass[:, 0])


def solution(mesh):
    return jax.shard_map(
        per_device,
        mesh=mesh,
        in_specs=(
            P(("grp", "cls"), None),
            P(("grp", "cls"), None),
            P(("grp", "cls")),
            P(("grp", "cls")),
            P(),
            P(),
            P("cls", None),
            P("cls"),
            P(),
        ),
        out_specs=(P("cls", None), P("cls"), P(("grp", "cls"))),
        check_vma=False,
    )
```
